32 devices in a mesh: parts: 2 (over y), mesh: 4 (over z), sub: 2 (over x), lat: 2 (over core).
Axes of the slice: x: 2, y: 2, z: 4, core: 2. Of those that a mesh axis runs over, the one named last changes fastest.
Arguments:
- node_state: bfloat16 [2048, 512], P(('parts', 'mesh', 'sub')), parts along dimension 0, may hold values from -6 to 6
- send_rows: int32 [16, 4, 32], P(('parts', 'mesh', 'sub')), parts along dimension 0, may hold values from 0 to 127
- edge_src: int32 [8192], P(('parts', 'mesh', 'sub')), parts along dimension 0, may hold values from 0 to 255, as said below
- edge_dst: int32 [8192], P(('parts', 'mesh', 'sub')), parts along dimension 0, may hold values from 0 to 127, as said below
- block_count: int32 [64], P(('parts', 'mesh', 'sub')), parts along dimension 0, may hold values from 1 to 128
- w_src: bfloat16 [512, 512], P(None, 'lat'), may hold values from -0.25 to 0.25
- w_dst: bfloat16 [512, 512], P(None, 'lat'), may hold values from -0.25 to 0.25
- hidden_bias: float32 [512], P('lat'), may hold values from -3 to 3
- w_out: bfloat16 [512, 512], P('lat'), may hold values from -0.25 to 0.25
- norm_gain: float32 [512], replicated, may hold values from 0.5 to 1.5
- cotangent: bfloat16 [2048, 512], P(('parts', 'mesh', 'sub')), parts along dimension 0, may hold values from -6 to 6
Outputs:
- updated: bfloat16 [2048, 512], P(('parts', 'mesh', 'sub')), parts along dimension 0
- node_grad: float32 [2048, 512], P(('parts', 'mesh', 'sub')), parts along dimension 0
- src_grad: float32 [1024, 512], P('parts', 'lat'), parts along dimension 0
- dst_grad: float32 [1024, 512], P('parts', 'lat'), parts along dimension 0
- out_grad: float32 [1024, 512], P(('parts', 'lat')), parts along dimension 0
- bias_grad: float32 [1024], P(('parts', 'lat')), parts along dimension 0
- gain_grad: float32 [1024], P('parts'), parts along dimension 0
The draws below stay inside these ranges and needn't reach their ends.
There are 2 independent parts, one for each index of `parts`. The reference program is written for one: setup_inputs(seed, part) draws one part's arguments, and reference() takes and returns one part's arrays. A program takes and returns all parts, laid end to end along the dimension named above; an argument that names none is the same for every part. Nothing has to cross between parts.
Inputs may be any that keep to these rules, and one draw needn't show every extreme that they name: `send_rows`: local row of the sending device. `edge_src`: below 128: a node of the edge's own device; 128 + d * 32 + c: the row that the neighbour of direction d sends in slot c. `edge_dst`: slot j of a device's 512 edge slots points to a node of rows (j // 256) * 64 to (j // 256 + 1) * 64 - 1 of that device.
All inputs are finite; a program needn't handle non-finite values.
Results may differ from the reference program's by a relative error of at most 0.008.
Values may be sent and summed in bfloat16 or wider, within the bound.
No kernel may reach another device: no remote copies, remote signals or barrier semaphores. Data moves between devices by JAX's collectives and lax.ppermute only.
A program may use at most 64 MiB of HBM per device.

```python
import jax
import jax.numpy as jnp
from jax import lax

D = 512
HID = 512
NODE_DEV = 128
HALO = 32
BLOCK = 128
EDGE_DEV = 512
PEERS = 8
NODES = 1024
EDGES = 4096
BLOCKS = 32
NODE_LAT = 64
EDGE_LAT = 256
N_MESH = 4
N_SUB = 2


def draw_edge_src(key, part):
    key = jax.random.fold_in(key, 11)
    pick_key, halo_key, local_key = jax.random.split(key, 3)
    local_slot = jnp.arange(EDGES, dtype=jnp.int32) % EDGE_DEV
    pick = jax.random.randint(pick_key, (EDGES,), 0, 6)
    halo_index = jax.random.randint(halo_key, (EDGES,), 0, 4 * HALO)
    local_index = jax.random.randint(local_key, (EDGES,), 0, NODE_DEV)
    chosen = jnp.where(pick == 0, NODE_DEV + halo_index, local_index)
    chosen = jnp.where(local_slot == EDGE_DEV - 1, NODE_DEV + 4 * HALO - 1, chosen)
    chosen = jnp.where(local_slot == EDGE_DEV - 2, 0, chosen)
    return chosen.astype(jnp.int32)


def draw_edge_dst(key, part):
    key = jax.random.fold_in(key, 23)
    local_slot = jnp.arange(EDGES, dtype=jnp.int32) % EDGE_DEV
    share = local_slot // EDGE_LAT
    offset = jax.random.randint(key, (EDGES,), 0, NODE_LAT)
    return (share * NODE_LAT + offset).astype(jnp.int32)


def plant(entries, key, smallest, high):
    spot = [jax.random.randint(jax.random.fold_in(key, axis), (), 0, length) for axis, length in enumerate(entries.shape)]
    main_axis = entries.shape.index(max(entries.shape))
    neighbour = spot[:main_axis] + [(spot[main_axis] + 1) % entries.shape[main_axis]] + spot[main_axis + 1:]
    return entries.at[tuple(spot)].set(smallest).at[tuple(neighbour)].set(high)


def steps_of(own_key, extent, cuts, low, largest):
    factor_of = 1.0
    for position, shards_of in cuts:
        draws = jax.random.uniform(jax.random.fold_in(jax.random.fold_in(own_key, 6), position), (shards_of,), jnp.float32, low / len(cuts), largest / len(cuts))
        factor_of = factor_of * jnp.repeat(jnp.exp(draws), extent[position] // shards_of).reshape((-1,) + (1,) * (len(extent) - 1 - position))
    return factor_of


def scatter_about(stream_key, dims, spread, bound, cuts=(), kind=jnp.bfloat16):
    values = jax.random.normal(stream_key, dims, jnp.float32) * spread
    if len(cuts) > 0:
        values = steps_of(stream_key, dims, cuts, -0.22, 0.18) * values
    return jnp.clip(values, min=-bound, max=bound).astype(kind)


def setup_inputs(seed: int = 0, part: int = 0) -> dict:
    splits = jax.random.split(jax.random.key(seed), 12)
    own_keys = jax.random.split(jax.random.fold_in(splits[11], part), 12)
    return {
        "node_state": scatter_about(own_keys[0], (NODES, D), 1.0, 6.0, ((0, 8),)),
        "send_rows": plant(jax.random.randint(own_keys[1], (PEERS, 4, HALO), 0, NODE_DEV), jax.random.fold_in(own_keys[1], 1), 0, NODE_DEV - 1).astype(jnp.int32),
        "edge_src": draw_edge_src(jax.random.fold_in(jax.random.fold_in(splits[11], part), 71), part),
        "edge_dst": draw_edge_dst(jax.random.fold_in(jax.random.fold_in(splits[11], part), 71), part),
        "block_count": plant(jax.random.randint(own_keys[4], (BLOCKS,), 1, BLOCK + 1), jax.random.fold_in(own_keys[4], 1), 1, BLOCK).astype(jnp.int32),
        "w_src": scatter_about(splits[5], (D, HID), D ** -0.5, 0.25, ((1, 2),)),
        "w_dst": scatter_about(splits[6], (D, HID), D ** -0.5, 0.25, ((1, 2),)),
        "hidden_bias": scatter_about(splits[7], (HID,), 0.5, 3.0, ((0, 2),), jnp.float32),
        "w_out": scatter_about(splits[8], (HID, D), HID ** -0.5, 0.25, ((0, 2),)),
        "norm_gain": jnp.clip(jax.random.uniform(splits[9], (D,), jnp.float32, 0.5, 1.5), 0.5, 1.5),
        "cotangent": scatter_about(own_keys[10], (NODES, D), 1.0, 6.0, ((0, 8),)),
    }


epsilon = 1e-05

def layer_norm(aggregate):
    center = aggregate - lax.optimization_barrier(jnp.mean(aggregate, axis=1, keepdims=True))
    variance = lax.optimization_barrier(jnp.mean(center * center, axis=1, keepdims=True))
    inverse = lax.rsqrt(variance + epsilon)
    return (center * inverse, inverse)

def reference(node_state, send_rows, edge_src, edge_dst, block_count, w_src, w_dst, hidden_bias, w_out, norm_gain, cotangent):
    total_edges = edge_src.shape[0]
    total_nodes = node_state.shape[0]
    positions = jnp.arange(total_edges, dtype=jnp.int32)
    owner = positions // EDGE_DEV
    mesh_pos = owner // N_SUB
    sub_pos = owner % N_SUB
    is_local = edge_src < NODE_DEV
    slot_index = jnp.maximum(edge_src - NODE_DEV, 0)
    direction = slot_index // HALO
    within = slot_index % HALO
    down_mesh = (mesh_pos - 1) % N_MESH * N_SUB + sub_pos
    up_mesh = (mesh_pos + 1) % N_MESH * N_SUB + sub_pos
    down_sub = mesh_pos * N_SUB + (sub_pos - 1) % N_SUB
    up_sub = mesh_pos * N_SUB + (sub_pos + 1) % N_SUB
    sender = jnp.where(direction == 0, down_mesh, jnp.where(direction == 1, up_mesh, jnp.where(direction == 2, down_sub, up_sub))).astype(jnp.int32)
    sent_row = send_rows[sender, direction, within]
    src_row = jnp.where(is_local, owner * NODE_DEV + edge_src, sender * NODE_DEV + sent_row).astype(jnp.int32)
    dst_row = (owner * NODE_DEV + edge_dst).astype(jnp.int32)
    usable = (positions % BLOCK < jnp.repeat(block_count, BLOCK)).astype(jnp.float32)
    source_rows = node_state[src_row]
    target_rows = node_state[dst_row]
    pre_act = jnp.dot(source_rows, w_src, preferred_element_type=jnp.float32) + jnp.dot(target_rows, w_dst, preferred_element_type=jnp.float32) + hidden_bias
    activated = jax.nn.silu(pre_act).astype(jnp.bfloat16)
    messages = jnp.dot(activated, w_out, preferred_element_type=jnp.float32) * usable[:, None]
    aggregate = jax.ops.segment_sum(messages, dst_row, num_segments=total_nodes)
    normed, inverse = layer_norm(aggregate)
    updated = (node_state.astype(jnp.float32) + norm_gain * normed).astype(jnp.bfloat16)
    upstream = cotangent.astype(jnp.float32)
    gain_grad = lax.optimization_barrier(jnp.sum(upstream * normed, axis=0))
    scaled = upstream * norm_gain
    agg_grad = inverse * (scaled - lax.optimization_barrier(jnp.mean(scaled, axis=1, keepdims=True)) - normed * lax.optimization_barrier(jnp.mean(scaled * normed, axis=1, keepdims=True)))
    message_grad = (usable[:, None] * agg_grad[dst_row]).astype(jnp.bfloat16)
    contract = (((0,), (0,)), ((), ()))
    out_grad = lax.dot_general(activated, message_grad, contract, preferred_element_type=jnp.float32)
    act_grad = lax.dot_general(message_grad, w_out, (((1,), (1,)), ((), ())), preferred_element_type=jnp.float32)
    sigmoid_pre = jax.nn.sigmoid(pre_act)
    pre_grad = (act_grad * sigmoid_pre * (1.0 + pre_act * (1.0 - sigmoid_pre))).astype(jnp.bfloat16)
    src_grad = lax.dot_general(source_rows, pre_grad, contract, preferred_element_type=jnp.float32)
    dst_grad = lax.dot_general(target_rows, pre_grad, contract, preferred_element_type=jnp.float32)
    bias_grad = lax.optimization_barrier(jnp.sum(pre_grad.astype(jnp.float32), axis=0))
    back_src = lax.dot_general(pre_grad, w_src, (((1,), (1,)), ((), ())), preferred_element_type=jnp.float32)
    back_dst = lax.dot_general(pre_grad, w_dst, (((1,), (1,)), ((), ())), preferred_element_type=jnp.float32)
    node_grad = upstream + jax.ops.segment_sum(back_src, src_row, num_segments=total_nodes) + jax.ops.segment_sum(back_dst, dst_row, num_segments=total_nodes)
    return (updated, node_grad, src_grad, dst_grad, out_grad, bias_grad, gain_grad)
```

```python
import functools

import jax
import jax.numpy as jnp
from jax import lax
from jax.experimental import pallas as pl
from jax.experimental.pallas import tpu as pltpu
from jax.sharding import PartitionSpec as P

BLOCK = 128
EPSILON = 1e-05
TAIL = 16
VMEM_LIMIT = 24 * 1024 * 1024

f32 = jnp.float32
bf16 = jnp.bfloat16

NN = (((1,), (0,)), ((), ()))
NT = (((1,), (1,)), ((), ()))
TN = (((0,), (0,)), ((), ()))


def dot(a, b, dims=NN):
    return lax.dot_general(a, b, dims, preferred_element_type=f32)


def iota(shape, dim):
    return lax.broadcasted_iota(jnp.int32, shape, dim)


def one_hot(condition):
    return jnp.where(condition, 1.0, 0.0).astype(bf16)


def split(x):
    high = x.astype(bf16)
    return high, (x - high.astype(f32)).astype(bf16)


def columns_of(row, lanes):
    return jnp.transpose(jnp.broadcast_to(row, (lanes, row.shape[1])))


def usable_row(count_ref, edges):
    lane = iota((1, BLOCK), 1)
    parts = [lane < count_ref[b] for b in range(edges // BLOCK)]
    return jnp.concatenate([jnp.where(p, 1, 0) for p in parts], axis=1)


def usable_columns(count_ref, edges, lanes):
    sub = iota((BLOCK, lanes), 0)
    return jnp.concatenate(
        [jnp.where(sub < count_ref[b], 1, 0) for b in range(edges // BLOCK)], axis=0
    )


def table_columns(row, rows):
    columns = columns_of(row, 128)
    lane = iota(columns.shape, 1)
    return [one_hot(columns == lane + 128 * b) for b in range(rows // 128)]


def send_kernel(node_ref, send_ref, *out_refs):
    node = node_ref[...]
    rows = node.shape[0]
    halo = send_ref.shape[1]
    pieces = []
    for d in range(4):
        pick = one_hot(iota((rows, halo), 0) == send_ref[d : d + 1, :])
        pieces.append(dot(pick, node, TN).astype(bf16))
    out_refs[0][...] = pieces[0]
    out_refs[1][...] = pieces[1]
    if len(out_refs) == 3:
        out_refs[2][0:halo, :] = pieces[2]
        out_refs[2][halo:, :] = pieces[3]
    else:
        out_refs[2][...] = pieces[2]
        out_refs[3][...] = pieces[3]


def forward_kernel(
    count_ref, node_ref, src_ref, dst_ref, w_src_ref, w_dst_ref, bias_ref, w_out_ref, *rest
):
    *halo_refs, factor_ref, hidden_ref, partial_ref = rest
    node = node_ref[...]
    rows = node.shape[0]
    edges = src_ref.shape[1]
    table = jnp.concatenate([node] + [r[...] for r in halo_refs], axis=0)
    picks = table_columns(src_ref[...], table.shape[0])
    source = dot(jnp.concatenate(picks, axis=1), table).astype(bf16)
    (target_pick,) = table_columns(dst_ref[...], rows)
    target = dot(target_pick, node).astype(bf16)
    pre = dot(source, w_src_ref[...]) + dot(target, w_dst_ref[...]) + bias_ref[...]
    sig = 0.5 + 0.5 * jnp.tanh(0.5 * pre)
    factor_ref[...] = sig * (1.0 + pre * (1.0 - sig))
    activated = (pre * sig).astype(bf16)
    used = usable_row(count_ref, edges)
    collect = one_hot((iota((rows, edges), 0) == dst_ref[...]) & (used > 0))
    hidden = dot(collect, activated)
    high, low = split(hidden)
    hidden_ref[...] = high
    partial_ref[...] = (dot(high, w_out_ref[...]) + dot(low, w_out_ref[...])).astype(bf16)


def backward_kernel(
    geometry,
    count_ref,
    node_ref,
    src_ref,
    dst_ref,
    w_out_ref,
    gain_ref,
    cot_ref,
    factor_ref,
    hidden_ref,
    own_ref,
    other_ref,
    *rest,
):
    peers, chunk, merged = geometry
    n_halo = 3 if merged else 4
    halo_refs = rest[:n_halo]
    updated_ref, message_ref, local_ref, target_ref = rest[n_halo : n_halo + 4]
    back_refs = rest[n_halo + 4 :]
    node = node_ref[...]
    rows, width = node.shape
    edges = src_ref.shape[1]
    aggregate = own_ref[...].astype(f32) + other_ref[...].astype(f32)
    center = aggregate - jnp.mean(aggregate, axis=1, keepdims=True)
    variance = jnp.mean(center * center, axis=1, keepdims=True)
    inverse = lax.rsqrt(variance + EPSILON)
    normed = center * inverse
    gain = gain_ref[...]
    updated_ref[...] = (node.astype(f32) + gain * normed).astype(bf16)
    upstream = cot_ref[...].astype(f32)
    gain_part = jnp.sum(upstream * normed, axis=0, keepdims=True)
    scaled = upstream * gain
    agg_grad = inverse * (
        scaled
        - jnp.mean(scaled, axis=1, keepdims=True)
        - normed * jnp.mean(scaled * normed, axis=1, keepdims=True)
    )
    agg_grad = agg_grad.astype(bf16)

    columns = columns_of(dst_ref[...], 128)
    used = usable_columns(count_ref, edges, 128)
    spread = one_hot((columns == iota(columns.shape, 1)) & (used > 0))
    message_grad = dot(spread, agg_grad).astype(bf16)
    act_grad = dot(message_grad, w_out_ref[...], NT)
    pre_grad = (act_grad * factor_ref[...]).astype(bf16)

    table = jnp.concatenate([node] + [r[...] for r in halo_refs], axis=0)
    size = table.shape[0]
    by_source = dot(one_hot(iota((size, edges), 0) == src_ref[...]), pre_grad)
    by_target = dot(one_hot(iota((rows, edges), 0) == dst_ref[...]), pre_grad)
    local_ref[...] = by_source[:rows]
    by_target_low = by_target.astype(bf16)
    target_ref[...] = by_target_low
    at = rows
    for ref in back_refs:
        ref[...] = by_source[at : at + ref.shape[0]].astype(bf16)
        at += ref.shape[0]

    hid = by_source.shape[1]
    bias_part = jnp.sum(by_target, axis=0, keepdims=True)
    src_part = dot(table, by_source.astype(bf16), TN).astype(bf16)
    dst_part = dot(node, by_target_low, TN).astype(bf16)
    out_part = dot(hidden_ref[...], agg_grad, TN).astype(bf16)
    blocks = [src_part, dst_part]
    for at in range(0, width, hid):
        blocks.append(out_part[:, at : at + hid])
    vectors = [bias_part] + [gain_part[:, at : at + hid] for at in range(0, width, hid)]
    tail = []
    for v in vectors:
        high = v.astype(bf16)
        tail += [high.astype(f32), (v - high.astype(f32))]
    tail.append(jnp.zeros((TAIL - len(tail), hid), f32))
    tail = jnp.concatenate(tail, axis=0).astype(bf16)
    done = 0
    for block in blocks:
        at = 0
        while at < block.shape[0]:
            peer, offset = divmod(done, chunk)
            take = min(chunk - offset, block.shape[0] - at)
            message_ref[peer, offset : offset + take, :] = block[at : at + take]
            at += take
            done += take
    while done < peers * chunk:
        peer, offset = divmod(done, chunk)
        take = chunk - offset
        message_ref[peer, offset : offset + take, :] = jnp.zeros((take, hid), bf16)
        done += take
    for peer in range(peers):
        message_ref[peer, chunk:, :] = tail


def sum_kernel(chunk, arrived_ref, out_ref, bias_ref, gain_ref):
    peers = arrived_ref.shape[0]
    total = arrived_ref[0].astype(f32)
    for peer in range(1, peers):
        total += arrived_ref[peer].astype(f32)
    low = total[:chunk].astype(bf16)
    for peer in range(peers):
        out_ref[peer] = low
    tail = total[chunk:]
    bias_ref[...] = tail[0:1] + tail[1:2]
    hid = tail.shape[1]
    for k in range(gain_ref.shape[1] // hid):
        gain_ref[:, k * hid : (k + 1) * hid] = tail[2 + 2 * k : 3 + 2 * k] + tail[3 + 2 * k : 4 + 2 * k]


def unpack_kernel(arrived_ref, src_ref, dst_ref, out_ref):
    hid = src_ref.shape[1]
    rows = src_ref.shape[0]
    src_ref[...] = arrived_ref[0:rows, :].astype(f32)
    dst_ref[...] = arrived_ref[rows : 2 * rows, :].astype(f32)
    at = 2 * rows
    for k in range(out_ref.shape[1] // hid):
        out_ref[:, k * hid : (k + 1) * hid] = arrived_ref[at : at + out_ref.shape[0], :].astype(f32)
        at += out_ref.shape[0]


def node_kernel(send_ref, local_ref, target_ref, w_src_ref, w_dst_ref, *rest):
    *back_refs, out_ref = rest
    rows = local_ref.shape[0]
    halo = send_ref.shape[1]
    returned = jnp.concatenate([r[...] for r in back_refs], axis=0)
    total = local_ref[...]
    for d in range(4):
        pick = one_hot(iota((rows, halo), 0) == send_ref[d : d + 1, :])
        total += dot(pick, returned[d * halo : (d + 1) * halo])
    out_ref[...] = (
        dot(total.astype(bf16), w_src_ref[...], NT) + dot(target_ref[...], w_dst_ref[...], NT)
    ).astype(bf16)


def finish_kernel(cot_ref, own_ref, other_ref, out_ref):
    out_ref[...] = cot_ref[...].astype(f32) + (
        own_ref[...].astype(f32) + other_ref[...].astype(f32)
    )


VMEM = pl.BlockSpec(memory_space=pltpu.VMEM)
SMEM = pl.BlockSpec(memory_space=pltpu.SMEM)


def shape(dims, dtype):
    return jax.ShapeDtypeStruct(dims, dtype)


def call(kernel, outs, *args, smem=0, flops=10**8):
    return pl.pallas_call(
        kernel,
        out_shape=outs,
        in_specs=[SMEM] * smem + [VMEM] * (len(args) - smem),
        out_specs=jax.tree.map(lambda _: VMEM, outs),
        compiler_params=pltpu.CompilerParams(vmem_limit_bytes=VMEM_LIMIT),
        cost_estimate=pl.CostEstimate(flops=flops, bytes_accessed=10**6, transcendentals=0),
    )(*args)


def shifted(x, axis, by):
    count = lax.axis_size(axis)
    return lax.ppermute(x, axis, [(i, (i + by) % count) for i in range(count)])


def shards(
    node_state,
    send_rows,
    edge_src,
    edge_dst,
    block_count,
    w_src,
    w_dst,
    hidden_bias,
    w_out,
    norm_gain,
    cotangent,
):
    rows, width = node_state.shape
    hid = w_src.shape[1]
    halo = send_rows.shape[2]
    edges = edge_src.shape[0]
    peers = lax.axis_size("mesh") * lax.axis_size("sub")
    merged = lax.axis_size("sub") == 2
    total_rows = 2 * width + (width // hid) * hid
    chunk = -(-total_rows // (peers * 16)) * 16

    send = send_rows[0]
    src = edge_src.reshape(1, edges)
    dst = edge_dst.reshape(1, edges)
    bias = hidden_bias.reshape(1, hid)
    gain = norm_gain.reshape(1, width)

    piece = [halo, halo, 2 * halo] if merged else [halo] * 4
    routes = [("mesh", 1), ("mesh", -1), ("sub", 1)] + ([] if merged else [("sub", -1)])

    outgoing = call(send_kernel, [shape((n, width), bf16) for n in piece], node_state, send)
    arrived = [shifted(x, axis, by) for x, (axis, by) in zip(outgoing, routes)]

    factor, hidden, partial = call(
        forward_kernel,
        [shape((edges, hid), f32), shape((rows, hid), bf16), shape((rows, width), bf16)],
        block_count, node_state, src, dst, w_src, w_dst, bias, w_out, *arrived,
        smem=1,
    )
    other = shifted(partial, "lat", 1)

    updated, message, local, target, *backs = call(
        functools.partial(backward_kernel, (peers, chunk, merged)),
        [
            shape((rows, width), bf16),
            shape((peers, chunk + TAIL, hid), bf16),
            shape((rows, hid), f32),
            shape((rows, hid), bf16),
        ]
        + [shape((n, hid), bf16) for n in piece],
        block_count, node_state, src, dst, w_out, gain, cotangent, factor, hidden, partial, other,
        *arrived,
        smem=1,
    )
    returned = [shifted(x, axis, -by) for x, (axis, by) in zip(backs, routes)]

    exchanged = lax.all_to_all(message, ("mesh", "sub"), 0, 0)

    node_part = call(
        node_kernel, shape((rows, width), bf16), send, local, target, w_src, w_dst, *returned
    )
    node_grad = call(
        finish_kernel, shape((rows, width), f32),
        cotangent, node_part, shifted(node_part, "lat", 1),
    )

    reduced, bias_grad, gain_grad = call(
        functools.partial(sum_kernel, chunk),
        [shape((peers, chunk, hid), bf16), shape((1, hid), f32), shape((1, width), f32)],
        exchanged,
    )
    gathered = lax.all_to_all(reduced, ("mesh", "sub"), 0, 0)
    src_grad, dst_grad, out_grad = call(
        unpack_kernel,
        [shape((width, hid), f32), shape((width, hid), f32), shape((hid, width), f32)],
        gathered.reshape(peers * chunk, hid),
    )
    return (
        updated, node_grad, src_grad, dst_grad, out_grad,
        bias_grad.reshape(hid), gain_grad.reshape(width),
    )


def solution(mesh):
    nodes = P(("parts", "mesh", "sub"), None)
    slots = P(("parts", "mesh", "sub"))
    in_specs = (
        nodes,
        P(("parts", "mesh", "sub"), None, None),
        slots,
        slots,
        slots,
        P(None, "lat"),
        P(None, "lat"),
        P("lat"),
        P("lat", None),
        P(),
        nodes,
    )
    out_specs = (
        nodes,
        nodes,
        P("parts", "lat"),
        P("parts", "lat"),
        P(("parts", "lat"), None),
        P(("parts", "lat")),
        P("parts"),
    )
    return jax.shard_map(shards, mesh=mesh, in_specs=in_specs, out_specs=out_specs, check_vma=False)
```

```python
import functools

import jax
import jax.numpy as jnp
from jax import lax
from jax.experimental import pallas as pl
from jax.experimental.pallas import tpu as pltpu
from jax.sharding import PartitionSpec as P

BLOCK = 128
EPSILON = 1e-05
TAIL = 16
VMEM_LIMIT = 24 * 1024 * 1024

f32 = jnp.float32
bf16 = jnp.bfloat16

NN = (((1,), (0,)), ((), ()))
NT = (((1,), (1,)), ((), ()))
TN = (((0,), (0,)), ((), ()))


def dot(a, b, dims=NN):
    return lax.dot_general(a, b, dims, preferred_element_type=f32)


def iota(shape, dim):
    return lax.broadcasted_iota(jnp.int32, shape, dim)


def one_hot(condition):
    return jnp.where(condition, 1.0, 0.0).astype(bf16)


def split(x):
    high = x.astype(bf16)
    return high, (x - high.astype(f32)).astype(bf16)


def columns_of(row, lanes):
    return jnp.transpose(jnp.broadcast_to(row, (lanes, row.shape[1])))


def usable_row(count_ref, edges):
    lane = iota((1, BLOCK), 1)
    parts = [lane < count_ref[b] for b in range(edges // BLOCK)]
    return jnp.concatenate([jnp.where(p, 1, 0) for p in parts], axis=1)


def usable_columns(count_ref, edges, lanes):
    sub = iota((BLOCK, lanes), 0)
    return jnp.concatenate(
        [jnp.where(sub < count_ref[b], 1, 0) for b in range(edges // BLOCK)], axis=0
    )


def table_columns(row, rows):
    columns = columns_of(row, 128)
    lane = iota(columns.shape, 1)
    return [one_hot(columns == lane + 128 * b) for b in range(rows // 128)]


def send_kernel(node_ref, send_ref, *out_refs):
    node = node_ref[...]
    rows = node.shape[0]
    halo = send_ref.shape[1]
    pieces = []
    for d in range(4):
        pick = one_hot(iota((rows, halo), 0) == send_ref[d : d + 1, :])
        pieces.append(dot(pick, node, TN).astype(bf16))
    out_refs[0][...] = pieces[0]
    out_refs[1][...] = pieces[1]
    if len(out_refs) == 3:
        out_refs[2][0:halo, :] = pieces[2]
        out_refs[2][halo:, :] = pieces[3]
    else:
        out_refs[2][...] = pieces[2]
        out_refs[3][...] = pieces[3]


def forward_kernel(
    count_ref, node_ref, src_ref, dst_ref, w_src_ref, w_dst_ref, bias_ref, w_out_ref, *rest
):
    *halo_refs, factor_ref, hidden_ref, partial_ref = rest
    node = node_ref[...]
    rows = node.shape[0]
    edges = src_ref.shape[1]
    table = jnp.concatenate([node] + [r[...] for r in halo_refs], axis=0)
    picks = table_columns(src_ref[...], table.shape[0])
    source = dot(jnp.concatenate(picks, axis=1), table).astype(bf16)
    (target_pick,) = table_columns(dst_ref[...], rows)
    target = dot(target_pick, node).astype(bf16)
    pre = dot(source, w_src_ref[...]) + dot(target, w_dst_ref[...]) + bias_ref[...]
    sig = 0.5 + 0.5 * jnp.tanh(0.5 * pre)
    factor_ref[...] = sig * (1.0 + pre * (1.0 - sig))
    activated = (pre * sig).astype(bf16)
    used = usable_row(count_ref, edges)
    collect = one_hot((iota((rows, edges), 0) == dst_ref[...]) & (used > 0))
    hidden = dot(collect, activated)
    high, low = split(hidden)
    hidden_ref[...] = high
    partial_ref[...] = (dot(high, w_out_ref[...]) + dot(low, w_out_ref[...])).astype(bf16)


def backward_kernel(
    geometry,
    count_ref,
    node_ref,
    src_ref,
    dst_ref,
    w_out_ref,
    gain_ref,
    cot_ref,
    factor_ref,
    hidden_ref,
    own_ref,
    other_ref,
    *rest,
):
    peers, chunk, n_halo, n_message, paired = geometry
    *rest, out_scratch = rest
    halo_refs = rest[:n_halo]
    updated_ref, local_ref, target_ref = rest[n_halo : n_halo + 3]
    back_refs = rest[n_halo + 3 : 2 * n_halo + 3]
    message_refs = rest[2 * n_halo + 3 :]
    node = node_ref[...]
    rows, width = node.shape
    edges = src_ref.shape[1]
    aggregate = own_ref[...].astype(f32) + other_ref[...].astype(f32)
    center = aggregate - jnp.mean(aggregate, axis=1, keepdims=True)
    variance = jnp.mean(center * center, axis=1, keepdims=True)
    inverse = lax.rsqrt(variance + EPSILON)
    normed = center * inverse
    gain = gain_ref[...]
    updated_ref[...] = (node.astype(f32) + gain * normed).astype(bf16)
    upstream = cot_ref[...].astype(f32)
    gain_part = jnp.sum(upstream * normed, axis=0, keepdims=True)
    scaled = upstream * gain
    agg_grad = inverse * (
        scaled
        - jnp.mean(scaled, axis=1, keepdims=True)
        - normed * jnp.mean(scaled * normed, axis=1, keepdims=True)
    )
    agg_grad = agg_grad.astype(bf16)

    columns = columns_of(dst_ref[...], 128)
    used = usable_columns(count_ref, edges, 128)
    spread = one_hot((columns == iota(columns.shape, 1)) & (used > 0))
    message_grad = dot(spread, agg_grad).astype(bf16)
    act_grad = dot(message_grad, w_out_ref[...], NT)
    pre_grad = (act_grad * factor_ref[...]).astype(bf16)

    table = jnp.concatenate([node] + [r[...] for r in halo_refs], axis=0)
    size = table.shape[0]
    by_source = dot(one_hot(iota((size, edges), 0) == src_ref[...]), pre_grad)
    by_target = dot(one_hot(iota((rows, edges), 0) == dst_ref[...]), pre_grad)
    local_ref[...] = by_source[:rows]
    by_target_low = by_target.astype(bf16)
    target_ref[...] = by_target_low
    at = rows
    for ref in back_refs:
        ref[...] = by_source[at : at + ref.shape[0]].astype(bf16)
        at += ref.shape[0]

    hid = by_source.shape[1]
    bias_part = jnp.sum(by_target, axis=0, keepdims=True)
    src_part = dot(table, by_source.astype(bf16), TN).astype(bf16)
    dst_part = dot(node, by_target_low, TN).astype(bf16)
    out_part = dot(hidden_ref[...], agg_grad, TN).astype(bf16)
    vectors = [bias_part] + [gain_part[:, at : at + hid] for at in range(0, width, hid)]
    tail = []
    for v in vectors:
        high = v.astype(bf16)
        tail += [high.astype(f32), (v - high.astype(f32))]
    tail.append(jnp.zeros((TAIL - len(tail), hid), f32))
    tail = jnp.concatenate(tail, axis=0).astype(bf16)

    if paired:
        send_ref, keep_ref, *out_refs = message_refs
        sub = lax.axis_index("sub")
        mesh = lax.axis_index("mesh")

        @pl.when(sub == 0)
        def _():
            send_ref[0:width, :] = dst_part
            keep_ref[0:width, :] = src_part

        @pl.when(sub == 1)
        def _():
            send_ref[0:width, :] = src_part
            keep_ref[0:width, :] = dst_part

        send_ref[width:, :] = tail
        keep_ref[width:, :] = tail
        out_scratch[...] = out_part
        strip = hid // len(out_refs)
        for k, ref in enumerate(out_refs):
            start = pl.multiple_of((mesh ^ k) * strip, strip)
            ref[...] = out_scratch[pl.ds(start, strip), :]
        return

    (message_ref,) = message_refs
    blocks = [src_part, dst_part]
    for at in range(0, width, hid):
        blocks.append(out_part[:, at : at + hid])
    done = 0
    for block in blocks:
        at = 0
        while at < block.shape[0]:
            peer, offset = divmod(done, chunk)
            take = min(chunk - offset, block.shape[0] - at)
            message_ref[peer, offset : offset + take, :] = block[at : at + take]
            at += take
            done += take
    while done < peers * chunk:
        peer, offset = divmod(done, chunk)
        take = chunk - offset
        message_ref[peer, offset : offset + take, :] = jnp.zeros((take, hid), bf16)
        done += take
    for peer in range(peers):
        message_ref[peer, chunk:, :] = tail


def tree(terms):
    while len(terms) > 1:
        terms = [terms[i] + terms[i + 1] for i in range(0, len(terms), 2)]
    return terms[0]


def turn_kernel(count, keep_ref, arrived_ref, *refs):
    out_terms = refs[:count]
    line_refs = refs[count : 2 * count]
    out_send_ref, out_keep_ref, scratch = refs[2 * count :]
    sub = lax.axis_index("sub")
    mesh = lax.axis_index("mesh")
    hid = keep_ref.shape[1]
    total = keep_ref[...].astype(f32) + arrived_ref[...].astype(f32)
    rows = total.shape[0] - TAIL
    strip = rows // count
    vectors = total[rows:]
    high = vectors.astype(bf16)
    low = (vectors - high.astype(f32)).astype(bf16)
    scratch[...] = total[:rows].astype(bf16)
    for k, ref in enumerate(line_refs):
        start = pl.multiple_of((mesh ^ k) * strip, strip)
        ref[0:strip, :] = scratch[pl.ds(start, strip), :]
        ref[strip : strip + TAIL, :] = high
        ref[strip + TAIL :, :] = low
    out = tree([r[...].astype(f32) for r in out_terms])
    left, right = out[:, :hid], out[:, hid:]
    out_send_ref[...] = jnp.where(sub == 0, right, left).astype(bf16)
    out_keep_ref[...] = jnp.where(sub == 0, left, right).astype(bf16)


def own_kernel(count, *refs):
    line_refs = refs[:count]
    out_keep_ref, out_arrived_ref, own_ref, bias_ref, gain_ref = refs[count:]
    total = tree([r[...].astype(f32) for r in line_refs])
    strip = own_ref.shape[0] - out_keep_ref.shape[0]
    own_ref[0:strip, :] = total[:strip].astype(bf16)
    own_ref[strip:, :] = (
        out_keep_ref[...].astype(f32) + out_arrived_ref[...].astype(f32)
    ).astype(bf16)
    tail = total[strip : strip + TAIL] + total[strip + TAIL :]
    write_vectors(tail, bias_ref, gain_ref)


def write_vectors(tail, bias_ref, gain_ref):
    bias_ref[...] = tail[0:1] + tail[1:2]
    hid = tail.shape[1]
    for k in range(gain_ref.shape[1] // hid):
        gain_ref[:, k * hid : (k + 1) * hid] = tail[2 + 2 * k : 3 + 2 * k] + tail[3 + 2 * k : 4 + 2 * k]


def place_kernel(count, *refs):
    mine, theirs = refs[:count], refs[count : 2 * count]
    src_ref, dst_ref, out_ref = refs[2 * count :]
    first = lax.axis_index("sub") == 0
    mesh = lax.axis_index("mesh")
    width, hid = src_ref.shape
    strip = width // count
    narrow = hid // count
    for k in range(count):
        a, b = mine[k][...], theirs[k][...]
        low = jnp.where(first, a, b).astype(f32)
        high = jnp.where(first, b, a).astype(f32)
        start = pl.multiple_of((mesh ^ k) * strip, strip)
        src_ref[pl.ds(start, strip), :] = low[:strip]
        dst_ref[pl.ds(start, strip), :] = high[:strip]
        start = pl.multiple_of((mesh ^ k) * narrow, narrow)
        out_ref[pl.ds(start, narrow), 0:hid] = low[strip:]
        out_ref[pl.ds(start, narrow), hid:] = high[strip:]


def sum_kernel(chunk, arrived_ref, out_ref, bias_ref, gain_ref):
    peers = arrived_ref.shape[0]
    total = arrived_ref[0].astype(f32)
    for peer in range(1, peers):
        total += arrived_ref[peer].astype(f32)
    low = total[:chunk].astype(bf16)
    for peer in range(peers):
        out_ref[peer] = low
    tail = total[chunk:]
    write_vectors(tail, bias_ref, gain_ref)


def unpack_kernel(arrived_ref, src_ref, dst_ref, out_ref):
    hid = src_ref.shape[1]
    rows = src_ref.shape[0]
    src_ref[...] = arrived_ref[0:rows, :].astype(f32)
    dst_ref[...] = arrived_ref[rows : 2 * rows, :].astype(f32)
    at = 2 * rows
    for k in range(out_ref.shape[1] // hid):
        out_ref[:, k * hid : (k + 1) * hid] = arrived_ref[at : at + out_ref.shape[0], :].astype(f32)
        at += out_ref.shape[0]


def node_kernel(send_ref, local_ref, target_ref, w_src_ref, w_dst_ref, *rest):
    *back_refs, out_ref = rest
    rows = local_ref.shape[0]
    halo = send_ref.shape[1]
    returned = jnp.concatenate([r[...] for r in back_refs], axis=0)
    total = local_ref[...]
    for d in range(4):
        pick = one_hot(iota((rows, halo), 0) == send_ref[d : d + 1, :])
        total += dot(pick, returned[d * halo : (d + 1) * halo])
    out_ref[...] = (
        dot(total.astype(bf16), w_src_ref[...], NT) + dot(target_ref[...], w_dst_ref[...], NT)
    ).astype(bf16)


def finish_kernel(cot_ref, own_ref, other_ref, out_ref):
    out_ref[...] = cot_ref[...].astype(f32) + (
        own_ref[...].astype(f32) + other_ref[...].astype(f32)
    )


VMEM = pl.BlockSpec(memory_space=pltpu.VMEM)
SMEM = pl.BlockSpec(memory_space=pltpu.SMEM)


def shape(dims, dtype):
    return jax.ShapeDtypeStruct(dims, dtype)


def call(kernel, outs, *args, smem=0, flops=10**8, scratch=()):
    return pl.pallas_call(
        kernel,
        out_shape=outs,
        in_specs=[SMEM] * smem + [VMEM] * (len(args) - smem),
        out_specs=jax.tree.map(lambda _: VMEM, outs),
        scratch_shapes=scratch,
        compiler_params=pltpu.CompilerParams(vmem_limit_bytes=VMEM_LIMIT),
        cost_estimate=pl.CostEstimate(flops=flops, bytes_accessed=10**6, transcendentals=0),
    )(*args)


def shifted(x, axis, by):
    count = lax.axis_size(axis)
    return lax.ppermute(x, axis, [(i, (i + by) % count) for i in range(count)])


def across(x, axis, k):
    count = lax.axis_size(axis)
    return lax.ppermute(x, axis, [(i, i ^ k) for i in range(count)])


def paired_sums(messages, lines, strip, narrow, width, hid):
    send, keep, *outs = messages
    out_terms = [outs[0]] + [across(outs[k], "mesh", k) for k in range(1, lines)]
    arrived = across(send, "sub", 1)
    *line, out_send, out_keep = call(
        functools.partial(turn_kernel, lines),
        [shape((strip + 2 * TAIL, hid), bf16)] * lines + [shape((narrow, hid), bf16)] * 2,
        keep, arrived, *out_terms,
        scratch=[pltpu.VMEM((width, hid), bf16)],
    )
    line_terms = [line[0]] + [across(line[k], "mesh", k) for k in range(1, lines)]
    own, bias_grad, gain_grad = call(
        functools.partial(own_kernel, lines),
        [shape((strip + narrow, hid), bf16), shape((1, hid), f32), shape((1, width), f32)],
        *line_terms, out_keep, across(out_send, "sub", 1),
    )
    mine = [own] + [across(own, "mesh", k) for k in range(1, lines)]
    theirs = [across(x, "sub", 1) for x in mine]
    grads = call(
        functools.partial(place_kernel, lines),
        [shape((width, hid), f32), shape((width, hid), f32), shape((hid, width), f32)],
        *mine, *theirs,
    )
    return (*grads, bias_grad, gain_grad)


def shards(
    node_state,
    send_rows,
    edge_src,
    edge_dst,
    block_count,
    w_src,
    w_dst,
    hidden_bias,
    w_out,
    norm_gain,
    cotangent,
):
    rows, width = node_state.shape
    hid = w_src.shape[1]
    halo = send_rows.shape[2]
    edges = edge_src.shape[0]
    peers = lax.axis_size("mesh") * lax.axis_size("sub")
    merged = lax.axis_size("sub") == 2
    total_rows = 2 * width + (width // hid) * hid
    chunk = -(-total_rows // (peers * 16)) * 16

    send = send_rows[0]
    src = edge_src.reshape(1, edges)
    dst = edge_dst.reshape(1, edges)
    bias = hidden_bias.reshape(1, hid)
    gain = norm_gain.reshape(1, width)

    piece = [halo, halo, 2 * halo] if merged else [halo] * 4
    routes = [("mesh", 1), ("mesh", -1), ("sub", 1)] + ([] if merged else [("sub", -1)])

    outgoing = call(send_kernel, [shape((n, width), bf16) for n in piece], node_state, send)
    arrived = [shifted(x, axis, by) for x, (axis, by) in zip(outgoing, routes)]

    factor, hidden, partial = call(
        forward_kernel,
        [shape((edges, hid), f32), shape((rows, hid), bf16), shape((rows, width), bf16)],
        block_count, node_state, src, dst, w_src, w_dst, bias, w_out, *arrived,
        smem=1,
    )
    other = shifted(partial, "lat", 1)

    lines = lax.axis_size("mesh")
    paired = merged and lines == 4
    if paired:
        strip = width // lines
        narrow = hid // lines
        message_shapes = [shape((width + TAIL, hid), bf16)] * 2 + [shape((narrow, width), bf16)] * lines
    else:
        message_shapes = [shape((peers, chunk + TAIL, hid), bf16)]
    n_halo = len(piece)
    updated, local, target, *rest = call(
        functools.partial(
            backward_kernel, (peers, chunk, n_halo, len(message_shapes), paired)
        ),
        [shape((rows, width), bf16), shape((rows, hid), f32), shape((rows, hid), bf16)]
        + [shape((n, hid), bf16) for n in piece]
        + message_shapes,
        block_count, node_state, src, dst, w_out, gain, cotangent, factor, hidden, partial, other,
        *arrived,
        smem=1,
        scratch=[pltpu.VMEM((hid, width), bf16)],
    )
    backs, messages = rest[:n_halo], rest[n_halo:]
    returned = [shifted(x, axis, -by) for x, (axis, by) in zip(backs, routes)]

    node_part = call(
        node_kernel, shape((rows, width), bf16), send, local, target, w_src, w_dst, *returned
    )
    node_grad = call(
        finish_kernel, shape((rows, width), f32),
        cotangent, node_part, shifted(node_part, "lat", 1),
    )

    if paired:
        src_grad, dst_grad, out_grad, bias_grad, gain_grad = paired_sums(
            messages, lines, strip, narrow, width, hid
        )
    else:
        exchanged = lax.all_to_all(messages[0], ("mesh", "sub"), 0, 0)
        reduced, bias_grad, gain_grad = call(
            functools.partial(sum_kernel, chunk),
            [shape((peers, chunk, hid), bf16), shape((1, hid), f32), shape((1, width), f32)],
            exchanged,
        )
        gathered = lax.all_to_all(reduced, ("mesh", "sub"), 0, 0)
        src_grad, dst_grad, out_grad = call(
            unpack_kernel,
            [shape((width, hid), f32), shape((width, hid), f32), shape((hid, width), f32)],
            gathered.reshape(peers * chunk, hid),
        )
    return (
        updated, node_grad, src_grad, dst_grad, out_grad,
        bias_grad.reshape(hid), gain_grad.reshape(width),
    )


def solution(mesh):
    nodes = P(("parts", "mesh", "sub"), None)
    slots = P(("parts", "mesh", "sub"))
    in_specs = (
        nodes,
        P(("parts", "mesh", "sub"), None, None),
        slots,
        slots,
        slots,
        P(None, "lat"),
        P(None, "lat"),
        P("lat"),
        P("lat", None),
        P(),
        nodes,
    )
    out_specs = (
        nodes,
        nodes,
        P("parts", "lat"),
        P("parts", "lat"),
        P(("parts", "lat"), None),
        P(("parts", "lat")),
        P("parts"),
    )
    return jax.shard_map(shards, mesh=mesh, in_specs=in_specs, out_specs=out_specs, check_vma=False)
```

```python
import functools

import jax
import jax.numpy as jnp
from jax import lax
from jax.experimental import pallas as pl
from jax.experimental.pallas import tpu as pltpu
from jax.sharding import PartitionSpec as P

BLOCK = 128
EPSILON = 1e-05
TAIL = 16
VMEM_LIMIT = 24 * 1024 * 1024

f32 = jnp.float32
bf16 = jnp.bfloat16

NN = (((1,), (0,)), ((), ()))
NT = (((1,), (1,)), ((), ()))
TN = (((0,), (0,)), ((), ()))


def dot(a, b, dims=NN):
    return lax.dot_general(a, b, dims, preferred_element_type=f32)


def iota(shape, dim):
    return lax.broadcasted_iota(jnp.int32, shape, dim)


def one_hot(condition):
    return jnp.where(condition, 1.0, 0.0).astype(bf16)


def split(x):
    high = x.astype(bf16)
    return high, (x - high.astype(f32)).astype(bf16)


def columns_of(row, lanes):
    return jnp.transpose(jnp.broadcast_to(row, (lanes, row.shape[1])))


def usable_row(count_ref, edges):
    lane = iota((1, BLOCK), 1)
    parts = [lane < count_ref[b] for b in range(edges // BLOCK)]
    return jnp.concatenate([jnp.where(p, 1, 0) for p in parts], axis=1)


def usable_columns(count_ref, edges, lanes):
    sub = iota((BLOCK, lanes), 0)
    return jnp.concatenate(
        [jnp.where(sub < count_ref[b], 1, 0) for b in range(edges // BLOCK)], axis=0
    )


def fetch(sems, *pairs):
    copies = [pltpu.make_async_copy(a, b, sems.at[i]) for i, (a, b) in enumerate(pairs)]
    for copy in copies:
        copy.start()
    return copies


def send_kernel(node_hbm, send_hbm, node_ref, send_ref, *rest):
    *out_refs, sems = rest
    for copy in fetch(sems, (node_hbm, node_ref), (send_hbm, send_ref)):
        copy.wait()
    node = node_ref[...]
    rows = node.shape[0]
    halo = send_ref.shape[2]
    pieces = []
    for d in range(4):
        pick = one_hot(iota((rows, halo), 0) == send_ref[0, d : d + 1, :])
        pieces.append(dot(pick, node, TN).astype(bf16))
    out_refs[0][...] = pieces[0]
    out_refs[1][...] = pieces[1]
    if len(out_refs) == 3:
        out_refs[2][0:halo, :] = pieces[2]
        out_refs[2][halo:, :] = pieces[3]
    else:
        out_refs[2][...] = pieces[2]
        out_refs[3][...] = pieces[3]


def local_kernel(
    count_ref, node_ref, src_hbm, dst_hbm, bias_hbm, w_src_hbm, w_dst_hbm, w_out_hbm, gain_hbm, cot_hbm,
    pre_ref, pick_ref, collect_ref, spread_ref, scatter_ref,
    w_src_ref, w_dst_ref, w_out_ref, gain_ref, cot_ref,
    src_ref, dst_ref, bias_ref, sems,
):
    copies = fetch(
        sems, (src_hbm, src_ref), (dst_hbm, dst_ref), (bias_hbm, bias_ref), (w_src_hbm, w_src_ref),
        (w_dst_hbm, w_dst_ref), (w_out_hbm, w_out_ref), (gain_hbm, gain_ref), (cot_hbm, cot_ref),
    )
    node = node_ref[...]
    rows = node.shape[0]
    edges = src_ref.shape[1]
    copies[0].wait()
    copies[1].wait()
    scatter_ref[...] = one_hot(iota(scatter_ref.shape, 0) == src_ref[...])
    used = usable_row(count_ref, edges) > 0
    collect_ref[...] = one_hot((iota((rows, edges), 0) == dst_ref[...]) & used)
    source = columns_of(src_ref[...], 128)
    target = columns_of(dst_ref[...], 128)
    lane = iota(source.shape, 1)
    used = usable_columns(count_ref, edges, 128) > 0
    near = one_hot(source == lane)
    pick_ref[...] = one_hot(source == lane + rows)
    spread_ref[...] = one_hot((target == lane) & used)
    both = jnp.concatenate([dot(near, node), dot(one_hot(target == lane), node)], axis=1).astype(bf16)
    copies[2].wait()
    copies[3].wait()
    copies[4].wait()
    weights = jnp.concatenate([w_src_ref[...], w_dst_ref[...]], axis=0)
    pre_ref[...] = dot(both, weights) + bias_ref[...]
    for copy in copies[5:]:
        copy.wait()


def twice(x):
    return jnp.concatenate([x, x], axis=1)


def stacked(x):
    return jnp.concatenate(split(x), axis=0)


def forward_kernel(pre_ref, pick_ref, collect_ref, w_src_ref, w_out_ref, *rest):
    *halo_refs, factor_ref, hidden_ref, partial_ref = rest
    halo = jnp.concatenate([r[...] for r in halo_refs], axis=0)
    far = stacked(dot(halo, w_src_ref[...]))
    pre = pre_ref[...] + dot(twice(pick_ref[...]), far)
    sig = 0.5 + 0.5 * jnp.tanh(0.5 * pre)
    factor_ref[...] = sig * (1.0 + pre * (1.0 - sig))
    hidden = dot(collect_ref[...], (pre * sig).astype(bf16))
    high, low = split(hidden)
    hidden_ref[...] = high
    w_out = w_out_ref[...]
    partial_ref[...] = (dot(high, w_out) + dot(low, w_out)).astype(bf16)


def backward_kernel(
    geometry,
    node_ref, collect_ref, spread_ref, scatter_ref, w_out_ref, gain_ref, cot_ref,
    factor_ref, hidden_ref, own_ref, other_ref,
    *rest,
):
    peers, chunk, n_halo, paired = geometry
    *rest, out_scratch, back_scratch = rest
    halo_refs = rest[:n_halo]
    updated_ref, local_ref, target_ref, *message_refs = rest[n_halo:]
    node = node_ref[...]
    rows, width = node.shape
    aggregate = own_ref[...].astype(f32) + other_ref[...].astype(f32)
    center = aggregate - jnp.mean(aggregate, axis=1, keepdims=True)
    variance = jnp.mean(center * center, axis=1, keepdims=True)
    inverse = lax.rsqrt(variance + EPSILON)
    normed = center * inverse
    gain = gain_ref[...]
    upstream = cot_ref[...].astype(f32)
    scaled = upstream * gain
    agg_grad = inverse * (
        scaled
        - jnp.mean(scaled, axis=1, keepdims=True)
        - normed * jnp.mean(scaled * normed, axis=1, keepdims=True)
    )
    agg_grad = agg_grad.astype(bf16)
    updated_ref[...] = (node.astype(f32) + gain * normed).astype(bf16)
    gain_part = jnp.sum(upstream * normed, axis=0, keepdims=True)

    act_grad = dot(twice(spread_ref[...]), stacked(dot(agg_grad, w_out_ref[...], NT)))
    pre_grad = (act_grad * factor_ref[...]).astype(bf16)

    table = jnp.concatenate([node] + [r[...] for r in halo_refs], axis=0)
    by_source = dot(scatter_ref[...], pre_grad)
    by_target = dot(collect_ref[...], pre_grad)
    local_ref[...] = by_source[:rows]
    by_target_low = by_target.astype(bf16)
    by_source_low = by_source.astype(bf16)
    target_ref[...] = by_target_low

    hid = by_source.shape[1]
    bias_part = jnp.sum(by_target, axis=0, keepdims=True)
    src_part = dot(table, by_source_low, TN).astype(bf16)
    dst_part = dot(node, by_target_low, TN).astype(bf16)
    out_part = dot(hidden_ref[...], agg_grad, TN).astype(bf16)
    vectors = [bias_part] + [gain_part[:, at : at + hid] for at in range(0, width, hid)]
    tail = tail_of(vectors)
    back = by_source_low[rows:]

    if paired:
        send_ref, keep_ref, *out_refs = message_refs
        sub = lax.axis_index("sub")
        mesh = lax.axis_index("mesh")

        @pl.when(sub == 0)
        def _():
            send_ref[0:width, :] = dst_part
            keep_ref[0:width, :] = src_part

        @pl.when(sub == 1)
        def _():
            send_ref[0:width, :] = src_part
            keep_ref[0:width, :] = dst_part

        halo = back.shape[0] // 4
        send_ref[width : width + TAIL, :] = tail
        keep_ref[width:, :] = tail
        send_ref[width + TAIL :, :] = back[2 * halo :]
        back_scratch[...] = back[: 2 * halo]
        out_scratch[...] = out_part
        strip = hid // len(out_refs)
        for k, ref in enumerate(out_refs):
            start = pl.multiple_of((mesh ^ k) * strip, strip)
            ref[0:strip, :] = out_scratch[pl.ds(start, strip), :]
            if k % 2 == 1:
                slot = (mesh + (k // 2) + 1) % 2
                start = pl.multiple_of(slot * halo, halo)
                rows_back = back_scratch[pl.ds(start, halo), :]
                ref[strip:, 0:hid] = rows_back[: halo // 2]
                ref[strip:, hid:] = rows_back[halo // 2 :]
        return

    message_ref, *back_refs = message_refs
    at = 0
    for ref in back_refs:
        ref[...] = back[at : at + ref.shape[0]]
        at += ref.shape[0]
    blocks = [src_part, dst_part]
    for at in range(0, width, hid):
        blocks.append(out_part[:, at : at + hid])
    done = 0
    for block in blocks:
        at = 0
        while at < block.shape[0]:
            peer, offset = divmod(done, chunk)
            take = min(chunk - offset, block.shape[0] - at)
            message_ref[peer, offset : offset + take, :] = block[at : at + take]
            at += take
            done += take
    while done < peers * chunk:
        peer, offset = divmod(done, chunk)
        take = chunk - offset
        message_ref[peer, offset : offset + take, :] = jnp.zeros((take, hid), bf16)
        done += take
    for peer in range(peers):
        message_ref[peer, chunk:, :] = tail


def tail_of(vectors):
    tail = []
    for v in vectors:
        high = v.astype(bf16).astype(f32)
        tail += [high, v - high]
    tail.append(jnp.zeros((TAIL - len(tail), vectors[0].shape[1]), f32))
    return jnp.concatenate(tail, axis=0).astype(bf16)


def tree(terms):
    while len(terms) > 1:
        terms = [terms[i] + terms[i + 1] for i in range(0, len(terms), 2)]
    return terms[0]


def turn_kernel(count, *refs):
    out_terms = refs[count - 1 :: -1]
    arrived_ref, keep_ref, *refs = refs[count:]
    refs = [None] * count + refs
    line_refs = refs[count : 2 * count]
    out_send_ref, out_keep_ref, scratch = refs[2 * count :]
    sub = lax.axis_index("sub")
    mesh = lax.axis_index("mesh")
    full, hid = keep_ref.shape
    total = keep_ref[...].astype(f32) + arrived_ref[0:full, :].astype(f32)
    rows = full - TAIL
    strip = rows // count
    tail = total[rows:]
    tail = tail_of([tail[at : at + 1] + tail[at + 1 : at + 2] for at in range(0, 6, 2)])
    scratch[...] = total[:rows].astype(bf16)
    for k, ref in enumerate(line_refs):
        start = pl.multiple_of((mesh ^ k) * strip, strip)
        ref[0:strip, :] = scratch[pl.ds(start, strip), :]
        ref[strip:, :] = tail
    out_strip = out_keep_ref.shape[0]
    out = tree([r[0:out_strip, :].astype(f32) for r in out_terms])
    left, right = out[:, :hid], out[:, hid:]
    out_send_ref[...] = jnp.where(sub == 0, right, left).astype(bf16)
    out_keep_ref[...] = jnp.where(sub == 0, left, right).astype(bf16)


def own_kernel(count, *refs):
    line_refs = refs[count - 1 :: -1]
    out_keep_ref, out_arrived_ref, own_ref, bias_ref, gain_ref = refs[count:]
    total = tree([r[...].astype(f32) for r in line_refs])
    strip = own_ref.shape[0] - out_keep_ref.shape[0]
    own_ref[0:strip, :] = total[:strip].astype(bf16)
    own_ref[strip:, :] = (
        out_keep_ref[...].astype(f32) + out_arrived_ref[...].astype(f32)
    ).astype(bf16)
    write_vectors(total[strip:], bias_ref, gain_ref)


def write_vectors(tail, bias_ref, gain_ref):
    bias_ref[...] = tail[0:1] + tail[1:2]
    hid = tail.shape[1]
    for k in range(gain_ref.shape[1] // hid):
        gain_ref[:, k * hid : (k + 1) * hid] = tail[2 + 2 * k : 3 + 2 * k] + tail[3 + 2 * k : 4 + 2 * k]


def place_kernel(count, *refs):
    mine, theirs = refs[:count], refs[count : 2 * count]
    src_ref, dst_ref, out_ref = refs[2 * count :]
    first = lax.axis_index("sub") == 0
    mesh = lax.axis_index("mesh")
    width, hid = src_ref.shape
    strip = width // count
    narrow = hid // count
    for k in range(count):
        a, b = mine[k][...], theirs[k][...]
        low = jnp.where(first, a, b).astype(f32)
        high = jnp.where(first, b, a).astype(f32)
        start = pl.multiple_of((mesh ^ k) * strip, strip)
        src_ref[pl.ds(start, strip), :] = low[:strip]
        dst_ref[pl.ds(start, strip), :] = high[:strip]
        start = pl.multiple_of((mesh ^ k) * narrow, narrow)
        out_ref[pl.ds(start, narrow), 0:hid] = low[strip:]
        out_ref[pl.ds(start, narrow), hid:] = high[strip:]


def sum_kernel(chunk, arrived_ref, out_ref, bias_ref, gain_ref):
    peers = arrived_ref.shape[0]
    total = arrived_ref[0].astype(f32)
    for peer in range(1, peers):
        total += arrived_ref[peer].astype(f32)
    low = total[:chunk].astype(bf16)
    for peer in range(peers):
        out_ref[peer] = low
    tail = total[chunk:]
    write_vectors(tail, bias_ref, gain_ref)


def unpack_kernel(arrived_ref, src_ref, dst_ref, out_ref):
    hid = src_ref.shape[1]
    rows = src_ref.shape[0]
    src_ref[...] = arrived_ref[0:rows, :].astype(f32)
    dst_ref[...] = arrived_ref[rows : 2 * rows, :].astype(f32)
    at = 2 * rows
    for k in range(out_ref.shape[1] // hid):
        out_ref[:, k * hid : (k + 1) * hid] = arrived_ref[at : at + out_ref.shape[0], :].astype(f32)
        at += out_ref.shape[0]


def node_part(send_ref, local_ref, target_ref, w_src_ref, w_dst_ref, returned, out_ref):
    rows = local_ref.shape[0]
    halo = send_ref.shape[2]
    picks = [one_hot(iota((rows, halo), 0) == send_ref[0, d : d + 1, :]) for d in range(4)]
    total = local_ref[...] + dot(jnp.concatenate(picks, axis=1), jnp.concatenate(returned, axis=0))
    out_ref[...] = (
        dot(total.astype(bf16), w_src_ref[...], NT) + dot(target_ref[...], w_dst_ref[...], NT)
    ).astype(bf16)


def node_kernel(send_ref, local_ref, target_ref, w_src_ref, w_dst_ref, *rest):
    *back_refs, out_ref = rest
    returned = [r[...] for r in back_refs]
    node_part(send_ref, local_ref, target_ref, w_src_ref, w_dst_ref, returned, out_ref)


def paired_node_kernel(
    send_ref, local_ref, target_ref, w_src_ref, w_dst_ref, three_ref, one_ref, pair_ref, out_ref
):
    even = lax.axis_index("mesh") % 2 == 0
    halo = send_ref.shape[2]
    hid = local_ref.shape[1]
    at = one_ref.shape[0] - halo // 2
    one, three = [
        jnp.concatenate([r[at:, :hid], r[at:, hid:]], axis=0) for r in (one_ref, three_ref)
    ]
    returned = [
        jnp.where(even, one, three), jnp.where(even, three, one), pair_ref[pair_ref.shape[0] - 2 * halo :, :]
    ]
    node_part(send_ref, local_ref, target_ref, w_src_ref, w_dst_ref, returned, out_ref)


def finish_kernel(cot_ref, own_ref, other_ref, out_ref):
    out_ref[...] = cot_ref[...].astype(f32) + (
        own_ref[...].astype(f32) + other_ref[...].astype(f32)
    )


VMEM = pl.BlockSpec(memory_space=pltpu.VMEM)
SMEM = pl.BlockSpec(memory_space=pltpu.SMEM)
HBM = pl.BlockSpec(memory_space=pltpu.HBM)


def shape(dims, dtype):
    return jax.ShapeDtypeStruct(dims, dtype)


def call(kernel, outs, *args, specs=None, flops=10**8, scratch=()):
    return pl.pallas_call(
        kernel,
        out_shape=outs,
        in_specs=specs or [VMEM] * len(args),
        out_specs=jax.tree.map(lambda _: VMEM, outs),
        scratch_shapes=scratch,
        compiler_params=pltpu.CompilerParams(vmem_limit_bytes=VMEM_LIMIT),
        cost_estimate=pl.CostEstimate(flops=flops, bytes_accessed=10**6, transcendentals=0),
    )(*args)


def shifted(x, axis, by):
    count = lax.axis_size(axis)
    return lax.ppermute(x, axis, [(i, (i + by) % count) for i in range(count)])


def across(x, axis, k):
    count = lax.axis_size(axis)
    return lax.ppermute(x, axis, [(i, i ^ k) for i in range(count)])


def paired_sums(messages, lines, strip, narrow, width, hid):
    send, keep, *outs = messages
    order = range(lines - 1, 0, -1)
    out_terms = {k: across(outs[k], "mesh", k) for k in order}
    arrived = across(send, "sub", 1)
    *line, out_send, out_keep = call(
        functools.partial(turn_kernel, lines),
        [shape((strip + TAIL, hid), bf16)] * lines + [shape((narrow, hid), bf16)] * 2,
        *[out_terms[k] for k in order], outs[0], arrived, keep,
        scratch=[pltpu.VMEM((width, hid), bf16)],
    )
    line_terms = {k: across(line[k], "mesh", k) for k in order}
    own, bias_grad, gain_grad = call(
        functools.partial(own_kernel, lines),
        [shape((strip + narrow, hid), bf16), shape((1, hid), f32), shape((1, width), f32)],
        *[line_terms[k] for k in order], line[0], out_keep, across(out_send, "sub", 1),
    )
    mine = {k: across(own, "mesh", k) for k in order}
    mine[0] = own
    theirs = {k: across(mine[k], "sub", 1) for k in mine}
    grads = call(
        functools.partial(place_kernel, lines),
        [shape((width, hid), f32), shape((width, hid), f32), shape((hid, width), f32)],
        *[mine[k] for k in range(lines)], *[theirs[k] for k in range(lines)],
    )
    return (*grads, bias_grad, gain_grad), (out_terms[3], out_terms[1], arrived)


def shards(
    node_state,
    send_rows,
    edge_src,
    edge_dst,
    block_count,
    w_src,
    w_dst,
    hidden_bias,
    w_out,
    norm_gain,
    cotangent,
):
    rows, width = node_state.shape
    hid = w_src.shape[1]
    halo = send_rows.shape[2]
    edges = edge_src.shape[0]
    peers = lax.axis_size("mesh") * lax.axis_size("sub")
    merged = lax.axis_size("sub") == 2
    total_rows = 2 * width + (width // hid) * hid
    chunk = -(-total_rows // (peers * 16)) * 16

    piece = [halo, halo, 2 * halo] if merged else [halo] * 4
    routes = [("mesh", 1), ("mesh", -1), ("sub", 1)] + ([] if merged else [("sub", -1)])
    n_halo = len(piece)

    node, send, *outgoing = call(
        send_kernel,
        [shape((rows, width), bf16), shape(send_rows.shape, jnp.int32)]
        + [shape((n, width), bf16) for n in piece],
        node_state, send_rows,
        specs=[HBM, HBM],
        scratch=[pltpu.SemaphoreType.DMA((2,))],
    )
    arrived = [shifted(x, axis, by) for x, (axis, by) in zip(outgoing, routes)]

    pre, pick, collect, spread, scatter, w_src, w_dst, w_out, gain, cot = call(
        local_kernel,
        [
            shape((edges, hid), f32),
            shape((edges, 4 * halo), bf16),
            shape((rows, edges), bf16),
            shape((edges, rows), bf16),
            shape((rows + 4 * halo, edges), bf16),
            shape(w_src.shape, bf16),
            shape(w_dst.shape, bf16),
            shape(w_out.shape, bf16),
            shape((1, width), f32),
            shape((rows, width), bf16),
        ],
        block_count, node, edge_src.reshape(1, edges), edge_dst.reshape(1, edges),
        hidden_bias.reshape(1, hid), w_src, w_dst, w_out, norm_gain.reshape(1, width), cotangent,
        specs=[SMEM, VMEM] + [HBM] * 8,
        scratch=[
            pltpu.VMEM((1, edges), jnp.int32),
            pltpu.VMEM((1, edges), jnp.int32),
            pltpu.VMEM((1, hid), f32),
            pltpu.SemaphoreType.DMA((8,)),
        ],
    )

    factor, hidden, partial = call(
        forward_kernel,
        [shape((edges, hid), f32), shape((rows, hid), bf16), shape((rows, width), bf16)],
        pre, pick, collect, w_src, w_out, *arrived,
    )
    other = shifted(partial, "lat", 1)

    lines = lax.axis_size("mesh")
    paired = merged and lines == 4
    if paired:
        strip = width // lines
        narrow = hid // lines
        message_shapes = [shape((width + TAIL + 2 * halo, hid), bf16), shape((width + TAIL, hid), bf16)]
        message_shapes += [shape((narrow + k % 2 * (halo // 2), width), bf16) for k in range(lines)]
    else:
        message_shapes = [shape((peers, chunk + TAIL, hid), bf16)]
        message_shapes += [shape((n, hid), bf16) for n in piece]
    updated, local, target, *messages = call(
        functools.partial(backward_kernel, (peers, chunk, n_halo, paired)),
        [shape((rows, width), bf16), shape((rows, hid), f32), shape((rows, hid), bf16)]
        + message_shapes,
        node, collect, spread, scatter, w_out, gain, cot, factor, hidden, partial, other, *arrived,
        scratch=[pltpu.VMEM((hid, width), bf16), pltpu.VMEM((2 * halo, hid), bf16)],
    )

    if paired:
        (src_grad, dst_grad, out_grad, bias_grad, gain_grad), returned = paired_sums(
            messages, lines, strip, narrow, width, hid
        )
    else:
        returned = [shifted(x, axis, -by) for x, (axis, by) in zip(messages[1:], routes)]
        exchanged = lax.all_to_all(messages[0], ("mesh", "sub"), 0, 0)
        reduced, bias_grad, gain_grad = call(
            functools.partial(sum_kernel, chunk),
            [shape((peers, chunk, hid), bf16), shape((1, hid), f32), shape((1, width), f32)],
            exchanged,
        )
        gathered = lax.all_to_all(reduced, ("mesh", "sub"), 0, 0)
        src_grad, dst_grad, out_grad = call(
            unpack_kernel,
            [shape((width, hid), f32), shape((width, hid), f32), shape((hid, width), f32)],
            gathered.reshape(peers * chunk, hid),
        )
    node_part = call(
        paired_node_kernel if paired else node_kernel,
        shape((rows, width), bf16),
        send, local, target, w_src, w_dst, *returned,
    )
    node_grad = call(
        finish_kernel, shape((rows, width), f32), cot, node_part, shifted(node_part, "lat", 1)
    )
    return (
        updated, node_grad, src_grad, dst_grad, out_grad,
        bias_grad.reshape(hid), gain_grad.reshape(width),
    )


def solution(mesh):
    nodes = P(("parts", "mesh", "sub"), None)
    slots = P(("parts", "mesh", "sub"))
    in_specs = (
        nodes,
        P(("parts", "mesh", "sub"), None, None),
        slots,
        slots,
        slots,
        P(None, "lat"),
        P(None, "lat"),
        P("lat"),
        P("lat", None),
        P(),
        nodes,
    )
    out_specs = (
        nodes,
        nodes,
        P("parts", "lat"),
        P("parts", "lat"),
        P(("parts", "lat"), None),
        P(("parts", "lat")),
        P("parts"),
    )
    return jax.shard_map(shards, mesh=mesh, in_specs=in_specs, out_specs=out_specs, check_vma=False)
```

```python
import functools

import jax
import jax.numpy as jnp
from jax import lax
from jax.experimental import pallas as pl
from jax.experimental.pallas import tpu as pltpu
from jax.sharding import PartitionSpec as P

BLOCK = 128
EPSILON = 1e-05
TAIL = 16
N_OPERANDS = 10
VMEM_LIMIT = 24 * 1024 * 1024

f32 = jnp.float32
bf16 = jnp.bfloat16

NN = (((1,), (0,)), ((), ()))
NT = (((1,), (1,)), ((), ()))
TN = (((0,), (0,)), ((), ()))


def dot(a, b, dims=NN):
    return lax.dot_general(a, b, dims, preferred_element_type=f32)


def iota(shape, dim):
    return lax.broadcasted_iota(jnp.int32, shape, dim)


def one_hot(condition):
    return jnp.where(condition, 1.0, 0.0).astype(bf16)


def split(x):
    high = x.astype(bf16)
    return high, (x - high.astype(f32)).astype(bf16)


def columns_of(row, lanes):
    return jnp.transpose(jnp.broadcast_to(row, (lanes, row.shape[1])))


def usable_row(count_ref, edges):
    lane = iota((1, BLOCK), 1)
    parts = [lane < count_ref[b] for b in range(edges // BLOCK)]
    return jnp.concatenate([jnp.where(p, 1, 0) for p in parts], axis=1)


def usable_columns(count_ref, edges, lanes):
    sub = iota((BLOCK, lanes), 0)
    return jnp.concatenate(
        [jnp.where(sub < count_ref[b], 1, 0) for b in range(edges // BLOCK)], axis=0
    )


def fetch(sems, *pairs):
    copies = [pltpu.make_async_copy(a, b, sems.at[i]) for i, (a, b) in enumerate(pairs)]
    for copy in copies:
        copy.start()
    return copies


def send_kernel(*refs):
    count = N_OPERANDS
    ins, outs, out_refs, sems = refs[:count], refs[count : 2 * count], refs[2 * count : -1], refs[-1]
    copies = fetch(sems, *zip(ins, outs))
    node_ref, send_ref = outs[:2]
    copies[0].wait()
    copies[1].wait()
    node = node_ref[...]
    rows = node.shape[0]
    halo = send_ref.shape[2]
    pieces = []
    for d in range(4):
        pick = one_hot(iota((rows, halo), 0) == send_ref[0, d : d + 1, :])
        pieces.append(dot(pick, node, TN).astype(bf16))
    out_refs[0][...] = pieces[0]
    out_refs[1][...] = pieces[1]
    if len(out_refs) == 3:
        out_refs[2][0:halo, :] = pieces[2]
        out_refs[2][halo:, :] = pieces[3]
    else:
        out_refs[2][...] = pieces[2]
        out_refs[3][...] = pieces[3]
    for copy in copies[2:]:
        copy.wait()


def local_kernel(
    count_ref, node_ref, src_ref, dst_ref, bias_ref, w_src_ref, w_dst_ref,
    pre_ref, pick_ref, collect_ref, spread_ref, scatter_ref,
):
    node = node_ref[...]
    rows = node.shape[0]
    edges = src_ref.shape[1]
    scatter_ref[...] = one_hot(iota(scatter_ref.shape, 0) == src_ref[...])
    used = usable_row(count_ref, edges) > 0
    collect_ref[...] = one_hot((iota((rows, edges), 0) == dst_ref[...]) & used)
    source = columns_of(src_ref[...], 128)
    target = columns_of(dst_ref[...], 128)
    lane = iota(source.shape, 1)
    used = usable_columns(count_ref, edges, 128) > 0
    near = one_hot(source == lane)
    pick_ref[...] = one_hot(source == lane + rows)
    spread_ref[...] = one_hot((target == lane) & used)
    both = jnp.concatenate([dot(near, node), dot(one_hot(target == lane), node)], axis=1).astype(bf16)
    weights = jnp.concatenate([w_src_ref[...], w_dst_ref[...]], axis=0)
    pre_ref[...] = dot(both, weights) + bias_ref[...]


def twice(x):
    return jnp.concatenate([x, x], axis=1)


def stacked(x):
    return jnp.concatenate(split(x), axis=0)


def forward_kernel(pre_ref, pick_ref, collect_ref, w_src_ref, w_out_ref, *rest):
    *halo_refs, factor_ref, hidden_ref, partial_ref = rest
    halo = jnp.concatenate([r[...] for r in halo_refs], axis=0)
    far = stacked(dot(halo, w_src_ref[...]))
    pre = pre_ref[...] + dot(twice(pick_ref[...]), far)
    sig = 0.5 + 0.5 * jnp.tanh(0.5 * pre)
    factor_ref[...] = sig * (1.0 + pre * (1.0 - sig))
    hidden = dot(collect_ref[...], (pre * sig).astype(bf16))
    high, low = split(hidden)
    hidden_ref[...] = high
    w_out = w_out_ref[...]
    partial_ref[...] = (dot(high, w_out) + dot(low, w_out)).astype(bf16)


def backward_kernel(
    geometry,
    node_ref, collect_ref, spread_ref, scatter_ref, w_out_ref, gain_ref, cot_ref,
    factor_ref, hidden_ref, own_ref, other_ref,
    *rest,
):
    peers, chunk, n_halo, paired = geometry
    *rest, out_scratch, back_scratch = rest
    halo_refs = rest[:n_halo]
    updated_ref, local_ref, target_ref, *message_refs = rest[n_halo:]
    node = node_ref[...]
    rows, width = node.shape
    aggregate = own_ref[...].astype(f32) + other_ref[...].astype(f32)
    center = aggregate - jnp.mean(aggregate, axis=1, keepdims=True)
    variance = jnp.mean(center * center, axis=1, keepdims=True)
    inverse = lax.rsqrt(variance + EPSILON)
    normed = center * inverse
    gain = gain_ref[...]
    upstream = cot_ref[...].astype(f32)
    scaled = upstream * gain
    agg_grad = inverse * (
        scaled
        - jnp.mean(scaled, axis=1, keepdims=True)
        - normed * jnp.mean(scaled * normed, axis=1, keepdims=True)
    )
    agg_grad = agg_grad.astype(bf16)
    updated_ref[...] = (node.astype(f32) + gain * normed).astype(bf16)
    gain_part = jnp.sum(upstream * normed, axis=0, keepdims=True)

    act_grad = dot(twice(spread_ref[...]), stacked(dot(agg_grad, w_out_ref[...], NT)))
    pre_grad = (act_grad * factor_ref[...]).astype(bf16)

    table = jnp.concatenate([node] + [r[...] for r in halo_refs], axis=0)
    by_source = dot(scatter_ref[...], pre_grad)
    by_target = dot(collect_ref[...], pre_grad)
    local_ref[...] = by_source[:rows]
    by_target_low = by_target.astype(bf16)
    by_source_low = by_source.astype(bf16)
    target_ref[...] = by_target_low

    hid = by_source.shape[1]
    bias_part = jnp.sum(by_target, axis=0, keepdims=True)
    src_part = dot(table, by_source_low, TN).astype(bf16)
    dst_part = dot(node, by_target_low, TN).astype(bf16)
    out_part = dot(hidden_ref[...], agg_grad, TN).astype(bf16)
    vectors = [bias_part] + [gain_part[:, at : at + hid] for at in range(0, width, hid)]
    tail = tail_of(vectors)
    back = by_source_low[rows:]

    if paired:
        send_ref, keep_ref, *out_refs = message_refs
        sub = lax.axis_index("sub")
        mesh = lax.axis_index("mesh")

        @pl.when(sub == 0)
        def _():
            send_ref[0:width, :] = dst_part
            keep_ref[0:width, :] = src_part

        @pl.when(sub == 1)
        def _():
            send_ref[0:width, :] = src_part
            keep_ref[0:width, :] = dst_part

        halo = back.shape[0] // 4
        send_ref[width : width + TAIL, :] = tail
        keep_ref[width:, :] = tail
        send_ref[width + TAIL :, :] = back[2 * halo :]
        back_scratch[...] = back[: 2 * halo]
        out_scratch[...] = out_part
        strip = hid // len(out_refs)
        for k, ref in enumerate(out_refs):
            start = pl.multiple_of((mesh ^ k) * strip, strip)
            ref[0:strip, :] = out_scratch[pl.ds(start, strip), :]
            if k % 2 == 1:
                slot = (mesh + (k // 2) + 1) % 2
                start = pl.multiple_of(slot * halo, halo)
                rows_back = back_scratch[pl.ds(start, halo), :]
                ref[strip:, 0:hid] = rows_back[: halo // 2]
                ref[strip:, hid:] = rows_back[halo // 2 :]
        return

    message_ref, *back_refs = message_refs
    at = 0
    for ref in back_refs:
        ref[...] = back[at : at + ref.shape[0]]
        at += ref.shape[0]
    blocks = [src_part, dst_part]
    for at in range(0, width, hid):
        blocks.append(out_part[:, at : at + hid])
    done = 0
    for block in blocks:
        at = 0
        while at < block.shape[0]:
            peer, offset = divmod(done, chunk)
            take = min(chunk - offset, block.shape[0] - at)
            message_ref[peer, offset : offset + take, :] = block[at : at + take]
            at += take
            done += take
    while done < peers * chunk:
        peer, offset = divmod(done, chunk)
        take = chunk - offset
        message_ref[peer, offset : offset + take, :] = jnp.zeros((take, hid), bf16)
        done += take
    for peer in range(peers):
        message_ref[peer, chunk:, :] = tail


def tail_of(vectors):
    tail = []
    for v in vectors:
        high = v.astype(bf16).astype(f32)
        tail += [high, v - high]
    tail.append(jnp.zeros((TAIL - len(tail), vectors[0].shape[1]), f32))
    return jnp.concatenate(tail, axis=0).astype(bf16)


def tree(terms):
    while len(terms) > 1:
        terms = [terms[i] + terms[i + 1] for i in range(0, len(terms), 2)]
    return terms[0]


def turn_kernel(count, arrived_ref, keep_ref, *refs):
    *line_refs, scratch = refs
    mesh = lax.axis_index("mesh")
    full = keep_ref.shape[0]
    total = keep_ref[...].astype(f32) + arrived_ref[0:full, :].astype(f32)
    rows = full - TAIL
    strip = rows // count
    tail = total[rows:]
    tail = tail_of([tail[at : at + 1] + tail[at + 1 : at + 2] for at in range(0, 6, 2)])
    scratch[...] = total[:rows].astype(bf16)
    for k, ref in enumerate(line_refs):
        start = pl.multiple_of((mesh ^ k) * strip, strip)
        ref[0:strip, :] = scratch[pl.ds(start, strip), :]
        ref[strip:, :] = tail


def line_kernel(*refs):
    *terms, out_ref = refs
    rows = out_ref.shape[0]
    out_ref[...] = tree([r[0:rows, :].astype(f32) for r in terms]).astype(bf16)


def pair_kernel(a_ref, b_ref, out_ref):
    out_ref[...] = (a_ref[...].astype(f32) + b_ref[...].astype(f32)).astype(bf16)


def own_kernel(*refs):
    *terms, own_ref, bias_ref, gain_ref = refs
    total = tree([r[...].astype(f32) for r in terms])
    strip = own_ref.shape[0]
    own_ref[...] = total[:strip].astype(bf16)
    write_vectors(total[strip:], bias_ref, gain_ref)


def write_vectors(tail, bias_ref, gain_ref):
    bias_ref[...] = tail[0:1] + tail[1:2]
    hid = tail.shape[1]
    for k in range(gain_ref.shape[1] // hid):
        gain_ref[:, k * hid : (k + 1) * hid] = tail[2 + 2 * k : 3 + 2 * k] + tail[3 + 2 * k : 4 + 2 * k]


def place_kernel(count, *refs):
    mine, theirs, outs = refs[:count], refs[count : 2 * count], refs[2 * count : 3 * count]
    src_ref, dst_ref, out_ref = refs[3 * count :]
    first = lax.axis_index("sub") == 0
    mesh = lax.axis_index("mesh")
    strip = mine[0].shape[0]
    narrow = outs[0].shape[0]
    for k in range(count):
        a, b = mine[k][...], theirs[k][...]
        start = pl.multiple_of((mesh ^ k) * strip, strip)
        src_ref[pl.ds(start, strip), :] = jnp.where(first, a, b).astype(f32)
        dst_ref[pl.ds(start, strip), :] = jnp.where(first, b, a).astype(f32)
        start = pl.multiple_of((mesh ^ k) * narrow, narrow)
        out_ref[pl.ds(start, narrow), :] = outs[k][...].astype(f32)


def sum_kernel(chunk, arrived_ref, out_ref, bias_ref, gain_ref):
    peers = arrived_ref.shape[0]
    total = arrived_ref[0].astype(f32)
    for peer in range(1, peers):
        total += arrived_ref[peer].astype(f32)
    low = total[:chunk].astype(bf16)
    for peer in range(peers):
        out_ref[peer] = low
    tail = total[chunk:]
    write_vectors(tail, bias_ref, gain_ref)


def unpack_kernel(arrived_ref, src_ref, dst_ref, out_ref):
    hid = src_ref.shape[1]
    rows = src_ref.shape[0]
    src_ref[...] = arrived_ref[0:rows, :].astype(f32)
    dst_ref[...] = arrived_ref[rows : 2 * rows, :].astype(f32)
    at = 2 * rows
    for k in range(out_ref.shape[1] // hid):
        out_ref[:, k * hid : (k + 1) * hid] = arrived_ref[at : at + out_ref.shape[0], :].astype(f32)
        at += out_ref.shape[0]


def node_part(send_ref, local_ref, target_ref, w_src_ref, w_dst_ref, returned, out_ref):
    rows = local_ref.shape[0]
    halo = send_ref.shape[2]
    picks = [one_hot(iota((rows, halo), 0) == send_ref[0, d : d + 1, :]) for d in range(4)]
    total = local_ref[...] + dot(jnp.concatenate(picks, axis=1), jnp.concatenate(returned, axis=0))
    out_ref[...] = (
        dot(total.astype(bf16), w_src_ref[...], NT) + dot(target_ref[...], w_dst_ref[...], NT)
    ).astype(bf16)


def node_kernel(send_ref, local_ref, target_ref, w_src_ref, w_dst_ref, *rest):
    *back_refs, out_ref = rest
    returned = [r[...] for r in back_refs]
    node_part(send_ref, local_ref, target_ref, w_src_ref, w_dst_ref, returned, out_ref)


def paired_node_kernel(
    send_ref, local_ref, target_ref, w_src_ref, w_dst_ref, three_ref, one_ref, pair_ref, out_ref
):
    even = lax.axis_index("mesh") % 2 == 0
    halo = send_ref.shape[2]
    hid = local_ref.shape[1]
    at = one_ref.shape[0] - halo // 2
    one, three = [
        jnp.concatenate([r[at:, :hid], r[at:, hid:]], axis=0) for r in (one_ref, three_ref)
    ]
    returned = [
        jnp.where(even, one, three), jnp.where(even, three, one), pair_ref[pair_ref.shape[0] - 2 * halo :, :]
    ]
    node_part(send_ref, local_ref, target_ref, w_src_ref, w_dst_ref, returned, out_ref)


def finish_kernel(cot_ref, own_ref, other_ref, out_ref):
    out_ref[...] = cot_ref[...].astype(f32) + (
        own_ref[...].astype(f32) + other_ref[...].astype(f32)
    )


VMEM = pl.BlockSpec(memory_space=pltpu.VMEM)
SMEM = pl.BlockSpec(memory_space=pltpu.SMEM)
HBM = pl.BlockSpec(memory_space=pltpu.HBM)


def shape(dims, dtype):
    return jax.ShapeDtypeStruct(dims, dtype)


def call(kernel, outs, *args, specs=None, flops=10**8, scratch=()):
    return pl.pallas_call(
        kernel,
        out_shape=outs,
        in_specs=specs or [VMEM] * len(args),
        out_specs=jax.tree.map(lambda _: VMEM, outs),
        scratch_shapes=scratch,
        compiler_params=pltpu.CompilerParams(vmem_limit_bytes=VMEM_LIMIT),
        cost_estimate=pl.CostEstimate(flops=flops, bytes_accessed=10**6, transcendentals=0),
    )(*args)


def shifted(x, axis, by):
    count = lax.axis_size(axis)
    return lax.ppermute(x, axis, [(i, (i + by) % count) for i in range(count)])


def across(x, axis, k):
    count = lax.axis_size(axis)
    return lax.ppermute(x, axis, [(i, i ^ k) for i in range(count)])


def gather_line(x, lines):
    three = across(x, "mesh", 3)
    one = across(x, "mesh", 1)
    return [x, one, across(three, "mesh", 1), three]


def paired_sums(messages, lines, strip, narrow, width, hid):
    send, keep, *outs = messages
    order = range(lines - 1, 0, -1)
    out_terms = {k: across(outs[k], "mesh", k) for k in order}
    arrived = across(send, "sub", 1)
    line = call(
        functools.partial(turn_kernel, lines),
        [shape((strip + TAIL, hid), bf16)] * lines,
        arrived, keep,
        scratch=[pltpu.VMEM((width, hid), bf16)],
    )
    line_terms = {k: across(line[k], "mesh", k) for k in order}
    quarter = call(
        line_kernel, shape((narrow, width), bf16), *[out_terms[k] for k in order], outs[0]
    )
    quarter = call(pair_kernel, shape((narrow, width), bf16), quarter, across(quarter, "sub", 1))
    own, bias_grad, gain_grad = call(
        own_kernel,
        [shape((strip, hid), bf16), shape((1, hid), f32), shape((1, width), f32)],
        *[line_terms[k] for k in order], line[0],
    )
    out = gather_line(quarter, lines)
    mine = gather_line(own, lines)
    theirs = [across(x, "sub", 1) for x in mine]
    grads = call(
        functools.partial(place_kernel, lines),
        [shape((width, hid), f32), shape((width, hid), f32), shape((hid, width), f32)],
        *mine, *theirs, *out,
    )
    return (*grads, bias_grad, gain_grad), (out_terms[3], out_terms[1], arrived)


def shards(
    node_state,
    send_rows,
    edge_src,
    edge_dst,
    block_count,
    w_src,
    w_dst,
    hidden_bias,
    w_out,
    norm_gain,
    cotangent,
):
    rows, width = node_state.shape
    hid = w_src.shape[1]
    halo = send_rows.shape[2]
    edges = edge_src.shape[0]
    peers = lax.axis_size("mesh") * lax.axis_size("sub")
    merged = lax.axis_size("sub") == 2
    total_rows = 2 * width + (width // hid) * hid
    chunk = -(-total_rows // (peers * 16)) * 16

    piece = [halo, halo, 2 * halo] if merged else [halo] * 4
    routes = [("mesh", 1), ("mesh", -1), ("sub", 1)] + ([] if merged else [("sub", -1)])
    n_halo = len(piece)

    operands = [
        node_state, send_rows, edge_src.reshape(1, edges), edge_dst.reshape(1, edges),
        hidden_bias.reshape(1, hid), w_src, w_dst, w_out, norm_gain.reshape(1, width), cotangent,
    ]
    node, send, src, dst, bias, w_src, w_dst, w_out, gain, cot, *outgoing = call(
        send_kernel,
        [shape(x.shape, x.dtype) for x in operands] + [shape((n, width), bf16) for n in piece],
        *[pltpu.with_memory_space_constraint(x, pltpu.HBM) for x in operands],
        specs=[HBM] * len(operands),
        scratch=[pltpu.SemaphoreType.DMA((N_OPERANDS,))],
    )
    arrived = [shifted(x, axis, by) for x, (axis, by) in zip(outgoing, routes)]

    pre, pick, collect, spread, scatter = call(
        local_kernel,
        [
            shape((edges, hid), f32),
            shape((edges, 4 * halo), bf16),
            shape((rows, edges), bf16),
            shape((edges, rows), bf16),
            shape((rows + 4 * halo, edges), bf16),
        ],
        block_count, node, src, dst, bias, w_src, w_dst,
        specs=[SMEM] + [VMEM] * 6,
    )

    factor, hidden, partial = call(
        forward_kernel,
        [shape((edges, hid), f32), shape((rows, hid), bf16), shape((rows, width), bf16)],
        pre, pick, collect, w_src, w_out, *arrived,
    )
    other = shifted(partial, "lat", 1)

    lines = lax.axis_size("mesh")
    paired = merged and lines == 4
    if paired:
        strip = width // lines
        narrow = hid // lines
        message_shapes = [shape((width + TAIL + 2 * halo, hid), bf16), shape((width + TAIL, hid), bf16)]
        message_shapes += [shape((narrow + k % 2 * (halo // 2), width), bf16) for k in range(lines)]
    else:
        message_shapes = [shape((peers, chunk + TAIL, hid), bf16)]
        message_shapes += [shape((n, hid), bf16) for n in piece]
    updated, local, target, *messages = call(
        functools.partial(backward_kernel, (peers, chunk, n_halo, paired)),
        [shape((rows, width), bf16), shape((rows, hid), f32), shape((rows, hid), bf16)]
        + message_shapes,
        node, collect, spread, scatter, w_out, gain, cot, factor, hidden, partial, other, *arrived,
        scratch=[pltpu.VMEM((hid, width), bf16), pltpu.VMEM((2 * halo, hid), bf16)],
    )

    if paired:
        (src_grad, dst_grad, out_grad, bias_grad, gain_grad), returned = paired_sums(
            messages, lines, strip, narrow, width, hid
        )
    else:
        returned = [shifted(x, axis, -by) for x, (axis, by) in zip(messages[1:], routes)]
        exchanged = lax.all_to_all(messages[0], ("mesh", "sub"), 0, 0)
        reduced, bias_grad, gain_grad = call(
            functools.partial(sum_kernel, chunk),
            [shape((peers, chunk, hid), bf16), shape((1, hid), f32), shape((1, width), f32)],
            exchanged,
        )
        gathered = lax.all_to_all(reduced, ("mesh", "sub"), 0, 0)
        src_grad, dst_grad, out_grad = call(
            unpack_kernel,
            [shape((width, hid), f32), shape((width, hid), f32), shape((hid, width), f32)],
            gathered.reshape(peers * chunk, hid),
        )
    node_part = call(
        paired_node_kernel if paired else node_kernel,
        shape((rows, width), bf16),
        send, local, target, w_src, w_dst, *returned,
    )
    node_grad = call(
        finish_kernel, shape((rows, width), f32), cot, node_part, shifted(node_part, "lat", 1)
    )
    return (
        updated, node_grad, src_grad, dst_grad, out_grad,
        bias_grad.reshape(hid), gain_grad.reshape(width),
    )


def solution(mesh):
    nodes = P(("parts", "mesh", "sub"), None)
    slots = P(("parts", "mesh", "sub"))
    in_specs = (
        nodes,
        P(("parts", "mesh", "sub"), None, None),
        slots,
        slots,
        slots,
        P(None, "lat"),
        P(None, "lat"),
        P("lat"),
        P("lat", None),
        P(),
        nodes,
    )
    out_specs = (
        nodes,
        nodes,
        P("parts", "lat"),
        P("parts", "lat"),
        P(("parts", "lat"), None),
        P(("parts", "lat")),
        P("parts"),
    )
    return jax.shard_map(shards, mesh=mesh, in_specs=in_specs, out_specs=out_specs, check_vma=False)
```

```python
import functools

import jax
import jax.numpy as jnp
from jax import lax
from jax.experimental import pallas as pl
from jax.experimental.pallas import tpu as pltpu
from jax.sharding import PartitionSpec as P

BLOCK = 128
EPSILON = 1e-05
TAIL = 16
N_FETCHED = 9
VMEM_LIMIT = 24 * 1024 * 1024

f32 = jnp.float32
bf16 = jnp.bfloat16

NN = (((1,), (0,)), ((), ()))
NT = (((1,), (1,)), ((), ()))
TN = (((0,), (0,)), ((), ()))


def dot(a, b, dims=NN):
    return lax.dot_general(a, b, dims, preferred_element_type=f32)


def iota(shape, dim):
    return lax.broadcasted_iota(jnp.int32, shape, dim)


def one_hot(condition):
    return jnp.where(condition, 1.0, 0.0).astype(bf16)


def split(x):
    high = x.astype(bf16)
    return high, (x - high.astype(f32)).astype(bf16)


def columns_of(row, lanes):
    return jnp.transpose(jnp.broadcast_to(row, (lanes, row.shape[1])))


def usable_row(count_ref, edges):
    lane = iota((1, BLOCK), 1)
    parts = [lane < count_ref[b] for b in range(edges // BLOCK)]
    return jnp.concatenate([jnp.where(p, 1, 0) for p in parts], axis=1)


def usable_columns(count_ref, edges, lanes):
    sub = iota((BLOCK, lanes), 0)
    return jnp.concatenate(
        [jnp.where(sub < count_ref[b], 1, 0) for b in range(edges // BLOCK)], axis=0
    )


def fetch(sems, *pairs):
    copies = [pltpu.make_async_copy(a, b, sems.at[i]) for i, (a, b) in enumerate(pairs)]
    for copy in copies:
        copy.start()
    return copies


def send_kernel(node_hbm, send_hbm, node_ref, send_ref, *rest):
    *out_refs, sems = rest
    for copy in fetch(sems, (node_hbm, node_ref), (send_hbm, send_ref)):
        copy.wait()
    node = node_ref[...]
    rows = node.shape[0]
    halo = send_ref.shape[2]
    pieces = []
    for d in range(4):
        pick = one_hot(iota((rows, halo), 0) == send_ref[0, d : d + 1, :])
        pieces.append(dot(pick, node, TN).astype(bf16))
    out_refs[0][...] = pieces[0]
    out_refs[1][...] = pieces[1]
    if len(out_refs) == 3:
        out_refs[2][0:halo, :] = pieces[2]
        out_refs[2][halo:, :] = pieces[3]
    else:
        out_refs[2][...] = pieces[2]
        out_refs[3][...] = pieces[3]


def local_kernel(*refs):
    node_ref, ins, refs = refs[0], refs[1 : 1 + N_FETCHED], refs[1 + N_FETCHED :]
    pre_ref, pick_ref, collect_ref, spread_ref, scatter_ref, *refs = refs
    w_src_ref, w_dst_ref, w_out_ref, gain_ref, cot_ref, count_ref, src_ref, dst_ref, bias_ref, sems = refs
    outs = (src_ref, dst_ref, count_ref, bias_ref, w_src_ref, w_dst_ref, w_out_ref, gain_ref, cot_ref)
    copies = fetch(sems, *zip(ins, outs))
    node = node_ref[...]
    rows = node.shape[0]
    edges = src_ref.shape[1]
    for copy in copies[:3]:
        copy.wait()
    scatter_ref[...] = one_hot(iota(scatter_ref.shape, 0) == src_ref[...])
    used = usable_row(count_ref, edges) > 0
    collect_ref[...] = one_hot((iota((rows, edges), 0) == dst_ref[...]) & used)
    source = columns_of(src_ref[...], 128)
    target = columns_of(dst_ref[...], 128)
    lane = iota(source.shape, 1)
    used = usable_columns(count_ref, edges, 128) > 0
    near = one_hot(source == lane)
    pick_ref[...] = one_hot(source == lane + rows)
    spread_ref[...] = one_hot((target == lane) & used)
    both = jnp.concatenate([dot(near, node), dot(one_hot(target == lane), node)], axis=1).astype(bf16)
    for copy in copies[3:]:
        copy.wait()
    weights = jnp.concatenate([w_src_ref[...], w_dst_ref[...]], axis=0)
    pre_ref[...] = dot(both, weights) + bias_ref[...]


def twice(x):
    return jnp.concatenate([x, x], axis=1)


def stacked(x):
    return jnp.concatenate(split(x), axis=0)


def forward_kernel(pre_ref, pick_ref, collect_ref, w_src_ref, w_out_ref, *rest):
    *halo_refs, factor_ref, hidden_ref, partial_ref = rest
    halo = jnp.concatenate([r[...] for r in halo_refs], axis=0)
    far = stacked(dot(halo, w_src_ref[...]))
    pre = pre_ref[...] + dot(twice(pick_ref[...]), far)
    sig = 0.5 + 0.5 * jnp.tanh(0.5 * pre)
    factor_ref[...] = sig * (1.0 + pre * (1.0 - sig))
    hidden = dot(collect_ref[...], (pre * sig).astype(bf16))
    high, low = split(hidden)
    hidden_ref[...] = high
    w_out = w_out_ref[...]
    partial_ref[...] = (dot(high, w_out) + dot(low, w_out)).astype(bf16)


def backward_kernel(
    geometry,
    node_ref, collect_ref, spread_ref, scatter_ref, w_out_ref, gain_ref, cot_ref,
    factor_ref, hidden_ref, own_ref, other_ref,
    *rest,
):
    peers, chunk, n_halo, paired = geometry
    *rest, out_scratch, back_scratch, pair_scratch = rest
    halo_refs = rest[:n_halo]
    normed_ref, local_ref, target_ref, *message_refs = rest[n_halo:]
    node = node_ref[...]
    rows, width = node.shape
    aggregate = own_ref[...].astype(f32) + other_ref[...].astype(f32)
    center = aggregate - jnp.mean(aggregate, axis=1, keepdims=True)
    variance = jnp.mean(center * center, axis=1, keepdims=True)
    inverse = lax.rsqrt(variance + EPSILON)
    normed = center * inverse
    gain = gain_ref[...]
    upstream = cot_ref[...].astype(f32)
    scaled = upstream * gain
    agg_grad = inverse * (
        scaled
        - jnp.mean(scaled, axis=1, keepdims=True)
        - normed * jnp.mean(scaled * normed, axis=1, keepdims=True)
    )
    agg_grad = agg_grad.astype(bf16)
    normed_ref[...] = normed
    gain_part = jnp.sum(upstream * normed, axis=0, keepdims=True)

    act_grad = dot(twice(spread_ref[...]), stacked(dot(agg_grad, w_out_ref[...], NT)))
    pre_grad = (act_grad * factor_ref[...]).astype(bf16)

    table = jnp.concatenate([node] + [r[...] for r in halo_refs], axis=0)
    by_source = dot(scatter_ref[...], pre_grad)
    by_target = dot(collect_ref[...], pre_grad)
    local_ref[...] = by_source[:rows]
    by_target_low = by_target.astype(bf16)
    by_source_low = by_source.astype(bf16)
    target_ref[...] = by_target_low

    hid = by_source.shape[1]
    bias_part = jnp.sum(by_target, axis=0, keepdims=True)
    src_part = dot(table, by_source_low, TN).astype(bf16)
    dst_part = dot(node, by_target_low, TN).astype(bf16)
    out_part = dot(hidden_ref[...], agg_grad, TN).astype(bf16)
    vectors = [bias_part] + [gain_part[:, at : at + hid] for at in range(0, width, hid)]
    tail = tail_of(vectors)
    back = by_source_low[rows:]

    if paired:
        far_send_ref, far_keep_ref, near_send_ref, near_keep_ref, *out_refs = message_refs
        sub = lax.axis_index("sub")
        mesh = lax.axis_index("mesh")
        lines = len(out_refs)
        halo = back.shape[0] // 4
        first = sub == 0
        pair_scratch[0] = jnp.where(first, dst_part, src_part)
        pair_scratch[1] = jnp.where(first, src_part, dst_part)
        strip = width // lines
        for slot, far_ref, near_ref in ((0, far_send_ref, near_send_ref), (1, far_keep_ref, near_keep_ref)):
            for at, k in enumerate((3, 2, 1, 0)):
                start = pl.multiple_of((mesh ^ k) * strip, strip)
                ref = far_ref if at < 2 else near_ref
                ref[at % 2 * strip : (at % 2 + 1) * strip, :] = pair_scratch[slot, pl.ds(start, strip), :]
            far_ref[2 * strip : 2 * strip + TAIL, :] = tail
        far_send_ref[2 * strip + TAIL :, :] = back[2 * halo :]
        back_scratch[...] = back[: 2 * halo]
        out_scratch[...] = out_part
        strip = hid // len(out_refs)
        for k, ref in enumerate(out_refs):
            start = pl.multiple_of((mesh ^ k) * strip, strip)
            ref[0:strip, :] = out_scratch[pl.ds(start, strip), :]
            if k % 2 == 1:
                slot = (mesh + (k // 2) + 1) % 2
                start = pl.multiple_of(slot * halo, halo)
                rows_back = back_scratch[pl.ds(start, halo), :]
                ref[strip:, 0:hid] = rows_back[: halo // 2]
                ref[strip:, hid:] = rows_back[halo // 2 :]
        return

    message_ref, *back_refs = message_refs
    at = 0
    for ref in back_refs:
        ref[...] = back[at : at + ref.shape[0]]
        at += ref.shape[0]
    blocks = [src_part, dst_part]
    for at in range(0, width, hid):
        blocks.append(out_part[:, at : at + hid])
    done = 0
    for block in blocks:
        at = 0
        while at < block.shape[0]:
            peer, offset = divmod(done, chunk)
            take = min(chunk - offset, block.shape[0] - at)
            message_ref[peer, offset : offset + take, :] = block[at : at + take]
            at += take
            done += take
    while done < peers * chunk:
        peer, offset = divmod(done, chunk)
        take = chunk - offset
        message_ref[peer, offset : offset + take, :] = jnp.zeros((take, hid), bf16)
        done += take
    for peer in range(peers):
        message_ref[peer, chunk:, :] = tail


def tail_of(vectors):
    tail = []
    for v in vectors:
        high = v.astype(bf16).astype(f32)
        tail += [high, v - high]
    tail.append(jnp.zeros((TAIL - len(tail), vectors[0].shape[1]), f32))
    return jnp.concatenate(tail, axis=0).astype(bf16)


def tree(terms):
    while len(terms) > 1:
        terms = [terms[i] + terms[i + 1] for i in range(0, len(terms), 2)]
    return terms[0]


def far_kernel(arrived_ref, keep_ref, three_ref, two_ref, tail_ref):
    full = keep_ref.shape[0]
    total = keep_ref[...].astype(f32) + arrived_ref[0:full, :].astype(f32)
    strip = three_ref.shape[0] - TAIL
    tail = total[2 * strip :]
    tail = tail_of([tail[at : at + 1] + tail[at + 1 : at + 2] for at in range(0, 6, 2)])
    for k, ref in enumerate((three_ref, two_ref)):
        ref[0:strip, :] = total[k * strip : (k + 1) * strip].astype(bf16)
        ref[strip:, :] = tail
    tail_ref[...] = tail


def near_kernel(arrived_ref, keep_ref, tail_ref, one_ref, zero_ref):
    full = keep_ref.shape[0]
    total = (keep_ref[...].astype(f32) + arrived_ref[...].astype(f32)).astype(bf16)
    strip = full // 2
    for k, ref in enumerate((one_ref, zero_ref)):
        ref[0:strip, :] = total[k * strip : (k + 1) * strip]
        ref[strip:, :] = tail_ref[...]


def line_kernel(*refs):
    *terms, _, send_ref, keep_ref = refs
    rows, hid = send_ref.shape
    total = tree([r[0:rows, :].astype(f32) for r in terms])
    first = lax.axis_index("sub") == 0
    left, right = total[:, :hid], total[:, hid:]
    send_ref[...] = jnp.where(first, right, left).astype(bf16)
    keep_ref[...] = jnp.where(first, left, right).astype(bf16)


def own_kernel(*refs):
    *terms, out_keep_ref, out_arrived_ref, _, own_ref, tail_ref = refs
    total = tree([r[...].astype(f32) for r in terms])
    strip = own_ref.shape[0] - out_keep_ref.shape[0]
    own_ref[0:strip, :] = total[:strip].astype(bf16)
    own_ref[strip:, :] = (
        out_keep_ref[...].astype(f32) + out_arrived_ref[...].astype(f32)
    ).astype(bf16)
    tail_ref[...] = total[strip:]


def write_vectors(tail, bias_ref, gain_ref):
    bias_ref[...] = tail[0:1] + tail[1:2]
    hid = tail.shape[1]
    for k in range(gain_ref.shape[1] // hid):
        gain_ref[:, k * hid : (k + 1) * hid] = tail[2 + 2 * k : 3 + 2 * k] + tail[3 + 2 * k : 4 + 2 * k]


def place_kernel(count, tail_ref, *refs):
    mine, theirs = refs[:count], refs[count : 2 * count]
    src_hbm, dst_hbm, out_hbm, bias_ref, gain_ref, src_ref, dst_ref, out_ref, sems = refs[2 * count :]
    first = lax.axis_index("sub") == 0
    mesh = lax.axis_index("mesh")
    strip, hid = src_ref.shape[1:]
    narrow = out_ref.shape[1]
    copies = []

    def put(ref, hbm, k, rows):
        start = pl.multiple_of((mesh ^ k) * rows, rows)
        copies.append(pltpu.make_async_copy(ref.at[k], hbm.at[pl.ds(start, rows)], sems.at[len(copies)]))
        copies[-1].start()

    for k in range(count):
        a, b = mine[k][...], theirs[k][...]
        low = jnp.where(first, a, b).astype(f32)
        high = jnp.where(first, b, a).astype(f32)
        src_ref[k] = low[:strip]
        put(src_ref, src_hbm, k, strip)
        dst_ref[k] = high[:strip]
        put(dst_ref, dst_hbm, k, strip)
        out_ref[k, :, 0:hid] = low[strip:]
        out_ref[k, :, hid:] = high[strip:]
        put(out_ref, out_hbm, k, narrow)
    write_vectors(tail_ref[...], bias_ref, gain_ref)
    for copy in copies:
        copy.wait()


def sum_kernel(chunk, arrived_ref, out_ref, bias_ref, gain_ref):
    peers = arrived_ref.shape[0]
    total = arrived_ref[0].astype(f32)
    for peer in range(1, peers):
        total += arrived_ref[peer].astype(f32)
    low = total[:chunk].astype(bf16)
    for peer in range(peers):
        out_ref[peer] = low
    tail = total[chunk:]
    write_vectors(tail, bias_ref, gain_ref)


def unpack_kernel(arrived_ref, src_ref, dst_ref, out_ref):
    hid = src_ref.shape[1]
    rows = src_ref.shape[0]
    src_ref[...] = arrived_ref[0:rows, :].astype(f32)
    dst_ref[...] = arrived_ref[rows : 2 * rows, :].astype(f32)
    at = 2 * rows
    for k in range(out_ref.shape[1] // hid):
        out_ref[:, k * hid : (k + 1) * hid] = arrived_ref[at : at + out_ref.shape[0], :].astype(f32)
        at += out_ref.shape[0]


def node_part(send_ref, local_ref, target_ref, w_src_ref, w_dst_ref, returned, out_ref):
    rows = local_ref.shape[0]
    halo = send_ref.shape[2]
    picks = [one_hot(iota((rows, halo), 0) == send_ref[0, d : d + 1, :]) for d in range(4)]
    total = local_ref[...] + dot(jnp.concatenate(picks, axis=1), jnp.concatenate(returned, axis=0))
    out_ref[...] = (
        dot(total.astype(bf16), w_src_ref[...], NT) + dot(target_ref[...], w_dst_ref[...], NT)
    ).astype(bf16)


def node_kernel(send_ref, local_ref, target_ref, w_src_ref, w_dst_ref, *rest):
    *back_refs, out_ref = rest
    returned = [r[...] for r in back_refs]
    node_part(send_ref, local_ref, target_ref, w_src_ref, w_dst_ref, returned, out_ref)


def paired_node_kernel(
    send_ref, local_ref, target_ref, w_src_ref, w_dst_ref, three_ref, one_ref, pair_ref, out_ref
):
    even = lax.axis_index("mesh") % 2 == 0
    halo = send_ref.shape[2]
    hid = local_ref.shape[1]
    at = one_ref.shape[0] - halo // 2
    one, three = [
        jnp.concatenate([r[at:, :hid], r[at:, hid:]], axis=0) for r in (one_ref, three_ref)
    ]
    returned = [
        jnp.where(even, one, three), jnp.where(even, three, one), pair_ref[pair_ref.shape[0] - 2 * halo :, :]
    ]
    node_part(send_ref, local_ref, target_ref, w_src_ref, w_dst_ref, returned, out_ref)


def finish_kernel(cot_ref, node_ref, gain_ref, normed_ref, own_ref, other_ref, grad_ref, updated_ref):
    grad_ref[...] = cot_ref[...].astype(f32) + (
        own_ref[...].astype(f32) + other_ref[...].astype(f32)
    )
    updated_ref[...] = (node_ref[...].astype(f32) + gain_ref[...] * normed_ref[...]).astype(bf16)


VMEM = pl.BlockSpec(memory_space=pltpu.VMEM)
SMEM = pl.BlockSpec(memory_space=pltpu.SMEM)
HBM = pl.BlockSpec(memory_space=pltpu.HBM)


def shape(dims, dtype):
    return jax.ShapeDtypeStruct(dims, dtype)


def call(kernel, outs, *args, specs=None, out_specs=None, flops=10**8, scratch=()):
    return pl.pallas_call(
        kernel,
        out_shape=outs,
        in_specs=specs or [VMEM] * len(args),
        out_specs=out_specs or jax.tree.map(lambda _: VMEM, outs),
        scratch_shapes=scratch,
        compiler_params=pltpu.CompilerParams(vmem_limit_bytes=VMEM_LIMIT),
        cost_estimate=pl.CostEstimate(flops=flops, bytes_accessed=10**6, transcendentals=0),
    )(*args)


def shifted(x, axis, by):
    count = lax.axis_size(axis)
    return lax.ppermute(x, axis, [(i, (i + by) % count) for i in range(count)])


def across(x, axis, k):
    count = lax.axis_size(axis)
    return lax.ppermute(x, axis, [(i, i ^ k) for i in range(count)])


def paired_sums(messages, lines, strip, narrow, width, hid, node_terms):
    far_send, far_keep, near_send, near_keep, *outs = messages
    order = range(lines - 1, 0, -1)
    block = shape((strip + TAIL, hid), bf16)
    far = across(far_send, "sub", 1)
    out_terms = {k: across(outs[k], "mesh", k) for k in order}
    near = across(near_send, "sub", 1)
    line = {}
    line[3], line[2], tail = call(far_kernel, [block, block, shape((TAIL, hid), bf16)], far, far_keep)
    line[1], line[0] = call(near_kernel, [block, block], near, near_keep, tail)
    line_terms = {k: across(line[k], "mesh", k) for k in order}
    out_send, out_keep = call(
        line_kernel,
        [shape((narrow, hid), bf16)] * 2,
        *[out_terms[k] for k in order], outs[0], line_terms[3],
    )
    node_part = node_terms(out_terms[3], out_terms[1], far)
    own, tail = call(
        own_kernel,
        [shape((strip + narrow, hid), bf16), shape((TAIL, hid), f32)],
        *[line_terms[k] for k in order], line[0], out_keep, across(out_send, "sub", 1),
        node_part,
    )
    mine = {k: across(own, "mesh", k) for k in order}
    mine[0] = own
    theirs = {k: across(mine[k], "sub", 1) for k in (0, 1, 3, 2)}
    grads = call(
        functools.partial(place_kernel, lines),
        [
            shape((width, hid), f32), shape((width, hid), f32), shape((hid, width), f32),
            shape((1, hid), f32), shape((1, width), f32),
        ],
        tail, *[mine[k] for k in range(lines)], *[theirs[k] for k in range(lines)],
        out_specs=[HBM] * 3 + [VMEM] * 2,
        scratch=[
            pltpu.VMEM((lines, strip, hid), f32),
            pltpu.VMEM((lines, strip, hid), f32),
            pltpu.VMEM((lines, narrow, width), f32),
            pltpu.SemaphoreType.DMA((3 * lines,)),
        ],
    )
    return grads, node_part


def shards(
    node_state,
    send_rows,
    edge_src,
    edge_dst,
    block_count,
    w_src,
    w_dst,
    hidden_bias,
    w_out,
    norm_gain,
    cotangent,
):
    rows, width = node_state.shape
    hid = w_src.shape[1]
    halo = send_rows.shape[2]
    edges = edge_src.shape[0]
    peers = lax.axis_size("mesh") * lax.axis_size("sub")
    merged = lax.axis_size("sub") == 2
    total_rows = 2 * width + (width // hid) * hid
    chunk = -(-total_rows // (peers * 16)) * 16

    piece = [halo, halo, 2 * halo] if merged else [halo] * 4
    routes = [("mesh", 1), ("mesh", -1), ("sub", 1)] + ([] if merged else [("sub", -1)])
    n_halo = len(piece)

    def in_hbm(x):
        return pltpu.with_memory_space_constraint(x, pltpu.HBM)

    node, send, *outgoing = call(
        send_kernel,
        [shape((rows, width), bf16), shape(send_rows.shape, jnp.int32)]
        + [shape((n, width), bf16) for n in piece],
        in_hbm(node_state), in_hbm(send_rows),
        specs=[HBM, HBM],
        scratch=[pltpu.SemaphoreType.DMA((2,))],
    )
    arrived = [shifted(x, axis, by) for x, (axis, by) in zip(outgoing, routes)]

    fetched = [
        edge_src.reshape(1, edges), edge_dst.reshape(1, edges), block_count,
        hidden_bias.reshape(1, hid), w_src, w_dst, w_out, norm_gain.reshape(1, width), cotangent,
    ]
    pre, pick, collect, spread, scatter, w_src, w_dst, w_out, gain, cot = call(
        local_kernel,
        [
            shape((edges, hid), f32),
            shape((edges, 4 * halo), bf16),
            shape((rows, edges), bf16),
            shape((edges, rows), bf16),
            shape((rows + 4 * halo, edges), bf16),
        ]
        + [shape(x.shape, x.dtype) for x in fetched[4:]],
        node, *[in_hbm(x) for x in fetched],
        specs=[VMEM] + [HBM] * len(fetched),
        scratch=[
            pltpu.SMEM(block_count.shape, jnp.int32),
            pltpu.VMEM((1, edges), jnp.int32),
            pltpu.VMEM((1, edges), jnp.int32),
            pltpu.VMEM((1, hid), f32),
            pltpu.SemaphoreType.DMA((N_FETCHED,)),
        ],
    )

    factor, hidden, partial = call(
        forward_kernel,
        [shape((edges, hid), f32), shape((rows, hid), bf16), shape((rows, width), bf16)],
        pre, pick, collect, w_src, w_out, *arrived,
    )
    other = shifted(partial, "lat", 1)

    lines = lax.axis_size("mesh")
    paired = merged and lines == 4
    if paired:
        strip = width // lines
        narrow = hid // lines
        message_shapes = [shape((2 * strip + TAIL + 2 * halo, hid), bf16), shape((2 * strip + TAIL, hid), bf16)]
        message_shapes += [shape((2 * strip, hid), bf16)] * 2
        message_shapes += [shape((narrow + k % 2 * (halo // 2), width), bf16) for k in range(lines)]
    else:
        message_shapes = [shape((peers, chunk + TAIL, hid), bf16)]
        message_shapes += [shape((n, hid), bf16) for n in piece]
    normed, local, target, *messages = call(
        functools.partial(backward_kernel, (peers, chunk, n_halo, paired)),
        [shape((rows, width), f32), shape((rows, hid), f32), shape((rows, hid), bf16)]
        + message_shapes,
        node, collect, spread, scatter, w_out, gain, cot, factor, hidden, partial, other, *arrived,
        scratch=[
            pltpu.VMEM((hid, width), bf16),
            pltpu.VMEM((2 * halo, hid), bf16),
            pltpu.VMEM((2, width, hid), bf16),
        ],
    )

    def node_terms(*returned):
        return call(
            paired_node_kernel if paired else node_kernel,
            shape((rows, width), bf16),
            send, local, target, w_src, w_dst, *returned,
        )

    if paired:
        (src_grad, dst_grad, out_grad, bias_grad, gain_grad), node_part = paired_sums(
            messages, lines, strip, narrow, width, hid, node_terms
        )
    else:
        node_part = node_terms(
            *[shifted(x, axis, -by) for x, (axis, by) in zip(messages[1:], routes)]
        )
        exchanged = lax.all_to_all(messages[0], ("mesh", "sub"), 0, 0)
        reduced, bias_grad, gain_grad = call(
            functools.partial(sum_kernel, chunk),
            [shape((peers, chunk, hid), bf16), shape((1, hid), f32), shape((1, width), f32)],
            exchanged,
        )
        gathered = lax.all_to_all(reduced, ("mesh", "sub"), 0, 0)
        src_grad, dst_grad, out_grad = call(
            unpack_kernel,
            [shape((width, hid), f32), shape((width, hid), f32), shape((hid, width), f32)],
            gathered.reshape(peers * chunk, hid),
        )
    node_grad, updated = call(
        finish_kernel,
        [shape((rows, width), f32), shape((rows, width), bf16)],
        cot, node, gain, normed, node_part, shifted(node_part, "lat", 1),
    )
    return (
        updated, node_grad, src_grad, dst_grad, out_grad,
        bias_grad.reshape(hid), gain_grad.reshape(width),
    )


def solution(mesh):
    nodes = P(("parts", "mesh", "sub"), None)
    slots = P(("parts", "mesh", "sub"))
    in_specs = (
        nodes,
        P(("parts", "mesh", "sub"), None, None),
        slots,
        slots,
        slots,
        P(None, "lat"),
        P(None, "lat"),
        P("lat"),
        P("lat", None),
        P(),
        nodes,
    )
    out_specs = (
        nodes,
        nodes,
        P("parts", "lat"),
        P("parts", "lat"),
        P(("parts", "lat"), None),
        P(("parts", "lat")),
        P("parts"),
    )
    return jax.shard_map(shards, mesh=mesh, in_specs=in_specs, out_specs=out_specs, check_vma=False)
```

```python
import functools

import jax
import jax.numpy as jnp
from jax import lax
from jax.experimental import pallas as pl
from jax.experimental.pallas import tpu as pltpu
from jax.sharding import PartitionSpec as P

BLOCK = 128
EPSILON = 1e-05
TAIL = 16
N_FETCHED = 9
VMEM_LIMIT = 24 * 1024 * 1024

f32 = jnp.float32
bf16 = jnp.bfloat16

NN = (((1,), (0,)), ((), ()))
NT = (((1,), (1,)), ((), ()))
TN = (((0,), (0,)), ((), ()))


def dot(a, b, dims=NN):
    return lax.dot_general(a, b, dims, preferred_element_type=f32)


def iota(shape, dim):
    return lax.broadcasted_iota(jnp.int32, shape, dim)


def one_hot(condition):
    return jnp.where(condition, 1.0, 0.0).astype(bf16)


def split(x):
    high = x.astype(bf16)
    return high, (x - high.astype(f32)).astype(bf16)


def columns_of(row, lanes):
    return jnp.transpose(jnp.broadcast_to(row, (lanes, row.shape[1])))


def usable_row(count_ref, edges):
    lane = iota((1, BLOCK), 1)
    parts = [lane < count_ref[b] for b in range(edges // BLOCK)]
    return jnp.concatenate([jnp.where(p, 1, 0) for p in parts], axis=1)


def usable_columns(count_ref, edges, lanes):
    sub = iota((BLOCK, lanes), 0)
    return jnp.concatenate(
        [jnp.where(sub < count_ref[b], 1, 0) for b in range(edges // BLOCK)], axis=0
    )


def fetch(sems, *pairs):
    copies = [pltpu.make_async_copy(a, b, sems.at[i]) for i, (a, b) in enumerate(pairs)]
    for copy in copies:
        copy.start()
    return copies


def send_kernel(paired, node_hbm, send_hbm, node_ref, send_ref, *rest):
    *out_refs, sems = rest
    for copy in fetch(sems, (node_hbm, node_ref), (send_hbm, send_ref)):
        copy.wait()
    node = node_ref[...]
    rows = node.shape[0]
    halo = send_ref.shape[2]
    chosen = [send_ref[0, d : d + 1, :] for d in range(4)]
    if paired:
        even = lax.axis_index("mesh") % 2 == 0
        chosen[:2] = jnp.where(even, chosen[1], chosen[0]), jnp.where(even, chosen[0], chosen[1])
    pieces = []
    for row in chosen:
        pick = one_hot(iota((rows, halo), 0) == row)
        pieces.append(dot(pick, node, TN).astype(bf16))
    out_refs[0][...] = pieces[0]
    out_refs[1][...] = pieces[1]
    if len(out_refs) == 3:
        out_refs[2][0:halo, :] = pieces[2]
        out_refs[2][halo:, :] = pieces[3]
    else:
        out_refs[2][...] = pieces[2]
        out_refs[3][...] = pieces[3]


def local_kernel(paired, *refs):
    node_ref, ins, refs = refs[0], refs[1 : 1 + N_FETCHED], refs[1 + N_FETCHED :]
    pre_ref, pick_ref, collect_ref, spread_ref, scatter_ref, *refs = refs
    w_src_ref, w_dst_ref, w_out_ref, gain_ref, cot_ref, count_ref, src_ref, dst_ref, bias_ref, sems = refs
    outs = (src_ref, dst_ref, count_ref, bias_ref, w_src_ref, w_dst_ref, w_out_ref, gain_ref, cot_ref)
    copies = fetch(sems, *zip(ins, outs))
    node = node_ref[...]
    rows = node.shape[0]
    edges = src_ref.shape[1]
    for copy in copies[:3]:
        copy.wait()
    src_row = src_ref[...]
    if paired:
        halo = (scatter_ref.shape[0] - rows) // 4
        odd = lax.axis_index("mesh") % 2 == 1
        step = jnp.where(src_row < rows + halo, halo, -halo)
        ring = (src_row >= rows) & (src_row < rows + 2 * halo)
        src_row = src_row + jnp.where(ring & odd, step, 0)
    scatter_ref[...] = one_hot(iota(scatter_ref.shape, 0) == src_row)
    used = usable_row(count_ref, edges) > 0
    collect_ref[...] = one_hot((iota((rows, edges), 0) == dst_ref[...]) & used)
    source = columns_of(src_row, 128)
    target = columns_of(dst_ref[...], 128)
    lane = iota(source.shape, 1)
    used = usable_columns(count_ref, edges, 128) > 0
    near = one_hot(source == lane)
    pick_ref[...] = one_hot(source == lane + rows)
    spread_ref[...] = one_hot((target == lane) & used)
    both = jnp.concatenate([dot(near, node), dot(one_hot(target == lane), node)], axis=1).astype(bf16)
    for copy in copies[3:]:
        copy.wait()
    weights = jnp.concatenate([w_src_ref[...], w_dst_ref[...]], axis=0)
    pre_ref[...] = dot(both, weights) + bias_ref[...]


def twice(x):
    return jnp.concatenate([x, x], axis=1)


def stacked(x):
    return jnp.concatenate(split(x), axis=0)


def forward_kernel(pre_ref, pick_ref, collect_ref, w_src_ref, w_out_ref, *rest):
    *halo_refs, factor_ref, hidden_ref, partial_ref = rest
    halo = jnp.concatenate([r[...] for r in halo_refs], axis=0)
    far = stacked(dot(halo, w_src_ref[...]))
    pre = pre_ref[...] + dot(twice(pick_ref[...]), far)
    sig = 0.5 + 0.5 * jnp.tanh(0.5 * pre)
    factor_ref[...] = sig * (1.0 + pre * (1.0 - sig))
    hidden = dot(collect_ref[...], (pre * sig).astype(bf16))
    high, low = split(hidden)
    hidden_ref[...] = high
    w_out = w_out_ref[...]
    partial_ref[...] = (dot(high, w_out) + dot(low, w_out)).astype(bf16)


def backward_kernel(
    geometry,
    node_ref, collect_ref, spread_ref, scatter_ref, w_out_ref, gain_ref, cot_ref,
    factor_ref, hidden_ref, own_ref, other_ref,
    *rest,
):
    peers, chunk, n_halo, paired = geometry
    *rest, out_scratch, pair_scratch = rest
    halo_refs = rest[:n_halo]
    normed_ref, local_ref, target_ref, *message_refs = rest[n_halo:]
    node = node_ref[...]
    rows, width = node.shape
    aggregate = own_ref[...].astype(f32) + other_ref[...].astype(f32)
    center = aggregate - jnp.mean(aggregate, axis=1, keepdims=True)
    variance = jnp.mean(center * center, axis=1, keepdims=True)
    inverse = lax.rsqrt(variance + EPSILON)
    normed = center * inverse
    gain = gain_ref[...]
    upstream = cot_ref[...].astype(f32)
    scaled = upstream * gain
    agg_grad = inverse * (
        scaled
        - jnp.mean(scaled, axis=1, keepdims=True)
        - normed * jnp.mean(scaled * normed, axis=1, keepdims=True)
    )
    agg_grad = agg_grad.astype(bf16)
    normed_ref[...] = normed
    gain_part = jnp.sum(upstream * normed, axis=0, keepdims=True)

    act_grad = dot(twice(spread_ref[...]), stacked(dot(agg_grad, w_out_ref[...], NT)))
    pre_grad = (act_grad * factor_ref[...]).astype(bf16)

    table = jnp.concatenate([node] + [r[...] for r in halo_refs], axis=0)
    by_source = dot(scatter_ref[...], pre_grad)
    by_target = dot(collect_ref[...], pre_grad)
    local_ref[...] = by_source[:rows]
    by_target_low = by_target.astype(bf16)
    by_source_low = by_source.astype(bf16)
    target_ref[...] = by_target_low

    hid = by_source.shape[1]
    bias_part = jnp.sum(by_target, axis=0, keepdims=True)
    src_part = dot(table, by_source_low, TN).astype(bf16)
    dst_part = dot(node, by_target_low, TN).astype(bf16)
    out_part = dot(hidden_ref[...], agg_grad, TN).astype(bf16)
    vectors = [bias_part] + [gain_part[:, at : at + hid] for at in range(0, width, hid)]
    tail = tail_of(vectors)
    back = by_source_low[rows:]

    if paired:
        far_send_ref, far_keep_ref, near_send_ref, near_keep_ref, *out_refs = message_refs
        sub = lax.axis_index("sub")
        mesh = lax.axis_index("mesh")
        lines = len(out_refs)
        halo = back.shape[0] // 4
        first = sub == 0
        pair_scratch[0] = jnp.where(first, dst_part, src_part)
        pair_scratch[1] = jnp.where(first, src_part, dst_part)
        strip = width // lines
        for slot, far_ref, near_ref in ((0, far_send_ref, near_send_ref), (1, far_keep_ref, near_keep_ref)):
            for at, k in enumerate((3, 2, 1, 0)):
                start = pl.multiple_of((mesh ^ k) * strip, strip)
                ref = far_ref if at < 2 else near_ref
                ref[at % 2 * strip : (at % 2 + 1) * strip, :] = pair_scratch[slot, pl.ds(start, strip), :]
            far_ref[2 * strip : 2 * strip + TAIL, :] = tail
        far_send_ref[2 * strip + TAIL :, :] = back[2 * halo :]
        out_scratch[...] = out_part
        strip = hid // lines
        for k, ref in enumerate(out_refs):
            start = pl.multiple_of((mesh ^ k) * strip, strip)
            ref[0:strip, :] = out_scratch[pl.ds(start, strip), :]
            if k % 2 == 1:
                rows_back = back[(1 - k // 2) * halo : (2 - k // 2) * halo]
                ref[strip:, 0:hid] = rows_back[: halo // 2]
                ref[strip:, hid:] = rows_back[halo // 2 :]
        return

    message_ref, *back_refs = message_refs
    at = 0
    for ref in back_refs:
        ref[...] = back[at : at + ref.shape[0]]
        at += ref.shape[0]
    blocks = [src_part, dst_part]
    for at in range(0, width, hid):
        blocks.append(out_part[:, at : at + hid])
    done = 0
    for block in blocks:
        at = 0
        while at < block.shape[0]:
            peer, offset = divmod(done, chunk)
            take = min(chunk - offset, block.shape[0] - at)
            message_ref[peer, offset : offset + take, :] = block[at : at + take]
            at += take
            done += take
    while done < peers * chunk:
        peer, offset = divmod(done, chunk)
        take = chunk - offset
        message_ref[peer, offset : offset + take, :] = jnp.zeros((take, hid), bf16)
        done += take
    for peer in range(peers):
        message_ref[peer, chunk:, :] = tail


def tail_of(vectors):
    tail = []
    for v in vectors:
        high = v.astype(bf16).astype(f32)
        tail += [high, v - high]
    tail.append(jnp.zeros((TAIL - len(tail), vectors[0].shape[1]), f32))
    return jnp.concatenate(tail, axis=0).astype(bf16)


def tree(terms):
    while len(terms) > 1:
        terms = [terms[i] + terms[i + 1] for i in range(0, len(terms), 2)]
    return terms[0]


def far_kernel(arrived_ref, keep_ref, three_ref, two_ref, tail_ref):
    full = keep_ref.shape[0]
    total = keep_ref[...].astype(f32) + arrived_ref[0:full, :].astype(f32)
    strip = three_ref.shape[0] - TAIL
    tail = total[2 * strip :]
    tail = tail_of([tail[at : at + 1] + tail[at + 1 : at + 2] for at in range(0, 6, 2)])
    for k, ref in enumerate((three_ref, two_ref)):
        ref[0:strip, :] = total[k * strip : (k + 1) * strip].astype(bf16)
        ref[strip:, :] = tail
    tail_ref[...] = tail


def near_kernel(arrived_ref, keep_ref, tail_ref, one_ref, zero_ref):
    full = keep_ref.shape[0]
    total = (keep_ref[...].astype(f32) + arrived_ref[...].astype(f32)).astype(bf16)
    strip = full // 2
    for k, ref in enumerate((one_ref, zero_ref)):
        ref[0:strip, :] = total[k * strip : (k + 1) * strip]
        ref[strip:, :] = tail_ref[...]


def line_kernel(*refs):
    *terms, _, send_ref, keep_ref = refs
    rows, hid = send_ref.shape
    total = tree([r[0:rows, :].astype(f32) for r in terms])
    first = lax.axis_index("sub") == 0
    left, right = total[:, :hid], total[:, hid:]
    send_ref[...] = jnp.where(first, right, left).astype(bf16)
    keep_ref[...] = jnp.where(first, left, right).astype(bf16)


def own_kernel(*refs):
    *terms, out_keep_ref, out_arrived_ref, _, own_ref, tail_ref = refs
    total = tree([r[...].astype(f32) for r in terms])
    strip = own_ref.shape[0] - out_keep_ref.shape[0]
    own_ref[0:strip, :] = total[:strip].astype(bf16)
    own_ref[strip:, :] = (
        out_keep_ref[...].astype(f32) + out_arrived_ref[...].astype(f32)
    ).astype(bf16)
    tail_ref[...] = total[strip:]


def write_vectors(tail, bias_ref, gain_ref):
    bias_ref[...] = tail[0:1] + tail[1:2]
    hid = tail.shape[1]
    for k in range(gain_ref.shape[1] // hid):
        gain_ref[:, k * hid : (k + 1) * hid] = tail[2 + 2 * k : 3 + 2 * k] + tail[3 + 2 * k : 4 + 2 * k]


def place_kernel(order, *refs):
    count = len(order)
    mine, theirs = refs[:count], refs[count : 2 * count]
    src_ref, dst_ref, out_ref = refs[2 * count :]
    first = lax.axis_index("sub") == 0
    mesh = lax.axis_index("mesh")
    width, hid = src_ref.shape
    strip = width // count
    narrow = hid // count
    for at, k in enumerate(order):
        a, b = mine[at][...], theirs[at][...]
        low = jnp.where(first, a, b).astype(f32)
        high = jnp.where(first, b, a).astype(f32)
        start = pl.multiple_of((mesh ^ k) * strip, strip)
        src_ref[pl.ds(start, strip), :] = low[:strip]
        dst_ref[pl.ds(start, strip), :] = high[:strip]
        start = pl.multiple_of((mesh ^ k) * narrow, narrow)
        out_ref[pl.ds(start, narrow), 0:hid] = low[strip:]
        out_ref[pl.ds(start, narrow), hid:] = high[strip:]


def sum_kernel(chunk, arrived_ref, out_ref, bias_ref, gain_ref):
    peers = arrived_ref.shape[0]
    total = arrived_ref[0].astype(f32)
    for peer in range(1, peers):
        total += arrived_ref[peer].astype(f32)
    low = total[:chunk].astype(bf16)
    for peer in range(peers):
        out_ref[peer] = low
    tail = total[chunk:]
    write_vectors(tail, bias_ref, gain_ref)


def unpack_kernel(arrived_ref, src_ref, dst_ref, out_ref):
    hid = src_ref.shape[1]
    rows = src_ref.shape[0]
    src_ref[...] = arrived_ref[0:rows, :].astype(f32)
    dst_ref[...] = arrived_ref[rows : 2 * rows, :].astype(f32)
    at = 2 * rows
    for k in range(out_ref.shape[1] // hid):
        out_ref[:, k * hid : (k + 1) * hid] = arrived_ref[at : at + out_ref.shape[0], :].astype(f32)
        at += out_ref.shape[0]


def node_part(send_ref, local_ref, target_ref, w_src_ref, w_dst_ref, returned, out_ref):
    rows = local_ref.shape[0]
    halo = send_ref.shape[2]
    picks = [one_hot(iota((rows, halo), 0) == send_ref[0, d : d + 1, :]) for d in range(4)]
    total = local_ref[...] + dot(jnp.concatenate(picks, axis=1), jnp.concatenate(returned, axis=0))
    out_ref[...] = (
        dot(total.astype(bf16), w_src_ref[...], NT) + dot(target_ref[...], w_dst_ref[...], NT)
    ).astype(bf16)


def node_kernel(send_ref, local_ref, target_ref, w_src_ref, w_dst_ref, *rest):
    *back_refs, out_ref = rest
    returned = [r[...] for r in back_refs]
    node_part(send_ref, local_ref, target_ref, w_src_ref, w_dst_ref, returned, out_ref)


def paired_node_kernel(
    send_ref, local_ref, target_ref, w_src_ref, w_dst_ref, three_ref, one_ref, pair_ref, out_ref
):
    even = lax.axis_index("mesh") % 2 == 0
    halo = send_ref.shape[2]
    hid = local_ref.shape[1]
    at = one_ref.shape[0] - halo // 2
    one, three = [
        jnp.concatenate([r[at:, :hid], r[at:, hid:]], axis=0) for r in (one_ref, three_ref)
    ]
    returned = [
        jnp.where(even, one, three), jnp.where(even, three, one), pair_ref[pair_ref.shape[0] - 2 * halo :, :]
    ]
    node_part(send_ref, local_ref, target_ref, w_src_ref, w_dst_ref, returned, out_ref)


def finish_kernel(cot_ref, node_ref, gain_ref, normed_ref, own_ref, other_ref, *rest):
    if len(rest) == 5:
        tail_ref, *rest, bias_out_ref, gain_out_ref = rest
        write_vectors(tail_ref[...], bias_out_ref, gain_out_ref)
    grad_ref, updated_ref = rest
    grad_ref[...] = cot_ref[...].astype(f32) + (
        own_ref[...].astype(f32) + other_ref[...].astype(f32)
    )
    updated_ref[...] = (node_ref[...].astype(f32) + gain_ref[...] * normed_ref[...]).astype(bf16)


VMEM = pl.BlockSpec(memory_space=pltpu.VMEM)
SMEM = pl.BlockSpec(memory_space=pltpu.SMEM)
HBM = pl.BlockSpec(memory_space=pltpu.HBM)


def shape(dims, dtype):
    return jax.ShapeDtypeStruct(dims, dtype)


def call(kernel, outs, *args, specs=None, out_specs=None, flops=10**8, scratch=()):
    return pl.pallas_call(
        kernel,
        out_shape=outs,
        in_specs=specs or [VMEM] * len(args),
        out_specs=out_specs or jax.tree.map(lambda _: VMEM, outs),
        scratch_shapes=scratch,
        compiler_params=pltpu.CompilerParams(vmem_limit_bytes=VMEM_LIMIT),
        cost_estimate=pl.CostEstimate(flops=flops, bytes_accessed=10**6, transcendentals=0),
    )(*args)


def shifted(x, axis, by):
    count = lax.axis_size(axis)
    return lax.ppermute(x, axis, [(i, (i + by) % count) for i in range(count)])


def across(x, axis, k):
    count = lax.axis_size(axis)
    return lax.ppermute(x, axis, [(i, i ^ k) for i in range(count)])


def paired_sums(messages, lines, strip, narrow, width, hid, node_terms):
    far_send, far_keep, near_send, near_keep, *outs = messages
    order = range(lines - 1, 0, -1)
    block = shape((strip + TAIL, hid), bf16)
    far = across(far_send, "sub", 1)
    out_terms = {k: across(outs[k], "mesh", k) for k in order}
    near = across(near_send, "sub", 1)
    line = {}
    line[3], line[2], tail = call(far_kernel, [block, block, shape((TAIL, hid), bf16)], far, far_keep)
    line[1], line[0] = call(near_kernel, [block, block], near, near_keep, tail)
    line_terms = {k: across(line[k], "mesh", k) for k in order}
    out_send, out_keep = call(
        line_kernel,
        [shape((narrow, hid), bf16)] * 2,
        *[out_terms[k] for k in order], outs[0], line_terms[2],
    )
    node_part = node_terms(out_terms[3], out_terms[1], far)
    own, tail = call(
        own_kernel,
        [shape((strip + narrow, hid), bf16), shape((TAIL, hid), f32)],
        *[line_terms[k] for k in (2, 3, 1)], line[0], out_keep, across(out_send, "sub", 1),
        node_part,
    )
    mine = {k: across(own, "mesh", k) for k in order}
    mine[0] = own
    theirs = {k: across(mine[k], "sub", 1) for k in mine}
    placed = (0, 3, 1, 2)
    grads = call(
        functools.partial(place_kernel, placed),
        [shape((width, hid), f32), shape((width, hid), f32), shape((hid, width), f32)],
        *[mine[k] for k in placed], *[theirs[k] for k in placed],
    )
    return (*grads, tail), node_part


def shards(
    node_state,
    send_rows,
    edge_src,
    edge_dst,
    block_count,
    w_src,
    w_dst,
    hidden_bias,
    w_out,
    norm_gain,
    cotangent,
):
    rows, width = node_state.shape
    hid = w_src.shape[1]
    halo = send_rows.shape[2]
    edges = edge_src.shape[0]
    peers = lax.axis_size("mesh") * lax.axis_size("sub")
    merged = lax.axis_size("sub") == 2
    total_rows = 2 * width + (width // hid) * hid
    chunk = -(-total_rows // (peers * 16)) * 16

    piece = [halo, halo, 2 * halo] if merged else [halo] * 4
    routes = [("mesh", 1), ("mesh", -1), ("sub", 1)] + ([] if merged else [("sub", -1)])
    n_halo = len(piece)
    lines = lax.axis_size("mesh")
    paired = merged and lines == 4

    def in_hbm(x):
        return pltpu.with_memory_space_constraint(x, pltpu.HBM)

    node, send, *outgoing = call(
        functools.partial(send_kernel, paired),
        [shape((rows, width), bf16), shape(send_rows.shape, jnp.int32)]
        + [shape((n, width), bf16) for n in piece],
        in_hbm(node_state), in_hbm(send_rows),
        specs=[HBM, HBM],
        scratch=[pltpu.SemaphoreType.DMA((2,))],
    )
    if paired:
        pair = across(outgoing[2], "sub", 1)
        one = across(outgoing[1], "mesh", 1)
        arrived = [across(outgoing[0], "mesh", 3), one, pair]
    else:
        arrived = [shifted(x, axis, by) for x, (axis, by) in zip(outgoing, routes)]

    fetched = [
        edge_src.reshape(1, edges), edge_dst.reshape(1, edges), block_count,
        hidden_bias.reshape(1, hid), w_src, w_dst, w_out, norm_gain.reshape(1, width), cotangent,
    ]
    pre, pick, collect, spread, scatter, w_src, w_dst, w_out, gain, cot = call(
        functools.partial(local_kernel, paired),
        [
            shape((edges, hid), f32),
            shape((edges, 4 * halo), bf16),
            shape((rows, edges), bf16),
            shape((edges, rows), bf16),
            shape((rows + 4 * halo, edges), bf16),
        ]
        + [shape(x.shape, x.dtype) for x in fetched[4:]],
        node, *[in_hbm(x) for x in fetched],
        specs=[VMEM] + [HBM] * len(fetched),
        scratch=[
            pltpu.SMEM(block_count.shape, jnp.int32),
            pltpu.VMEM((1, edges), jnp.int32),
            pltpu.VMEM((1, edges), jnp.int32),
            pltpu.VMEM((1, hid), f32),
            pltpu.SemaphoreType.DMA((N_FETCHED,)),
        ],
    )

    factor, hidden, partial = call(
        forward_kernel,
        [shape((edges, hid), f32), shape((rows, hid), bf16), shape((rows, width), bf16)],
        pre, pick, collect, w_src, w_out, *arrived,
    )
    other = shifted(partial, "lat", 1)

    if paired:
        strip = width // lines
        narrow = hid // lines
        message_shapes = [shape((2 * strip + TAIL + 2 * halo, hid), bf16), shape((2 * strip + TAIL, hid), bf16)]
        message_shapes += [shape((2 * strip, hid), bf16)] * 2
        message_shapes += [shape((narrow + k % 2 * (halo // 2), width), bf16) for k in range(lines)]
    else:
        message_shapes = [shape((peers, chunk + TAIL, hid), bf16)]
        message_shapes += [shape((n, hid), bf16) for n in piece]
    normed, local, target, *messages = call(
        functools.partial(backward_kernel, (peers, chunk, n_halo, paired)),
        [shape((rows, width), f32), shape((rows, hid), f32), shape((rows, hid), bf16)]
        + message_shapes,
        node, collect, spread, scatter, w_out, gain, cot, factor, hidden, partial, other, *arrived,
        scratch=[
            pltpu.VMEM((hid, width), bf16),
            pltpu.VMEM((2, width, hid), bf16),
        ],
    )

    def node_terms(*returned):
        return call(
            paired_node_kernel if paired else node_kernel,
            shape((rows, width), bf16),
            send, local, target, w_src, w_dst, *returned,
        )

    if paired:
        (src_grad, dst_grad, out_grad, tail), node_part = paired_sums(
            messages, lines, strip, narrow, width, hid, node_terms
        )
    else:
        node_part = node_terms(
            *[shifted(x, axis, -by) for x, (axis, by) in zip(messages[1:], routes)]
        )
        exchanged = lax.all_to_all(messages[0], ("mesh", "sub"), 0, 0)
        reduced, bias_grad, gain_grad = call(
            functools.partial(sum_kernel, chunk),
            [shape((peers, chunk, hid), bf16), shape((1, hid), f32), shape((1, width), f32)],
            exchanged,
        )
        gathered = lax.all_to_all(reduced, ("mesh", "sub"), 0, 0)
        src_grad, dst_grad, out_grad = call(
            unpack_kernel,
            [shape((width, hid), f32), shape((width, hid), f32), shape((hid, width), f32)],
            gathered.reshape(peers * chunk, hid),
        )
    finished = [shape((rows, width), f32), shape((rows, width), bf16)]
    ends = [cot, node, gain, normed, node_part, shifted(node_part, "lat", 1)]
    if paired:
        node_grad, updated, bias_grad, gain_grad = call(
            finish_kernel, finished + [shape((1, hid), f32), shape((1, width), f32)], *ends, tail
        )
    else:
        node_grad, updated = call(finish_kernel, finished, *ends)
    return (
        updated, node_grad, src_grad, dst_grad, out_grad,
        bias_grad.reshape(hid), gain_grad.reshape(width),
    )


def solution(mesh):
    nodes = P(("parts", "mesh", "sub"), None)
    slots = P(("parts", "mesh", "sub"))
    in_specs = (
        nodes,
        P(("parts", "mesh", "sub"), None, None),
        slots,
        slots,
        slots,
        P(None, "lat"),
        P(None, "lat"),
        P("lat"),
        P("lat", None),
        P(),
        nodes,
    )
    out_specs = (
        nodes,
        nodes,
        P("parts", "lat"),
        P("parts", "lat"),
        P(("parts", "lat"), None),
        P(("parts", "lat")),
        P("parts"),
    )
    return jax.shard_map(shards, mesh=mesh, in_specs=in_specs, out_specs=out_specs, check_vma=False)
```

```python
import functools

import jax
import jax.numpy as jnp
from jax import lax
from jax.experimental import pallas as pl
from jax.experimental.pallas import tpu as pltpu
from jax.sharding import PartitionSpec as P

BLOCK = 128
EPSILON = 1e-05
TAIL = 16
N_FETCHED = 9
VMEM_LIMIT = 24 * 1024 * 1024

f32 = jnp.float32
bf16 = jnp.bfloat16

NN = (((1,), (0,)), ((), ()))
NT = (((1,), (1,)), ((), ()))
TN = (((0,), (0,)), ((), ()))


def dot(a, b, dims=NN):
    return lax.dot_general(a, b, dims, preferred_element_type=f32)


def iota(shape, dim):
    return lax.broadcasted_iota(jnp.int32, shape, dim)


def one_hot(condition):
    return jnp.where(condition, 1.0, 0.0).astype(bf16)


def split(x):
    high = x.astype(bf16)
    return high, (x - high.astype(f32)).astype(bf16)


def columns_of(row, lanes):
    return jnp.transpose(jnp.broadcast_to(row, (lanes, row.shape[1])))


def usable_row(count_ref, edges):
    lane = iota((1, BLOCK), 1)
    parts = [lane < count_ref[b] for b in range(edges // BLOCK)]
    return jnp.concatenate([jnp.where(p, 1, 0) for p in parts], axis=1)


def usable_columns(count_ref, edges, lanes):
    sub = iota((BLOCK, lanes), 0)
    return jnp.concatenate(
        [jnp.where(sub < count_ref[b], 1, 0) for b in range(edges // BLOCK)], axis=0
    )


def fetch(sems, *pairs):
    copies = [pltpu.make_async_copy(a, b, sems.at[i]) for i, (a, b) in enumerate(pairs)]
    for copy in copies:
        copy.start()
    return copies


def send_kernel(node_hbm, send_hbm, node_ref, send_ref, *rest):
    *out_refs, sems = rest
    for copy in fetch(sems, (node_hbm, node_ref), (send_hbm, send_ref)):
        copy.wait()
    node = node_ref[...]
    rows = node.shape[0]
    halo = send_ref.shape[2]
    pieces = []
    for d in range(4):
        pick = one_hot(iota((rows, halo), 0) == send_ref[0, d : d + 1, :])
        pieces.append(dot(pick, node, TN).astype(bf16))
    out_refs[0][...] = pieces[0]
    out_refs[1][...] = pieces[1]
    if len(out_refs) == 3:
        out_refs[2][0:halo, :] = pieces[2]
        out_refs[2][halo:, :] = pieces[3]
    else:
        out_refs[2][...] = pieces[2]
        out_refs[3][...] = pieces[3]


def local_kernel(*refs):
    node_ref, ins, refs = refs[0], refs[1 : 1 + N_FETCHED], refs[1 + N_FETCHED :]
    pre_ref, pick_ref, collect_ref, spread_ref, scatter_ref, *refs = refs
    w_src_ref, w_dst_ref, w_out_ref, gain_ref, cot_ref, count_ref, src_ref, dst_ref, bias_ref, sems = refs
    outs = (src_ref, dst_ref, count_ref, bias_ref, w_src_ref, w_dst_ref, w_out_ref, gain_ref, cot_ref)
    copies = fetch(sems, *zip(ins, outs))
    node = node_ref[...]
    rows = node.shape[0]
    edges = src_ref.shape[1]
    for copy in copies[:3]:
        copy.wait()
    scatter_ref[...] = one_hot(iota(scatter_ref.shape, 0) == src_ref[...])
    used = usable_row(count_ref, edges) > 0
    collect_ref[...] = one_hot((iota((rows, edges), 0) == dst_ref[...]) & used)
    source = columns_of(src_ref[...], 128)
    target = columns_of(dst_ref[...], 128)
    lane = iota(source.shape, 1)
    used = usable_columns(count_ref, edges, 128) > 0
    near = one_hot(source == lane)
    pick_ref[...] = one_hot(source == lane + rows)
    spread_ref[...] = one_hot((target == lane) & used)
    both = jnp.concatenate([dot(near, node), dot(one_hot(target == lane), node)], axis=1).astype(bf16)
    for copy in copies[3:]:
        copy.wait()
    weights = jnp.concatenate([w_src_ref[...], w_dst_ref[...]], axis=0)
    pre_ref[...] = dot(both, weights) + bias_ref[...]


def twice(x):
    return jnp.concatenate([x, x], axis=1)


def stacked(x):
    return jnp.concatenate(split(x), axis=0)


def forward_kernel(pre_ref, pick_ref, collect_ref, w_src_ref, w_out_ref, *rest):
    *halo_refs, factor_ref, hidden_ref, partial_ref = rest
    halo = jnp.concatenate([r[...] for r in halo_refs], axis=0)
    far = stacked(dot(halo, w_src_ref[...]))
    pre = pre_ref[...] + dot(twice(pick_ref[...]), far)
    sig = 0.5 + 0.5 * jnp.tanh(0.5 * pre)
    factor_ref[...] = sig * (1.0 + pre * (1.0 - sig))
    hidden = dot(collect_ref[...], (pre * sig).astype(bf16))
    high, low = split(hidden)
    hidden_ref[...] = high
    w_out = w_out_ref[...]
    partial_ref[...] = (dot(high, w_out) + dot(low, w_out)).astype(bf16)


def backward_kernel(
    geometry,
    node_ref, collect_ref, spread_ref, scatter_ref, w_out_ref, gain_ref, cot_ref,
    factor_ref, hidden_ref, own_ref, other_ref,
    *rest,
):
    peers, chunk, n_halo, paired = geometry
    *rest, out_scratch, back_scratch, pair_scratch = rest
    halo_refs = rest[:n_halo]
    normed_ref, local_ref, target_ref, *message_refs = rest[n_halo:]
    node = node_ref[...]
    rows, width = node.shape
    aggregate = own_ref[...].astype(f32) + other_ref[...].astype(f32)
    center = aggregate - jnp.mean(aggregate, axis=1, keepdims=True)
    variance = jnp.mean(center * center, axis=1, keepdims=True)
    inverse = lax.rsqrt(variance + EPSILON)
    normed = center * inverse
    gain = gain_ref[...]
    upstream = cot_ref[...].astype(f32)
    scaled = upstream * gain
    agg_grad = inverse * (
        scaled
        - jnp.mean(scaled, axis=1, keepdims=True)
        - normed * jnp.mean(scaled * normed, axis=1, keepdims=True)
    )
    agg_grad = agg_grad.astype(bf16)
    normed_ref[...] = normed
    gain_part = jnp.sum(upstream * normed, axis=0, keepdims=True)

    act_grad = dot(twice(spread_ref[...]), stacked(dot(agg_grad, w_out_ref[...], NT)))
    pre_grad = (act_grad * factor_ref[...]).astype(bf16)

    table = jnp.concatenate([node] + [r[...] for r in halo_refs], axis=0)
    by_source = dot(scatter_ref[...], pre_grad)
    by_target = dot(collect_ref[...], pre_grad)
    local_ref[...] = by_source[:rows]
    by_target_low = by_target.astype(bf16)
    by_source_low = by_source.astype(bf16)
    target_ref[...] = by_target_low

    hid = by_source.shape[1]
    bias_part = jnp.sum(by_target, axis=0, keepdims=True)
    src_part = dot(table, by_source_low, TN).astype(bf16)
    dst_part = dot(node, by_target_low, TN).astype(bf16)
    out_part = dot(hidden_ref[...], agg_grad, TN).astype(bf16)
    vectors = [bias_part] + [gain_part[:, at : at + hid] for at in range(0, width, hid)]
    tail = tail_of(vectors)
    back = by_source_low[rows:]

    if paired:
        far_send_ref, far_keep_ref, near_send_ref, near_keep_ref, *out_refs = message_refs
        sub = lax.axis_index("sub")
        mesh = lax.axis_index("mesh")
        lines = len(out_refs)
        halo = back.shape[0] // 4
        first = sub == 0
        pair_scratch[0] = jnp.where(first, dst_part, src_part)
        pair_scratch[1] = jnp.where(first, src_part, dst_part)
        strip = width // lines
        for slot, far_ref, near_ref in ((0, far_send_ref, near_send_ref), (1, far_keep_ref, near_keep_ref)):
            for at, k in enumerate((3, 2, 1, 0)):
                start = pl.multiple_of((mesh ^ k) * strip, strip)
                ref = far_ref if at < 2 else near_ref
                ref[at % 2 * strip : (at % 2 + 1) * strip, :] = pair_scratch[slot, pl.ds(start, strip), :]
            far_ref[2 * strip : 2 * strip + TAIL, :] = tail
        far_send_ref[2 * strip + TAIL :, :] = back[2 * halo :]
        back_scratch[...] = back[: 2 * halo]
        out_scratch[...] = out_part
        strip = hid // len(out_refs)
        for k, ref in enumerate(out_refs):
            start = pl.multiple_of((mesh ^ k) * strip, strip)
            ref[0:strip, :] = out_scratch[pl.ds(start, strip), :]
            if k % 2 == 1:
                slot = (mesh + (k // 2) + 1) % 2
                start = pl.multiple_of(slot * halo, halo)
                rows_back = back_scratch[pl.ds(start, halo), :]
                ref[strip:, 0:hid] = rows_back[: halo // 2]
                ref[strip:, hid:] = rows_back[halo // 2 :]
        return

    message_ref, *back_refs = message_refs
    at = 0
    for ref in back_refs:
        ref[...] = back[at : at + ref.shape[0]]
        at += ref.shape[0]
    blocks = [src_part, dst_part]
    for at in range(0, width, hid):
        blocks.append(out_part[:, at : at + hid])
    done = 0
    for block in blocks:
        at = 0
        while at < block.shape[0]:
            peer, offset = divmod(done, chunk)
            take = min(chunk - offset, block.shape[0] - at)
            message_ref[peer, offset : offset + take, :] = block[at : at + take]
            at += take
            done += take
    while done < peers * chunk:
        peer, offset = divmod(done, chunk)
        take = chunk - offset
        message_ref[peer, offset : offset + take, :] = jnp.zeros((take, hid), bf16)
        done += take
    for peer in range(peers):
        message_ref[peer, chunk:, :] = tail


def tail_of(vectors):
    tail = []
    for v in vectors:
        high = v.astype(bf16).astype(f32)
        tail += [high, v - high]
    tail.append(jnp.zeros((TAIL - len(tail), vectors[0].shape[1]), f32))
    return jnp.concatenate(tail, axis=0).astype(bf16)


def tree(terms):
    while len(terms) > 1:
        terms = [terms[i] + terms[i + 1] for i in range(0, len(terms), 2)]
    return terms[0]


def far_kernel(arrived_ref, keep_ref, three_ref, two_ref, tail_ref):
    full = keep_ref.shape[0]
    total = keep_ref[...].astype(f32) + arrived_ref[0:full, :].astype(f32)
    strip = three_ref.shape[0] - TAIL
    tail = total[2 * strip :]
    tail = tail_of([tail[at : at + 1] + tail[at + 1 : at + 2] for at in range(0, 6, 2)])
    for k, ref in enumerate((three_ref, two_ref)):
        ref[0:strip, :] = total[k * strip : (k + 1) * strip].astype(bf16)
        ref[strip:, :] = tail
    tail_ref[...] = tail


def near_kernel(arrived_ref, keep_ref, tail_ref, one_ref, zero_ref):
    full = keep_ref.shape[0]
    total = (keep_ref[...].astype(f32) + arrived_ref[...].astype(f32)).astype(bf16)
    strip = full // 2
    for k, ref in enumerate((one_ref, zero_ref)):
        ref[0:strip, :] = total[k * strip : (k + 1) * strip]
        ref[strip:, :] = tail_ref[...]


def line_kernel(*refs):
    *terms, _, send_ref, keep_ref = refs
    rows, hid = send_ref.shape
    total = tree([r[0:rows, :].astype(f32) for r in terms])
    first = lax.axis_index("sub") == 0
    left, right = total[:, :hid], total[:, hid:]
    send_ref[...] = jnp.where(first, right, left).astype(bf16)
    keep_ref[...] = jnp.where(first, left, right).astype(bf16)


def own_kernel(*refs):
    *terms, out_keep_ref, out_arrived_ref, _, own_ref, tail_ref = refs
    total = tree([r[...].astype(f32) for r in terms])
    strip = own_ref.shape[0] - out_keep_ref.shape[0]
    own_ref[0:strip, :] = total[:strip].astype(bf16)
    own_ref[strip:, :] = (
        out_keep_ref[...].astype(f32) + out_arrived_ref[...].astype(f32)
    ).astype(bf16)
    tail_ref[...] = total[strip:]


def write_vectors(tail, bias_ref, gain_ref):
    bias_ref[...] = tail[0:1] + tail[1:2]
    hid = tail.shape[1]
    for k in range(gain_ref.shape[1] // hid):
        gain_ref[:, k * hid : (k + 1) * hid] = tail[2 + 2 * k : 3 + 2 * k] + tail[3 + 2 * k : 4 + 2 * k]


def relay_kernel(strip_ref, _, out_ref):
    out_ref[...] = strip_ref[...]


def place_kernel(order, *refs):
    count = len(order)
    mine, theirs = refs[:count], refs[count : 2 * count]
    src_ref, dst_ref, out_ref = refs[2 * count :]
    first = lax.axis_index("sub") == 0
    mesh = lax.axis_index("mesh")
    width, hid = src_ref.shape
    strip = width // count
    narrow = hid // count
    for at, k in enumerate(order):
        a, b = mine[at][...], theirs[at][...]
        low = jnp.where(first, a, b).astype(f32)
        high = jnp.where(first, b, a).astype(f32)
        start = pl.multiple_of((mesh ^ k) * strip, strip)
        src_ref[pl.ds(start, strip), :] = low[:strip]
        dst_ref[pl.ds(start, strip), :] = high[:strip]
        start = pl.multiple_of((mesh ^ k) * narrow, narrow)
        out_ref[pl.ds(start, narrow), 0:hid] = low[strip:]
        out_ref[pl.ds(start, narrow), hid:] = high[strip:]


def sum_kernel(chunk, arrived_ref, out_ref, bias_ref, gain_ref):
    peers = arrived_ref.shape[0]
    total = arrived_ref[0].astype(f32)
    for peer in range(1, peers):
        total += arrived_ref[peer].astype(f32)
    low = total[:chunk].astype(bf16)
    for peer in range(peers):
        out_ref[peer] = low
    tail = total[chunk:]
    write_vectors(tail, bias_ref, gain_ref)


def unpack_kernel(arrived_ref, src_ref, dst_ref, out_ref):
    hid = src_ref.shape[1]
    rows = src_ref.shape[0]
    src_ref[...] = arrived_ref[0:rows, :].astype(f32)
    dst_ref[...] = arrived_ref[rows : 2 * rows, :].astype(f32)
    at = 2 * rows
    for k in range(out_ref.shape[1] // hid):
        out_ref[:, k * hid : (k + 1) * hid] = arrived_ref[at : at + out_ref.shape[0], :].astype(f32)
        at += out_ref.shape[0]


def node_part(send_ref, local_ref, target_ref, w_src_ref, w_dst_ref, returned, out_ref):
    rows = local_ref.shape[0]
    halo = send_ref.shape[2]
    picks = [one_hot(iota((rows, halo), 0) == send_ref[0, d : d + 1, :]) for d in range(4)]
    total = local_ref[...] + dot(jnp.concatenate(picks, axis=1), jnp.concatenate(returned, axis=0))
    out_ref[...] = (
        dot(total.astype(bf16), w_src_ref[...], NT) + dot(target_ref[...], w_dst_ref[...], NT)
    ).astype(bf16)


def node_kernel(send_ref, local_ref, target_ref, w_src_ref, w_dst_ref, *rest):
    *back_refs, out_ref = rest
    returned = [r[...] for r in back_refs]
    node_part(send_ref, local_ref, target_ref, w_src_ref, w_dst_ref, returned, out_ref)


def paired_node_kernel(
    send_ref, local_ref, target_ref, w_src_ref, w_dst_ref, three_ref, one_ref, pair_ref, out_ref
):
    even = lax.axis_index("mesh") % 2 == 0
    halo = send_ref.shape[2]
    hid = local_ref.shape[1]
    at = one_ref.shape[0] - halo // 2
    one, three = [
        jnp.concatenate([r[at:, :hid], r[at:, hid:]], axis=0) for r in (one_ref, three_ref)
    ]
    returned = [
        jnp.where(even, one, three), jnp.where(even, three, one), pair_ref[pair_ref.shape[0] - 2 * halo :, :]
    ]
    node_part(send_ref, local_ref, target_ref, w_src_ref, w_dst_ref, returned, out_ref)


def finish_kernel(cot_ref, node_ref, gain_ref, normed_ref, own_ref, other_ref, *rest):
    if len(rest) == 5:
        tail_ref, *rest, bias_out_ref, gain_out_ref = rest
        write_vectors(tail_ref[...], bias_out_ref, gain_out_ref)
    grad_ref, updated_ref = rest
    grad_ref[...] = cot_ref[...].astype(f32) + (
        own_ref[...].astype(f32) + other_ref[...].astype(f32)
    )
    updated_ref[...] = (node_ref[...].astype(f32) + gain_ref[...] * normed_ref[...]).astype(bf16)


VMEM = pl.BlockSpec(memory_space=pltpu.VMEM)
SMEM = pl.BlockSpec(memory_space=pltpu.SMEM)
HBM = pl.BlockSpec(memory_space=pltpu.HBM)


def shape(dims, dtype):
    return jax.ShapeDtypeStruct(dims, dtype)


def call(kernel, outs, *args, specs=None, out_specs=None, flops=10**8, scratch=()):
    return pl.pallas_call(
        kernel,
        out_shape=outs,
        in_specs=specs or [VMEM] * len(args),
        out_specs=out_specs or jax.tree.map(lambda _: VMEM, outs),
        scratch_shapes=scratch,
        compiler_params=pltpu.CompilerParams(vmem_limit_bytes=VMEM_LIMIT),
        cost_estimate=pl.CostEstimate(flops=flops, bytes_accessed=10**6, transcendentals=0),
    )(*args)


def shifted(x, axis, by):
    count = lax.axis_size(axis)
    return lax.ppermute(x, axis, [(i, (i + by) % count) for i in range(count)])


def across(x, axis, k):
    count = lax.axis_size(axis)
    return lax.ppermute(x, axis, [(i, i ^ k) for i in range(count)])


def paired_sums(messages, lines, strip, narrow, width, hid, node_terms):
    far_send, far_keep, near_send, near_keep, *outs = messages
    order = range(lines - 1, 0, -1)
    block = shape((strip + TAIL, hid), bf16)
    far = across(far_send, "sub", 1)
    out_terms = {k: across(outs[k], "mesh", k) for k in order}
    near = across(near_send, "sub", 1)
    line = {}
    line[3], line[2], tail = call(far_kernel, [block, block, shape((TAIL, hid), bf16)], far, far_keep)
    line[1], line[0] = call(near_kernel, [block, block], near, near_keep, tail)
    line_terms = {k: across(line[k], "mesh", k) for k in order}
    out_send, out_keep = call(
        line_kernel,
        [shape((narrow, hid), bf16)] * 2,
        *[out_terms[k] for k in order], outs[0], line_terms[3],
    )
    node_part = node_terms(out_terms[3], out_terms[1], far)
    own, tail = call(
        own_kernel,
        [shape((strip + narrow, hid), bf16), shape((TAIL, hid), f32)],
        *[line_terms[k] for k in (3, 2, 1)], line[0], out_keep, across(out_send, "sub", 1),
        node_part,
    )
    mine = {k: across(own, "mesh", k) for k in order}
    mine[0] = own
    theirs = {0: across(own, "sub", 1)}
    first = call(relay_kernel, shape(own.shape, bf16), mine[2], theirs[0])
    theirs |= {k: across(first if k == 2 else mine[k], "sub", 1) for k in order}
    placed = (0, 3, 1, 2)
    grads = call(
        functools.partial(place_kernel, placed),
        [shape((width, hid), f32), shape((width, hid), f32), shape((hid, width), f32)],
        *[mine[k] for k in placed], *[theirs[k] for k in placed],
    )
    return (*grads, tail), node_part


def shards(
    node_state,
    send_rows,
    edge_src,
    edge_dst,
    block_count,
    w_src,
    w_dst,
    hidden_bias,
    w_out,
    norm_gain,
    cotangent,
):
    rows, width = node_state.shape
    hid = w_src.shape[1]
    halo = send_rows.shape[2]
    edges = edge_src.shape[0]
    peers = lax.axis_size("mesh") * lax.axis_size("sub")
    merged = lax.axis_size("sub") == 2
    total_rows = 2 * width + (width // hid) * hid
    chunk = -(-total_rows // (peers * 16)) * 16

    piece = [halo, halo, 2 * halo] if merged else [halo] * 4
    routes = [("mesh", 1), ("mesh", -1), ("sub", 1)] + ([] if merged else [("sub", -1)])
    n_halo = len(piece)

    def in_hbm(x):
        return pltpu.with_memory_space_constraint(x, pltpu.HBM)

    node, send, *outgoing = call(
        send_kernel,
        [shape((rows, width), bf16), shape(send_rows.shape, jnp.int32)]
        + [shape((n, width), bf16) for n in piece],
        in_hbm(node_state), in_hbm(send_rows),
        specs=[HBM, HBM],
        scratch=[pltpu.SemaphoreType.DMA((2,))],
    )
    arrived = [shifted(x, axis, by) for x, (axis, by) in zip(outgoing, routes)]

    fetched = [
        edge_src.reshape(1, edges), edge_dst.reshape(1, edges), block_count,
        hidden_bias.reshape(1, hid), w_src, w_dst, w_out, norm_gain.reshape(1, width), cotangent,
    ]
    pre, pick, collect, spread, scatter, w_src, w_dst, w_out, gain, cot = call(
        local_kernel,
        [
            shape((edges, hid), f32),
            shape((edges, 4 * halo), bf16),
            shape((rows, edges), bf16),
            shape((edges, rows), bf16),
            shape((rows + 4 * halo, edges), bf16),
        ]
        + [shape(x.shape, x.dtype) for x in fetched[4:]],
        node, *[in_hbm(x) for x in fetched],
        specs=[VMEM] + [HBM] * len(fetched),
        scratch=[
            pltpu.SMEM(block_count.shape, jnp.int32),
            pltpu.VMEM((1, edges), jnp.int32),
            pltpu.VMEM((1, edges), jnp.int32),
            pltpu.VMEM((1, hid), f32),
            pltpu.SemaphoreType.DMA((N_FETCHED,)),
        ],
    )

    factor, hidden, partial = call(
        forward_kernel,
        [shape((edges, hid), f32), shape((rows, hid), bf16), shape((rows, width), bf16)],
        pre, pick, collect, w_src, w_out, *arrived,
    )
    other = shifted(partial, "lat", 1)

    lines = lax.axis_size("mesh")
    paired = merged and lines == 4
    if paired:
        strip = width // lines
        narrow = hid // lines
        message_shapes = [shape((2 * strip + TAIL + 2 * halo, hid), bf16), shape((2 * strip + TAIL, hid), bf16)]
        message_shapes += [shape((2 * strip, hid), bf16)] * 2
        message_shapes += [shape((narrow + k % 2 * (halo // 2), width), bf16) for k in range(lines)]
    else:
        message_shapes = [shape((peers, chunk + TAIL, hid), bf16)]
        message_shapes += [shape((n, hid), bf16) for n in piece]
    normed, local, target, *messages = call(
        functools.partial(backward_kernel, (peers, chunk, n_halo, paired)),
        [shape((rows, width), f32), shape((rows, hid), f32), shape((rows, hid), bf16)]
        + message_shapes,
        node, collect, spread, scatter, w_out, gain, cot, factor, hidden, partial, other, *arrived,
        scratch=[
            pltpu.VMEM((hid, width), bf16),
            pltpu.VMEM((2 * halo, hid), bf16),
            pltpu.VMEM((2, width, hid), bf16),
        ],
    )

    def node_terms(*returned):
        return call(
            paired_node_kernel if paired else node_kernel,
            shape((rows, width), bf16),
            send, local, target, w_src, w_dst, *returned,
        )

    if paired:
        (src_grad, dst_grad, out_grad, tail), node_part = paired_sums(
            messages, lines, strip, narrow, width, hid, node_terms
        )
    else:
        node_part = node_terms(
            *[shifted(x, axis, -by) for x, (axis, by) in zip(messages[1:], routes)]
        )
        exchanged = lax.all_to_all(messages[0], ("mesh", "sub"), 0, 0)
        reduced, bias_grad, gain_grad = call(
            functools.partial(sum_kernel, chunk),
            [shape((peers, chunk, hid), bf16), shape((1, hid), f32), shape((1, width), f32)],
            exchanged,
        )
        gathered = lax.all_to_all(reduced, ("mesh", "sub"), 0, 0)
        src_grad, dst_grad, out_grad = call(
            unpack_kernel,
            [shape((width, hid), f32), shape((width, hid), f32), shape((hid, width), f32)],
            gathered.reshape(peers * chunk, hid),
        )
    finished = [shape((rows, width), f32), shape((rows, width), bf16)]
    ends = [cot, node, gain, normed, node_part, shifted(node_part, "lat", 1)]
    if paired:
        node_grad, updated, bias_grad, gain_grad = call(
            finish_kernel, finished + [shape((1, hid), f32), shape((1, width), f32)], *ends, tail
        )
    else:
        node_grad, updated = call(finish_kernel, finished, *ends)
    return (
        updated, node_grad, src_grad, dst_grad, out_grad,
        bias_grad.reshape(hid), gain_grad.reshape(width),
    )


def solution(mesh):
    nodes = P(("parts", "mesh", "sub"), None)
    slots = P(("parts", "mesh", "sub"))
    in_specs = (
        nodes,
        P(("parts", "mesh", "sub"), None, None),
        slots,
        slots,
        slots,
        P(None, "lat"),
        P(None, "lat"),
        P("lat"),
        P("lat", None),
        P(),
        nodes,
    )
    out_specs = (
        nodes,
        nodes,
        P("parts", "lat"),
        P("parts", "lat"),
        P(("parts", "lat"), None),
        P(("parts", "lat")),
        P("parts"),
    )
    return jax.shard_map(shards, mesh=mesh, in_specs=in_specs, out_specs=out_specs, check_vma=False)
```

```python
import functools

import jax
import jax.numpy as jnp
from jax import lax
from jax.experimental import pallas as pl
from jax.experimental.pallas import tpu as pltpu
from jax.sharding import PartitionSpec as P

BLOCK = 128
EPSILON = 1e-05
TAIL = 16
N_FETCHED = 9
VMEM_LIMIT = 24 * 1024 * 1024

f32 = jnp.float32
bf16 = jnp.bfloat16

NN = (((1,), (0,)), ((), ()))
NT = (((1,), (1,)), ((), ()))
TN = (((0,), (0,)), ((), ()))


def dot(a, b, dims=NN):
    return lax.dot_general(a, b, dims, preferred_element_type=f32)


def iota(shape, dim):
    return lax.broadcasted_iota(jnp.int32, shape, dim)


def one_hot(condition):
    return jnp.where(condition, 1.0, 0.0).astype(bf16)


def split(x):
    high = x.astype(bf16)
    return high, (x - high.astype(f32)).astype(bf16)


def columns_of(row, lanes):
    return jnp.transpose(jnp.broadcast_to(row, (lanes, row.shape[1])))


def usable_row(count_ref, edges):
    lane = iota((1, BLOCK), 1)
    parts = [lane < count_ref[b] for b in range(edges // BLOCK)]
    return jnp.concatenate([jnp.where(p, 1, 0) for p in parts], axis=1)


def usable_columns(count_ref, edges, lanes):
    sub = iota((BLOCK, lanes), 0)
    return jnp.concatenate(
        [jnp.where(sub < count_ref[b], 1, 0) for b in range(edges // BLOCK)], axis=0
    )


def fetch(sems, *pairs):
    copies = [pltpu.make_async_copy(a, b, sems.at[i]) for i, (a, b) in enumerate(pairs)]
    for copy in copies:
        copy.start()
    return copies


def send_kernel(node_hbm, send_hbm, node_ref, send_ref, *rest):
    *out_refs, sems = rest
    for copy in fetch(sems, (node_hbm, node_ref), (send_hbm, send_ref)):
        copy.wait()
    node = node_ref[...]
    rows = node.shape[0]
    halo = send_ref.shape[2]
    pieces = []
    for d in range(4):
        pick = one_hot(iota((rows, halo), 0) == send_ref[0, d : d + 1, :])
        pieces.append(dot(pick, node, TN).astype(bf16))
    out_refs[0][...] = pieces[0]
    out_refs[1][...] = pieces[1]
    if len(out_refs) == 3:
        out_refs[2][0:halo, :] = pieces[2]
        out_refs[2][halo:, :] = pieces[3]
    else:
        out_refs[2][...] = pieces[2]
        out_refs[3][...] = pieces[3]


def local_kernel(*refs):
    node_ref, ins, refs = refs[0], refs[1 : 1 + N_FETCHED], refs[1 + N_FETCHED :]
    pre_ref, pick_ref, collect_ref, spread_ref, scatter_ref, *refs = refs
    w_src_ref, w_dst_ref, w_out_ref, gain_ref, cot_ref, count_ref, src_ref, dst_ref, bias_ref, sems = refs
    outs = (src_ref, dst_ref, count_ref, bias_ref, w_src_ref, w_dst_ref, w_out_ref, gain_ref, cot_ref)
    copies = fetch(sems, *zip(ins, outs))
    node = node_ref[...]
    rows = node.shape[0]
    edges = src_ref.shape[1]
    for copy in copies[:3]:
        copy.wait()
    scatter_ref[...] = one_hot(iota(scatter_ref.shape, 0) == src_ref[...])
    used = usable_row(count_ref, edges) > 0
    collect_ref[...] = one_hot((iota((rows, edges), 0) == dst_ref[...]) & used)
    source = columns_of(src_ref[...], 128)
    target = columns_of(dst_ref[...], 128)
    lane = iota(source.shape, 1)
    used = usable_columns(count_ref, edges, 128) > 0
    near = one_hot(source == lane)
    pick_ref[...] = one_hot(source == lane + rows)
    spread_ref[...] = one_hot((target == lane) & used)
    both = jnp.concatenate([dot(near, node), dot(one_hot(target == lane), node)], axis=1).astype(bf16)
    for copy in copies[3:]:
        copy.wait()
    weights = jnp.concatenate([w_src_ref[...], w_dst_ref[...]], axis=0)
    pre_ref[...] = dot(both, weights) + bias_ref[...]


def twice(x):
    return jnp.concatenate([x, x], axis=1)


def stacked(x):
    return jnp.concatenate(split(x), axis=0)


def forward_kernel(pre_ref, pick_ref, collect_ref, w_src_ref, w_out_ref, *rest):
    *halo_refs, factor_ref, hidden_ref, partial_ref = rest
    halo = jnp.concatenate([r[...] for r in halo_refs], axis=0)
    far = stacked(dot(halo, w_src_ref[...]))
    pre = pre_ref[...] + dot(twice(pick_ref[...]), far)
    sig = 0.5 + 0.5 * jnp.tanh(0.5 * pre)
    factor_ref[...] = sig * (1.0 + pre * (1.0 - sig))
    hidden = dot(collect_ref[...], (pre * sig).astype(bf16))
    high, low = split(hidden)
    hidden_ref[...] = high
    w_out = w_out_ref[...]
    partial_ref[...] = (dot(high, w_out) + dot(low, w_out)).astype(bf16)


def backward_kernel(
    geometry,
    node_ref, collect_ref, spread_ref, scatter_ref, w_out_ref, gain_ref, cot_ref,
    factor_ref, hidden_ref, own_ref, other_ref,
    *rest,
):
    peers, chunk, n_halo, paired = geometry
    *rest, out_scratch, back_scratch, pair_scratch = rest
    halo_refs = rest[:n_halo]
    normed_ref, local_ref, target_ref, *message_refs = rest[n_halo:]
    node = node_ref[...]
    rows, width = node.shape
    aggregate = own_ref[...].astype(f32) + other_ref[...].astype(f32)
    center = aggregate - jnp.mean(aggregate, axis=1, keepdims=True)
    variance = jnp.mean(center * center, axis=1, keepdims=True)
    inverse = lax.rsqrt(variance + EPSILON)
    normed = center * inverse
    gain = gain_ref[...]
    upstream = cot_ref[...].astype(f32)
    scaled = upstream * gain
    agg_grad = inverse * (
        scaled
        - jnp.mean(scaled, axis=1, keepdims=True)
        - normed * jnp.mean(scaled * normed, axis=1, keepdims=True)
    )
    agg_grad = agg_grad.astype(bf16)
    normed_ref[...] = normed
    gain_part = jnp.sum(upstream * normed, axis=0, keepdims=True)

    act_grad = dot(twice(spread_ref[...]), stacked(dot(agg_grad, w_out_ref[...], NT)))
    pre_grad = (act_grad * factor_ref[...]).astype(bf16)

    table = jnp.concatenate([node] + [r[...] for r in halo_refs], axis=0)
    by_source = dot(scatter_ref[...], pre_grad)
    by_target = dot(collect_ref[...], pre_grad)
    local_ref[...] = by_source[:rows]
    by_target_low = by_target.astype(bf16)
    by_source_low = by_source.astype(bf16)
    target_ref[...] = by_target_low

    hid = by_source.shape[1]
    bias_part = jnp.sum(by_target, axis=0, keepdims=True)
    src_part = dot(table, by_source_low, TN).astype(bf16)
    dst_part = dot(node, by_target_low, TN).astype(bf16)
    out_part = dot(hidden_ref[...], agg_grad, TN).astype(bf16)
    vectors = [bias_part] + [gain_part[:, at : at + hid] for at in range(0, width, hid)]
    tail = tail_of(vectors)
    back = by_source_low[rows:]

    if paired:
        sends, keeps, out_refs = message_refs[:3], message_refs[3:6], message_refs[6:]
        sub = lax.axis_index("sub")
        mesh = lax.axis_index("mesh")
        lines = len(out_refs)
        halo = back.shape[0] // 4
        first = sub == 0
        pair_scratch[0] = jnp.where(first, dst_part, src_part)
        pair_scratch[1] = jnp.where(first, src_part, dst_part)
        strip = width // lines
        for slot, (far_ref, one_ref, zero_ref) in enumerate((sends, keeps)):
            places = ((far_ref, 0, 3), (far_ref, strip, 2), (one_ref, 0, 1), (zero_ref, 0, 0))
            for ref, at, k in places:
                start = pl.multiple_of((mesh ^ k) * strip, strip)
                ref[at : at + strip, :] = pair_scratch[slot, pl.ds(start, strip), :]
            far_ref[2 * strip :, :] = tail
        sends[2][strip:, :] = back[2 * halo :]
        back_scratch[...] = back[: 2 * halo]
        out_scratch[...] = out_part
        strip = hid // len(out_refs)
        for k, ref in enumerate(out_refs):
            start = pl.multiple_of((mesh ^ k) * strip, strip)
            ref[0:strip, :] = out_scratch[pl.ds(start, strip), :]
            if k % 2 == 1:
                slot = (mesh + (k // 2) + 1) % 2
                start = pl.multiple_of(slot * halo, halo)
                rows_back = back_scratch[pl.ds(start, halo), :]
                ref[strip:, 0:hid] = rows_back[: halo // 2]
                ref[strip:, hid:] = rows_back[halo // 2 :]
        return

    message_ref, *back_refs = message_refs
    at = 0
    for ref in back_refs:
        ref[...] = back[at : at + ref.shape[0]]
        at += ref.shape[0]
    blocks = [src_part, dst_part]
    for at in range(0, width, hid):
        blocks.append(out_part[:, at : at + hid])
    done = 0
    for block in blocks:
        at = 0
        while at < block.shape[0]:
            peer, offset = divmod(done, chunk)
            take = min(chunk - offset, block.shape[0] - at)
            message_ref[peer, offset : offset + take, :] = block[at : at + take]
            at += take
            done += take
    while done < peers * chunk:
        peer, offset = divmod(done, chunk)
        take = chunk - offset
        message_ref[peer, offset : offset + take, :] = jnp.zeros((take, hid), bf16)
        done += take
    for peer in range(peers):
        message_ref[peer, chunk:, :] = tail


def tail_of(vectors):
    tail = []
    for v in vectors:
        high = v.astype(bf16).astype(f32)
        tail += [high, v - high]
    tail.append(jnp.zeros((TAIL - len(tail), vectors[0].shape[1]), f32))
    return jnp.concatenate(tail, axis=0).astype(bf16)


def tree(terms):
    while len(terms) > 1:
        terms = [terms[i] + terms[i + 1] for i in range(0, len(terms), 2)]
    return terms[0]


def far_kernel(arrived_ref, keep_ref, three_ref, two_ref, tail_ref):
    total = keep_ref[...].astype(f32) + arrived_ref[...].astype(f32)
    strip = three_ref.shape[0] - TAIL
    tail = total[2 * strip :]
    tail = tail_of([tail[at : at + 1] + tail[at + 1 : at + 2] for at in range(0, 6, 2)])
    for k, ref in enumerate((three_ref, two_ref)):
        ref[0:strip, :] = total[k * strip : (k + 1) * strip].astype(bf16)
        ref[strip:, :] = tail
    tail_ref[...] = tail


def near_kernel(arrived_ref, keep_ref, tail_ref, one_ref):
    strip = keep_ref.shape[0]
    one_ref[0:strip, :] = (keep_ref[...].astype(f32) + arrived_ref[...].astype(f32)).astype(bf16)
    one_ref[strip:, :] = tail_ref[...]


def line_kernel(*refs):
    *terms, _, send_ref, keep_ref = refs
    rows, hid = send_ref.shape
    total = tree([r[0:rows, :].astype(f32) for r in terms])
    first = lax.axis_index("sub") == 0
    left, right = total[:, :hid], total[:, hid:]
    send_ref[...] = jnp.where(first, right, left).astype(bf16)
    keep_ref[...] = jnp.where(first, left, right).astype(bf16)


def own_kernel(*refs):
    *terms, keep_ref, arrived_ref, vectors_ref, out_keep_ref, out_arrived_ref, _, own_ref, tail_ref = refs
    strip = keep_ref.shape[0]
    zero = (keep_ref[...].astype(f32) + arrived_ref[0:strip, :].astype(f32)).astype(bf16)
    total = tree([r[0:strip, :].astype(f32) for r in terms] + [zero.astype(f32)])
    own_ref[0:strip, :] = total.astype(bf16)
    own_ref[strip:, :] = (
        out_keep_ref[...].astype(f32) + out_arrived_ref[...].astype(f32)
    ).astype(bf16)
    tail_ref[...] = tree([r[strip:, :].astype(f32) for r in terms] + [vectors_ref[...].astype(f32)])


def write_vectors(tail, bias_ref, gain_ref):
    bias_ref[...] = tail[0:1] + tail[1:2]
    hid = tail.shape[1]
    for k in range(gain_ref.shape[1] // hid):
        gain_ref[:, k * hid : (k + 1) * hid] = tail[2 + 2 * k : 3 + 2 * k] + tail[3 + 2 * k : 4 + 2 * k]


def relay_kernel(strip_ref, _, out_ref):
    out_ref[...] = strip_ref[...]


def place_kernel(order, *refs):
    count = len(order)
    mine, theirs = refs[:count], refs[count : 2 * count]
    src_ref, dst_ref, out_ref = refs[2 * count :]
    first = lax.axis_index("sub") == 0
    mesh = lax.axis_index("mesh")
    width, hid = src_ref.shape
    strip = width // count
    narrow = hid // count
    for at, k in enumerate(order):
        a, b = mine[at][...], theirs[at][...]
        low = jnp.where(first, a, b).astype(f32)
        high = jnp.where(first, b, a).astype(f32)
        start = pl.multiple_of((mesh ^ k) * strip, strip)
        src_ref[pl.ds(start, strip), :] = low[:strip]
        dst_ref[pl.ds(start, strip), :] = high[:strip]
        start = pl.multiple_of((mesh ^ k) * narrow, narrow)
        out_ref[pl.ds(start, narrow), 0:hid] = low[strip:]
        out_ref[pl.ds(start, narrow), hid:] = high[strip:]


def sum_kernel(chunk, arrived_ref, out_ref, bias_ref, gain_ref):
    peers = arrived_ref.shape[0]
    total = arrived_ref[0].astype(f32)
    for peer in range(1, peers):
        total += arrived_ref[peer].astype(f32)
    low = total[:chunk].astype(bf16)
    for peer in range(peers):
        out_ref[peer] = low
    tail = total[chunk:]
    write_vectors(tail, bias_ref, gain_ref)


def unpack_kernel(arrived_ref, src_ref, dst_ref, out_ref):
    hid = src_ref.shape[1]
    rows = src_ref.shape[0]
    src_ref[...] = arrived_ref[0:rows, :].astype(f32)
    dst_ref[...] = arrived_ref[rows : 2 * rows, :].astype(f32)
    at = 2 * rows
    for k in range(out_ref.shape[1] // hid):
        out_ref[:, k * hid : (k + 1) * hid] = arrived_ref[at : at + out_ref.shape[0], :].astype(f32)
        at += out_ref.shape[0]


def node_part(send_ref, local_ref, target_ref, w_src_ref, w_dst_ref, returned, out_ref):
    rows = local_ref.shape[0]
    halo = send_ref.shape[2]
    picks = [one_hot(iota((rows, halo), 0) == send_ref[0, d : d + 1, :]) for d in range(4)]
    total = local_ref[...] + dot(jnp.concatenate(picks, axis=1), jnp.concatenate(returned, axis=0))
    out_ref[...] = (
        dot(total.astype(bf16), w_src_ref[...], NT) + dot(target_ref[...], w_dst_ref[...], NT)
    ).astype(bf16)


def node_kernel(send_ref, local_ref, target_ref, w_src_ref, w_dst_ref, *rest):
    *back_refs, out_ref = rest
    returned = [r[...] for r in back_refs]
    node_part(send_ref, local_ref, target_ref, w_src_ref, w_dst_ref, returned, out_ref)


def paired_node_kernel(
    send_ref, local_ref, target_ref, w_src_ref, w_dst_ref, three_ref, one_ref, pair_ref, out_ref
):
    even = lax.axis_index("mesh") % 2 == 0
    halo = send_ref.shape[2]
    hid = local_ref.shape[1]
    at = one_ref.shape[0] - halo // 2
    one, three = [
        jnp.concatenate([r[at:, :hid], r[at:, hid:]], axis=0) for r in (one_ref, three_ref)
    ]
    returned = [
        jnp.where(even, one, three), jnp.where(even, three, one), pair_ref[pair_ref.shape[0] - 2 * halo :, :]
    ]
    node_part(send_ref, local_ref, target_ref, w_src_ref, w_dst_ref, returned, out_ref)


def finish_kernel(cot_ref, node_ref, gain_ref, normed_ref, own_ref, other_ref, *rest):
    if len(rest) == 5:
        tail_ref, *rest, bias_out_ref, gain_out_ref = rest
        write_vectors(tail_ref[...], bias_out_ref, gain_out_ref)
    grad_ref, updated_ref = rest
    grad_ref[...] = cot_ref[...].astype(f32) + (
        own_ref[...].astype(f32) + other_ref[...].astype(f32)
    )
    updated_ref[...] = (node_ref[...].astype(f32) + gain_ref[...] * normed_ref[...]).astype(bf16)


VMEM = pl.BlockSpec(memory_space=pltpu.VMEM)
SMEM = pl.BlockSpec(memory_space=pltpu.SMEM)
HBM = pl.BlockSpec(memory_space=pltpu.HBM)


def shape(dims, dtype):
    return jax.ShapeDtypeStruct(dims, dtype)


def call(kernel, outs, *args, specs=None, out_specs=None, flops=10**8, scratch=()):
    return pl.pallas_call(
        kernel,
        out_shape=outs,
        in_specs=specs or [VMEM] * len(args),
        out_specs=out_specs or jax.tree.map(lambda _: VMEM, outs),
        scratch_shapes=scratch,
        compiler_params=pltpu.CompilerParams(vmem_limit_bytes=VMEM_LIMIT),
        cost_estimate=pl.CostEstimate(flops=flops, bytes_accessed=10**6, transcendentals=0),
    )(*args)


def shifted(x, axis, by):
    count = lax.axis_size(axis)
    return lax.ppermute(x, axis, [(i, (i + by) % count) for i in range(count)])


def across(x, axis, k):
    count = lax.axis_size(axis)
    return lax.ppermute(x, axis, [(i, i ^ k) for i in range(count)])


def paired_sums(messages, lines, strip, narrow, width, hid, node_terms):
    sends, keeps, outs = messages[:3], messages[3:6], messages[6:]
    order = range(lines - 1, 0, -1)
    block = shape((strip + TAIL, hid), bf16)
    far = across(sends[0], "sub", 1)
    out_terms = {k: across(outs[k], "mesh", k) for k in order}
    one = across(sends[1], "sub", 1)
    zero = across(sends[2], "sub", 1)
    line = {}
    line[3], line[2], tail = call(far_kernel, [block, block, shape((TAIL, hid), bf16)], far, keeps[0])
    line[1] = call(near_kernel, block, one, keeps[1], tail)
    line_terms = {k: across(line[k], "mesh", k) for k in order}
    out_send, out_keep = call(
        line_kernel,
        [shape((narrow, hid), bf16)] * 2,
        *[out_terms[k] for k in order], outs[0], line[1],
    )
    node_part = node_terms(out_terms[3], out_terms[1], zero)
    own, tail = call(
        own_kernel,
        [shape((strip + narrow, hid), bf16), shape((TAIL, hid), f32)],
        *[line_terms[k] for k in order], keeps[2], zero, tail, out_keep, across(out_send, "sub", 1),
        node_part,
    )
    mine = {k: across(own, "mesh", k) for k in order}
    mine[0] = own
    theirs = {0: across(own, "sub", 1)}
    first = call(relay_kernel, shape(own.shape, bf16), mine[2], theirs[0])
    theirs |= {k: across(first if k == 2 else mine[k], "sub", 1) for k in order}
    placed = (0, 3, 1, 2)
    grads = call(
        functools.partial(place_kernel, placed),
        [shape((width, hid), f32), shape((width, hid), f32), shape((hid, width), f32)],
        *[mine[k] for k in placed], *[theirs[k] for k in placed],
    )
    return (*grads, tail), node_part


def shards(
    node_state,
    send_rows,
    edge_src,
    edge_dst,
    block_count,
    w_src,
    w_dst,
    hidden_bias,
    w_out,
    norm_gain,
    cotangent,
):
    rows, width = node_state.shape
    hid = w_src.shape[1]
    halo = send_rows.shape[2]
    edges = edge_src.shape[0]
    peers = lax.axis_size("mesh") * lax.axis_size("sub")
    merged = lax.axis_size("sub") == 2
    total_rows = 2 * width + (width // hid) * hid
    chunk = -(-total_rows // (peers * 16)) * 16

    piece = [halo, halo, 2 * halo] if merged else [halo] * 4
    routes = [("mesh", 1), ("mesh", -1), ("sub", 1)] + ([] if merged else [("sub", -1)])
    n_halo = len(piece)

    def in_hbm(x):
        return pltpu.with_memory_space_constraint(x, pltpu.HBM)

    node, send, *outgoing = call(
        send_kernel,
        [shape((rows, width), bf16), shape(send_rows.shape, jnp.int32)]
        + [shape((n, width), bf16) for n in piece],
        in_hbm(node_state), in_hbm(send_rows),
        specs=[HBM, HBM],
        scratch=[pltpu.SemaphoreType.DMA((2,))],
    )
    arrived = [shifted(x, axis, by) for x, (axis, by) in zip(outgoing, routes)]

    fetched = [
        edge_src.reshape(1, edges), edge_dst.reshape(1, edges), block_count,
        hidden_bias.reshape(1, hid), w_src, w_dst, w_out, norm_gain.reshape(1, width), cotangent,
    ]
    pre, pick, collect, spread, scatter, w_src, w_dst, w_out, gain, cot = call(
        local_kernel,
        [
            shape((edges, hid), f32),
            shape((edges, 4 * halo), bf16),
            shape((rows, edges), bf16),
            shape((edges, rows), bf16),
            shape((rows + 4 * halo, edges), bf16),
        ]
        + [shape(x.shape, x.dtype) for x in fetched[4:]],
        node, *[in_hbm(x) for x in fetched],
        specs=[VMEM] + [HBM] * len(fetched),
        scratch=[
            pltpu.SMEM(block_count.shape, jnp.int32),
            pltpu.VMEM((1, edges), jnp.int32),
            pltpu.VMEM((1, edges), jnp.int32),
            pltpu.VMEM((1, hid), f32),
            pltpu.SemaphoreType.DMA((N_FETCHED,)),
        ],
    )

    factor, hidden, partial = call(
        forward_kernel,
        [shape((edges, hid), f32), shape((rows, hid), bf16), shape((rows, width), bf16)],
        pre, pick, collect, w_src, w_out, *arrived,
    )
    other = shifted(partial, "lat", 1)

    lines = lax.axis_size("mesh")
    paired = merged and lines == 4
    if paired:
        strip = width // lines
        narrow = hid // lines
        rows_of = (2 * strip + TAIL, strip, strip + 2 * halo, 2 * strip + TAIL, strip, strip)
        message_shapes = [shape((n, hid), bf16) for n in rows_of]
        message_shapes += [shape((narrow + k % 2 * (halo // 2), width), bf16) for k in range(lines)]
    else:
        message_shapes = [shape((peers, chunk + TAIL, hid), bf16)]
        message_shapes += [shape((n, hid), bf16) for n in piece]
    normed, local, target, *messages = call(
        functools.partial(backward_kernel, (peers, chunk, n_halo, paired)),
        [shape((rows, width), f32), shape((rows, hid), f32), shape((rows, hid), bf16)]
        + message_shapes,
        node, collect, spread, scatter, w_out, gain, cot, factor, hidden, partial, other, *arrived,
        scratch=[
            pltpu.VMEM((hid, width), bf16),
            pltpu.VMEM((2 * halo, hid), bf16),
            pltpu.VMEM((2, width, hid), bf16),
        ],
    )

    def node_terms(*returned):
        return call(
            paired_node_kernel if paired else node_kernel,
            shape((rows, width), bf16),
            send, local, target, w_src, w_dst, *returned,
        )

    if paired:
        (src_grad, dst_grad, out_grad, tail), node_part = paired_sums(
            messages, lines, strip, narrow, width, hid, node_terms
        )
    else:
        node_part = node_terms(
            *[shifted(x, axis, -by) for x, (axis, by) in zip(messages[1:], routes)]
        )
        exchanged = lax.all_to_all(messages[0], ("mesh", "sub"), 0, 0)
        reduced, bias_grad, gain_grad = call(
            functools.partial(sum_kernel, chunk),
            [shape((peers, chunk, hid), bf16), shape((1, hid), f32), shape((1, width), f32)],
            exchanged,
        )
        gathered = lax.all_to_all(reduced, ("mesh", "sub"), 0, 0)
        src_grad, dst_grad, out_grad = call(
            unpack_kernel,
            [shape((width, hid), f32), shape((width, hid), f32), shape((hid, width), f32)],
            gathered.reshape(peers * chunk, hid),
        )
    finished = [shape((rows, width), f32), shape((rows, width), bf16)]
    ends = [cot, node, gain, normed, node_part, shifted(node_part, "lat", 1)]
    if paired:
        node_grad, updated, bias_grad, gain_grad = call(
            finish_kernel, finished + [shape((1, hid), f32), shape((1, width), f32)], *ends, tail
        )
    else:
        node_grad, updated = call(finish_kernel, finished, *ends)
    return (
        updated, node_grad, src_grad, dst_grad, out_grad,
        bias_grad.reshape(hid), gain_grad.reshape(width),
    )


def solution(mesh):
    nodes = P(("parts", "mesh", "sub"), None)
    slots = P(("parts", "mesh", "sub"))
    in_specs = (
        nodes,
        P(("parts", "mesh", "sub"), None, None),
        slots,
        slots,
        slots,
        P(None, "lat"),
        P(None, "lat"),
        P("lat"),
        P("lat", None),
        P(),
        nodes,
    )
    out_specs = (
        nodes,
        nodes,
        P("parts", "lat"),
        P("parts", "lat"),
        P(("parts", "lat"), None),
        P(("parts", "lat")),
        P("parts"),
    )
    return jax.shard_map(shards, mesh=mesh, in_specs=in_specs, out_specs=out_specs, check_vma=False)
```

```python
import functools

import jax
import jax.numpy as jnp
from jax import lax
from jax.experimental import pallas as pl
from jax.experimental.pallas import tpu as pltpu
from jax.sharding import PartitionSpec as P

BLOCK = 128
EPSILON = 1e-05
TAIL = 16
N_FETCHED = 9
VMEM_LIMIT = 24 * 1024 * 1024

f32 = jnp.float32
bf16 = jnp.bfloat16

NN = (((1,), (0,)), ((), ()))
NT = (((1,), (1,)), ((), ()))
TN = (((0,), (0,)), ((), ()))


def dot(a, b, dims=NN):
    return lax.dot_general(a, b, dims, preferred_element_type=f32)


def iota(shape, dim):
    return lax.broadcasted_iota(jnp.int32, shape, dim)


def one_hot(condition):
    return jnp.where(condition, 1.0, 0.0).astype(bf16)


def split(x):
    high = x.astype(bf16)
    return high, (x - high.astype(f32)).astype(bf16)


def columns_of(row, lanes):
    return jnp.transpose(jnp.broadcast_to(row, (lanes, row.shape[1])))


def usable_row(count_ref, edges):
    lane = iota((1, BLOCK), 1)
    parts = [lane < count_ref[b] for b in range(edges // BLOCK)]
    return jnp.concatenate([jnp.where(p, 1, 0) for p in parts], axis=1)


def usable_columns(count_ref, edges, lanes):
    sub = iota((BLOCK, lanes), 0)
    return jnp.concatenate(
        [jnp.where(sub < count_ref[b], 1, 0) for b in range(edges // BLOCK)], axis=0
    )


def fetch(sems, *pairs):
    copies = [pltpu.make_async_copy(a, b, sems.at[i]) for i, (a, b) in enumerate(pairs)]
    for copy in copies:
        copy.start()
    return copies


def send_kernel(node_hbm, send_hbm, node_ref, send_ref, *rest):
    *out_refs, sems = rest
    for copy in fetch(sems, (node_hbm, node_ref), (send_hbm, send_ref)):
        copy.wait()
    node = node_ref[...]
    rows = node.shape[0]
    halo = send_ref.shape[2]
    pieces = []
    for d in range(4):
        pick = one_hot(iota((rows, halo), 0) == send_ref[0, d : d + 1, :])
        pieces.append(dot(pick, node, TN).astype(bf16))
    out_refs[0][...] = pieces[0]
    out_refs[1][...] = pieces[1]
    if len(out_refs) == 3:
        out_refs[2][0:halo, :] = pieces[2]
        out_refs[2][halo:, :] = pieces[3]
    else:
        out_refs[2][...] = pieces[2]
        out_refs[3][...] = pieces[3]


def local_kernel(*refs):
    node_ref, ins, refs = refs[0], refs[1 : 1 + N_FETCHED], refs[1 + N_FETCHED :]
    pre_ref, pick_ref, collect_ref, spread_ref, scatter_ref, *refs = refs
    w_src_ref, w_dst_ref, w_out_ref, gain_ref, cot_ref, count_ref, src_ref, dst_ref, bias_ref, sems = refs
    outs = (src_ref, dst_ref, count_ref, bias_ref, w_src_ref, w_dst_ref, w_out_ref, gain_ref, cot_ref)
    copies = fetch(sems, *zip(ins, outs))
    node = node_ref[...]
    rows = node.shape[0]
    edges = src_ref.shape[1]
    for copy in copies[:3]:
        copy.wait()
    scatter_ref[...] = one_hot(iota(scatter_ref.shape, 0) == src_ref[...])
    used = usable_row(count_ref, edges) > 0
    collect_ref[...] = one_hot((iota((rows, edges), 0) == dst_ref[...]) & used)
    source = columns_of(src_ref[...], 128)
    target = columns_of(dst_ref[...], 128)
    lane = iota(source.shape, 1)
    used = usable_columns(count_ref, edges, 128) > 0
    near = one_hot(source == lane)
    pick_ref[...] = one_hot(source == lane + rows)
    spread_ref[...] = one_hot((target == lane) & used)
    both = jnp.concatenate([dot(near, node), dot(one_hot(target == lane), node)], axis=1).astype(bf16)
    for copy in copies[3:]:
        copy.wait()
    weights = jnp.concatenate([w_src_ref[...], w_dst_ref[...]], axis=0)
    pre_ref[...] = dot(both, weights) + bias_ref[...]


def twice(x):
    return jnp.concatenate([x, x], axis=1)


def stacked(x):
    return jnp.concatenate(split(x), axis=0)


def forward_kernel(pre_ref, pick_ref, collect_ref, w_src_ref, w_out_ref, *rest):
    *halo_refs, factor_ref, hidden_ref, partial_ref = rest
    halo = jnp.concatenate([r[...] for r in halo_refs], axis=0)
    far = stacked(dot(halo, w_src_ref[...]))
    pre = pre_ref[...] + dot(twice(pick_ref[...]), far)
    sig = 0.5 + 0.5 * jnp.tanh(0.5 * pre)
    factor_ref[...] = sig * (1.0 + pre * (1.0 - sig))
    hidden = dot(collect_ref[...], (pre * sig).astype(bf16))
    high, low = split(hidden)
    hidden_ref[...] = high
    w_out = w_out_ref[...]
    partial_ref[...] = (dot(high, w_out) + dot(low, w_out)).astype(bf16)


def backward_kernel(
    geometry,
    node_ref, collect_ref, spread_ref, scatter_ref, w_out_ref, gain_ref, cot_ref,
    factor_ref, hidden_ref, own_ref, other_ref,
    *rest,
):
    peers, chunk, n_halo, paired = geometry
    *rest, out_scratch, back_scratch, pair_scratch = rest
    halo_refs = rest[:n_halo]
    normed_ref, local_ref, target_ref, *message_refs = rest[n_halo:]
    node = node_ref[...]
    rows, width = node.shape
    aggregate = own_ref[...].astype(f32) + other_ref[...].astype(f32)
    center = aggregate - jnp.mean(aggregate, axis=1, keepdims=True)
    variance = jnp.mean(center * center, axis=1, keepdims=True)
    inverse = lax.rsqrt(variance + EPSILON)
    normed = center * inverse
    gain = gain_ref[...]
    upstream = cot_ref[...].astype(f32)
    scaled = upstream * gain
    agg_grad = inverse * (
        scaled
        - jnp.mean(scaled, axis=1, keepdims=True)
        - normed * jnp.mean(scaled * normed, axis=1, keepdims=True)
    )
    agg_grad = agg_grad.astype(bf16)
    normed_ref[...] = normed
    gain_part = jnp.sum(upstream * normed, axis=0, keepdims=True)

    act_grad = dot(twice(spread_ref[...]), stacked(dot(agg_grad, w_out_ref[...], NT)))
    pre_grad = (act_grad * factor_ref[...]).astype(bf16)

    table = jnp.concatenate([node] + [r[...] for r in halo_refs], axis=0)
    by_source = dot(scatter_ref[...], pre_grad)
    by_target = dot(collect_ref[...], pre_grad)
    local_ref[...] = by_source[:rows]
    by_target_low = by_target.astype(bf16)
    by_source_low = by_source.astype(bf16)
    target_ref[...] = by_target_low

    hid = by_source.shape[1]
    bias_part = jnp.sum(by_target, axis=0, keepdims=True)
    src_part = dot(table, by_source_low, TN).astype(bf16)
    dst_part = dot(node, by_target_low, TN).astype(bf16)
    out_part = dot(hidden_ref[...], agg_grad, TN).astype(bf16)
    vectors = [bias_part] + [gain_part[:, at : at + hid] for at in range(0, width, hid)]
    tail = tail_of(vectors)
    back = by_source_low[rows:]

    if paired:
        sends, keeps, out_refs = message_refs[:3], message_refs[3:6], message_refs[6:]
        sub = lax.axis_index("sub")
        mesh = lax.axis_index("mesh")
        lines = len(out_refs)
        halo = back.shape[0] // 4
        first = sub == 0
        pair_scratch[0] = jnp.where(first, dst_part, src_part)
        pair_scratch[1] = jnp.where(first, src_part, dst_part)
        strip = width // lines
        for slot, (far_ref, one_ref, zero_ref) in enumerate((sends, keeps)):
            places = ((far_ref, 0, 3), (far_ref, strip, 2), (one_ref, 0, 1), (zero_ref, 0, 0))
            for ref, at, k in places:
                start = pl.multiple_of((mesh ^ k) * strip, strip)
                ref[at : at + strip, :] = pair_scratch[slot, pl.ds(start, strip), :]
            far_ref[2 * strip :, :] = tail
        sends[2][strip:, :] = back[2 * halo :]
        back_scratch[...] = back[: 2 * halo]
        out_scratch[...] = out_part
        strip = hid // len(out_refs)
        for k, ref in enumerate(out_refs):
            start = pl.multiple_of((mesh ^ k) * strip, strip)
            ref[0:strip, :] = out_scratch[pl.ds(start, strip), :]
            if k % 2 == 1:
                slot = (mesh + (k // 2) + 1) % 2
                start = pl.multiple_of(slot * halo, halo)
                rows_back = back_scratch[pl.ds(start, halo), :]
                ref[strip:, 0:hid] = rows_back[: halo // 2]
                ref[strip:, hid:] = rows_back[halo // 2 :]
        return

    message_ref, *back_refs = message_refs
    at = 0
    for ref in back_refs:
        ref[...] = back[at : at + ref.shape[0]]
        at += ref.shape[0]
    blocks = [src_part, dst_part]
    for at in range(0, width, hid):
        blocks.append(out_part[:, at : at + hid])
    done = 0
    for block in blocks:
        at = 0
        while at < block.shape[0]:
            peer, offset = divmod(done, chunk)
            take = min(chunk - offset, block.shape[0] - at)
            message_ref[peer, offset : offset + take, :] = block[at : at + take]
            at += take
            done += take
    while done < peers * chunk:
        peer, offset = divmod(done, chunk)
        take = chunk - offset
        message_ref[peer, offset : offset + take, :] = jnp.zeros((take, hid), bf16)
        done += take
    for peer in range(peers):
        message_ref[peer, chunk:, :] = tail


def tail_of(vectors):
    tail = []
    for v in vectors:
        high = v.astype(bf16).astype(f32)
        tail += [high, v - high]
    tail.append(jnp.zeros((TAIL - len(tail), vectors[0].shape[1]), f32))
    return jnp.concatenate(tail, axis=0).astype(bf16)


def tree(terms):
    while len(terms) > 1:
        terms = [terms[i] + terms[i + 1] for i in range(0, len(terms), 2)]
    return terms[0]


def far_kernel(arrived_ref, keep_ref, three_ref, two_ref, tail_ref):
    total = keep_ref[...].astype(f32) + arrived_ref[...].astype(f32)
    strip = three_ref.shape[0] - TAIL
    tail = total[2 * strip :]
    tail = tail_of([tail[at : at + 1] + tail[at + 1 : at + 2] for at in range(0, 6, 2)])
    for k, ref in enumerate((three_ref, two_ref)):
        ref[0:strip, :] = total[k * strip : (k + 1) * strip].astype(bf16)
        ref[strip:, :] = tail
    tail_ref[...] = tail


def near_kernel(arrived_ref, keep_ref, tail_ref, one_ref):
    strip = keep_ref.shape[0]
    one_ref[0:strip, :] = (keep_ref[...].astype(f32) + arrived_ref[...].astype(f32)).astype(bf16)
    one_ref[strip:, :] = tail_ref[...]


def line_kernel(*refs):
    *terms, _, send_ref, keep_ref = refs
    rows, hid = send_ref.shape
    total = tree([r[0:rows, :].astype(f32) for r in terms])
    first = lax.axis_index("sub") == 0
    left, right = total[:, :hid], total[:, hid:]
    send_ref[...] = jnp.where(first, right, left).astype(bf16)
    keep_ref[...] = jnp.where(first, left, right).astype(bf16)


def own_kernel(*refs):
    *terms, keep_ref, arrived_ref, vectors_ref, out_keep_ref, out_arrived_ref, _, own_ref, tail_ref = refs
    strip = keep_ref.shape[0]
    zero = (keep_ref[...].astype(f32) + arrived_ref[0:strip, :].astype(f32)).astype(bf16)
    total = tree([r[0:strip, :].astype(f32) for r in terms] + [zero.astype(f32)])
    own_ref[0:strip, :] = total.astype(bf16)
    own_ref[strip:, :] = (
        out_keep_ref[...].astype(f32) + out_arrived_ref[...].astype(f32)
    ).astype(bf16)
    tail_ref[...] = tree([r[strip:, :].astype(f32) for r in terms] + [vectors_ref[...].astype(f32)])


def write_vectors(tail, bias_ref, gain_ref):
    bias_ref[...] = tail[0:1] + tail[1:2]
    hid = tail.shape[1]
    for k in range(gain_ref.shape[1] // hid):
        gain_ref[:, k * hid : (k + 1) * hid] = tail[2 + 2 * k : 3 + 2 * k] + tail[3 + 2 * k : 4 + 2 * k]


def place_kernel(order, *refs):
    count = len(order)
    mine, theirs = refs[:count], refs[count : 2 * count]
    src_ref, dst_ref, out_ref = refs[2 * count :]
    first = lax.axis_index("sub") == 0
    mesh = lax.axis_index("mesh")
    width, hid = src_ref.shape
    strip = width // count
    narrow = hid // count
    for at, k in enumerate(order):
        a, b = mine[at][...], theirs[at][...]
        low = jnp.where(first, a, b).astype(f32)
        high = jnp.where(first, b, a).astype(f32)
        start = pl.multiple_of((mesh ^ k) * strip, strip)
        src_ref[pl.ds(start, strip), :] = low[:strip]
        dst_ref[pl.ds(start, strip), :] = high[:strip]
        start = pl.multiple_of((mesh ^ k) * narrow, narrow)
        out_ref[pl.ds(start, narrow), 0:hid] = low[strip:]
        out_ref[pl.ds(start, narrow), hid:] = high[strip:]


def sum_kernel(chunk, arrived_ref, out_ref, bias_ref, gain_ref):
    peers = arrived_ref.shape[0]
    total = arrived_ref[0].astype(f32)
    for peer in range(1, peers):
        total += arrived_ref[peer].astype(f32)
    low = total[:chunk].astype(bf16)
    for peer in range(peers):
        out_ref[peer] = low
    tail = total[chunk:]
    write_vectors(tail, bias_ref, gain_ref)


def unpack_kernel(arrived_ref, src_ref, dst_ref, out_ref):
    hid = src_ref.shape[1]
    rows = src_ref.shape[0]
    src_ref[...] = arrived_ref[0:rows, :].astype(f32)
    dst_ref[...] = arrived_ref[rows : 2 * rows, :].astype(f32)
    at = 2 * rows
    for k in range(out_ref.shape[1] // hid):
        out_ref[:, k * hid : (k + 1) * hid] = arrived_ref[at : at + out_ref.shape[0], :].astype(f32)
        at += out_ref.shape[0]


def node_part(send_ref, local_ref, target_ref, w_src_ref, w_dst_ref, returned, out_ref):
    rows = local_ref.shape[0]
    halo = send_ref.shape[2]
    picks = [one_hot(iota((rows, halo), 0) == send_ref[0, d : d + 1, :]) for d in range(4)]
    total = local_ref[...] + dot(jnp.concatenate(picks, axis=1), jnp.concatenate(returned, axis=0))
    out_ref[...] = (
        dot(total.astype(bf16), w_src_ref[...], NT) + dot(target_ref[...], w_dst_ref[...], NT)
    ).astype(bf16)


def node_kernel(send_ref, local_ref, target_ref, w_src_ref, w_dst_ref, *rest):
    *back_refs, out_ref = rest
    returned = [r[...] for r in back_refs]
    node_part(send_ref, local_ref, target_ref, w_src_ref, w_dst_ref, returned, out_ref)


def paired_node_kernel(
    send_ref, local_ref, target_ref, w_src_ref, w_dst_ref, three_ref, one_ref, pair_ref, out_ref
):
    even = lax.axis_index("mesh") % 2 == 0
    halo = send_ref.shape[2]
    hid = local_ref.shape[1]
    at = one_ref.shape[0] - halo // 2
    one, three = [
        jnp.concatenate([r[at:, :hid], r[at:, hid:]], axis=0) for r in (one_ref, three_ref)
    ]
    returned = [
        jnp.where(even, one, three), jnp.where(even, three, one), pair_ref[pair_ref.shape[0] - 2 * halo :, :]
    ]
    node_part(send_ref, local_ref, target_ref, w_src_ref, w_dst_ref, returned, out_ref)


def finish_kernel(cot_ref, node_ref, gain_ref, normed_ref, own_ref, other_ref, *rest):
    if len(rest) == 5:
        tail_ref, *rest, bias_out_ref, gain_out_ref = rest
        write_vectors(tail_ref[...], bias_out_ref, gain_out_ref)
    grad_ref, updated_ref = rest
    grad_ref[...] = cot_ref[...].astype(f32) + (
        own_ref[...].astype(f32) + other_ref[...].astype(f32)
    )
    updated_ref[...] = (node_ref[...].astype(f32) + gain_ref[...] * normed_ref[...]).astype(bf16)


VMEM = pl.BlockSpec(memory_space=pltpu.VMEM)
SMEM = pl.BlockSpec(memory_space=pltpu.SMEM)
HBM = pl.BlockSpec(memory_space=pltpu.HBM)


def shape(dims, dtype):
    return jax.ShapeDtypeStruct(dims, dtype)


def call(kernel, outs, *args, specs=None, out_specs=None, flops=10**8, scratch=()):
    return pl.pallas_call(
        kernel,
        out_shape=outs,
        in_specs=specs or [VMEM] * len(args),
        out_specs=out_specs or jax.tree.map(lambda _: VMEM, outs),
        scratch_shapes=scratch,
        compiler_params=pltpu.CompilerParams(vmem_limit_bytes=VMEM_LIMIT),
        cost_estimate=pl.CostEstimate(flops=flops, bytes_accessed=10**6, transcendentals=0),
    )(*args)


def shifted(x, axis, by):
    count = lax.axis_size(axis)
    return lax.ppermute(x, axis, [(i, (i + by) % count) for i in range(count)])


def across(x, axis, k):
    count = lax.axis_size(axis)
    return lax.ppermute(x, axis, [(i, i ^ k) for i in range(count)])


def paired_sums(messages, lines, strip, narrow, width, hid, node_terms):
    sends, keeps, outs = messages[:3], messages[3:6], messages[6:]
    order = range(lines - 1, 0, -1)
    block = shape((strip + TAIL, hid), bf16)
    far = across(sends[0], "sub", 1)
    out_terms = {k: across(outs[k], "mesh", k) for k in order}
    one = across(sends[1], "sub", 1)
    zero = across(sends[2], "sub", 1)
    line = {}
    line[3], line[2], tail = call(far_kernel, [block, block, shape((TAIL, hid), bf16)], far, keeps[0])
    line[1] = call(near_kernel, block, one, keeps[1], tail)
    line_terms = {k: across(line[k], "mesh", k) for k in order}
    out_send, out_keep = call(
        line_kernel,
        [shape((narrow, hid), bf16)] * 2,
        *[out_terms[k] for k in order], outs[0], line[1],
    )
    node_part = node_terms(out_terms[3], out_terms[1], zero)
    own, tail = call(
        own_kernel,
        [shape((strip + narrow, hid), bf16), shape((TAIL, hid), f32)],
        *[line_terms[k] for k in order], keeps[2], zero, tail, out_keep, across(out_send, "sub", 1),
        node_part,
    )
    mine = {k: across(own, "mesh", k) for k in order}
    mine[0] = own
    theirs = {0: across(own, "sub", 1)}
    theirs[1] = across(theirs[0], "mesh", 1)
    theirs |= {k: across(mine[k], "sub", 1) for k in (3, 2)}
    placed = (0, 3, 1, 2)
    grads = call(
        functools.partial(place_kernel, placed),
        [shape((width, hid), f32), shape((width, hid), f32), shape((hid, width), f32)],
        *[mine[k] for k in placed], *[theirs[k] for k in placed],
    )
    return (*grads, tail), node_part


def shards(
    node_state,
    send_rows,
    edge_src,
    edge_dst,
    block_count,
    w_src,
    w_dst,
    hidden_bias,
    w_out,
    norm_gain,
    cotangent,
):
    rows, width = node_state.shape
    hid = w_src.shape[1]
    halo = send_rows.shape[2]
    edges = edge_src.shape[0]
    peers = lax.axis_size("mesh") * lax.axis_size("sub")
    merged = lax.axis_size("sub") == 2
    total_rows = 2 * width + (width // hid) * hid
    chunk = -(-total_rows // (peers * 16)) * 16

    piece = [halo, halo, 2 * halo] if merged else [halo] * 4
    routes = [("mesh", 1), ("mesh", -1), ("sub", 1)] + ([] if merged else [("sub", -1)])
    n_halo = len(piece)

    def in_hbm(x):
        return pltpu.with_memory_space_constraint(x, pltpu.HBM)

    node, send, *outgoing = call(
        send_kernel,
        [shape((rows, width), bf16), shape(send_rows.shape, jnp.int32)]
        + [shape((n, width), bf16) for n in piece],
        in_hbm(node_state), in_hbm(send_rows),
        specs=[HBM, HBM],
        scratch=[pltpu.SemaphoreType.DMA((2,))],
    )
    arrived = [shifted(x, axis, by) for x, (axis, by) in zip(outgoing, routes)]

    fetched = [
        edge_src.reshape(1, edges), edge_dst.reshape(1, edges), block_count,
        hidden_bias.reshape(1, hid), w_src, w_dst, w_out, norm_gain.reshape(1, width), cotangent,
    ]
    pre, pick, collect, spread, scatter, w_src, w_dst, w_out, gain, cot = call(
        local_kernel,
        [
            shape((edges, hid), f32),
            shape((edges, 4 * halo), bf16),
            shape((rows, edges), bf16),
            shape((edges, rows), bf16),
            shape((rows + 4 * halo, edges), bf16),
        ]
        + [shape(x.shape, x.dtype) for x in fetched[4:]],
        node, *[in_hbm(x) for x in fetched],
        specs=[VMEM] + [HBM] * len(fetched),
        scratch=[
            pltpu.SMEM(block_count.shape, jnp.int32),
            pltpu.VMEM((1, edges), jnp.int32),
            pltpu.VMEM((1, edges), jnp.int32),
            pltpu.VMEM((1, hid), f32),
            pltpu.SemaphoreType.DMA((N_FETCHED,)),
        ],
    )

    factor, hidden, partial = call(
        forward_kernel,
        [shape((edges, hid), f32), shape((rows, hid), bf16), shape((rows, width), bf16)],
        pre, pick, collect, w_src, w_out, *arrived,
    )
    other = shifted(partial, "lat", 1)

    lines = lax.axis_size("mesh")
    paired = merged and lines == 4
    if paired:
        strip = width // lines
        narrow = hid // lines
        rows_of = (2 * strip + TAIL, strip, strip + 2 * halo, 2 * strip + TAIL, strip, strip)
        message_shapes = [shape((n, hid), bf16) for n in rows_of]
        message_shapes += [shape((narrow + k % 2 * (halo // 2), width), bf16) for k in range(lines)]
    else:
        message_shapes = [shape((peers, chunk + TAIL, hid), bf16)]
        message_shapes += [shape((n, hid), bf16) for n in piece]
    normed, local, target, *messages = call(
        functools.partial(backward_kernel, (peers, chunk, n_halo, paired)),
        [shape((rows, width), f32), shape((rows, hid), f32), shape((rows, hid), bf16)]
        + message_shapes,
        node, collect, spread, scatter, w_out, gain, cot, factor, hidden, partial, other, *arrived,
        scratch=[
            pltpu.VMEM((hid, width), bf16),
            pltpu.VMEM((2 * halo, hid), bf16),
            pltpu.VMEM((2, width, hid), bf16),
        ],
    )

    def node_terms(*returned):
        return call(
            paired_node_kernel if paired else node_kernel,
            shape((rows, width), bf16),
            send, local, target, w_src, w_dst, *returned,
        )

    if paired:
        (src_grad, dst_grad, out_grad, tail), node_part = paired_sums(
            messages, lines, strip, narrow, width, hid, node_terms
        )
    else:
        node_part = node_terms(
            *[shifted(x, axis, -by) for x, (axis, by) in zip(messages[1:], routes)]
        )
        exchanged = lax.all_to_all(messages[0], ("mesh", "sub"), 0, 0)
        reduced, bias_grad, gain_grad = call(
            functools.partial(sum_kernel, chunk),
            [shape((peers, chunk, hid), bf16), shape((1, hid), f32), shape((1, width), f32)],
            exchanged,
        )
        gathered = lax.all_to_all(reduced, ("mesh", "sub"), 0, 0)
        src_grad, dst_grad, out_grad = call(
            unpack_kernel,
            [shape((width, hid), f32), shape((width, hid), f32), shape((hid, width), f32)],
            gathered.reshape(peers * chunk, hid),
        )
    finished = [shape((rows, width), f32), shape((rows, width), bf16)]
    ends = [cot, node, gain, normed, node_part, shifted(node_part, "lat", 1)]
    if paired:
        node_grad, updated, bias_grad, gain_grad = call(
            finish_kernel, finished + [shape((1, hid), f32), shape((1, width), f32)], *ends, tail
        )
    else:
        node_grad, updated = call(finish_kernel, finished, *ends)
    return (
        updated, node_grad, src_grad, dst_grad, out_grad,
        bias_grad.reshape(hid), gain_grad.reshape(width),
    )


def solution(mesh):
    nodes = P(("parts", "mesh", "sub"), None)
    slots = P(("parts", "mesh", "sub"))
    in_specs = (
        nodes,
        P(("parts", "mesh", "sub"), None, None),
        slots,
        slots,
        slots,
        P(None, "lat"),
        P(None, "lat"),
        P("lat"),
        P("lat", None),
        P(),
        nodes,
    )
    out_specs = (
        nodes,
        nodes,
        P("parts", "lat"),
        P("parts", "lat"),
        P(("parts", "lat"), None),
        P(("parts", "lat")),
        P("parts"),
    )
    return jax.shard_map(shards, mesh=mesh, in_specs=in_specs, out_specs=out_specs, check_vma=False)
```

```python
import functools

import jax
import jax.numpy as jnp
from jax import lax
from jax.experimental import pallas as pl
from jax.experimental.pallas import tpu as pltpu
from jax.sharding import PartitionSpec as P

BLOCK = 128
EPSILON = 1e-05
TAIL = 16
CUT = 32
N_FETCHED = 9
VMEM_LIMIT = 24 * 1024 * 1024

f32 = jnp.float32
bf16 = jnp.bfloat16

NN = (((1,), (0,)), ((), ()))
NT = (((1,), (1,)), ((), ()))
TN = (((0,), (0,)), ((), ()))


def dot(a, b, dims=NN):
    return lax.dot_general(a, b, dims, preferred_element_type=f32)


def iota(shape, dim):
    return lax.broadcasted_iota(jnp.int32, shape, dim)


def one_hot(condition):
    return jnp.where(condition, 1.0, 0.0).astype(bf16)


def split(x):
    high = x.astype(bf16)
    return high, (x - high.astype(f32)).astype(bf16)


def columns_of(row, lanes):
    return jnp.transpose(jnp.broadcast_to(row, (lanes, row.shape[1])))


def usable_row(count_ref, edges):
    lane = iota((1, BLOCK), 1)
    parts = [lane < count_ref[b] for b in range(edges // BLOCK)]
    return jnp.concatenate([jnp.where(p, 1, 0) for p in parts], axis=1)


def usable_columns(count_ref, edges, lanes):
    sub = iota((BLOCK, lanes), 0)
    return jnp.concatenate(
        [jnp.where(sub < count_ref[b], 1, 0) for b in range(edges // BLOCK)], axis=0
    )


def fetch(sems, *pairs):
    copies = [pltpu.make_async_copy(a, b, sems.at[i]) for i, (a, b) in enumerate(pairs)]
    for copy in copies:
        copy.start()
    return copies


def send_kernel(node_hbm, send_hbm, node_ref, send_ref, *rest):
    *out_refs, sems = rest
    for copy in fetch(sems, (node_hbm, node_ref), (send_hbm, send_ref)):
        copy.wait()
    node = node_ref[...]
    rows = node.shape[0]
    halo = send_ref.shape[2]
    pieces = []
    for d in range(4):
        pick = one_hot(iota((rows, halo), 0) == send_ref[0, d : d + 1, :])
        pieces.append(dot(pick, node, TN).astype(bf16))
    out_refs[0][...] = pieces[0]
    out_refs[1][...] = pieces[1]
    if len(out_refs) == 3:
        out_refs[2][0:halo, :] = pieces[2]
        out_refs[2][halo:, :] = pieces[3]
    else:
        out_refs[2][...] = pieces[2]
        out_refs[3][...] = pieces[3]


def local_kernel(*refs):
    node_ref, ins, refs = refs[0], refs[1 : 1 + N_FETCHED], refs[1 + N_FETCHED :]
    pre_ref, pick_ref, collect_ref, spread_ref, scatter_ref, *refs = refs
    w_src_ref, w_dst_ref, w_out_ref, gain_ref, cot_ref, count_ref, src_ref, dst_ref, bias_ref, sems = refs
    outs = (src_ref, dst_ref, count_ref, bias_ref, w_src_ref, w_dst_ref, w_out_ref, gain_ref, cot_ref)
    copies = fetch(sems, *zip(ins, outs))
    node = node_ref[...]
    rows = node.shape[0]
    edges = src_ref.shape[1]
    for copy in copies[:3]:
        copy.wait()
    scatter_ref[...] = one_hot(iota(scatter_ref.shape, 0) == src_ref[...])
    used = usable_row(count_ref, edges) > 0
    collect_ref[...] = one_hot((iota((rows, edges), 0) == dst_ref[...]) & used)
    source = columns_of(src_ref[...], 128)
    target = columns_of(dst_ref[...], 128)
    lane = iota(source.shape, 1)
    used = usable_columns(count_ref, edges, 128) > 0
    near = one_hot(source == lane)
    pick_ref[...] = one_hot(source == lane + rows)
    spread_ref[...] = one_hot((target == lane) & used)
    both = jnp.concatenate([dot(near, node), dot(one_hot(target == lane), node)], axis=1).astype(bf16)
    for copy in copies[3:]:
        copy.wait()
    weights = jnp.concatenate([w_src_ref[...], w_dst_ref[...]], axis=0)
    pre_ref[...] = dot(both, weights) + bias_ref[...]


def twice(x):
    return jnp.concatenate([x, x], axis=1)


def stacked(x):
    return jnp.concatenate(split(x), axis=0)


def forward_kernel(pre_ref, pick_ref, collect_ref, w_src_ref, w_out_ref, *rest):
    *halo_refs, factor_ref, hidden_ref, partial_ref = rest
    halo = jnp.concatenate([r[...] for r in halo_refs], axis=0)
    far = stacked(dot(halo, w_src_ref[...]))
    pre = pre_ref[...] + dot(twice(pick_ref[...]), far)
    sig = 0.5 + 0.5 * jnp.tanh(0.5 * pre)
    factor_ref[...] = sig * (1.0 + pre * (1.0 - sig))
    hidden = dot(collect_ref[...], (pre * sig).astype(bf16))
    high, low = split(hidden)
    hidden_ref[...] = high
    w_out = w_out_ref[...]
    partial_ref[...] = (dot(high, w_out) + dot(low, w_out)).astype(bf16)


def backward_kernel(
    geometry,
    node_ref, collect_ref, spread_ref, scatter_ref, w_out_ref, gain_ref, cot_ref,
    factor_ref, hidden_ref, own_ref, other_ref,
    *rest,
):
    peers, chunk, n_halo, paired = geometry
    *rest, out_scratch, back_scratch, pair_scratch = rest
    halo_refs = rest[:n_halo]
    normed_ref, local_ref, target_ref, *message_refs = rest[n_halo:]
    node = node_ref[...]
    rows, width = node.shape
    aggregate = own_ref[...].astype(f32) + other_ref[...].astype(f32)
    center = aggregate - jnp.mean(aggregate, axis=1, keepdims=True)
    variance = jnp.mean(center * center, axis=1, keepdims=True)
    inverse = lax.rsqrt(variance + EPSILON)
    normed = center * inverse
    gain = gain_ref[...]
    upstream = cot_ref[...].astype(f32)
    scaled = upstream * gain
    agg_grad = inverse * (
        scaled
        - jnp.mean(scaled, axis=1, keepdims=True)
        - normed * jnp.mean(scaled * normed, axis=1, keepdims=True)
    )
    agg_grad = agg_grad.astype(bf16)
    normed_ref[...] = normed
    gain_part = jnp.sum(upstream * normed, axis=0, keepdims=True)

    act_grad = dot(twice(spread_ref[...]), stacked(dot(agg_grad, w_out_ref[...], NT)))
    pre_grad = (act_grad * factor_ref[...]).astype(bf16)

    table = jnp.concatenate([node] + [r[...] for r in halo_refs], axis=0)
    by_source = dot(scatter_ref[...], pre_grad)
    by_target = dot(collect_ref[...], pre_grad)
    local_ref[...] = by_source[:rows]
    by_target_low = by_target.astype(bf16)
    by_source_low = by_source.astype(bf16)
    target_ref[...] = by_target_low

    hid = by_source.shape[1]
    bias_part = jnp.sum(by_target, axis=0, keepdims=True)
    src_part = dot(table, by_source_low, TN).astype(bf16)
    dst_part = dot(node, by_target_low, TN).astype(bf16)
    out_part = dot(hidden_ref[...], agg_grad, TN).astype(bf16)
    vectors = [bias_part] + [gain_part[:, at : at + hid] for at in range(0, width, hid)]
    tail = tail_of(vectors)
    back = by_source_low[rows:]

    if paired:
        sends, keeps, out_refs = message_refs[:3], message_refs[3:6], message_refs[6:]
        sub = lax.axis_index("sub")
        mesh = lax.axis_index("mesh")
        lines = len(out_refs)
        halo = back.shape[0] // 4
        first = sub == 0
        pair_scratch[0] = jnp.where(first, dst_part, src_part)
        pair_scratch[1] = jnp.where(first, src_part, dst_part)
        strip = width // lines
        for slot, (far_ref, one_ref, zero_ref) in enumerate((sends, keeps)):
            cut = strip - CUT
            places = (
                (far_ref, 0, 3, 0, strip), (far_ref, strip, 2, 0, strip), (far_ref, 2 * strip + TAIL, 1, cut, CUT),
                (one_ref, 0, 1, 0, cut), (zero_ref, 0, 0, 0, strip),
            )
            for ref, at, k, begin, size in places:
                start = pl.multiple_of((mesh ^ k) * strip + begin, 16)
                ref[at : at + size, :] = pair_scratch[slot, pl.ds(start, size), :]
            far_ref[2 * strip : 2 * strip + TAIL, :] = tail
        sends[2][strip:, :] = back[2 * halo :]
        back_scratch[...] = back[: 2 * halo]
        out_scratch[...] = out_part
        strip = hid // len(out_refs)
        for k, ref in enumerate(out_refs):
            start = pl.multiple_of((mesh ^ k) * strip, strip)
            ref[0:strip, :] = out_scratch[pl.ds(start, strip), :]
            if k % 2 == 1:
                slot = (mesh + (k // 2) + 1) % 2
                start = pl.multiple_of(slot * halo, halo)
                rows_back = back_scratch[pl.ds(start, halo), :]
                ref[strip:, 0:hid] = rows_back[: halo // 2]
                ref[strip:, hid:] = rows_back[halo // 2 :]
        return

    message_ref, *back_refs = message_refs
    at = 0
    for ref in back_refs:
        ref[...] = back[at : at + ref.shape[0]]
        at += ref.shape[0]
    blocks = [src_part, dst_part]
    for at in range(0, width, hid):
        blocks.append(out_part[:, at : at + hid])
    done = 0
    for block in blocks:
        at = 0
        while at < block.shape[0]:
            peer, offset = divmod(done, chunk)
            take = min(chunk - offset, block.shape[0] - at)
            message_ref[peer, offset : offset + take, :] = block[at : at + take]
            at += take
            done += take
    while done < peers * chunk:
        peer, offset = divmod(done, chunk)
        take = chunk - offset
        message_ref[peer, offset : offset + take, :] = jnp.zeros((take, hid), bf16)
        done += take
    for peer in range(peers):
        message_ref[peer, chunk:, :] = tail


def tail_of(vectors):
    tail = []
    for v in vectors:
        high = v.astype(bf16).astype(f32)
        tail += [high, v - high]
    tail.append(jnp.zeros((TAIL - len(tail), vectors[0].shape[1]), f32))
    return jnp.concatenate(tail, axis=0).astype(bf16)


def tree(terms):
    while len(terms) > 1:
        terms = [terms[i] + terms[i + 1] for i in range(0, len(terms), 2)]
    return terms[0]


def far_kernel(arrived_ref, keep_ref, three_ref, two_ref, tail_ref):
    total = keep_ref[...].astype(f32) + arrived_ref[...].astype(f32)
    strip = three_ref.shape[0] - TAIL
    tail = total[2 * strip : 2 * strip + TAIL]
    tail = tail_of([tail[at : at + 1] + tail[at + 1 : at + 2] for at in range(0, 6, 2)])
    for k, ref in enumerate((three_ref, two_ref)):
        ref[0:strip, :] = total[k * strip : (k + 1) * strip].astype(bf16)
        ref[strip:, :] = tail
    tail_ref[0:TAIL, :] = tail
    tail_ref[TAIL:, :] = total[2 * strip + TAIL :].astype(bf16)


def near_kernel(arrived_ref, keep_ref, tail_ref, one_ref):
    cut = keep_ref.shape[0]
    one_ref[0:cut, :] = (keep_ref[...].astype(f32) + arrived_ref[...].astype(f32)).astype(bf16)
    one_ref[cut : cut + CUT, :] = tail_ref[TAIL:, :]
    one_ref[cut + CUT :, :] = tail_ref[0:TAIL, :]


def line_kernel(*refs):
    *terms, _, send_ref, keep_ref = refs
    rows, hid = send_ref.shape
    total = tree([r[0:rows, :].astype(f32) for r in terms])
    first = lax.axis_index("sub") == 0
    left, right = total[:, :hid], total[:, hid:]
    send_ref[...] = jnp.where(first, right, left).astype(bf16)
    keep_ref[...] = jnp.where(first, left, right).astype(bf16)


def own_kernel(*refs):
    *terms, keep_ref, arrived_ref, vectors_ref, out_keep_ref, out_arrived_ref, _, own_ref, tail_ref = refs
    strip = keep_ref.shape[0]
    zero = (keep_ref[...].astype(f32) + arrived_ref[0:strip, :].astype(f32)).astype(bf16)
    total = tree([r[0:strip, :].astype(f32) for r in terms] + [zero.astype(f32)])
    own_ref[0:strip, :] = total.astype(bf16)
    own_ref[strip:, :] = (
        out_keep_ref[...].astype(f32) + out_arrived_ref[...].astype(f32)
    ).astype(bf16)
    tail_ref[...] = tree([r[strip:, :].astype(f32) for r in terms] + [vectors_ref[0:TAIL, :].astype(f32)])


def write_vectors(tail, bias_ref, gain_ref):
    bias_ref[...] = tail[0:1] + tail[1:2]
    hid = tail.shape[1]
    for k in range(gain_ref.shape[1] // hid):
        gain_ref[:, k * hid : (k + 1) * hid] = tail[2 + 2 * k : 3 + 2 * k] + tail[3 + 2 * k : 4 + 2 * k]


def place_kernel(order, *refs):
    count = len(order)
    mine, theirs = refs[:count], refs[count : 2 * count]
    src_ref, dst_ref, out_ref = refs[2 * count :]
    first = lax.axis_index("sub") == 0
    mesh = lax.axis_index("mesh")
    width, hid = src_ref.shape
    strip = width // count
    narrow = hid // count
    for at, k in enumerate(order):
        a, b = mine[at][...], theirs[at][...]
        low = jnp.where(first, a, b).astype(f32)
        high = jnp.where(first, b, a).astype(f32)
        start = pl.multiple_of((mesh ^ k) * strip, strip)
        src_ref[pl.ds(start, strip), :] = low[:strip]
        dst_ref[pl.ds(start, strip), :] = high[:strip]
        start = pl.multiple_of((mesh ^ k) * narrow, narrow)
        out_ref[pl.ds(start, narrow), 0:hid] = low[strip:]
        out_ref[pl.ds(start, narrow), hid:] = high[strip:]


def sum_kernel(chunk, arrived_ref, out_ref, bias_ref, gain_ref):
    peers = arrived_ref.shape[0]
    total = arrived_ref[0].astype(f32)
    for peer in range(1, peers):
        total += arrived_ref[peer].astype(f32)
    low = total[:chunk].astype(bf16)
    for peer in range(peers):
        out_ref[peer] = low
    tail = total[chunk:]
    write_vectors(tail, bias_ref, gain_ref)


def unpack_kernel(arrived_ref, src_ref, dst_ref, out_ref):
    hid = src_ref.shape[1]
    rows = src_ref.shape[0]
    src_ref[...] = arrived_ref[0:rows, :].astype(f32)
    dst_ref[...] = arrived_ref[rows : 2 * rows, :].astype(f32)
    at = 2 * rows
    for k in range(out_ref.shape[1] // hid):
        out_ref[:, k * hid : (k + 1) * hid] = arrived_ref[at : at + out_ref.shape[0], :].astype(f32)
        at += out_ref.shape[0]


def node_part(send_ref, local_ref, target_ref, w_src_ref, w_dst_ref, returned, out_ref):
    rows = local_ref.shape[0]
    halo = send_ref.shape[2]
    picks = [one_hot(iota((rows, halo), 0) == send_ref[0, d : d + 1, :]) for d in range(4)]
    total = local_ref[...] + dot(jnp.concatenate(picks, axis=1), jnp.concatenate(returned, axis=0))
    out_ref[...] = (
        dot(total.astype(bf16), w_src_ref[...], NT) + dot(target_ref[...], w_dst_ref[...], NT)
    ).astype(bf16)


def node_kernel(send_ref, local_ref, target_ref, w_src_ref, w_dst_ref, *rest):
    *back_refs, out_ref = rest
    returned = [r[...] for r in back_refs]
    node_part(send_ref, local_ref, target_ref, w_src_ref, w_dst_ref, returned, out_ref)


def paired_node_kernel(
    send_ref, local_ref, target_ref, w_src_ref, w_dst_ref, three_ref, one_ref, pair_ref, out_ref
):
    even = lax.axis_index("mesh") % 2 == 0
    halo = send_ref.shape[2]
    hid = local_ref.shape[1]
    at = one_ref.shape[0] - halo // 2
    one, three = [
        jnp.concatenate([r[at:, :hid], r[at:, hid:]], axis=0) for r in (one_ref, three_ref)
    ]
    returned = [
        jnp.where(even, one, three), jnp.where(even, three, one), pair_ref[pair_ref.shape[0] - 2 * halo :, :]
    ]
    node_part(send_ref, local_ref, target_ref, w_src_ref, w_dst_ref, returned, out_ref)


def finish_kernel(cot_ref, node_ref, gain_ref, normed_ref, own_ref, other_ref, *rest):
    if len(rest) == 5:
        tail_ref, *rest, bias_out_ref, gain_out_ref = rest
        write_vectors(tail_ref[...], bias_out_ref, gain_out_ref)
    grad_ref, updated_ref = rest
    grad_ref[...] = cot_ref[...].astype(f32) + (
        own_ref[...].astype(f32) + other_ref[...].astype(f32)
    )
    updated_ref[...] = (node_ref[...].astype(f32) + gain_ref[...] * normed_ref[...]).astype(bf16)


VMEM = pl.BlockSpec(memory_space=pltpu.VMEM)
SMEM = pl.BlockSpec(memory_space=pltpu.SMEM)
HBM = pl.BlockSpec(memory_space=pltpu.HBM)


def shape(dims, dtype):
    return jax.ShapeDtypeStruct(dims, dtype)


def call(kernel, outs, *args, specs=None, out_specs=None, flops=10**8, scratch=()):
    return pl.pallas_call(
        kernel,
        out_shape=outs,
        in_specs=specs or [VMEM] * len(args),
        out_specs=out_specs or jax.tree.map(lambda _: VMEM, outs),
        scratch_shapes=scratch,
        compiler_params=pltpu.CompilerParams(vmem_limit_bytes=VMEM_LIMIT),
        cost_estimate=pl.CostEstimate(flops=flops, bytes_accessed=10**6, transcendentals=0),
    )(*args)


def shifted(x, axis, by):
    count = lax.axis_size(axis)
    return lax.ppermute(x, axis, [(i, (i + by) % count) for i in range(count)])


def across(x, axis, k):
    count = lax.axis_size(axis)
    return lax.ppermute(x, axis, [(i, i ^ k) for i in range(count)])


def diagonal(x):
    lines, pairs = lax.axis_size("mesh"), lax.axis_size("sub")
    moves = [(m * pairs + p, (m ^ 1) * pairs + (p ^ 1)) for m in range(lines) for p in range(pairs)]
    return lax.ppermute(x, ("mesh", "sub"), moves)


def paired_sums(messages, lines, strip, narrow, width, hid, node_terms):
    sends, keeps, outs = messages[:3], messages[3:6], messages[6:]
    order = range(lines - 1, 0, -1)
    block = shape((strip + TAIL, hid), bf16)
    far = across(sends[0], "sub", 1)
    out_terms = {k: across(outs[k], "mesh", k) for k in order}
    one = across(sends[1], "sub", 1)
    zero = across(sends[2], "sub", 1)
    line = {}
    line[3], line[2], tail = call(far_kernel, [block, block, shape((TAIL + CUT, hid), bf16)], far, keeps[0])
    line[1] = call(near_kernel, block, one, keeps[1], tail)
    line_terms = {k: across(line[k], "mesh", k) for k in order}
    out_send, out_keep = call(
        line_kernel,
        [shape((narrow, hid), bf16)] * 2,
        *[out_terms[k] for k in order], outs[0], line[1],
    )
    node_part = node_terms(out_terms[3], out_terms[1], zero)
    own, tail = call(
        own_kernel,
        [shape((strip + narrow, hid), bf16), shape((TAIL, hid), f32)],
        *[line_terms[k] for k in order], keeps[2], zero, tail, out_keep, across(out_send, "sub", 1),
        node_part,
    )
    mine = {k: across(own, "mesh", k) for k in order}
    mine[0] = own
    theirs = {0: across(own, "sub", 1), 1: diagonal(own)}
    theirs |= {k: across(mine[k], "sub", 1) for k in (3, 2)}
    placed = (0, 3, 1, 2)
    grads = call(
        functools.partial(place_kernel, placed),
        [shape((width, hid), f32), shape((width, hid), f32), shape((hid, width), f32)],
        *[mine[k] for k in placed], *[theirs[k] for k in placed],
    )
    return (*grads, tail), node_part


def shards(
    node_state,
    send_rows,
    edge_src,
    edge_dst,
    block_count,
    w_src,
    w_dst,
    hidden_bias,
    w_out,
    norm_gain,
    cotangent,
):
    rows, width = node_state.shape
    hid = w_src.shape[1]
    halo = send_rows.shape[2]
    edges = edge_src.shape[0]
    peers = lax.axis_size("mesh") * lax.axis_size("sub")
    merged = lax.axis_size("sub") == 2
    total_rows = 2 * width + (width // hid) * hid
    chunk = -(-total_rows // (peers * 16)) * 16

    piece = [halo, halo, 2 * halo] if merged else [halo] * 4
    routes = [("mesh", 1), ("mesh", -1), ("sub", 1)] + ([] if merged else [("sub", -1)])
    n_halo = len(piece)

    def in_hbm(x):
        return pltpu.with_memory_space_constraint(x, pltpu.HBM)

    node, send, *outgoing = call(
        send_kernel,
        [shape((rows, width), bf16), shape(send_rows.shape, jnp.int32)]
        + [shape((n, width), bf16) for n in piece],
        in_hbm(node_state), in_hbm(send_rows),
        specs=[HBM, HBM],
        scratch=[pltpu.SemaphoreType.DMA((2,))],
    )
    arrived = [shifted(x, axis, by) for x, (axis, by) in zip(outgoing, routes)]

    fetched = [
        edge_src.reshape(1, edges), edge_dst.reshape(1, edges), block_count,
        hidden_bias.reshape(1, hid), w_src, w_dst, w_out, norm_gain.reshape(1, width), cotangent,
    ]
    pre, pick, collect, spread, scatter, w_src, w_dst, w_out, gain, cot = call(
        local_kernel,
        [
            shape((edges, hid), f32),
            shape((edges, 4 * halo), bf16),
            shape((rows, edges), bf16),
            shape((edges, rows), bf16),
            shape((rows + 4 * halo, edges), bf16),
        ]
        + [shape(x.shape, x.dtype) for x in fetched[4:]],
        node, *[in_hbm(x) for x in fetched],
        specs=[VMEM] + [HBM] * len(fetched),
        scratch=[
            pltpu.SMEM(block_count.shape, jnp.int32),
            pltpu.VMEM((1, edges), jnp.int32),
            pltpu.VMEM((1, edges), jnp.int32),
            pltpu.VMEM((1, hid), f32),
            pltpu.SemaphoreType.DMA((N_FETCHED,)),
        ],
    )

    factor, hidden, partial = call(
        forward_kernel,
        [shape((edges, hid), f32), shape((rows, hid), bf16), shape((rows, width), bf16)],
        pre, pick, collect, w_src, w_out, *arrived,
    )
    other = shifted(partial, "lat", 1)

    lines = lax.axis_size("mesh")
    paired = merged and lines == 4
    if paired:
        strip = width // lines
        narrow = hid // lines
        far_rows, cut = 2 * strip + TAIL + CUT, strip - CUT
        rows_of = (far_rows, cut, strip + 2 * halo, far_rows, cut, strip)
        message_shapes = [shape((n, hid), bf16) for n in rows_of]
        message_shapes += [shape((narrow + k % 2 * (halo // 2), width), bf16) for k in range(lines)]
    else:
        message_shapes = [shape((peers, chunk + TAIL, hid), bf16)]
        message_shapes += [shape((n, hid), bf16) for n in piece]
    normed, local, target, *messages = call(
        functools.partial(backward_kernel, (peers, chunk, n_halo, paired)),
        [shape((rows, width), f32), shape((rows, hid), f32), shape((rows, hid), bf16)]
        + message_shapes,
        node, collect, spread, scatter, w_out, gain, cot, factor, hidden, partial, other, *arrived,
        scratch=[
            pltpu.VMEM((hid, width), bf16),
            pltpu.VMEM((2 * halo, hid), bf16),
            pltpu.VMEM((2, width, hid), bf16),
        ],
    )

    def node_terms(*returned):
        return call(
            paired_node_kernel if paired else node_kernel,
            shape((rows, width), bf16),
            send, local, target, w_src, w_dst, *returned,
        )

    if paired:
        (src_grad, dst_grad, out_grad, tail), node_part = paired_sums(
            messages, lines, strip, narrow, width, hid, node_terms
        )
    else:
        node_part = node_terms(
            *[shifted(x, axis, -by) for x, (axis, by) in zip(messages[1:], routes)]
        )
        exchanged = lax.all_to_all(messages[0], ("mesh", "sub"), 0, 0)
        reduced, bias_grad, gain_grad = call(
            functools.partial(sum_kernel, chunk),
            [shape((peers, chunk, hid), bf16), shape((1, hid), f32), shape((1, width), f32)],
            exchanged,
        )
        gathered = lax.all_to_all(reduced, ("mesh", "sub"), 0, 0)
        src_grad, dst_grad, out_grad = call(
            unpack_kernel,
            [shape((width, hid), f32), shape((width, hid), f32), shape((hid, width), f32)],
            gathered.reshape(peers * chunk, hid),
        )
    finished = [shape((rows, width), f32), shape((rows, width), bf16)]
    ends = [cot, node, gain, normed, node_part, shifted(node_part, "lat", 1)]
    if paired:
        node_grad, updated, bias_grad, gain_grad = call(
            finish_kernel, finished + [shape((1, hid), f32), shape((1, width), f32)], *ends, tail
        )
    else:
        node_grad, updated = call(finish_kernel, finished, *ends)
    return (
        updated, node_grad, src_grad, dst_grad, out_grad,
        bias_grad.reshape(hid), gain_grad.reshape(width),
    )


def solution(mesh):
    nodes = P(("parts", "mesh", "sub"), None)
    slots = P(("parts", "mesh", "sub"))
    in_specs = (
        nodes,
        P(("parts", "mesh", "sub"), None, None),
        slots,
        slots,
        slots,
        P(None, "lat"),
        P(None, "lat"),
        P("lat"),
        P("lat", None),
        P(),
        nodes,
    )
    out_specs = (
        nodes,
        nodes,
        P("parts", "lat"),
        P("parts", "lat"),
        P(("parts", "lat"), None),
        P(("parts", "lat")),
        P("parts"),
    )
    return jax.shard_map(shards, mesh=mesh, in_specs=in_specs, out_specs=out_specs, check_vma=False)
```

```python
import functools

import jax
import jax.numpy as jnp
from jax import lax
from jax.experimental import pallas as pl
from jax.experimental.pallas import tpu as pltpu
from jax.sharding import PartitionSpec as P

BLOCK = 128
EPSILON = 1e-05
TAIL = 16
N_FETCHED = 9
VMEM_LIMIT = 24 * 1024 * 1024

f32 = jnp.float32
bf16 = jnp.bfloat16

NN = (((1,), (0,)), ((), ()))
NT = (((1,), (1,)), ((), ()))
TN = (((0,), (0,)), ((), ()))


def dot(a, b, dims=NN):
    return lax.dot_general(a, b, dims, preferred_element_type=f32)


def iota(shape, dim):
    return lax.broadcasted_iota(jnp.int32, shape, dim)


def one_hot(condition):
    return jnp.where(condition, 1.0, 0.0).astype(bf16)


def split(x):
    high = x.astype(bf16)
    return high, (x - high.astype(f32)).astype(bf16)


def columns_of(row, lanes):
    return jnp.transpose(jnp.broadcast_to(row, (lanes, row.shape[1])))


def usable_row(count_ref, edges):
    lane = iota((1, BLOCK), 1)
    parts = [lane < count_ref[b] for b in range(edges // BLOCK)]
    return jnp.concatenate([jnp.where(p, 1, 0) for p in parts], axis=1)


def usable_columns(count_ref, edges, lanes):
    sub = iota((BLOCK, lanes), 0)
    return jnp.concatenate(
        [jnp.where(sub < count_ref[b], 1, 0) for b in range(edges // BLOCK)], axis=0
    )


def fetch(sems, *pairs):
    copies = [pltpu.make_async_copy(a, b, sems.at[i]) for i, (a, b) in enumerate(pairs)]
    for copy in copies:
        copy.start()
    return copies


def send_kernel(node_hbm, send_hbm, node_ref, send_ref, *rest):
    *out_refs, sems = rest
    for copy in fetch(sems, (node_hbm, node_ref), (send_hbm, send_ref)):
        copy.wait()
    node = node_ref[...]
    rows = node.shape[0]
    halo = send_ref.shape[2]
    pieces = []
    for d in range(4):
        pick = one_hot(iota((rows, halo), 0) == send_ref[0, d : d + 1, :])
        pieces.append(dot(pick, node, TN).astype(bf16))
    out_refs[0][...] = pieces[0]
    out_refs[1][...] = pieces[1]
    if len(out_refs) == 3:
        out_refs[2][0:halo, :] = pieces[2]
        out_refs[2][halo:, :] = pieces[3]
    else:
        out_refs[2][...] = pieces[2]
        out_refs[3][...] = pieces[3]


def local_kernel(*refs):
    node_ref, w_src_other_ref, w_dst_other_ref, bias_other_ref, *refs = refs
    ins, refs = refs[:N_FETCHED], refs[N_FETCHED:]
    pre_ref, pick_ref, collect_ref, spread_ref, scatter_ref, *refs = refs
    w_src_ref, w_dst_ref, w_out_ref, gain_ref, cot_ref, count_ref, src_ref, dst_ref, bias_ref, sems = refs
    outs = (src_ref, dst_ref, count_ref, bias_ref, w_src_ref, w_dst_ref, w_out_ref, gain_ref, cot_ref)
    copies = fetch(sems, *zip(ins, outs))
    node = node_ref[...]
    rows = node.shape[0]
    edges = src_ref.shape[1]
    for copy in copies:
        copy.wait()
    weights = [w_src_ref[...], w_src_other_ref[...], w_dst_ref[...], w_dst_other_ref[...]]
    projected = dot(node, jnp.concatenate(weights, axis=1))
    both = projected.shape[1] // 2
    projected = jnp.concatenate([projected[:, :both], projected[:, both:]], axis=0)
    high, low = split(projected)
    src_row = src_ref[...]
    scatter_ref[...] = one_hot(iota(scatter_ref.shape, 0) == src_row)
    used = usable_row(count_ref, edges) > 0
    collect_ref[...] = one_hot((iota((rows, edges), 0) == dst_ref[...]) & used)
    source = columns_of(src_row, 128)
    target = columns_of(dst_ref[...], 128)
    lane = iota(source.shape, 1)
    used = usable_columns(count_ref, edges, 128) > 0
    near = one_hot(source == lane)
    pick_ref[...] = one_hot(source == lane + rows)
    spread_ref[...] = one_hot((target == lane) & used)
    ends = jnp.concatenate([near, one_hot(target == lane)], axis=1)
    bias = jnp.concatenate([bias_ref[...], bias_other_ref[...]], axis=1)
    pre_ref[...] = dot(ends, high) + dot(ends, low) + bias


def twice(x):
    return jnp.concatenate([x, x], axis=1)


def stacked(x):
    return jnp.concatenate(split(x), axis=0)


def edge_kernel(
    geometry,
    node_ref, pre_ref, pick_ref, collect_ref, spread_ref, scatter_ref,
    w_src_ref, w_src_other_ref, w_out_ref, w_out_other_ref, gain_ref, cot_ref,
    *rest,
):
    peers, chunk, n_halo, paired = geometry
    *rest, out_scratch, back_scratch, pair_scratch = rest
    halo_refs = rest[:n_halo]
    normed_ref, local_ref, target_ref, *message_refs = rest[n_halo:]
    node = node_ref[...]
    rows, width = node.shape
    hid = w_src_ref.shape[1]
    halo_rows = jnp.concatenate([r[...] for r in halo_refs], axis=0)

    weights = jnp.concatenate([w_src_ref[...], w_src_other_ref[...]], axis=1)
    far = stacked(dot(halo_rows, weights))
    pre = pre_ref[...] + dot(twice(pick_ref[...]), far)
    sig = 0.5 + 0.5 * jnp.tanh(0.5 * pre)
    hidden = dot(collect_ref[...], (pre * sig).astype(bf16))
    pre, sig = pre[:, :hid], sig[:, :hid]
    factor = sig * (1.0 + pre * (1.0 - sig))
    hidden_low, parts = None, []
    for at, w_ref in ((0, w_out_ref), (hid, w_out_other_ref)):
        high, low = split(hidden[:, at : at + hid])
        hidden_low = high if at == 0 else hidden_low
        w_out = w_ref[...]
        parts.append(dot(high, w_out) + dot(low, w_out))
    aggregate = parts[0] + parts[1]

    center = aggregate - jnp.mean(aggregate, axis=1, keepdims=True)
    variance = jnp.mean(center * center, axis=1, keepdims=True)
    inverse = lax.rsqrt(variance + EPSILON)
    normed = center * inverse
    gain = gain_ref[...]
    upstream = cot_ref[...].astype(f32)
    scaled = upstream * gain
    agg_grad = inverse * (
        scaled
        - jnp.mean(scaled, axis=1, keepdims=True)
        - normed * jnp.mean(scaled * normed, axis=1, keepdims=True)
    )
    agg_grad = agg_grad.astype(bf16)
    normed_ref[...] = normed
    gain_part = jnp.sum(upstream * normed, axis=0, keepdims=True)

    act_grad = dot(twice(spread_ref[...]), stacked(dot(agg_grad, w_out_ref[...], NT)))
    pre_grad = (act_grad * factor).astype(bf16)

    table = jnp.concatenate([node, halo_rows], axis=0)
    by_source = dot(scatter_ref[...], pre_grad)
    by_target = dot(collect_ref[...], pre_grad)
    local_ref[...] = by_source[:rows]
    by_target_low = by_target.astype(bf16)
    by_source_low = by_source.astype(bf16)
    target_ref[...] = by_target_low

    bias_part = jnp.sum(by_target, axis=0, keepdims=True)
    src_part = dot(table, by_source_low, TN).astype(bf16)
    dst_part = dot(node, by_target_low, TN).astype(bf16)
    out_part = dot(hidden_low, agg_grad, TN).astype(bf16)
    vectors = [bias_part] + [gain_part[:, at : at + hid] for at in range(0, width, hid)]
    tail = tail_of(vectors)
    back = by_source_low[rows:]

    if paired:
        sends, keeps, out_refs = message_refs[:3], message_refs[3:6], message_refs[6:]
        sub = lax.axis_index("sub")
        mesh = lax.axis_index("mesh")
        lines = len(out_refs)
        halo = back.shape[0] // 4
        first = sub == 0
        pair_scratch[0] = jnp.where(first, dst_part, src_part)
        pair_scratch[1] = jnp.where(first, src_part, dst_part)
        strip = width // lines
        for slot, (far_ref, one_ref, zero_ref) in enumerate((sends, keeps)):
            places = ((far_ref, 0, 3), (far_ref, strip, 2), (one_ref, 0, 1), (zero_ref, 0, 0))
            for ref, at, k in places:
                start = pl.multiple_of((mesh ^ k) * strip, strip)
                ref[at : at + strip, :] = pair_scratch[slot, pl.ds(start, strip), :]
            far_ref[2 * strip :, :] = tail
        sends[2][strip:, :] = back[2 * halo :]
        back_scratch[...] = back[: 2 * halo]
        out_scratch[...] = out_part
        strip = hid // len(out_refs)
        for k, ref in enumerate(out_refs):
            start = pl.multiple_of((mesh ^ k) * strip, strip)
            ref[0:strip, :] = out_scratch[pl.ds(start, strip), :]
            if k % 2 == 1:
                slot = (mesh + (k // 2) + 1) % 2
                start = pl.multiple_of(slot * halo, halo)
                rows_back = back_scratch[pl.ds(start, halo), :]
                ref[strip:, 0:hid] = rows_back[: halo // 2]
                ref[strip:, hid:] = rows_back[halo // 2 :]
        return

    message_ref, *back_refs = message_refs
    at = 0
    for ref in back_refs:
        ref[...] = back[at : at + ref.shape[0]]
        at += ref.shape[0]
    blocks = [src_part, dst_part]
    for at in range(0, width, hid):
        blocks.append(out_part[:, at : at + hid])
    done = 0
    for block in blocks:
        at = 0
        while at < block.shape[0]:
            peer, offset = divmod(done, chunk)
            take = min(chunk - offset, block.shape[0] - at)
            message_ref[peer, offset : offset + take, :] = block[at : at + take]
            at += take
            done += take
    while done < peers * chunk:
        peer, offset = divmod(done, chunk)
        take = chunk - offset
        message_ref[peer, offset : offset + take, :] = jnp.zeros((take, hid), bf16)
        done += take
    for peer in range(peers):
        message_ref[peer, chunk:, :] = tail


def tail_of(vectors):
    tail = []
    for v in vectors:
        high = v.astype(bf16).astype(f32)
        tail += [high, v - high]
    tail.append(jnp.zeros((TAIL - len(tail), vectors[0].shape[1]), f32))
    return jnp.concatenate(tail, axis=0).astype(bf16)


def tree(terms):
    while len(terms) > 1:
        terms = [terms[i] + terms[i + 1] for i in range(0, len(terms), 2)]
    return terms[0]


def far_kernel(arrived_ref, keep_ref, three_ref, two_ref, tail_ref):
    total = keep_ref[...].astype(f32) + arrived_ref[...].astype(f32)
    strip = three_ref.shape[0] - TAIL
    tail = total[2 * strip :]
    tail = tail_of([tail[at : at + 1] + tail[at + 1 : at + 2] for at in range(0, 6, 2)])
    for k, ref in enumerate((three_ref, two_ref)):
        ref[0:strip, :] = total[k * strip : (k + 1) * strip].astype(bf16)
        ref[strip:, :] = tail
    tail_ref[...] = tail


def near_kernel(arrived_ref, keep_ref, tail_ref, one_ref):
    strip = keep_ref.shape[0]
    one_ref[0:strip, :] = (keep_ref[...].astype(f32) + arrived_ref[...].astype(f32)).astype(bf16)
    one_ref[strip:, :] = tail_ref[...]


def line_kernel(*refs):
    *terms, _, send_ref, keep_ref = refs
    rows, hid = send_ref.shape
    total = tree([r[0:rows, :].astype(f32) for r in terms])
    first = lax.axis_index("sub") == 0
    left, right = total[:, :hid], total[:, hid:]
    send_ref[...] = jnp.where(first, right, left).astype(bf16)
    keep_ref[...] = jnp.where(first, left, right).astype(bf16)


def own_kernel(*refs):
    *terms, keep_ref, arrived_ref, vectors_ref, out_keep_ref, out_arrived_ref, _, own_ref, tail_ref = refs
    strip = keep_ref.shape[0]
    zero = (keep_ref[...].astype(f32) + arrived_ref[0:strip, :].astype(f32)).astype(bf16)
    total = tree([r[0:strip, :].astype(f32) for r in terms] + [zero.astype(f32)])
    own_ref[0:strip, :] = total.astype(bf16)
    own_ref[strip:, :] = (
        out_keep_ref[...].astype(f32) + out_arrived_ref[...].astype(f32)
    ).astype(bf16)
    tail_ref[...] = tree([r[strip:, :].astype(f32) for r in terms] + [vectors_ref[...].astype(f32)])


def write_vectors(tail, bias_ref, gain_ref):
    bias_ref[...] = tail[0:1] + tail[1:2]
    hid = tail.shape[1]
    for k in range(gain_ref.shape[1] // hid):
        gain_ref[:, k * hid : (k + 1) * hid] = tail[2 + 2 * k : 3 + 2 * k] + tail[3 + 2 * k : 4 + 2 * k]


def relay_kernel(*refs):
    *_, strip_ref, out_ref = refs
    out_ref[...] = strip_ref[...]


def place_kernel(lines, which, a_ref, b_ref, c_ref, d_ref, *refs):
    src_hbm, dst_hbm, out_hbm, src_ref, dst_ref, out_ref, sems = refs[-7:]
    first = lax.axis_index("sub") == 0
    mesh = lax.axis_index("mesh")
    strip, hid = src_ref.shape[1:]
    narrow = out_ref.shape[1]
    copies = []

    def put(ref, hbm, at, rows):
        start = pl.multiple_of((mesh ^ which[at]) * rows, rows)
        copies.append(pltpu.make_async_copy(ref.at[at], hbm.at[pl.ds(start, rows)], sems.at[len(copies)]))
        copies[-1].start()

    for at, (mine_ref, theirs_ref) in enumerate(((a_ref, c_ref), (b_ref, d_ref))):
        mine, theirs = mine_ref[...], theirs_ref[...]
        low = jnp.where(first, mine, theirs).astype(f32)
        high = jnp.where(first, theirs, mine).astype(f32)
        src_ref[at] = low[:strip]
        put(src_ref, src_hbm, at, strip)
        dst_ref[at] = high[:strip]
        put(dst_ref, dst_hbm, at, strip)
        out_ref[at, :, 0:hid] = low[strip:]
        out_ref[at, :, hid:] = high[strip:]
        put(out_ref, out_hbm, at, narrow)
    for copy in copies:
        copy.wait()


def sum_kernel(chunk, arrived_ref, out_ref, bias_ref, gain_ref):
    peers = arrived_ref.shape[0]
    total = arrived_ref[0].astype(f32)
    for peer in range(1, peers):
        total += arrived_ref[peer].astype(f32)
    low = total[:chunk].astype(bf16)
    for peer in range(peers):
        out_ref[peer] = low
    tail = total[chunk:]
    write_vectors(tail, bias_ref, gain_ref)


def unpack_kernel(arrived_ref, src_ref, dst_ref, out_ref):
    hid = src_ref.shape[1]
    rows = src_ref.shape[0]
    src_ref[...] = arrived_ref[0:rows, :].astype(f32)
    dst_ref[...] = arrived_ref[rows : 2 * rows, :].astype(f32)
    at = 2 * rows
    for k in range(out_ref.shape[1] // hid):
        out_ref[:, k * hid : (k + 1) * hid] = arrived_ref[at : at + out_ref.shape[0], :].astype(f32)
        at += out_ref.shape[0]


def node_part(send_ref, local_ref, target_ref, w_src_ref, w_dst_ref, returned, out_ref):
    rows = local_ref.shape[0]
    halo = send_ref.shape[2]
    picks = [one_hot(iota((rows, halo), 0) == send_ref[0, d : d + 1, :]) for d in range(4)]
    total = local_ref[...] + dot(jnp.concatenate(picks, axis=1), jnp.concatenate(returned, axis=0))
    out_ref[...] = (
        dot(total.astype(bf16), w_src_ref[...], NT) + dot(target_ref[...], w_dst_ref[...], NT)
    ).astype(bf16)


def node_kernel(send_ref, local_ref, target_ref, w_src_ref, w_dst_ref, *rest):
    *back_refs, out_ref = rest
    returned = [r[...] for r in back_refs]
    node_part(send_ref, local_ref, target_ref, w_src_ref, w_dst_ref, returned, out_ref)


def paired_node_kernel(
    send_ref, local_ref, target_ref, w_src_ref, w_dst_ref, three_ref, one_ref, pair_ref, out_ref
):
    even = lax.axis_index("mesh") % 2 == 0
    halo = send_ref.shape[2]
    hid = local_ref.shape[1]
    at = one_ref.shape[0] - halo // 2
    one, three = [
        jnp.concatenate([r[at:, :hid], r[at:, hid:]], axis=0) for r in (one_ref, three_ref)
    ]
    returned = [
        jnp.where(even, one, three), jnp.where(even, three, one), pair_ref[pair_ref.shape[0] - 2 * halo :, :]
    ]
    node_part(send_ref, local_ref, target_ref, w_src_ref, w_dst_ref, returned, out_ref)


def finish_kernel(cot_ref, node_ref, gain_ref, normed_ref, own_ref, other_ref, *rest):
    if len(rest) == 5:
        tail_ref, *rest, bias_out_ref, gain_out_ref = rest
        write_vectors(tail_ref[...], bias_out_ref, gain_out_ref)
    grad_ref, updated_ref = rest
    grad_ref[...] = cot_ref[...].astype(f32) + (
        own_ref[...].astype(f32) + other_ref[...].astype(f32)
    )
    updated_ref[...] = (node_ref[...].astype(f32) + gain_ref[...] * normed_ref[...]).astype(bf16)


VMEM = pl.BlockSpec(memory_space=pltpu.VMEM)
SMEM = pl.BlockSpec(memory_space=pltpu.SMEM)
HBM = pl.BlockSpec(memory_space=pltpu.HBM)


def shape(dims, dtype):
    return jax.ShapeDtypeStruct(dims, dtype)


def call(kernel, outs, *args, specs=None, out_specs=None, flops=10**8, scratch=(), **options):
    return pl.pallas_call(
        kernel,
        out_shape=outs,
        in_specs=specs or [VMEM] * len(args),
        out_specs=out_specs or jax.tree.map(lambda _: VMEM, outs),
        scratch_shapes=scratch,
        **options,
        compiler_params=pltpu.CompilerParams(vmem_limit_bytes=VMEM_LIMIT),
        cost_estimate=pl.CostEstimate(flops=flops, bytes_accessed=10**6, transcendentals=0),
    )(*args)


def shifted(x, axis, by):
    count = lax.axis_size(axis)
    return lax.ppermute(x, axis, [(i, (i + by) % count) for i in range(count)])


def across(x, axis, k):
    count = lax.axis_size(axis)
    return lax.ppermute(x, axis, [(i, i ^ k) for i in range(count)])


def diagonal(x):
    lines, pairs = lax.axis_size("mesh"), lax.axis_size("sub")
    moves = [(m * pairs + p, (m ^ 1) * pairs + (p ^ 1)) for m in range(lines) for p in range(pairs)]
    return lax.ppermute(x, ("mesh", "sub"), moves)


def paired_sums(messages, lines, strip, narrow, width, hid, node_terms):
    sends, keeps, outs = messages[:3], messages[3:6], messages[6:]
    order = range(lines - 1, 0, -1)
    block = shape((strip + TAIL, hid), bf16)
    far = across(sends[0], "sub", 1)
    out_terms = {k: across(outs[k], "mesh", k) for k in order}
    one = across(sends[1], "sub", 1)
    zero = across(sends[2], "sub", 1)
    line = {}
    line[3], line[2], tail = call(far_kernel, [block, block, shape((TAIL, hid), bf16)], far, keeps[0])
    line[1] = call(near_kernel, block, one, keeps[1], tail)
    line_terms = {k: across(line[k], "mesh", k) for k in order}
    out_send, out_keep = call(
        line_kernel,
        [shape((narrow, hid), bf16)] * 2,
        *[out_terms[k] for k in order], outs[0], line[1],
    )
    node_part = node_terms(out_terms[3], out_terms[1], zero)
    own, tail = call(
        own_kernel,
        [shape((strip + narrow, hid), bf16), shape((TAIL, hid), f32)],
        *[line_terms[k] for k in order], keeps[2], zero, tail, out_keep, across(out_send, "sub", 1),
        node_part,
    )
    mine = {k: across(own, "mesh", k) for k in order}
    mine[0] = own
    theirs = {0: across(own, "sub", 1), 1: diagonal(own)}
    early = (mine[0], mine[1], theirs[0], theirs[1])
    theirs[2] = across(mine[2], "sub", 1)
    last = call(relay_kernel, shape(own.shape, bf16), *early, mine[3])
    theirs[3] = across(last, "sub", 1)
    wholes = [shape((width, hid), f32), shape((width, hid), f32), shape((hid, width), f32)]
    scratch = [
        pltpu.VMEM((2, strip, hid), f32), pltpu.VMEM((2, strip, hid), f32), pltpu.VMEM((2, narrow, width), f32),
        pltpu.SemaphoreType.DMA((6,)),
    ]
    grads = call(
        functools.partial(place_kernel, lines, (0, 1)), wholes, *early,
        out_specs=[HBM] * 3, scratch=scratch, flops=10**8,
    )
    grads = call(
        functools.partial(place_kernel, lines, (3, 2)), wholes,
        mine[3], mine[2], theirs[3], theirs[2], *grads,
        specs=[VMEM] * 4 + [HBM] * 3, out_specs=[HBM] * 3, scratch=scratch,
        input_output_aliases={4: 0, 5: 1, 6: 2},
    )
    return (*grads, tail), node_part


def shards(
    node_state,
    send_rows,
    edge_src,
    edge_dst,
    block_count,
    w_src,
    w_dst,
    hidden_bias,
    w_out,
    norm_gain,
    cotangent,
):
    rows, width = node_state.shape
    hid = w_src.shape[1]
    halo = send_rows.shape[2]
    edges = edge_src.shape[0]
    peers = lax.axis_size("mesh") * lax.axis_size("sub")
    merged = lax.axis_size("sub") == 2
    total_rows = 2 * width + (width // hid) * hid
    chunk = -(-total_rows // (peers * 16)) * 16

    piece = [halo, halo, 2 * halo] if merged else [halo] * 4
    routes = [("mesh", 1), ("mesh", -1), ("sub", 1)] + ([] if merged else [("sub", -1)])
    n_halo = len(piece)

    def in_hbm(x):
        return pltpu.with_memory_space_constraint(x, pltpu.HBM)

    node, send, *outgoing = call(
        send_kernel,
        [shape((rows, width), bf16), shape(send_rows.shape, jnp.int32)]
        + [shape((n, width), bf16) for n in piece],
        in_hbm(node_state), in_hbm(send_rows),
        specs=[HBM, HBM],
        scratch=[pltpu.SemaphoreType.DMA((2,))],
    )
    arrived = [shifted(x, axis, by) for x, (axis, by) in zip(outgoing, routes)]

    fetched = [
        edge_src.reshape(1, edges), edge_dst.reshape(1, edges), block_count,
        hidden_bias.reshape(1, hid), w_src, w_dst, w_out, norm_gain.reshape(1, width), cotangent,
    ]
    w_src_other, w_dst_other, w_out_other = [shifted(w, "lat", 1) for w in (w_src, w_dst, w_out)]
    bias_other = shifted(fetched[3], "lat", 1)
    pre, pick, collect, spread, scatter, w_src, w_dst, w_out, gain, cot = call(
        local_kernel,
        [
            shape((edges, 2 * hid), f32),
            shape((edges, 4 * halo), bf16),
            shape((rows, edges), bf16),
            shape((edges, rows), bf16),
            shape((rows + 4 * halo, edges), bf16),
        ]
        + [shape(x.shape, x.dtype) for x in fetched[4:]],
        node, w_src_other, w_dst_other, bias_other, *[in_hbm(x) for x in fetched],
        specs=[VMEM] * 4 + [HBM] * len(fetched),
        scratch=[
            pltpu.SMEM(block_count.shape, jnp.int32),
            pltpu.VMEM((1, edges), jnp.int32),
            pltpu.VMEM((1, edges), jnp.int32),
            pltpu.VMEM((1, hid), f32),
            pltpu.SemaphoreType.DMA((N_FETCHED,)),
        ],
    )


    lines = lax.axis_size("mesh")
    paired = merged and lines == 4
    if paired:
        strip = width // lines
        narrow = hid // lines
        rows_of = (2 * strip + TAIL, strip, strip + 2 * halo, 2 * strip + TAIL, strip, strip)
        message_shapes = [shape((n, hid), bf16) for n in rows_of]
        message_shapes += [shape((narrow + k % 2 * (halo // 2), width), bf16) for k in range(lines)]
    else:
        message_shapes = [shape((peers, chunk + TAIL, hid), bf16)]
        message_shapes += [shape((n, hid), bf16) for n in piece]
    normed, local, target, *messages = call(
        functools.partial(edge_kernel, (peers, chunk, n_halo, paired)),
        [shape((rows, width), f32), shape((rows, hid), f32), shape((rows, hid), bf16)]
        + message_shapes,
        node, pre, pick, collect, spread, scatter, w_src, w_src_other, w_out, w_out_other, gain, cot, *arrived,
        scratch=[
            pltpu.VMEM((hid, width), bf16),
            pltpu.VMEM((2 * halo, hid), bf16),
            pltpu.VMEM((2, width, hid), bf16),
        ],
    )

    def node_terms(*returned):
        return call(
            paired_node_kernel if paired else node_kernel,
            shape((rows, width), bf16),
            send, local, target, w_src, w_dst, *returned,
        )

    if paired:
        (src_grad, dst_grad, out_grad, tail), node_part = paired_sums(
            messages, lines, strip, narrow, width, hid, node_terms
        )
    else:
        node_part = node_terms(
            *[shifted(x, axis, -by) for x, (axis, by) in zip(messages[1:], routes)]
        )
        exchanged = lax.all_to_all(messages[0], ("mesh", "sub"), 0, 0)
        reduced, bias_grad, gain_grad = call(
            functools.partial(sum_kernel, chunk),
            [shape((peers, chunk, hid), bf16), shape((1, hid), f32), shape((1, width), f32)],
            exchanged,
        )
        gathered = lax.all_to_all(reduced, ("mesh", "sub"), 0, 0)
        src_grad, dst_grad, out_grad = call(
            unpack_kernel,
            [shape((width, hid), f32), shape((width, hid), f32), shape((hid, width), f32)],
            gathered.reshape(peers * chunk, hid),
        )
    finished = [shape((rows, width), f32), shape((rows, width), bf16)]
    ends = [cot, node, gain, normed, node_part, shifted(node_part, "lat", 1)]
    if paired:
        node_grad, updated, bias_grad, gain_grad = call(
            finish_kernel, finished + [shape((1, hid), f32), shape((1, width), f32)], *ends, tail
        )
    else:
        node_grad, updated = call(finish_kernel, finished, *ends)
    return (
        updated, node_grad, src_grad, dst_grad, out_grad,
        bias_grad.reshape(hid), gain_grad.reshape(width),
    )


def solution(mesh):
    nodes = P(("parts", "mesh", "sub"), None)
    slots = P(("parts", "mesh", "sub"))
    in_specs = (
        nodes,
        P(("parts", "mesh", "sub"), None, None),
        slots,
        slots,
        slots,
        P(None, "lat"),
        P(None, "lat"),
        P("lat"),
        P("lat", None),
        P(),
        nodes,
    )
    out_specs = (
        nodes,
        nodes,
        P("parts", "lat"),
        P("parts", "lat"),
        P(("parts", "lat"), None),
        P(("parts", "lat")),
        P("parts"),
    )
    return jax.shard_map(shards, mesh=mesh, in_specs=in_specs, out_specs=out_specs, check_vma=False)
```

```python
import functools

import jax
import jax.numpy as jnp
from jax import lax
from jax.experimental import pallas as pl
from jax.experimental.pallas import tpu as pltpu
from jax.sharding import PartitionSpec as P

BLOCK = 128
EPSILON = 1e-05
TAIL = 16
N_FETCHED = 9
VMEM_LIMIT = 24 * 1024 * 1024

f32 = jnp.float32
bf16 = jnp.bfloat16

NN = (((1,), (0,)), ((), ()))
NT = (((1,), (1,)), ((), ()))
TN = (((0,), (0,)), ((), ()))


def dot(a, b, dims=NN):
    return lax.dot_general(a, b, dims, preferred_element_type=f32)


def iota(shape, dim):
    return lax.broadcasted_iota(jnp.int32, shape, dim)


def one_hot(condition):
    return jnp.where(condition, 1.0, 0.0).astype(bf16)


def split(x):
    high = x.astype(bf16)
    return high, (x - high.astype(f32)).astype(bf16)


def columns_of(row, lanes):
    return jnp.transpose(jnp.broadcast_to(row, (lanes, row.shape[1])))


def usable_row(count_ref, edges):
    lane = iota((1, BLOCK), 1)
    parts = [lane < count_ref[b] for b in range(edges // BLOCK)]
    return jnp.concatenate([jnp.where(p, 1, 0) for p in parts], axis=1)


def usable_columns(count_ref, edges, lanes):
    sub = iota((BLOCK, lanes), 0)
    return jnp.concatenate(
        [jnp.where(sub < count_ref[b], 1, 0) for b in range(edges // BLOCK)], axis=0
    )


def fetch(sems, *pairs):
    copies = [pltpu.make_async_copy(a, b, sems.at[i]) for i, (a, b) in enumerate(pairs)]
    for copy in copies:
        copy.start()
    return copies


def send_kernel(node_hbm, send_hbm, node_ref, send_ref, *rest):
    *out_refs, sems = rest
    for copy in fetch(sems, (node_hbm, node_ref), (send_hbm, send_ref)):
        copy.wait()
    node = node_ref[...]
    rows = node.shape[0]
    halo = send_ref.shape[2]
    pieces = []
    for d in range(4):
        pick = one_hot(iota((rows, halo), 0) == send_ref[0, d : d + 1, :])
        pieces.append(dot(pick, node, TN).astype(bf16))
    out_refs[0][...] = pieces[0]
    out_refs[1][...] = pieces[1]
    if len(out_refs) == 3:
        out_refs[2][0:halo, :] = pieces[2]
        out_refs[2][halo:, :] = pieces[3]
    else:
        out_refs[2][...] = pieces[2]
        out_refs[3][...] = pieces[3]


def local_kernel(*refs):
    node_ref, ins, refs = refs[0], refs[1 : 1 + N_FETCHED], refs[1 + N_FETCHED :]
    pre_ref, pick_ref, collect_ref, spread_ref, scatter_ref, *refs = refs
    w_src_ref, w_dst_ref, w_out_ref, gain_ref, cot_ref, count_ref, src_ref, dst_ref, bias_ref, sems = refs
    outs = (src_ref, dst_ref, count_ref, bias_ref, w_src_ref, w_dst_ref, w_out_ref, gain_ref, cot_ref)
    copies = fetch(sems, *zip(ins, outs))
    node = node_ref[...]
    rows = node.shape[0]
    edges = src_ref.shape[1]
    for copy in copies[:3]:
        copy.wait()
    scatter_ref[...] = one_hot(iota(scatter_ref.shape, 0) == src_ref[...])
    used = usable_row(count_ref, edges) > 0
    collect_ref[...] = one_hot((iota((rows, edges), 0) == dst_ref[...]) & used)
    source = columns_of(src_ref[...], 128)
    target = columns_of(dst_ref[...], 128)
    lane = iota(source.shape, 1)
    used = usable_columns(count_ref, edges, 128) > 0
    near = one_hot(source == lane)
    pick_ref[...] = one_hot(source == lane + rows)
    spread_ref[...] = one_hot((target == lane) & used)
    both = jnp.concatenate([dot(near, node), dot(one_hot(target == lane), node)], axis=1).astype(bf16)
    for copy in copies[3:]:
        copy.wait()
    weights = jnp.concatenate([w_src_ref[...], w_dst_ref[...]], axis=0)
    pre_ref[...] = dot(both, weights) + bias_ref[...]


def twice(x):
    return jnp.concatenate([x, x], axis=1)


def stacked(x):
    return jnp.concatenate(split(x), axis=0)


def forward_kernel(pre_ref, pick_ref, collect_ref, w_src_ref, w_out_ref, *rest):
    *halo_refs, factor_ref, hidden_ref, partial_ref = rest
    halo = jnp.concatenate([r[...] for r in halo_refs], axis=0)
    far = stacked(dot(halo, w_src_ref[...]))
    pre = pre_ref[...] + dot(twice(pick_ref[...]), far)
    sig = 0.5 + 0.5 * jnp.tanh(0.5 * pre)
    factor_ref[...] = sig * (1.0 + pre * (1.0 - sig))
    hidden = dot(collect_ref[...], (pre * sig).astype(bf16))
    high, low = split(hidden)
    hidden_ref[...] = high
    w_out = w_out_ref[...]
    partial_ref[...] = (dot(high, w_out) + dot(low, w_out)).astype(bf16)


def backward_kernel(
    geometry,
    node_ref, collect_ref, spread_ref, scatter_ref, w_out_ref, gain_ref, cot_ref,
    factor_ref, hidden_ref, own_ref, other_ref,
    *rest,
):
    peers, chunk, n_halo, paired = geometry
    *rest, out_scratch, back_scratch, pair_scratch = rest
    halo_refs = rest[:n_halo]
    normed_ref, local_ref, target_ref, *message_refs = rest[n_halo:]
    node = node_ref[...]
    rows, width = node.shape
    aggregate = own_ref[...].astype(f32) + other_ref[...].astype(f32)
    center = aggregate - jnp.mean(aggregate, axis=1, keepdims=True)
    variance = jnp.mean(center * center, axis=1, keepdims=True)
    inverse = lax.rsqrt(variance + EPSILON)
    normed = center * inverse
    gain = gain_ref[...]
    upstream = cot_ref[...].astype(f32)
    scaled = upstream * gain
    agg_grad = inverse * (
        scaled
        - jnp.mean(scaled, axis=1, keepdims=True)
        - normed * jnp.mean(scaled * normed, axis=1, keepdims=True)
    )
    agg_grad = agg_grad.astype(bf16)
    normed_ref[...] = normed
    gain_part = jnp.sum(upstream * normed, axis=0, keepdims=True)

    act_grad = dot(twice(spread_ref[...]), stacked(dot(agg_grad, w_out_ref[...], NT)))
    pre_grad = (act_grad * factor_ref[...]).astype(bf16)

    table = jnp.concatenate([node] + [r[...] for r in halo_refs], axis=0)
    by_source = dot(scatter_ref[...], pre_grad)
    by_target = dot(collect_ref[...], pre_grad)
    local_ref[...] = by_source[:rows]
    by_target_low = by_target.astype(bf16)
    by_source_low = by_source.astype(bf16)
    target_ref[...] = by_target_low

    hid = by_source.shape[1]
    bias_part = jnp.sum(by_target, axis=0, keepdims=True)
    src_part = dot(table, by_source_low, TN).astype(bf16)
    dst_part = dot(node, by_target_low, TN).astype(bf16)
    out_part = dot(hidden_ref[...], agg_grad, TN).astype(bf16)
    vectors = [bias_part] + [gain_part[:, at : at + hid] for at in range(0, width, hid)]
    tail = tail_of(vectors)
    back = by_source_low[rows:]

    if paired:
        sends, keeps, out_refs = message_refs[:3], message_refs[3:6], message_refs[6:]
        sub = lax.axis_index("sub")
        mesh = lax.axis_index("mesh")
        lines = len(out_refs)
        halo = back.shape[0] // 4
        first = sub == 0
        pair_scratch[0] = jnp.where(first, dst_part, src_part)
        pair_scratch[1] = jnp.where(first, src_part, dst_part)
        strip = width // lines
        for slot, (far_ref, one_ref, zero_ref) in enumerate((sends, keeps)):
            places = ((far_ref, 0, 3), (far_ref, strip, 2), (one_ref, 0, 1), (zero_ref, 0, 0))
            for ref, at, k in places:
                start = pl.multiple_of((mesh ^ k) * strip, strip)
                ref[at : at + strip, :] = pair_scratch[slot, pl.ds(start, strip), :]
            far_ref[2 * strip :, :] = tail
        sends[2][strip:, :] = back[2 * halo :]
        back_scratch[...] = back[: 2 * halo]
        out_scratch[...] = out_part
        strip = hid // len(out_refs)
        for k, ref in enumerate(out_refs):
            start = pl.multiple_of((mesh ^ k) * strip, strip)
            ref[0:strip, :] = out_scratch[pl.ds(start, strip), :]
            if k % 2 == 1:
                slot = (mesh + (k // 2) + 1) % 2
                start = pl.multiple_of(slot * halo, halo)
                rows_back = back_scratch[pl.ds(start, halo), :]
                ref[strip:, 0:hid] = rows_back[: halo // 2]
                ref[strip:, hid:] = rows_back[halo // 2 :]
        return

    message_ref, *back_refs = message_refs
    at = 0
    for ref in back_refs:
        ref[...] = back[at : at + ref.shape[0]]
        at += ref.shape[0]
    blocks = [src_part, dst_part]
    for at in range(0, width, hid):
        blocks.append(out_part[:, at : at + hid])
    done = 0
    for block in blocks:
        at = 0
        while at < block.shape[0]:
            peer, offset = divmod(done, chunk)
            take = min(chunk - offset, block.shape[0] - at)
            message_ref[peer, offset : offset + take, :] = block[at : at + take]
            at += take
            done += take
    while done < peers * chunk:
        peer, offset = divmod(done, chunk)
        take = chunk - offset
        message_ref[peer, offset : offset + take, :] = jnp.zeros((take, hid), bf16)
        done += take
    for peer in range(peers):
        message_ref[peer, chunk:, :] = tail


def tail_of(vectors):
    tail = []
    for v in vectors:
        high = v.astype(bf16).astype(f32)
        tail += [high, v - high]
    tail.append(jnp.zeros((TAIL - len(tail), vectors[0].shape[1]), f32))
    return jnp.concatenate(tail, axis=0).astype(bf16)


def tree(terms):
    while len(terms) > 1:
        terms = [terms[i] + terms[i + 1] for i in range(0, len(terms), 2)]
    return terms[0]


def far_kernel(arrived_ref, keep_ref, three_ref, two_ref, tail_ref):
    total = keep_ref[...].astype(f32) + arrived_ref[...].astype(f32)
    strip = three_ref.shape[0] - TAIL
    tail = total[2 * strip :]
    tail = tail_of([tail[at : at + 1] + tail[at + 1 : at + 2] for at in range(0, 6, 2)])
    for k, ref in enumerate((three_ref, two_ref)):
        ref[0:strip, :] = total[k * strip : (k + 1) * strip].astype(bf16)
        ref[strip:, :] = tail
    tail_ref[...] = tail


def near_kernel(arrived_ref, keep_ref, tail_ref, one_ref):
    strip = keep_ref.shape[0]
    one_ref[0:strip, :] = (keep_ref[...].astype(f32) + arrived_ref[...].astype(f32)).astype(bf16)
    one_ref[strip:, :] = tail_ref[...]


def line_kernel(*refs):
    *terms, _, send_ref, keep_ref = refs
    rows, hid = send_ref.shape
    total = tree([r[0:rows, :].astype(f32) for r in terms])
    first = lax.axis_index("sub") == 0
    left, right = total[:, :hid], total[:, hid:]
    send_ref[...] = jnp.where(first, right, left).astype(bf16)
    keep_ref[...] = jnp.where(first, left, right).astype(bf16)


def own_kernel(*refs):
    *terms, keep_ref, arrived_ref, vectors_ref, out_keep_ref, out_arrived_ref, _, own_ref, tail_ref = refs
    strip = keep_ref.shape[0]
    zero = (keep_ref[...].astype(f32) + arrived_ref[0:strip, :].astype(f32)).astype(bf16)
    total = tree([r[0:strip, :].astype(f32) for r in terms] + [zero.astype(f32)])
    own_ref[0:strip, :] = total.astype(bf16)
    own_ref[strip:, :] = (
        out_keep_ref[...].astype(f32) + out_arrived_ref[...].astype(f32)
    ).astype(bf16)
    tail_ref[...] = tree([r[strip:, :].astype(f32) for r in terms] + [vectors_ref[...].astype(f32)])


def write_vectors(tail, bias_ref, gain_ref):
    bias_ref[...] = tail[0:1] + tail[1:2]
    hid = tail.shape[1]
    for k in range(gain_ref.shape[1] // hid):
        gain_ref[:, k * hid : (k + 1) * hid] = tail[2 + 2 * k : 3 + 2 * k] + tail[3 + 2 * k : 4 + 2 * k]


def relay_kernel(*refs):
    *_, strip_ref, out_ref = refs
    out_ref[...] = strip_ref[...]


def place_kernel(lines, which, a_ref, b_ref, c_ref, d_ref, *refs):
    src_hbm, dst_hbm, out_hbm, src_ref, dst_ref, out_ref, sems = refs[-7:]
    first = lax.axis_index("sub") == 0
    mesh = lax.axis_index("mesh")
    strip, hid = src_ref.shape[1:]
    narrow = out_ref.shape[1]
    copies = []

    def put(ref, hbm, at, rows):
        start = pl.multiple_of((mesh ^ which[at]) * rows, rows)
        copies.append(pltpu.make_async_copy(ref.at[at], hbm.at[pl.ds(start, rows)], sems.at[len(copies)]))
        copies[-1].start()

    for at, (mine_ref, theirs_ref) in enumerate(((a_ref, c_ref), (b_ref, d_ref))):
        mine, theirs = mine_ref[...], theirs_ref[...]
        low = jnp.where(first, mine, theirs).astype(f32)
        high = jnp.where(first, theirs, mine).astype(f32)
        src_ref[at] = low[:strip]
        put(src_ref, src_hbm, at, strip)
        dst_ref[at] = high[:strip]
        put(dst_ref, dst_hbm, at, strip)
        out_ref[at, :, 0:hid] = low[strip:]
        out_ref[at, :, hid:] = high[strip:]
        put(out_ref, out_hbm, at, narrow)
    for copy in copies:
        copy.wait()


def sum_kernel(chunk, arrived_ref, out_ref, bias_ref, gain_ref):
    peers = arrived_ref.shape[0]
    total = arrived_ref[0].astype(f32)
    for peer in range(1, peers):
        total += arrived_ref[peer].astype(f32)
    low = total[:chunk].astype(bf16)
    for peer in range(peers):
        out_ref[peer] = low
    tail = total[chunk:]
    write_vectors(tail, bias_ref, gain_ref)


def unpack_kernel(arrived_ref, src_ref, dst_ref, out_ref):
    hid = src_ref.shape[1]
    rows = src_ref.shape[0]
    src_ref[...] = arrived_ref[0:rows, :].astype(f32)
    dst_ref[...] = arrived_ref[rows : 2 * rows, :].astype(f32)
    at = 2 * rows
    for k in range(out_ref.shape[1] // hid):
        out_ref[:, k * hid : (k + 1) * hid] = arrived_ref[at : at + out_ref.shape[0], :].astype(f32)
        at += out_ref.shape[0]


def node_part(send_ref, local_ref, target_ref, w_src_ref, w_dst_ref, returned, out_ref):
    rows = local_ref.shape[0]
    halo = send_ref.shape[2]
    picks = [one_hot(iota((rows, halo), 0) == send_ref[0, d : d + 1, :]) for d in range(4)]
    total = local_ref[...] + dot(jnp.concatenate(picks, axis=1), jnp.concatenate(returned, axis=0))
    out_ref[...] = (
        dot(total.astype(bf16), w_src_ref[...], NT) + dot(target_ref[...], w_dst_ref[...], NT)
    ).astype(bf16)


def node_kernel(send_ref, local_ref, target_ref, w_src_ref, w_dst_ref, *rest):
    *back_refs, out_ref = rest
    returned = [r[...] for r in back_refs]
    node_part(send_ref, local_ref, target_ref, w_src_ref, w_dst_ref, returned, out_ref)


def paired_node_kernel(
    send_ref, local_ref, target_ref, w_src_ref, w_dst_ref, three_ref, one_ref, pair_ref, out_ref
):
    even = lax.axis_index("mesh") % 2 == 0
    halo = send_ref.shape[2]
    hid = local_ref.shape[1]
    at = one_ref.shape[0] - halo // 2
    one, three = [
        jnp.concatenate([r[at:, :hid], r[at:, hid:]], axis=0) for r in (one_ref, three_ref)
    ]
    returned = [
        jnp.where(even, one, three), jnp.where(even, three, one), pair_ref[pair_ref.shape[0] - 2 * halo :, :]
    ]
    node_part(send_ref, local_ref, target_ref, w_src_ref, w_dst_ref, returned, out_ref)


def finish_kernel(cot_ref, node_ref, gain_ref, normed_ref, own_ref, other_ref, *rest):
    if len(rest) == 5:
        tail_ref, *rest, bias_out_ref, gain_out_ref = rest
        write_vectors(tail_ref[...], bias_out_ref, gain_out_ref)
    grad_ref, updated_ref = rest
    grad_ref[...] = cot_ref[...].astype(f32) + (
        own_ref[...].astype(f32) + other_ref[...].astype(f32)
    )
    updated_ref[...] = (node_ref[...].astype(f32) + gain_ref[...] * normed_ref[...]).astype(bf16)


VMEM = pl.BlockSpec(memory_space=pltpu.VMEM)
SMEM = pl.BlockSpec(memory_space=pltpu.SMEM)
HBM = pl.BlockSpec(memory_space=pltpu.HBM)


def shape(dims, dtype):
    return jax.ShapeDtypeStruct(dims, dtype)


def call(kernel, outs, *args, specs=None, out_specs=None, flops=10**8, scratch=(), **options):
    return pl.pallas_call(
        kernel,
        out_shape=outs,
        in_specs=specs or [VMEM] * len(args),
        out_specs=out_specs or jax.tree.map(lambda _: VMEM, outs),
        scratch_shapes=scratch,
        **options,
        compiler_params=pltpu.CompilerParams(vmem_limit_bytes=VMEM_LIMIT),
        cost_estimate=pl.CostEstimate(flops=flops, bytes_accessed=10**6, transcendentals=0),
    )(*args)


def shifted(x, axis, by):
    count = lax.axis_size(axis)
    return lax.ppermute(x, axis, [(i, (i + by) % count) for i in range(count)])


def across(x, axis, k):
    count = lax.axis_size(axis)
    return lax.ppermute(x, axis, [(i, i ^ k) for i in range(count)])


def diagonal(x):
    lines, pairs = lax.axis_size("mesh"), lax.axis_size("sub")
    moves = [(m * pairs + p, (m ^ 1) * pairs + (p ^ 1)) for m in range(lines) for p in range(pairs)]
    return lax.ppermute(x, ("mesh", "sub"), moves)


def paired_sums(messages, lines, strip, narrow, width, hid, node_terms):
    sends, keeps, outs = messages[:3], messages[3:6], messages[6:]
    order = range(lines - 1, 0, -1)
    block = shape((strip + TAIL, hid), bf16)
    far = across(sends[0], "sub", 1)
    out_terms = {k: across(outs[k], "mesh", k) for k in order}
    one = across(sends[1], "sub", 1)
    zero = across(sends[2], "sub", 1)
    line = {}
    line[3], line[2], tail = call(far_kernel, [block, block, shape((TAIL, hid), bf16)], far, keeps[0])
    line[1] = call(near_kernel, block, one, keeps[1], tail)
    line_terms = {k: across(line[k], "mesh", k) for k in order}
    out_send, out_keep = call(
        line_kernel,
        [shape((narrow, hid), bf16)] * 2,
        *[out_terms[k] for k in order], outs[0], line[1],
    )
    node_part = node_terms(out_terms[3], out_terms[1], zero)
    own, tail = call(
        own_kernel,
        [shape((strip + narrow, hid), bf16), shape((TAIL, hid), f32)],
        *[line_terms[k] for k in order], keeps[2], zero, tail, out_keep, across(out_send, "sub", 1),
        node_part,
    )
    mine = {k: across(own, "mesh", k) for k in order}
    mine[0] = own
    theirs = {0: across(own, "sub", 1), 1: diagonal(own)}
    early = (mine[0], mine[1], theirs[0], theirs[1])
    theirs[2] = across(mine[2], "sub", 1)
    last = call(relay_kernel, shape(own.shape, bf16), *early, mine[3])
    theirs[3] = across(last, "sub", 1)
    wholes = [shape((width, hid), f32), shape((width, hid), f32), shape((hid, width), f32)]
    scratch = [
        pltpu.VMEM((2, strip, hid), f32), pltpu.VMEM((2, strip, hid), f32), pltpu.VMEM((2, narrow, width), f32),
        pltpu.SemaphoreType.DMA((6,)),
    ]
    grads = call(
        functools.partial(place_kernel, lines, (0, 1)), wholes, *early,
        out_specs=[HBM] * 3, scratch=scratch, flops=10**8,
    )
    grads = call(
        functools.partial(place_kernel, lines, (3, 2)), wholes,
        mine[3], mine[2], theirs[3], theirs[2], *grads,
        specs=[VMEM] * 4 + [HBM] * 3, out_specs=[HBM] * 3, scratch=scratch,
        input_output_aliases={4: 0, 5: 1, 6: 2},
    )
    return (*grads, tail), node_part


def shards(
    node_state,
    send_rows,
    edge_src,
    edge_dst,
    block_count,
    w_src,
    w_dst,
    hidden_bias,
    w_out,
    norm_gain,
    cotangent,
):
    rows, width = node_state.shape
    hid = w_src.shape[1]
    halo = send_rows.shape[2]
    edges = edge_src.shape[0]
    peers = lax.axis_size("mesh") * lax.axis_size("sub")
    merged = lax.axis_size("sub") == 2
    total_rows = 2 * width + (width // hid) * hid
    chunk = -(-total_rows // (peers * 16)) * 16

    piece = [halo, halo, 2 * halo] if merged else [halo] * 4
    routes = [("mesh", 1), ("mesh", -1), ("sub", 1)] + ([] if merged else [("sub", -1)])
    n_halo = len(piece)

    def in_hbm(x):
        return pltpu.with_memory_space_constraint(x, pltpu.HBM)

    node, send, *outgoing = call(
        send_kernel,
        [shape((rows, width), bf16), shape(send_rows.shape, jnp.int32)]
        + [shape((n, width), bf16) for n in piece],
        in_hbm(node_state), in_hbm(send_rows),
        specs=[HBM, HBM],
        scratch=[pltpu.SemaphoreType.DMA((2,))],
    )
    arrived = [shifted(x, axis, by) for x, (axis, by) in zip(outgoing, routes)]

    fetched = [
        edge_src.reshape(1, edges), edge_dst.reshape(1, edges), block_count,
        hidden_bias.reshape(1, hid), w_src, w_dst, w_out, norm_gain.reshape(1, width), cotangent,
    ]
    pre, pick, collect, spread, scatter, w_src, w_dst, w_out, gain, cot = call(
        local_kernel,
        [
            shape((edges, hid), f32),
            shape((edges, 4 * halo), bf16),
            shape((rows, edges), bf16),
            shape((edges, rows), bf16),
            shape((rows + 4 * halo, edges), bf16),
        ]
        + [shape(x.shape, x.dtype) for x in fetched[4:]],
        node, *[in_hbm(x) for x in fetched],
        specs=[VMEM] + [HBM] * len(fetched),
        scratch=[
            pltpu.SMEM(block_count.shape, jnp.int32),
            pltpu.VMEM((1, edges), jnp.int32),
            pltpu.VMEM((1, edges), jnp.int32),
            pltpu.VMEM((1, hid), f32),
            pltpu.SemaphoreType.DMA((N_FETCHED,)),
        ],
    )

    factor, hidden, partial = call(
        forward_kernel,
        [shape((edges, hid), f32), shape((rows, hid), bf16), shape((rows, width), bf16)],
        pre, pick, collect, w_src, w_out, *arrived,
    )
    other = shifted(partial, "lat", 1)

    lines = lax.axis_size("mesh")
    paired = merged and lines == 4
    if paired:
        strip = width // lines
        narrow = hid // lines
        rows_of = (2 * strip + TAIL, strip, strip + 2 * halo, 2 * strip + TAIL, strip, strip)
        message_shapes = [shape((n, hid), bf16) for n in rows_of]
        message_shapes += [shape((narrow + k % 2 * (halo // 2), width), bf16) for k in range(lines)]
    else:
        message_shapes = [shape((peers, chunk + TAIL, hid), bf16)]
        message_shapes += [shape((n, hid), bf16) for n in piece]
    normed, local, target, *messages = call(
        functools.partial(backward_kernel, (peers, chunk, n_halo, paired)),
        [shape((rows, width), f32), shape((rows, hid), f32), shape((rows, hid), bf16)]
        + message_shapes,
        node, collect, spread, scatter, w_out, gain, cot, factor, hidden, partial, other, *arrived,
        scratch=[
            pltpu.VMEM((hid, width), bf16),
            pltpu.VMEM((2 * halo, hid), bf16),
            pltpu.VMEM((2, width, hid), bf16),
        ],
    )

    def node_terms(*returned):
        return call(
            paired_node_kernel if paired else node_kernel,
            shape((rows, width), bf16),
            send, local, target, w_src, w_dst, *returned,
        )

    if paired:
        (src_grad, dst_grad, out_grad, tail), node_part = paired_sums(
            messages, lines, strip, narrow, width, hid, node_terms
        )
    else:
        node_part = node_terms(
            *[shifted(x, axis, -by) for x, (axis, by) in zip(messages[1:], routes)]
        )
        exchanged = lax.all_to_all(messages[0], ("mesh", "sub"), 0, 0)
        reduced, bias_grad, gain_grad = call(
            functools.partial(sum_kernel, chunk),
            [shape((peers, chunk, hid), bf16), shape((1, hid), f32), shape((1, width), f32)],
            exchanged,
        )
        gathered = lax.all_to_all(reduced, ("mesh", "sub"), 0, 0)
        src_grad, dst_grad, out_grad = call(
            unpack_kernel,
            [shape((width, hid), f32), shape((width, hid), f32), shape((hid, width), f32)],
            gathered.reshape(peers * chunk, hid),
        )
    finished = [shape((rows, width), f32), shape((rows, width), bf16)]
    ends = [cot, node, gain, normed, node_part, shifted(node_part, "lat", 1)]
    if paired:
        node_grad, updated, bias_grad, gain_grad = call(
            finish_kernel, finished + [shape((1, hid), f32), shape((1, width), f32)], *ends, tail
        )
    else:
        node_grad, updated = call(finish_kernel, finished, *ends)
    return (
        updated, node_grad, src_grad, dst_grad, out_grad,
        bias_grad.reshape(hid), gain_grad.reshape(width),
    )


def solution(mesh):
    nodes = P(("parts", "mesh", "sub"), None)
    slots = P(("parts", "mesh", "sub"))
    in_specs = (
        nodes,
        P(("parts", "mesh", "sub"), None, None),
        slots,
        slots,
        slots,
        P(None, "lat"),
        P(None, "lat"),
        P("lat"),
        P("lat", None),
        P(),
        nodes,
    )
    out_specs = (
        nodes,
        nodes,
        P("parts", "lat"),
        P("parts", "lat"),
        P(("parts", "lat"), None),
        P(("parts", "lat")),
        P("parts"),
    )
    return jax.shard_map(shards, mesh=mesh, in_specs=in_specs, out_specs=out_specs, check_vma=False)
```

```python
import functools

import jax
import jax.numpy as jnp
from jax import lax
from jax.experimental import pallas as pl
from jax.experimental.pallas import tpu as pltpu
from jax.sharding import PartitionSpec as P

BLOCK = 128
EPSILON = 1e-05
TAIL = 16
N_FETCHED = 9
VMEM_LIMIT = 24 * 1024 * 1024

f32 = jnp.float32
bf16 = jnp.bfloat16

NN = (((1,), (0,)), ((), ()))
NT = (((1,), (1,)), ((), ()))
TN = (((0,), (0,)), ((), ()))


def dot(a, b, dims=NN):
    return lax.dot_general(a, b, dims, preferred_element_type=f32)


def iota(shape, dim):
    return lax.broadcasted_iota(jnp.int32, shape, dim)


def one_hot(condition):
    return jnp.where(condition, 1.0, 0.0).astype(bf16)


def split(x):
    high = x.astype(bf16)
    return high, (x - high.astype(f32)).astype(bf16)


def columns_of(row, lanes):
    return jnp.transpose(jnp.broadcast_to(row, (lanes, row.shape[1])))


def usable_row(count_ref, edges):
    lane = iota((1, BLOCK), 1)
    parts = [lane < count_ref[b] for b in range(edges // BLOCK)]
    return jnp.concatenate([jnp.where(p, 1, 0) for p in parts], axis=1)


def usable_columns(count_ref, edges, lanes):
    sub = iota((BLOCK, lanes), 0)
    return jnp.concatenate(
        [jnp.where(sub < count_ref[b], 1, 0) for b in range(edges // BLOCK)], axis=0
    )


def fetch(sems, *pairs):
    copies = [pltpu.make_async_copy(a, b, sems.at[i]) for i, (a, b) in enumerate(pairs)]
    for copy in copies:
        copy.start()
    return copies


def send_kernel(node_hbm, send_hbm, node_ref, send_ref, *rest):
    *out_refs, sems = rest
    for copy in fetch(sems, (node_hbm, node_ref), (send_hbm, send_ref)):
        copy.wait()
    node = node_ref[...]
    rows = node.shape[0]
    halo = send_ref.shape[2]
    pieces = []
    for d in range(4):
        pick = one_hot(iota((rows, halo), 0) == send_ref[0, d : d + 1, :])
        pieces.append(dot(pick, node, TN).astype(bf16))
    out_refs[0][...] = pieces[0]
    out_refs[1][...] = pieces[1]
    if len(out_refs) == 3:
        out_refs[2][0:halo, :] = pieces[2]
        out_refs[2][halo:, :] = pieces[3]
    else:
        out_refs[2][...] = pieces[2]
        out_refs[3][...] = pieces[3]


def local_kernel(*refs):
    node_ref, ins, refs = refs[0], refs[1 : 1 + N_FETCHED], refs[1 + N_FETCHED :]
    pre_ref, pick_ref, collect_ref, spread_ref, scatter_ref, *refs = refs
    w_src_ref, w_dst_ref, w_out_ref, gain_ref, cot_ref, count_ref, src_ref, dst_ref, bias_ref, sems = refs
    outs = (src_ref, dst_ref, count_ref, bias_ref, w_src_ref, w_dst_ref, w_out_ref, gain_ref, cot_ref)
    copies = fetch(sems, *zip(ins, outs))
    node = node_ref[...]
    rows = node.shape[0]
    edges = src_ref.shape[1]
    for copy in copies[:3]:
        copy.wait()
    scatter_ref[...] = one_hot(iota(scatter_ref.shape, 0) == src_ref[...])
    used = usable_row(count_ref, edges) > 0
    collect_ref[...] = one_hot((iota((rows, edges), 0) == dst_ref[...]) & used)
    source = columns_of(src_ref[...], 128)
    target = columns_of(dst_ref[...], 128)
    lane = iota(source.shape, 1)
    used = usable_columns(count_ref, edges, 128) > 0
    near = one_hot(source == lane)
    pick_ref[...] = one_hot(source == lane + rows)
    spread_ref[...] = one_hot((target == lane) & used)
    both = jnp.concatenate([dot(near, node), dot(one_hot(target == lane), node)], axis=1).astype(bf16)
    for copy in copies[3:]:
        copy.wait()
    weights = jnp.concatenate([w_src_ref[...], w_dst_ref[...]], axis=0)
    pre_ref[...] = dot(both, weights) + bias_ref[...]


def twice(x):
    return jnp.concatenate([x, x], axis=1)


def stacked(x):
    return jnp.concatenate(split(x), axis=0)


def forward_kernel(pre_ref, pick_ref, collect_ref, w_src_ref, w_out_ref, *rest):
    *halo_refs, factor_ref, hidden_ref, partial_ref = rest
    halo = jnp.concatenate([r[...] for r in halo_refs], axis=0)
    far = stacked(dot(halo, w_src_ref[...]))
    pre = pre_ref[...] + dot(twice(pick_ref[...]), far)
    sig = 0.5 + 0.5 * jnp.tanh(0.5 * pre)
    factor_ref[...] = sig * (1.0 + pre * (1.0 - sig))
    hidden = dot(collect_ref[...], (pre * sig).astype(bf16))
    high, low = split(hidden)
    hidden_ref[...] = high
    w_out = w_out_ref[...]
    partial_ref[...] = (dot(high, w_out) + dot(low, w_out)).astype(bf16)


def backward_kernel(
    geometry,
    node_ref, collect_ref, spread_ref, scatter_ref, w_out_ref, gain_ref, cot_ref,
    factor_ref, hidden_ref, own_ref, other_ref,
    *rest,
):
    peers, chunk, n_halo, paired = geometry
    *rest, out_scratch, back_scratch, pair_scratch = rest
    halo_refs = rest[:n_halo]
    normed_ref, local_ref, target_ref, *message_refs = rest[n_halo:]
    node = node_ref[...]
    rows, width = node.shape
    aggregate = own_ref[...].astype(f32) + other_ref[...].astype(f32)
    center = aggregate - jnp.mean(aggregate, axis=1, keepdims=True)
    variance = jnp.mean(center * center, axis=1, keepdims=True)
    inverse = lax.rsqrt(variance + EPSILON)
    normed = center * inverse
    gain = gain_ref[...]
    upstream = cot_ref[...].astype(f32)
    scaled = upstream * gain
    agg_grad = inverse * (
        scaled
        - jnp.mean(scaled, axis=1, keepdims=True)
        - normed * jnp.mean(scaled * normed, axis=1, keepdims=True)
    )
    agg_grad = agg_grad.astype(bf16)
    normed_ref[...] = normed
    gain_part = jnp.sum(upstream * normed, axis=0, keepdims=True)

    act_grad = dot(twice(spread_ref[...]), stacked(dot(agg_grad, w_out_ref[...], NT)))
    pre_grad = (act_grad * factor_ref[...]).astype(bf16)

    table = jnp.concatenate([node] + [r[...] for r in halo_refs], axis=0)
    by_source = dot(scatter_ref[...], pre_grad)
    by_target = dot(collect_ref[...], pre_grad)
    local_ref[...] = by_source[:rows]
    by_target_low = by_target.astype(bf16)
    by_source_low = by_source.astype(bf16)
    target_ref[...] = by_target_low

    hid = by_source.shape[1]
    bias_part = jnp.sum(by_target, axis=0, keepdims=True)
    src_part = dot(table, by_source_low, TN).astype(bf16)
    dst_part = dot(node, by_target_low, TN).astype(bf16)
    out_part = dot(hidden_ref[...], agg_grad, TN).astype(bf16)
    vectors = [bias_part] + [gain_part[:, at : at + hid] for at in range(0, width, hid)]
    tail = tail_of(vectors)
    back = by_source_low[rows:]

    if paired:
        sends, keeps, out_refs = message_refs[:2], message_refs[2:4], message_refs[4:]
        sub = lax.axis_index("sub")
        mesh = lax.axis_index("mesh")
        lines = len(out_refs)
        halo = back.shape[0] // 4
        first = sub == 0
        pair_scratch[0] = jnp.where(first, dst_part, src_part)
        pair_scratch[1] = jnp.where(first, src_part, dst_part)
        strip = width // lines
        for slot, (far_ref, zero_ref) in enumerate((sends, keeps)):
            places = [(far_ref, at, k) for at, k in enumerate((3, 2, 1))] + [(zero_ref, 0, 0)]
            for ref, at, k in places:
                start = pl.multiple_of((mesh ^ k) * strip, strip)
                ref[at * strip : (at + 1) * strip, :] = pair_scratch[slot, pl.ds(start, strip), :]
            far_ref[3 * strip :, :] = tail
        sends[1][strip:, :] = back[2 * halo :]
        back_scratch[...] = back[: 2 * halo]
        out_scratch[...] = out_part
        strip = hid // len(out_refs)
        for k, ref in enumerate(out_refs):
            start = pl.multiple_of((mesh ^ k) * strip, strip)
            ref[0:strip, :] = out_scratch[pl.ds(start, strip), :]
            if k % 2 == 1:
                slot = (mesh + (k // 2) + 1) % 2
                start = pl.multiple_of(slot * halo, halo)
                rows_back = back_scratch[pl.ds(start, halo), :]
                ref[strip:, 0:hid] = rows_back[: halo // 2]
                ref[strip:, hid:] = rows_back[halo // 2 :]
        return

    message_ref, *back_refs = message_refs
    at = 0
    for ref in back_refs:
        ref[...] = back[at : at + ref.shape[0]]
        at += ref.shape[0]
    blocks = [src_part, dst_part]
    for at in range(0, width, hid):
        blocks.append(out_part[:, at : at + hid])
    done = 0
    for block in blocks:
        at = 0
        while at < block.shape[0]:
            peer, offset = divmod(done, chunk)
            take = min(chunk - offset, block.shape[0] - at)
            message_ref[peer, offset : offset + take, :] = block[at : at + take]
            at += take
            done += take
    while done < peers * chunk:
        peer, offset = divmod(done, chunk)
        take = chunk - offset
        message_ref[peer, offset : offset + take, :] = jnp.zeros((take, hid), bf16)
        done += take
    for peer in range(peers):
        message_ref[peer, chunk:, :] = tail


def tail_of(vectors):
    tail = []
    for v in vectors:
        high = v.astype(bf16).astype(f32)
        tail += [high, v - high]
    tail.append(jnp.zeros((TAIL - len(tail), vectors[0].shape[1]), f32))
    return jnp.concatenate(tail, axis=0).astype(bf16)


def tree(terms):
    while len(terms) > 1:
        terms = [terms[i] + terms[i + 1] for i in range(0, len(terms), 2)]
    return terms[0]


def far_kernel(arrived_ref, keep_ref, *refs):
    *line_refs, tail_ref = refs
    total = keep_ref[...].astype(f32) + arrived_ref[...].astype(f32)
    strip = line_refs[0].shape[0] - TAIL
    tail = total[len(line_refs) * strip :]
    tail = tail_of([tail[at : at + 1] + tail[at + 1 : at + 2] for at in range(0, 6, 2)])
    for k, ref in enumerate(line_refs):
        ref[0:strip, :] = total[k * strip : (k + 1) * strip].astype(bf16)
        ref[strip:, :] = tail
    tail_ref[...] = tail


def line_kernel(*refs):
    *terms, _, send_ref, keep_ref = refs
    rows, hid = send_ref.shape
    total = tree([r[0:rows, :].astype(f32) for r in terms])
    first = lax.axis_index("sub") == 0
    left, right = total[:, :hid], total[:, hid:]
    send_ref[...] = jnp.where(first, right, left).astype(bf16)
    keep_ref[...] = jnp.where(first, left, right).astype(bf16)


def own_kernel(*refs):
    *terms, keep_ref, arrived_ref, vectors_ref, out_keep_ref, out_arrived_ref, _, own_ref, tail_ref = refs
    strip = keep_ref.shape[0]
    zero = (keep_ref[...].astype(f32) + arrived_ref[0:strip, :].astype(f32)).astype(bf16)
    total = tree([r[0:strip, :].astype(f32) for r in terms] + [zero.astype(f32)])
    own_ref[0:strip, :] = total.astype(bf16)
    own_ref[strip:, :] = (
        out_keep_ref[...].astype(f32) + out_arrived_ref[...].astype(f32)
    ).astype(bf16)
    tail_ref[...] = tree([r[strip:, :].astype(f32) for r in terms] + [vectors_ref[...].astype(f32)])


def write_vectors(tail, bias_ref, gain_ref):
    bias_ref[...] = tail[0:1] + tail[1:2]
    hid = tail.shape[1]
    for k in range(gain_ref.shape[1] // hid):
        gain_ref[:, k * hid : (k + 1) * hid] = tail[2 + 2 * k : 3 + 2 * k] + tail[3 + 2 * k : 4 + 2 * k]


def relay_kernel(*refs):
    *_, strip_ref, out_ref = refs
    out_ref[...] = strip_ref[...]


def place_kernel(lines, which, a_ref, b_ref, c_ref, d_ref, *refs):
    src_hbm, dst_hbm, out_hbm, src_ref, dst_ref, out_ref, sems = refs[-7:]
    first = lax.axis_index("sub") == 0
    mesh = lax.axis_index("mesh")
    strip, hid = src_ref.shape[1:]
    narrow = out_ref.shape[1]
    copies = []

    def put(ref, hbm, at, rows):
        start = pl.multiple_of((mesh ^ which[at]) * rows, rows)
        copies.append(pltpu.make_async_copy(ref.at[at], hbm.at[pl.ds(start, rows)], sems.at[len(copies)]))
        copies[-1].start()

    for at, (mine_ref, theirs_ref) in enumerate(((a_ref, c_ref), (b_ref, d_ref))):
        mine, theirs = mine_ref[...], theirs_ref[...]
        low = jnp.where(first, mine, theirs).astype(f32)
        high = jnp.where(first, theirs, mine).astype(f32)
        src_ref[at] = low[:strip]
        put(src_ref, src_hbm, at, strip)
        dst_ref[at] = high[:strip]
        put(dst_ref, dst_hbm, at, strip)
        out_ref[at, :, 0:hid] = low[strip:]
        out_ref[at, :, hid:] = high[strip:]
        put(out_ref, out_hbm, at, narrow)
    for copy in copies:
        copy.wait()


def sum_kernel(chunk, arrived_ref, out_ref, bias_ref, gain_ref):
    peers = arrived_ref.shape[0]
    total = arrived_ref[0].astype(f32)
    for peer in range(1, peers):
        total += arrived_ref[peer].astype(f32)
    low = total[:chunk].astype(bf16)
    for peer in range(peers):
        out_ref[peer] = low
    tail = total[chunk:]
    write_vectors(tail, bias_ref, gain_ref)


def unpack_kernel(arrived_ref, src_ref, dst_ref, out_ref):
    hid = src_ref.shape[1]
    rows = src_ref.shape[0]
    src_ref[...] = arrived_ref[0:rows, :].astype(f32)
    dst_ref[...] = arrived_ref[rows : 2 * rows, :].astype(f32)
    at = 2 * rows
    for k in range(out_ref.shape[1] // hid):
        out_ref[:, k * hid : (k + 1) * hid] = arrived_ref[at : at + out_ref.shape[0], :].astype(f32)
        at += out_ref.shape[0]


def node_part(send_ref, local_ref, target_ref, w_src_ref, w_dst_ref, returned, out_ref):
    rows = local_ref.shape[0]
    halo = send_ref.shape[2]
    picks = [one_hot(iota((rows, halo), 0) == send_ref[0, d : d + 1, :]) for d in range(4)]
    total = local_ref[...] + dot(jnp.concatenate(picks, axis=1), jnp.concatenate(returned, axis=0))
    out_ref[...] = (
        dot(total.astype(bf16), w_src_ref[...], NT) + dot(target_ref[...], w_dst_ref[...], NT)
    ).astype(bf16)


def node_kernel(send_ref, local_ref, target_ref, w_src_ref, w_dst_ref, *rest):
    *back_refs, out_ref = rest
    returned = [r[...] for r in back_refs]
    node_part(send_ref, local_ref, target_ref, w_src_ref, w_dst_ref, returned, out_ref)


def paired_node_kernel(
    send_ref, local_ref, target_ref, w_src_ref, w_dst_ref, three_ref, one_ref, pair_ref, out_ref
):
    even = lax.axis_index("mesh") % 2 == 0
    halo = send_ref.shape[2]
    hid = local_ref.shape[1]
    at = one_ref.shape[0] - halo // 2
    one, three = [
        jnp.concatenate([r[at:, :hid], r[at:, hid:]], axis=0) for r in (one_ref, three_ref)
    ]
    returned = [
        jnp.where(even, one, three), jnp.where(even, three, one), pair_ref[pair_ref.shape[0] - 2 * halo :, :]
    ]
    node_part(send_ref, local_ref, target_ref, w_src_ref, w_dst_ref, returned, out_ref)


def finish_kernel(cot_ref, node_ref, gain_ref, normed_ref, own_ref, other_ref, *rest):
    if len(rest) == 5:
        tail_ref, *rest, bias_out_ref, gain_out_ref = rest
        write_vectors(tail_ref[...], bias_out_ref, gain_out_ref)
    grad_ref, updated_ref = rest
    grad_ref[...] = cot_ref[...].astype(f32) + (
        own_ref[...].astype(f32) + other_ref[...].astype(f32)
    )
    updated_ref[...] = (node_ref[...].astype(f32) + gain_ref[...] * normed_ref[...]).astype(bf16)


VMEM = pl.BlockSpec(memory_space=pltpu.VMEM)
SMEM = pl.BlockSpec(memory_space=pltpu.SMEM)
HBM = pl.BlockSpec(memory_space=pltpu.HBM)


def shape(dims, dtype):
    return jax.ShapeDtypeStruct(dims, dtype)


def call(kernel, outs, *args, specs=None, out_specs=None, flops=10**8, scratch=(), **options):
    return pl.pallas_call(
        kernel,
        out_shape=outs,
        in_specs=specs or [VMEM] * len(args),
        out_specs=out_specs or jax.tree.map(lambda _: VMEM, outs),
        scratch_shapes=scratch,
        **options,
        compiler_params=pltpu.CompilerParams(vmem_limit_bytes=VMEM_LIMIT),
        cost_estimate=pl.CostEstimate(flops=flops, bytes_accessed=10**6, transcendentals=0),
    )(*args)


def shifted(x, axis, by):
    count = lax.axis_size(axis)
    return lax.ppermute(x, axis, [(i, (i + by) % count) for i in range(count)])


def across(x, axis, k):
    count = lax.axis_size(axis)
    return lax.ppermute(x, axis, [(i, i ^ k) for i in range(count)])


def paired_sums(messages, lines, strip, narrow, width, hid, node_terms):
    sends, keeps, outs = messages[:2], messages[2:4], messages[4:]
    order = range(lines - 1, 0, -1)
    block = shape((strip + TAIL, hid), bf16)
    far = across(sends[0], "sub", 1)
    out_terms = {k: across(outs[k], "mesh", k) for k in order}
    zero = across(sends[1], "sub", 1)
    line = {}
    line[3], line[2], line[1], tail = call(
        far_kernel, [block] * 3 + [shape((TAIL, hid), bf16)], far, keeps[0]
    )
    line_terms = {k: across(line[k], "mesh", k) for k in order}
    out_send, out_keep = call(
        line_kernel,
        [shape((narrow, hid), bf16)] * 2,
        *[out_terms[k] for k in order], outs[0], line[1],
    )
    node_part = node_terms(out_terms[3], out_terms[1], zero)
    own, tail = call(
        own_kernel,
        [shape((strip + narrow, hid), bf16), shape((TAIL, hid), f32)],
        *[line_terms[k] for k in order], keeps[1], zero, tail, out_keep, across(out_send, "sub", 1),
        node_part,
    )
    mine = {k: across(own, "mesh", k) for k in order}
    mine[0] = own
    theirs = {0: across(own, "sub", 1)}
    theirs[1] = across(theirs[0], "mesh", 1)
    early = (mine[0], mine[1], theirs[0], theirs[1])
    theirs[2] = across(mine[2], "sub", 1)
    theirs[3] = across(mine[3], "sub", 1)
    wholes = [shape((width, hid), f32), shape((width, hid), f32), shape((hid, width), f32)]
    scratch = [
        pltpu.VMEM((2, strip, hid), f32), pltpu.VMEM((2, strip, hid), f32), pltpu.VMEM((2, narrow, width), f32),
        pltpu.SemaphoreType.DMA((6,)),
    ]
    grads = call(
        functools.partial(place_kernel, lines, (0, 1)), wholes, *early,
        out_specs=[HBM] * 3, scratch=scratch, flops=10**8,
    )
    grads = call(
        functools.partial(place_kernel, lines, (3, 2)), wholes,
        mine[3], mine[2], theirs[3], theirs[2], *grads,
        specs=[VMEM] * 4 + [HBM] * 3, out_specs=[HBM] * 3, scratch=scratch,
        input_output_aliases={4: 0, 5: 1, 6: 2},
    )
    return (*grads, tail), node_part


def shards(
    node_state,
    send_rows,
    edge_src,
    edge_dst,
    block_count,
    w_src,
    w_dst,
    hidden_bias,
    w_out,
    norm_gain,
    cotangent,
):
    rows, width = node_state.shape
    hid = w_src.shape[1]
    halo = send_rows.shape[2]
    edges = edge_src.shape[0]
    peers = lax.axis_size("mesh") * lax.axis_size("sub")
    merged = lax.axis_size("sub") == 2
    total_rows = 2 * width + (width // hid) * hid
    chunk = -(-total_rows // (peers * 16)) * 16

    piece = [halo, halo, 2 * halo] if merged else [halo] * 4
    routes = [("mesh", 1), ("mesh", -1), ("sub", 1)] + ([] if merged else [("sub", -1)])
    n_halo = len(piece)

    def in_hbm(x):
        return pltpu.with_memory_space_constraint(x, pltpu.HBM)

    node, send, *outgoing = call(
        send_kernel,
        [shape((rows, width), bf16), shape(send_rows.shape, jnp.int32)]
        + [shape((n, width), bf16) for n in piece],
        in_hbm(node_state), in_hbm(send_rows),
        specs=[HBM, HBM],
        scratch=[pltpu.SemaphoreType.DMA((2,))],
    )
    arrived = [shifted(x, axis, by) for x, (axis, by) in zip(outgoing, routes)]

    fetched = [
        edge_src.reshape(1, edges), edge_dst.reshape(1, edges), block_count,
        hidden_bias.reshape(1, hid), w_src, w_dst, w_out, norm_gain.reshape(1, width), cotangent,
    ]
    pre, pick, collect, spread, scatter, w_src, w_dst, w_out, gain, cot = call(
        local_kernel,
        [
            shape((edges, hid), f32),
            shape((edges, 4 * halo), bf16),
            shape((rows, edges), bf16),
            shape((edges, rows), bf16),
            shape((rows + 4 * halo, edges), bf16),
        ]
        + [shape(x.shape, x.dtype) for x in fetched[4:]],
        node, *[in_hbm(x) for x in fetched],
        specs=[VMEM] + [HBM] * len(fetched),
        scratch=[
            pltpu.SMEM(block_count.shape, jnp.int32),
            pltpu.VMEM((1, edges), jnp.int32),
            pltpu.VMEM((1, edges), jnp.int32),
            pltpu.VMEM((1, hid), f32),
            pltpu.SemaphoreType.DMA((N_FETCHED,)),
        ],
    )

    factor, hidden, partial = call(
        forward_kernel,
        [shape((edges, hid), f32), shape((rows, hid), bf16), shape((rows, width), bf16)],
        pre, pick, collect, w_src, w_out, *arrived,
    )
    other = shifted(partial, "lat", 1)

    lines = lax.axis_size("mesh")
    paired = merged and lines == 4
    if paired:
        strip = width // lines
        narrow = hid // lines
        rows_of = (3 * strip + TAIL, strip + 2 * halo, 3 * strip + TAIL, strip)
        message_shapes = [shape((n, hid), bf16) for n in rows_of]
        message_shapes += [shape((narrow + k % 2 * (halo // 2), width), bf16) for k in range(lines)]
    else:
        message_shapes = [shape((peers, chunk + TAIL, hid), bf16)]
        message_shapes += [shape((n, hid), bf16) for n in piece]
    normed, local, target, *messages = call(
        functools.partial(backward_kernel, (peers, chunk, n_halo, paired)),
        [shape((rows, width), f32), shape((rows, hid), f32), shape((rows, hid), bf16)]
        + message_shapes,
        node, collect, spread, scatter, w_out, gain, cot, factor, hidden, partial, other, *arrived,
        scratch=[
            pltpu.VMEM((hid, width), bf16),
            pltpu.VMEM((2 * halo, hid), bf16),
            pltpu.VMEM((2, width, hid), bf16),
        ],
    )

    def node_terms(*returned):
        return call(
            paired_node_kernel if paired else node_kernel,
            shape((rows, width), bf16),
            send, local, target, w_src, w_dst, *returned,
        )

    if paired:
        (src_grad, dst_grad, out_grad, tail), node_part = paired_sums(
            messages, lines, strip, narrow, width, hid, node_terms
        )
    else:
        node_part = node_terms(
            *[shifted(x, axis, -by) for x, (axis, by) in zip(messages[1:], routes)]
        )
        exchanged = lax.all_to_all(messages[0], ("mesh", "sub"), 0, 0)
        reduced, bias_grad, gain_grad = call(
            functools.partial(sum_kernel, chunk),
            [shape((peers, chunk, hid), bf16), shape((1, hid), f32), shape((1, width), f32)],
            exchanged,
        )
        gathered = lax.all_to_all(reduced, ("mesh", "sub"), 0, 0)
        src_grad, dst_grad, out_grad = call(
            unpack_kernel,
            [shape((width, hid), f32), shape((width, hid), f32), shape((hid, width), f32)],
            gathered.reshape(peers * chunk, hid),
        )
    finished = [shape((rows, width), f32), shape((rows, width), bf16)]
    ends = [cot, node, gain, normed, node_part, shifted(node_part, "lat", 1)]
    if paired:
        node_grad, updated, bias_grad, gain_grad = call(
            finish_kernel, finished + [shape((1, hid), f32), shape((1, width), f32)], *ends, tail
        )
    else:
        node_grad, updated = call(finish_kernel, finished, *ends)
    return (
        updated, node_grad, src_grad, dst_grad, out_grad,
        bias_grad.reshape(hid), gain_grad.reshape(width),
    )


def solution(mesh):
    nodes = P(("parts", "mesh", "sub"), None)
    slots = P(("parts", "mesh", "sub"))
    in_specs = (
        nodes,
        P(("parts", "mesh", "sub"), None, None),
        slots,
        slots,
        slots,
        P(None, "lat"),
        P(None, "lat"),
        P("lat"),
        P("lat", None),
        P(),
        nodes,
    )
    out_specs = (
        nodes,
        nodes,
        P("parts", "lat"),
        P("parts", "lat"),
        P(("parts", "lat"), None),
        P(("parts", "lat")),
        P("parts"),
    )
    return jax.shard_map(shards, mesh=mesh, in_specs=in_specs, out_specs=out_specs, check_vma=False)
```

```python
import functools

import jax
import jax.numpy as jnp
from jax import lax
from jax.experimental import pallas as pl
from jax.experimental.pallas import tpu as pltpu
from jax.sharding import PartitionSpec as P

BLOCK = 128
EPSILON = 1e-05
TAIL = 16
N_FETCHED = 9
VMEM_LIMIT = 24 * 1024 * 1024

f32 = jnp.float32
bf16 = jnp.bfloat16

NN = (((1,), (0,)), ((), ()))
NT = (((1,), (1,)), ((), ()))
TN = (((0,), (0,)), ((), ()))


def dot(a, b, dims=NN):
    return lax.dot_general(a, b, dims, preferred_element_type=f32)


def iota(shape, dim):
    return lax.broadcasted_iota(jnp.int32, shape, dim)


def one_hot(condition):
    return jnp.where(condition, 1.0, 0.0).astype(bf16)


def split(x):
    high = x.astype(bf16)
    return high, (x - high.astype(f32)).astype(bf16)


def columns_of(row, lanes):
    return jnp.transpose(jnp.broadcast_to(row, (lanes, row.shape[1])))


def usable_row(count_ref, edges):
    lane = iota((1, BLOCK), 1)
    parts = [lane < count_ref[b] for b in range(edges // BLOCK)]
    return jnp.concatenate([jnp.where(p, 1, 0) for p in parts], axis=1)


def usable_columns(count_ref, edges, lanes):
    sub = iota((BLOCK, lanes), 0)
    return jnp.concatenate(
        [jnp.where(sub < count_ref[b], 1, 0) for b in range(edges // BLOCK)], axis=0
    )


def fetch(sems, *pairs):
    copies = [pltpu.make_async_copy(a, b, sems.at[i]) for i, (a, b) in enumerate(pairs)]
    for copy in copies:
        copy.start()
    return copies


def send_kernel(node_hbm, send_hbm, node_ref, send_ref, *rest):
    *out_refs, sems = rest
    for copy in fetch(sems, (node_hbm, node_ref), (send_hbm, send_ref)):
        copy.wait()
    node = node_ref[...]
    rows = node.shape[0]
    halo = send_ref.shape[2]
    pieces = []
    for d in range(4):
        pick = one_hot(iota((rows, halo), 0) == send_ref[0, d : d + 1, :])
        pieces.append(dot(pick, node, TN).astype(bf16))
    out_refs[0][...] = pieces[0]
    out_refs[1][...] = pieces[1]
    if len(out_refs) == 3:
        out_refs[2][0:halo, :] = pieces[2]
        out_refs[2][halo:, :] = pieces[3]
    else:
        out_refs[2][...] = pieces[2]
        out_refs[3][...] = pieces[3]


def local_kernel(*refs):
    node_ref, ins, refs = refs[0], refs[1 : 1 + N_FETCHED], refs[1 + N_FETCHED :]
    pre_ref, pick_ref, collect_ref, spread_ref, scatter_ref, *refs = refs
    w_src_ref, w_dst_ref, w_out_ref, gain_ref, cot_ref, count_ref, src_ref, dst_ref, bias_ref, sems = refs
    outs = (src_ref, dst_ref, count_ref, bias_ref, w_src_ref, w_dst_ref, w_out_ref, gain_ref, cot_ref)
    copies = fetch(sems, *zip(ins, outs))
    node = node_ref[...]
    rows = node.shape[0]
    edges = src_ref.shape[1]
    for copy in copies[:3]:
        copy.wait()
    scatter_ref[...] = one_hot(iota(scatter_ref.shape, 0) == src_ref[...])
    used = usable_row(count_ref, edges) > 0
    collect_ref[...] = one_hot((iota((rows, edges), 0) == dst_ref[...]) & used)
    source = columns_of(src_ref[...], 128)
    target = columns_of(dst_ref[...], 128)
    lane = iota(source.shape, 1)
    used = usable_columns(count_ref, edges, 128) > 0
    near = one_hot(source == lane)
    pick_ref[...] = one_hot(source == lane + rows)
    spread_ref[...] = one_hot((target == lane) & used)
    both = jnp.concatenate([dot(near, node), dot(one_hot(target == lane), node)], axis=1).astype(bf16)
    for copy in copies[3:]:
        copy.wait()
    weights = jnp.concatenate([w_src_ref[...], w_dst_ref[...]], axis=0)
    pre_ref[...] = dot(both, weights) + bias_ref[...]


def twice(x):
    return jnp.concatenate([x, x], axis=1)


def stacked(x):
    return jnp.concatenate(split(x), axis=0)


def forward_kernel(pre_ref, pick_ref, collect_ref, w_src_ref, w_out_ref, *rest):
    *halo_refs, factor_ref, hidden_ref, partial_ref = rest
    halo = jnp.concatenate([r[...] for r in halo_refs], axis=0)
    far = stacked(dot(halo, w_src_ref[...]))
    pre = pre_ref[...] + dot(twice(pick_ref[...]), far)
    sig = 0.5 + 0.5 * jnp.tanh(0.5 * pre)
    factor_ref[...] = sig * (1.0 + pre * (1.0 - sig))
    hidden = dot(collect_ref[...], (pre * sig).astype(bf16))
    high, low = split(hidden)
    hidden_ref[...] = high
    w_out = w_out_ref[...]
    partial_ref[...] = (dot(high, w_out) + dot(low, w_out)).astype(bf16)


def backward_kernel(
    geometry,
    node_ref, collect_ref, spread_ref, scatter_ref, w_out_ref, gain_ref, cot_ref,
    factor_ref, hidden_ref, own_ref, other_ref,
    *rest,
):
    peers, chunk, n_halo, paired = geometry
    *rest, out_scratch, back_scratch, pair_scratch = rest
    halo_refs = rest[:n_halo]
    normed_ref, local_ref, target_ref, *message_refs = rest[n_halo:]
    node = node_ref[...]
    rows, width = node.shape
    aggregate = own_ref[...].astype(f32) + other_ref[...].astype(f32)
    center = aggregate - jnp.mean(aggregate, axis=1, keepdims=True)
    variance = jnp.mean(center * center, axis=1, keepdims=True)
    inverse = lax.rsqrt(variance + EPSILON)
    normed = center * inverse
    gain = gain_ref[...]
    upstream = cot_ref[...].astype(f32)
    scaled = upstream * gain
    agg_grad = inverse * (
        scaled
        - jnp.mean(scaled, axis=1, keepdims=True)
        - normed * jnp.mean(scaled * normed, axis=1, keepdims=True)
    )
    agg_grad = agg_grad.astype(bf16)
    normed_ref[...] = normed
    gain_part = jnp.sum(upstream * normed, axis=0, keepdims=True)

    act_grad = dot(twice(spread_ref[...]), stacked(dot(agg_grad, w_out_ref[...], NT)))
    pre_grad = (act_grad * factor_ref[...]).astype(bf16)

    table = jnp.concatenate([node] + [r[...] for r in halo_refs], axis=0)
    by_source = dot(scatter_ref[...], pre_grad)
    by_target = dot(collect_ref[...], pre_grad)
    local_ref[...] = by_source[:rows]
    by_target_low = by_target.astype(bf16)
    by_source_low = by_source.astype(bf16)
    target_ref[...] = by_target_low

    hid = by_source.shape[1]
    bias_part = jnp.sum(by_target, axis=0, keepdims=True)
    src_part = dot(table, by_source_low, TN).astype(bf16)
    dst_part = dot(node, by_target_low, TN).astype(bf16)
    out_part = dot(hidden_ref[...], agg_grad, TN).astype(bf16)
    vectors = [bias_part] + [gain_part[:, at : at + hid] for at in range(0, width, hid)]
    tail = tail_of(vectors)
    back = by_source_low[rows:]

    if paired:
        sends, keeps, out_refs = message_refs[:2], message_refs[2:4], message_refs[4:]
        sub = lax.axis_index("sub")
        mesh = lax.axis_index("mesh")
        lines = len(out_refs)
        halo = back.shape[0] // 4
        first = sub == 0
        pair_scratch[0] = jnp.where(first, dst_part, src_part)
        pair_scratch[1] = jnp.where(first, src_part, dst_part)
        strip = width // lines
        for slot, (far_ref, zero_ref) in enumerate((sends, keeps)):
            places = [(far_ref, at, k) for at, k in enumerate((3, 2, 1))] + [(zero_ref, 0, 0)]
            for ref, at, k in places:
                start = pl.multiple_of((mesh ^ k) * strip, strip)
                ref[at * strip : (at + 1) * strip, :] = pair_scratch[slot, pl.ds(start, strip), :]
            far_ref[3 * strip :, :] = tail
        sends[1][strip:, :] = back[2 * halo :]
        back_scratch[...] = back[: 2 * halo]
        out_scratch[...] = out_part
        strip = hid // len(out_refs)
        for k, ref in enumerate(out_refs):
            start = pl.multiple_of((mesh ^ k) * strip, strip)
            ref[0:strip, :] = out_scratch[pl.ds(start, strip), :]
            if k % 2 == 1:
                slot = (mesh + (k // 2) + 1) % 2
                start = pl.multiple_of(slot * halo, halo)
                rows_back = back_scratch[pl.ds(start, halo), :]
                ref[strip:, 0:hid] = rows_back[: halo // 2]
                ref[strip:, hid:] = rows_back[halo // 2 :]
        return

    message_ref, *back_refs = message_refs
    at = 0
    for ref in back_refs:
        ref[...] = back[at : at + ref.shape[0]]
        at += ref.shape[0]
    blocks = [src_part, dst_part]
    for at in range(0, width, hid):
        blocks.append(out_part[:, at : at + hid])
    done = 0
    for block in blocks:
        at = 0
        while at < block.shape[0]:
            peer, offset = divmod(done, chunk)
            take = min(chunk - offset, block.shape[0] - at)
            message_ref[peer, offset : offset + take, :] = block[at : at + take]
            at += take
            done += take
    while done < peers * chunk:
        peer, offset = divmod(done, chunk)
        take = chunk - offset
        message_ref[peer, offset : offset + take, :] = jnp.zeros((take, hid), bf16)
        done += take
    for peer in range(peers):
        message_ref[peer, chunk:, :] = tail


def tail_of(vectors):
    tail = []
    for v in vectors:
        high = v.astype(bf16).astype(f32)
        tail += [high, v - high]
    tail.append(jnp.zeros((TAIL - len(tail), vectors[0].shape[1]), f32))
    return jnp.concatenate(tail, axis=0).astype(bf16)


def tree(terms):
    while len(terms) > 1:
        terms = [terms[i] + terms[i + 1] for i in range(0, len(terms), 2)]
    return terms[0]


def far_kernel(arrived_ref, keep_ref, *refs):
    *line_refs, tail_ref = refs
    total = keep_ref[...].astype(f32) + arrived_ref[...].astype(f32)
    strip = line_refs[0].shape[0] - TAIL
    tail = total[len(line_refs) * strip :]
    tail = tail_of([tail[at : at + 1] + tail[at + 1 : at + 2] for at in range(0, 6, 2)])
    for k, ref in enumerate(line_refs):
        ref[0:strip, :] = total[k * strip : (k + 1) * strip].astype(bf16)
        ref[strip:, :] = tail
    tail_ref[...] = tail


def line_kernel(*refs):
    *terms, _, send_ref, keep_ref = refs
    rows, hid = send_ref.shape
    total = tree([r[0:rows, :].astype(f32) for r in terms])
    first = lax.axis_index("sub") == 0
    left, right = total[:, :hid], total[:, hid:]
    send_ref[...] = jnp.where(first, right, left).astype(bf16)
    keep_ref[...] = jnp.where(first, left, right).astype(bf16)


def own_kernel(*refs):
    *terms, keep_ref, arrived_ref, vectors_ref, out_keep_ref, out_arrived_ref, _, own_ref, tail_ref = refs
    strip = keep_ref.shape[0]
    zero = (keep_ref[...].astype(f32) + arrived_ref[0:strip, :].astype(f32)).astype(bf16)
    total = tree([r[0:strip, :].astype(f32) for r in terms] + [zero.astype(f32)])
    own_ref[0:strip, :] = total.astype(bf16)
    own_ref[strip:, :] = (
        out_keep_ref[...].astype(f32) + out_arrived_ref[...].astype(f32)
    ).astype(bf16)
    tail_ref[...] = tree([r[strip:, :].astype(f32) for r in terms] + [vectors_ref[...].astype(f32)])


def write_vectors(tail, bias_ref, gain_ref):
    bias_ref[...] = tail[0:1] + tail[1:2]
    hid = tail.shape[1]
    for k in range(gain_ref.shape[1] // hid):
        gain_ref[:, k * hid : (k + 1) * hid] = tail[2 + 2 * k : 3 + 2 * k] + tail[3 + 2 * k : 4 + 2 * k]


def relay_kernel(*refs):
    *_, strip_ref, out_ref = refs
    out_ref[...] = strip_ref[...]


def place_kernel(lines, which, a_ref, b_ref, c_ref, d_ref, *refs):
    src_hbm, dst_hbm, out_hbm, src_ref, dst_ref, out_ref, sems = refs[-7:]
    first = lax.axis_index("sub") == 0
    mesh = lax.axis_index("mesh")
    strip, hid = src_ref.shape[1:]
    narrow = out_ref.shape[1]
    copies = []

    def put(ref, hbm, at, rows):
        start = pl.multiple_of((mesh ^ which[at]) * rows, rows)
        copies.append(pltpu.make_async_copy(ref.at[at], hbm.at[pl.ds(start, rows)], sems.at[len(copies)]))
        copies[-1].start()

    for at, (mine_ref, theirs_ref) in enumerate(((a_ref, c_ref), (b_ref, d_ref))):
        mine, theirs = mine_ref[...], theirs_ref[...]
        low = jnp.where(first, mine, theirs).astype(f32)
        high = jnp.where(first, theirs, mine).astype(f32)
        src_ref[at] = low[:strip]
        put(src_ref, src_hbm, at, strip)
        dst_ref[at] = high[:strip]
        put(dst_ref, dst_hbm, at, strip)
        out_ref[at, :, 0:hid] = low[strip:]
        out_ref[at, :, hid:] = high[strip:]
        put(out_ref, out_hbm, at, narrow)
    for copy in copies:
        copy.wait()


def sum_kernel(chunk, arrived_ref, out_ref, bias_ref, gain_ref):
    peers = arrived_ref.shape[0]
    total = arrived_ref[0].astype(f32)
    for peer in range(1, peers):
        total += arrived_ref[peer].astype(f32)
    low = total[:chunk].astype(bf16)
    for peer in range(peers):
        out_ref[peer] = low
    tail = total[chunk:]
    write_vectors(tail, bias_ref, gain_ref)


def unpack_kernel(arrived_ref, src_ref, dst_ref, out_ref):
    hid = src_ref.shape[1]
    rows = src_ref.shape[0]
    src_ref[...] = arrived_ref[0:rows, :].astype(f32)
    dst_ref[...] = arrived_ref[rows : 2 * rows, :].astype(f32)
    at = 2 * rows
    for k in range(out_ref.shape[1] // hid):
        out_ref[:, k * hid : (k + 1) * hid] = arrived_ref[at : at + out_ref.shape[0], :].astype(f32)
        at += out_ref.shape[0]


def node_part(send_ref, local_ref, target_ref, w_src_ref, w_dst_ref, returned, out_ref):
    rows = local_ref.shape[0]
    halo = send_ref.shape[2]
    picks = [one_hot(iota((rows, halo), 0) == send_ref[0, d : d + 1, :]) for d in range(4)]
    total = local_ref[...] + dot(jnp.concatenate(picks, axis=1), jnp.concatenate(returned, axis=0))
    out_ref[...] = (
        dot(total.astype(bf16), w_src_ref[...], NT) + dot(target_ref[...], w_dst_ref[...], NT)
    ).astype(bf16)


def node_kernel(send_ref, local_ref, target_ref, w_src_ref, w_dst_ref, *rest):
    *back_refs, out_ref = rest
    returned = [r[...] for r in back_refs]
    node_part(send_ref, local_ref, target_ref, w_src_ref, w_dst_ref, returned, out_ref)


def paired_node_kernel(
    send_ref, local_ref, target_ref, w_src_ref, w_dst_ref, three_ref, one_ref, pair_ref, out_ref
):
    even = lax.axis_index("mesh") % 2 == 0
    halo = send_ref.shape[2]
    hid = local_ref.shape[1]
    at = one_ref.shape[0] - halo // 2
    one, three = [
        jnp.concatenate([r[at:, :hid], r[at:, hid:]], axis=0) for r in (one_ref, three_ref)
    ]
    returned = [
        jnp.where(even, one, three), jnp.where(even, three, one), pair_ref[pair_ref.shape[0] - 2 * halo :, :]
    ]
    node_part(send_ref, local_ref, target_ref, w_src_ref, w_dst_ref, returned, out_ref)


def finish_kernel(cot_ref, node_ref, gain_ref, normed_ref, own_ref, other_ref, *rest):
    if len(rest) == 5:
        tail_ref, *rest, bias_out_ref, gain_out_ref = rest
        write_vectors(tail_ref[...], bias_out_ref, gain_out_ref)
    grad_ref, updated_ref = rest
    grad_ref[...] = cot_ref[...].astype(f32) + (
        own_ref[...].astype(f32) + other_ref[...].astype(f32)
    )
    updated_ref[...] = (node_ref[...].astype(f32) + gain_ref[...] * normed_ref[...]).astype(bf16)


VMEM = pl.BlockSpec(memory_space=pltpu.VMEM)
SMEM = pl.BlockSpec(memory_space=pltpu.SMEM)
HBM = pl.BlockSpec(memory_space=pltpu.HBM)


def shape(dims, dtype):
    return jax.ShapeDtypeStruct(dims, dtype)


def call(kernel, outs, *args, specs=None, out_specs=None, flops=10**8, scratch=(), **options):
    return pl.pallas_call(
        kernel,
        out_shape=outs,
        in_specs=specs or [VMEM] * len(args),
        out_specs=out_specs or jax.tree.map(lambda _: VMEM, outs),
        scratch_shapes=scratch,
        **options,
        compiler_params=pltpu.CompilerParams(vmem_limit_bytes=VMEM_LIMIT),
        cost_estimate=pl.CostEstimate(flops=flops, bytes_accessed=10**6, transcendentals=0),
    )(*args)


def shifted(x, axis, by):
    count = lax.axis_size(axis)
    return lax.ppermute(x, axis, [(i, (i + by) % count) for i in range(count)])


def across(x, axis, k):
    count = lax.axis_size(axis)
    return lax.ppermute(x, axis, [(i, i ^ k) for i in range(count)])


def diagonal(x):
    lines, pairs = lax.axis_size("mesh"), lax.axis_size("sub")
    moves = [(m * pairs + p, (m ^ 1) * pairs + (p ^ 1)) for m in range(lines) for p in range(pairs)]
    return lax.ppermute(x, ("mesh", "sub"), moves)


def paired_sums(messages, lines, strip, narrow, width, hid, node_terms):
    sends, keeps, outs = messages[:2], messages[2:4], messages[4:]
    order = range(lines - 1, 0, -1)
    block = shape((strip + TAIL, hid), bf16)
    far = across(sends[0], "sub", 1)
    out_terms = {k: across(outs[k], "mesh", k) for k in order}
    zero = across(sends[1], "sub", 1)
    line = {}
    line[3], line[2], line[1], tail = call(
        far_kernel, [block] * 3 + [shape((TAIL, hid), bf16)], far, keeps[0]
    )
    line_terms = {k: across(line[k], "mesh", k) for k in order}
    out_send, out_keep = call(
        line_kernel,
        [shape((narrow, hid), bf16)] * 2,
        *[out_terms[k] for k in order], outs[0], line[1],
    )
    node_part = node_terms(out_terms[3], out_terms[1], zero)
    own, tail = call(
        own_kernel,
        [shape((strip + narrow, hid), bf16), shape((TAIL, hid), f32)],
        *[line_terms[k] for k in order], keeps[1], zero, tail, out_keep, across(out_send, "sub", 1),
        node_part,
    )
    mine = {k: across(own, "mesh", k) for k in order}
    mine[0] = own
    theirs = {0: across(own, "sub", 1), 1: diagonal(own)}
    early = (mine[0], mine[1], theirs[0], theirs[1])
    theirs[2] = across(mine[2], "sub", 1)
    theirs[3] = across(mine[3], "sub", 1)
    wholes = [shape((width, hid), f32), shape((width, hid), f32), shape((hid, width), f32)]
    scratch = [
        pltpu.VMEM((2, strip, hid), f32), pltpu.VMEM((2, strip, hid), f32), pltpu.VMEM((2, narrow, width), f32),
        pltpu.SemaphoreType.DMA((6,)),
    ]
    grads = call(
        functools.partial(place_kernel, lines, (0, 1)), wholes, *early,
        out_specs=[HBM] * 3, scratch=scratch, flops=10**8,
    )
    grads = call(
        functools.partial(place_kernel, lines, (2, 3)), wholes,
        mine[2], mine[3], theirs[2], theirs[3], *grads,
        specs=[VMEM] * 4 + [HBM] * 3, out_specs=[HBM] * 3, scratch=scratch,
        input_output_aliases={4: 0, 5: 1, 6: 2},
    )
    return (*grads, tail), node_part


def shards(
    node_state,
    send_rows,
    edge_src,
    edge_dst,
    block_count,
    w_src,
    w_dst,
    hidden_bias,
    w_out,
    norm_gain,
    cotangent,
):
    rows, width = node_state.shape
    hid = w_src.shape[1]
    halo = send_rows.shape[2]
    edges = edge_src.shape[0]
    peers = lax.axis_size("mesh") * lax.axis_size("sub")
    merged = lax.axis_size("sub") == 2
    total_rows = 2 * width + (width // hid) * hid
    chunk = -(-total_rows // (peers * 16)) * 16

    piece = [halo, halo, 2 * halo] if merged else [halo] * 4
    routes = [("mesh", 1), ("mesh", -1), ("sub", 1)] + ([] if merged else [("sub", -1)])
    n_halo = len(piece)

    def in_hbm(x):
        return pltpu.with_memory_space_constraint(x, pltpu.HBM)

    node, send, *outgoing = call(
        send_kernel,
        [shape((rows, width), bf16), shape(send_rows.shape, jnp.int32)]
        + [shape((n, width), bf16) for n in piece],
        in_hbm(node_state), in_hbm(send_rows),
        specs=[HBM, HBM],
        scratch=[pltpu.SemaphoreType.DMA((2,))],
    )
    arrived = [shifted(x, axis, by) for x, (axis, by) in zip(outgoing, routes)]

    fetched = [
        edge_src.reshape(1, edges), edge_dst.reshape(1, edges), block_count,
        hidden_bias.reshape(1, hid), w_src, w_dst, w_out, norm_gain.reshape(1, width), cotangent,
    ]
    pre, pick, collect, spread, scatter, w_src, w_dst, w_out, gain, cot = call(
        local_kernel,
        [
            shape((edges, hid), f32),
            shape((edges, 4 * halo), bf16),
            shape((rows, edges), bf16),
            shape((edges, rows), bf16),
            shape((rows + 4 * halo, edges), bf16),
        ]
        + [shape(x.shape, x.dtype) for x in fetched[4:]],
        node, *[in_hbm(x) for x in fetched],
        specs=[VMEM] + [HBM] * len(fetched),
        scratch=[
            pltpu.SMEM(block_count.shape, jnp.int32),
            pltpu.VMEM((1, edges), jnp.int32),
            pltpu.VMEM((1, edges), jnp.int32),
            pltpu.VMEM((1, hid), f32),
            pltpu.SemaphoreType.DMA((N_FETCHED,)),
        ],
    )

    factor, hidden, partial = call(
        forward_kernel,
        [shape((edges, hid), f32), shape((rows, hid), bf16), shape((rows, width), bf16)],
        pre, pick, collect, w_src, w_out, *arrived,
    )
    other = shifted(partial, "lat", 1)

    lines = lax.axis_size("mesh")
    paired = merged and lines == 4
    if paired:
        strip = width // lines
        narrow = hid // lines
        rows_of = (3 * strip + TAIL, strip + 2 * halo, 3 * strip + TAIL, strip)
        message_shapes = [shape((n, hid), bf16) for n in rows_of]
        message_shapes += [shape((narrow + k % 2 * (halo // 2), width), bf16) for k in range(lines)]
    else:
        message_shapes = [shape((peers, chunk + TAIL, hid), bf16)]
        message_shapes += [shape((n, hid), bf16) for n in piece]
    normed, local, target, *messages = call(
        functools.partial(backward_kernel, (peers, chunk, n_halo, paired)),
        [shape((rows, width), f32), shape((rows, hid), f32), shape((rows, hid), bf16)]
        + message_shapes,
        node, collect, spread, scatter, w_out, gain, cot, factor, hidden, partial, other, *arrived,
        scratch=[
            pltpu.VMEM((hid, width), bf16),
            pltpu.VMEM((2 * halo, hid), bf16),
            pltpu.VMEM((2, width, hid), bf16),
        ],
    )

    def node_terms(*returned):
        return call(
            paired_node_kernel if paired else node_kernel,
            shape((rows, width), bf16),
            send, local, target, w_src, w_dst, *returned,
        )

    if paired:
        (src_grad, dst_grad, out_grad, tail), node_part = paired_sums(
            messages, lines, strip, narrow, width, hid, node_terms
        )
    else:
        node_part = node_terms(
            *[shifted(x, axis, -by) for x, (axis, by) in zip(messages[1:], routes)]
        )
        exchanged = lax.all_to_all(messages[0], ("mesh", "sub"), 0, 0)
        reduced, bias_grad, gain_grad = call(
            functools.partial(sum_kernel, chunk),
            [shape((peers, chunk, hid), bf16), shape((1, hid), f32), shape((1, width), f32)],
            exchanged,
        )
        gathered = lax.all_to_all(reduced, ("mesh", "sub"), 0, 0)
        src_grad, dst_grad, out_grad = call(
            unpack_kernel,
            [shape((width, hid), f32), shape((width, hid), f32), shape((hid, width), f32)],
            gathered.reshape(peers * chunk, hid),
        )
    finished = [shape((rows, width), f32), shape((rows, width), bf16)]
    ends = [cot, node, gain, normed, node_part, shifted(node_part, "lat", 1)]
    if paired:
        node_grad, updated, bias_grad, gain_grad = call(
            finish_kernel, finished + [shape((1, hid), f32), shape((1, width), f32)], *ends, tail
        )
    else:
        node_grad, updated = call(finish_kernel, finished, *ends)
    return (
        updated, node_grad, src_grad, dst_grad, out_grad,
        bias_grad.reshape(hid), gain_grad.reshape(width),
    )


def solution(mesh):
    nodes = P(("parts", "mesh", "sub"), None)
    slots = P(("parts", "mesh", "sub"))
    in_specs = (
        nodes,
        P(("parts", "mesh", "sub"), None, None),
        slots,
        slots,
        slots,
        P(None, "lat"),
        P(None, "lat"),
        P("lat"),
        P("lat", None),
        P(),
        nodes,
    )
    out_specs = (
        nodes,
        nodes,
        P("parts", "lat"),
        P("parts", "lat"),
        P(("parts", "lat"), None),
        P(("parts", "lat")),
        P("parts"),
    )
    return jax.shard_map(shards, mesh=mesh, in_specs=in_specs, out_specs=out_specs, check_vma=False)
```

```python
import functools

import jax
import jax.numpy as jnp
from jax import lax
from jax.experimental import pallas as pl
from jax.experimental.pallas import tpu as pltpu
from jax.sharding import PartitionSpec as P

BLOCK = 128
EPSILON = 1e-05
TAIL = 16
N_FETCHED = 5
VMEM_LIMIT = 24 * 1024 * 1024

f32 = jnp.float32
bf16 = jnp.bfloat16

NN = (((1,), (0,)), ((), ()))
NT = (((1,), (1,)), ((), ()))
TN = (((0,), (0,)), ((), ()))


def dot(a, b, dims=NN):
    return lax.dot_general(a, b, dims, preferred_element_type=f32)


def iota(shape, dim):
    return lax.broadcasted_iota(jnp.int32, shape, dim)


def one_hot(condition):
    return jnp.where(condition, 1.0, 0.0).astype(bf16)


def split(x):
    high = x.astype(bf16)
    return high, (x - high.astype(f32)).astype(bf16)


def columns_of(row, lanes):
    return jnp.transpose(jnp.broadcast_to(row, (lanes, row.shape[1])))


def usable_row(count_ref, edges):
    lane = iota((1, BLOCK), 1)
    parts = [lane < count_ref[b] for b in range(edges // BLOCK)]
    return jnp.concatenate([jnp.where(p, 1, 0) for p in parts], axis=1)


def usable_columns(count_ref, edges, lanes):
    sub = iota((BLOCK, lanes), 0)
    return jnp.concatenate(
        [jnp.where(sub < count_ref[b], 1, 0) for b in range(edges // BLOCK)], axis=0
    )


def fetch(sems, *pairs):
    copies = [pltpu.make_async_copy(a, b, sems.at[i]) for i, (a, b) in enumerate(pairs)]
    for copy in copies:
        copy.start()
    return copies


def send_kernel(
    node_hbm, send_hbm, w_src_hbm, w_dst_hbm, w_out_hbm, bias_hbm,
    node_ref, send_ref, packed_ref, *rest,
):
    *out_refs, bias_ref, sems = rest
    hid = packed_ref.shape[1]
    width = w_src_hbm.shape[0]
    pairs = [(node_hbm, node_ref), (send_hbm, send_ref), (bias_hbm, bias_ref)]
    pairs += [(w_src_hbm, packed_ref.at[pl.ds(0, width)]), (w_dst_hbm, packed_ref.at[pl.ds(width, width)])]
    for k in range(width // hid):
        target = packed_ref.at[pl.ds(2 * width + k * hid, hid)]
        pairs.append((w_out_hbm.at[:, pl.ds(k * hid, hid)], target))
    copies = fetch(sems, *pairs)
    copies[0].wait()
    copies[1].wait()
    node = node_ref[...]
    rows = node.shape[0]
    halo = send_ref.shape[2]
    pieces = []
    for d in range(4):
        pick = one_hot(iota((rows, halo), 0) == send_ref[0, d : d + 1, :])
        pieces.append(dot(pick, node, TN).astype(bf16))
    out_refs[0][...] = pieces[0]
    out_refs[1][...] = pieces[1]
    if len(out_refs) == 3:
        out_refs[2][0:halo, :] = pieces[2]
        out_refs[2][halo:, :] = pieces[3]
    else:
        out_refs[2][...] = pieces[2]
        out_refs[3][...] = pieces[3]
    copies[2].wait()
    bias = bias_ref[...]
    parts = []
    for _ in range(3):
        parts.append(bias.astype(bf16).astype(f32))
        bias = bias - parts[-1]
    parts.append(jnp.zeros((TAIL - 3, hid), f32))
    packed_ref[packed_ref.shape[0] - TAIL :, :] = jnp.concatenate(parts, axis=0).astype(bf16)
    for copy in copies[3:]:
        copy.wait()


def unpacked(ref, width):
    hid = ref.shape[1]
    w_out = [ref[at : at + hid, :] for at in range(2 * width, 3 * width, hid)]
    tail = ref[ref.shape[0] - TAIL :, :].astype(f32)
    bias = tail[0:1] + tail[1:2] + tail[2:3]
    return ref[0:width, :], ref[width : 2 * width, :], jnp.concatenate(w_out, axis=1), bias


def local_kernel(node_ref, packed_ref, other_ref, *refs):
    ins, refs = refs[:N_FETCHED], refs[N_FETCHED:]
    pre_ref, pick_ref, collect_ref, spread_ref, scatter_ref, *refs = refs
    gain_ref, cot_ref, count_ref, src_ref, dst_ref, sems = refs
    copies = fetch(sems, *zip(ins, (src_ref, dst_ref, count_ref, gain_ref, cot_ref)))
    node = node_ref[...]
    rows, width = node.shape
    w_src, w_dst, _, bias = unpacked(packed_ref, width)
    w_src_other, w_dst_other, _, bias_other = unpacked(other_ref, width)
    projected = dot(node, jnp.concatenate([w_src, w_src_other, w_dst, w_dst_other], axis=1))
    both = projected.shape[1] // 2
    projected = jnp.concatenate([projected[:, :both], projected[:, both:]], axis=0)
    high, low = split(projected)
    for copy in copies:
        copy.wait()
    edges = src_ref.shape[1]
    scatter_ref[...] = one_hot(iota(scatter_ref.shape, 0) == src_ref[...])
    used = usable_row(count_ref, edges) > 0
    collect_ref[...] = one_hot((iota((rows, edges), 0) == dst_ref[...]) & used)
    source = columns_of(src_ref[...], 128)
    target = columns_of(dst_ref[...], 128)
    lane = iota(source.shape, 1)
    used = usable_columns(count_ref, edges, 128) > 0
    near = one_hot(source == lane)
    pick_ref[...] = one_hot(source == lane + rows)
    spread_ref[...] = one_hot((target == lane) & used)
    ends = jnp.concatenate([near, one_hot(target == lane)], axis=1)
    pre_ref[...] = dot(ends, high) + dot(ends, low) + jnp.concatenate([bias, bias_other], axis=1)


def twice(x):
    return jnp.concatenate([x, x], axis=1)


def stacked(x):
    return jnp.concatenate(split(x), axis=0)


def edge_kernel(
    geometry,
    node_ref, pre_ref, pick_ref, collect_ref, spread_ref, scatter_ref, packed_ref, other_ref, gain_ref, cot_ref,
    *rest,
):
    peers, chunk, n_halo, paired = geometry
    *rest, out_scratch, back_scratch, pair_scratch = rest
    halo_refs = rest[:n_halo]
    normed_ref, local_ref, target_ref, *message_refs = rest[n_halo:]
    node = node_ref[...]
    rows, width = node.shape
    hid = packed_ref.shape[1]
    halo_rows = jnp.concatenate([r[...] for r in halo_refs], axis=0)
    w_src, _, w_out, _ = unpacked(packed_ref, width)
    w_src_other, _, w_out_other, _ = unpacked(other_ref, width)

    far = stacked(dot(halo_rows, jnp.concatenate([w_src, w_src_other], axis=1)))
    pre = pre_ref[...] + dot(twice(pick_ref[...]), far)
    sig = 0.5 + 0.5 * jnp.tanh(0.5 * pre)
    hidden = dot(collect_ref[...], (pre * sig).astype(bf16))
    pre, sig = pre[:, :hid], sig[:, :hid]
    factor = sig * (1.0 + pre * (1.0 - sig))
    parts = []
    for at, w in ((0, w_out), (hid, w_out_other)):
        high, low = split(hidden[:, at : at + hid])
        parts.append(dot(high, w) + dot(low, w))
    hidden_low = hidden[:, :hid].astype(bf16)
    aggregate = parts[0] + parts[1]

    center = aggregate - jnp.mean(aggregate, axis=1, keepdims=True)
    variance = jnp.mean(center * center, axis=1, keepdims=True)
    inverse = lax.rsqrt(variance + EPSILON)
    normed = center * inverse
    gain = gain_ref[...]
    upstream = cot_ref[...].astype(f32)
    scaled = upstream * gain
    agg_grad = inverse * (
        scaled
        - jnp.mean(scaled, axis=1, keepdims=True)
        - normed * jnp.mean(scaled * normed, axis=1, keepdims=True)
    )
    agg_grad = agg_grad.astype(bf16)
    normed_ref[...] = normed
    gain_part = jnp.sum(upstream * normed, axis=0, keepdims=True)

    act_grad = dot(twice(spread_ref[...]), stacked(dot(agg_grad, w_out, NT)))
    pre_grad = (act_grad * factor).astype(bf16)

    table = jnp.concatenate([node, halo_rows], axis=0)
    by_source = dot(scatter_ref[...], pre_grad)
    by_target = dot(collect_ref[...], pre_grad)
    local_ref[...] = by_source[:rows]
    by_target_low = by_target.astype(bf16)
    by_source_low = by_source.astype(bf16)
    target_ref[...] = by_target_low

    bias_part = jnp.sum(by_target, axis=0, keepdims=True)
    src_part = dot(table, by_source_low, TN).astype(bf16)
    dst_part = dot(node, by_target_low, TN).astype(bf16)
    out_part = dot(hidden_low, agg_grad, TN).astype(bf16)
    vectors = [bias_part] + [gain_part[:, at : at + hid] for at in range(0, width, hid)]
    tail = tail_of(vectors)
    back = by_source_low[rows:]

    if paired:
        sends, keeps, out_refs = message_refs[:2], message_refs[2:4], message_refs[4:]
        sub = lax.axis_index("sub")
        mesh = lax.axis_index("mesh")
        lines = len(out_refs)
        halo = back.shape[0] // 4
        first = sub == 0
        pair_scratch[0] = jnp.where(first, dst_part, src_part)
        pair_scratch[1] = jnp.where(first, src_part, dst_part)
        strip = width // lines
        for slot, (far_ref, zero_ref) in enumerate((sends, keeps)):
            places = [(far_ref, at, k) for at, k in enumerate((3, 2, 1))] + [(zero_ref, 0, 0)]
            for ref, at, k in places:
                start = pl.multiple_of((mesh ^ k) * strip, strip)
                ref[at * strip : (at + 1) * strip, :] = pair_scratch[slot, pl.ds(start, strip), :]
            far_ref[3 * strip :, :] = tail
        sends[1][strip:, :] = back[2 * halo :]
        back_scratch[...] = back[: 2 * halo]
        out_scratch[...] = out_part
        strip = hid // len(out_refs)
        for k, ref in enumerate(out_refs):
            start = pl.multiple_of((mesh ^ k) * strip, strip)
            ref[0:strip, :] = out_scratch[pl.ds(start, strip), :]
            if k % 2 == 1:
                slot = (mesh + (k // 2) + 1) % 2
                start = pl.multiple_of(slot * halo, halo)
                rows_back = back_scratch[pl.ds(start, halo), :]
                ref[strip:, 0:hid] = rows_back[: halo // 2]
                ref[strip:, hid:] = rows_back[halo // 2 :]
        return

    message_ref, *back_refs = message_refs
    at = 0
    for ref in back_refs:
        ref[...] = back[at : at + ref.shape[0]]
        at += ref.shape[0]
    blocks = [src_part, dst_part]
    for at in range(0, width, hid):
        blocks.append(out_part[:, at : at + hid])
    done = 0
    for block in blocks:
        at = 0
        while at < block.shape[0]:
            peer, offset = divmod(done, chunk)
            take = min(chunk - offset, block.shape[0] - at)
            message_ref[peer, offset : offset + take, :] = block[at : at + take]
            at += take
            done += take
    while done < peers * chunk:
        peer, offset = divmod(done, chunk)
        take = chunk - offset
        message_ref[peer, offset : offset + take, :] = jnp.zeros((take, hid), bf16)
        done += take
    for peer in range(peers):
        message_ref[peer, chunk:, :] = tail


def tail_of(vectors):
    tail = []
    for v in vectors:
        high = v.astype(bf16).astype(f32)
        tail += [high, v - high]
    tail.append(jnp.zeros((TAIL - len(tail), vectors[0].shape[1]), f32))
    return jnp.concatenate(tail, axis=0).astype(bf16)


def tree(terms):
    while len(terms) > 1:
        terms = [terms[i] + terms[i + 1] for i in range(0, len(terms), 2)]
    return terms[0]


def far_kernel(arrived_ref, keep_ref, *refs):
    *line_refs, tail_ref = refs
    total = keep_ref[...].astype(f32) + arrived_ref[...].astype(f32)
    strip = line_refs[0].shape[0] - TAIL
    tail = total[len(line_refs) * strip :]
    tail = tail_of([tail[at : at + 1] + tail[at + 1 : at + 2] for at in range(0, 6, 2)])
    for k, ref in enumerate(line_refs):
        ref[0:strip, :] = total[k * strip : (k + 1) * strip].astype(bf16)
        ref[strip:, :] = tail
    tail_ref[...] = tail


def line_kernel(*refs):
    *terms, _, send_ref, keep_ref = refs
    rows, hid = send_ref.shape
    total = tree([r[0:rows, :].astype(f32) for r in terms])
    first = lax.axis_index("sub") == 0
    left, right = total[:, :hid], total[:, hid:]
    send_ref[...] = jnp.where(first, right, left).astype(bf16)
    keep_ref[...] = jnp.where(first, left, right).astype(bf16)


def own_kernel(*refs):
    *terms, keep_ref, arrived_ref, vectors_ref, out_keep_ref, out_arrived_ref, _, own_ref, tail_ref = refs
    strip = keep_ref.shape[0]
    zero = (keep_ref[...].astype(f32) + arrived_ref[0:strip, :].astype(f32)).astype(bf16)
    total = tree([r[0:strip, :].astype(f32) for r in terms] + [zero.astype(f32)])
    own_ref[0:strip, :] = total.astype(bf16)
    own_ref[strip:, :] = (
        out_keep_ref[...].astype(f32) + out_arrived_ref[...].astype(f32)
    ).astype(bf16)
    tail_ref[...] = tree([r[strip:, :].astype(f32) for r in terms] + [vectors_ref[...].astype(f32)])


def write_vectors(tail, bias_ref, gain_ref):
    bias_ref[...] = tail[0:1] + tail[1:2]
    hid = tail.shape[1]
    for k in range(gain_ref.shape[1] // hid):
        gain_ref[:, k * hid : (k + 1) * hid] = tail[2 + 2 * k : 3 + 2 * k] + tail[3 + 2 * k : 4 + 2 * k]


def relay_kernel(*refs):
    *_, strip_ref, out_ref = refs
    out_ref[...] = strip_ref[...]


def place_kernel(lines, which, a_ref, b_ref, c_ref, d_ref, *refs):
    src_hbm, dst_hbm, out_hbm, src_ref, dst_ref, out_ref, sems = refs[-7:]
    first = lax.axis_index("sub") == 0
    mesh = lax.axis_index("mesh")
    strip, hid = src_ref.shape[1:]
    narrow = out_ref.shape[1]
    copies = []

    def put(ref, hbm, at, rows):
        start = pl.multiple_of((mesh ^ which[at]) * rows, rows)
        copies.append(pltpu.make_async_copy(ref.at[at], hbm.at[pl.ds(start, rows)], sems.at[len(copies)]))
        copies[-1].start()

    for at, (mine_ref, theirs_ref) in enumerate(((a_ref, c_ref), (b_ref, d_ref))):
        mine, theirs = mine_ref[...], theirs_ref[...]
        low = jnp.where(first, mine, theirs).astype(f32)
        high = jnp.where(first, theirs, mine).astype(f32)
        src_ref[at] = low[:strip]
        put(src_ref, src_hbm, at, strip)
        dst_ref[at] = high[:strip]
        put(dst_ref, dst_hbm, at, strip)
        out_ref[at, :, 0:hid] = low[strip:]
        out_ref[at, :, hid:] = high[strip:]
        put(out_ref, out_hbm, at, narrow)
    for copy in copies:
        copy.wait()


def sum_kernel(chunk, arrived_ref, out_ref, bias_ref, gain_ref):
    peers = arrived_ref.shape[0]
    total = arrived_ref[0].astype(f32)
    for peer in range(1, peers):
        total += arrived_ref[peer].astype(f32)
    low = total[:chunk].astype(bf16)
    for peer in range(peers):
        out_ref[peer] = low
    tail = total[chunk:]
    write_vectors(tail, bias_ref, gain_ref)


def unpack_kernel(arrived_ref, src_ref, dst_ref, out_ref):
    hid = src_ref.shape[1]
    rows = src_ref.shape[0]
    src_ref[...] = arrived_ref[0:rows, :].astype(f32)
    dst_ref[...] = arrived_ref[rows : 2 * rows, :].astype(f32)
    at = 2 * rows
    for k in range(out_ref.shape[1] // hid):
        out_ref[:, k * hid : (k + 1) * hid] = arrived_ref[at : at + out_ref.shape[0], :].astype(f32)
        at += out_ref.shape[0]


def node_part(send_ref, local_ref, target_ref, packed_ref, returned, out_ref):
    rows = local_ref.shape[0]
    halo = send_ref.shape[2]
    picks = [one_hot(iota((rows, halo), 0) == send_ref[0, d : d + 1, :]) for d in range(4)]
    total = local_ref[...] + dot(jnp.concatenate(picks, axis=1), jnp.concatenate(returned, axis=0))
    w_src, w_dst, _, _ = unpacked(packed_ref, out_ref.shape[1])
    out_ref[...] = (dot(total.astype(bf16), w_src, NT) + dot(target_ref[...], w_dst, NT)).astype(bf16)


def node_kernel(send_ref, local_ref, target_ref, packed_ref, *rest):
    *back_refs, out_ref = rest
    returned = [r[...] for r in back_refs]
    node_part(send_ref, local_ref, target_ref, packed_ref, returned, out_ref)


def paired_node_kernel(
    send_ref, local_ref, target_ref, packed_ref, three_ref, one_ref, pair_ref, out_ref
):
    even = lax.axis_index("mesh") % 2 == 0
    halo = send_ref.shape[2]
    hid = local_ref.shape[1]
    at = one_ref.shape[0] - halo // 2
    one, three = [
        jnp.concatenate([r[at:, :hid], r[at:, hid:]], axis=0) for r in (one_ref, three_ref)
    ]
    returned = [
        jnp.where(even, one, three), jnp.where(even, three, one), pair_ref[pair_ref.shape[0] - 2 * halo :, :]
    ]
    node_part(send_ref, local_ref, target_ref, packed_ref, returned, out_ref)


def finish_kernel(cot_ref, node_ref, gain_ref, normed_ref, own_ref, other_ref, *rest):
    if len(rest) == 5:
        tail_ref, *rest, bias_out_ref, gain_out_ref = rest
        write_vectors(tail_ref[...], bias_out_ref, gain_out_ref)
    grad_ref, updated_ref = rest
    grad_ref[...] = cot_ref[...].astype(f32) + (
        own_ref[...].astype(f32) + other_ref[...].astype(f32)
    )
    updated_ref[...] = (node_ref[...].astype(f32) + gain_ref[...] * normed_ref[...]).astype(bf16)


VMEM = pl.BlockSpec(memory_space=pltpu.VMEM)
SMEM = pl.BlockSpec(memory_space=pltpu.SMEM)
HBM = pl.BlockSpec(memory_space=pltpu.HBM)


def shape(dims, dtype):
    return jax.ShapeDtypeStruct(dims, dtype)


def call(kernel, outs, *args, specs=None, out_specs=None, flops=10**8, scratch=(), **options):
    return pl.pallas_call(
        kernel,
        out_shape=outs,
        in_specs=specs or [VMEM] * len(args),
        out_specs=out_specs or jax.tree.map(lambda _: VMEM, outs),
        scratch_shapes=scratch,
        **options,
        compiler_params=pltpu.CompilerParams(vmem_limit_bytes=VMEM_LIMIT),
        cost_estimate=pl.CostEstimate(flops=flops, bytes_accessed=10**6, transcendentals=0),
    )(*args)


def shifted(x, axis, by):
    count = lax.axis_size(axis)
    return lax.ppermute(x, axis, [(i, (i + by) % count) for i in range(count)])


def across(x, axis, k):
    count = lax.axis_size(axis)
    return lax.ppermute(x, axis, [(i, i ^ k) for i in range(count)])


def diagonal(x):
    lines, pairs = lax.axis_size("mesh"), lax.axis_size("sub")
    moves = [(m * pairs + p, (m ^ 1) * pairs + (p ^ 1)) for m in range(lines) for p in range(pairs)]
    return lax.ppermute(x, ("mesh", "sub"), moves)


def paired_sums(messages, lines, strip, narrow, width, hid, node_terms):
    sends, keeps, outs = messages[:2], messages[2:4], messages[4:]
    order = range(lines - 1, 0, -1)
    block = shape((strip + TAIL, hid), bf16)
    far = across(sends[0], "sub", 1)
    out_terms = {k: across(outs[k], "mesh", k) for k in order}
    zero = across(sends[1], "sub", 1)
    line = {}
    line[3], line[2], line[1], tail = call(
        far_kernel, [block] * 3 + [shape((TAIL, hid), bf16)], far, keeps[0]
    )
    line_terms = {k: across(line[k], "mesh", k) for k in order}
    out_send, out_keep = call(
        line_kernel,
        [shape((narrow, hid), bf16)] * 2,
        *[out_terms[k] for k in order], outs[0], line[1],
    )
    node_part = node_terms(out_terms[3], out_terms[1], zero)
    own, tail = call(
        own_kernel,
        [shape((strip + narrow, hid), bf16), shape((TAIL, hid), f32)],
        *[line_terms[k] for k in order], keeps[1], zero, tail, out_keep, across(out_send, "sub", 1),
        node_part,
    )
    mine = {k: across(own, "mesh", k) for k in order}
    mine[0] = own
    theirs = {0: across(own, "sub", 1), 1: diagonal(own)}
    early = (mine[0], mine[1], theirs[0], theirs[1])
    theirs[2] = across(mine[2], "sub", 1)
    theirs[3] = across(mine[3], "sub", 1)
    wholes = [shape((width, hid), f32), shape((width, hid), f32), shape((hid, width), f32)]
    scratch = [
        pltpu.VMEM((2, strip, hid), f32), pltpu.VMEM((2, strip, hid), f32), pltpu.VMEM((2, narrow, width), f32),
        pltpu.SemaphoreType.DMA((6,)),
    ]
    grads = call(
        functools.partial(place_kernel, lines, (0, 1)), wholes, *early,
        out_specs=[HBM] * 3, scratch=scratch, flops=10**8,
    )
    grads = call(
        functools.partial(place_kernel, lines, (2, 3)), wholes,
        mine[2], mine[3], theirs[2], theirs[3], *grads,
        specs=[VMEM] * 4 + [HBM] * 3, out_specs=[HBM] * 3, scratch=scratch,
        input_output_aliases={4: 0, 5: 1, 6: 2},
    )
    return (*grads, tail), node_part


def shards(
    node_state,
    send_rows,
    edge_src,
    edge_dst,
    block_count,
    w_src,
    w_dst,
    hidden_bias,
    w_out,
    norm_gain,
    cotangent,
):
    rows, width = node_state.shape
    hid = w_src.shape[1]
    halo = send_rows.shape[2]
    edges = edge_src.shape[0]
    peers = lax.axis_size("mesh") * lax.axis_size("sub")
    merged = lax.axis_size("sub") == 2
    total_rows = 2 * width + (width // hid) * hid
    chunk = -(-total_rows // (peers * 16)) * 16

    piece = [halo, halo, 2 * halo] if merged else [halo] * 4
    routes = [("mesh", 1), ("mesh", -1), ("sub", 1)] + ([] if merged else [("sub", -1)])
    n_halo = len(piece)

    def in_hbm(x):
        return pltpu.with_memory_space_constraint(x, pltpu.HBM)

    bias = hidden_bias.reshape(1, hid)
    operands = [node_state, send_rows, w_src, w_dst, w_out, bias]
    node, send, packed, *outgoing = call(
        send_kernel,
        [
            shape((rows, width), bf16),
            shape(send_rows.shape, jnp.int32),
            shape((3 * width + TAIL, hid), bf16),
        ]
        + [shape((n, width), bf16) for n in piece],
        *[in_hbm(x) for x in operands],
        specs=[HBM] * len(operands),
        scratch=[pltpu.VMEM((1, hid), f32), pltpu.SemaphoreType.DMA((5 + width // hid,))],
    )
    arrived = [shifted(x, axis, by) for x, (axis, by) in zip(outgoing, routes)]

    other = shifted(packed, "lat", 1)

    fetched = [
        edge_src.reshape(1, edges), edge_dst.reshape(1, edges), block_count,
        norm_gain.reshape(1, width), cotangent,
    ]
    pre, pick, collect, spread, scatter, gain, cot = call(
        local_kernel,
        [
            shape((edges, 2 * hid), f32),
            shape((edges, 4 * halo), bf16),
            shape((rows, edges), bf16),
            shape((edges, rows), bf16),
            shape((rows + 4 * halo, edges), bf16),
            shape((1, width), f32),
            shape((rows, width), bf16),
        ],
        node, packed, other, *[in_hbm(x) for x in fetched],
        specs=[VMEM] * 3 + [HBM] * len(fetched),
        scratch=[
            pltpu.SMEM(block_count.shape, jnp.int32),
            pltpu.VMEM((1, edges), jnp.int32),
            pltpu.VMEM((1, edges), jnp.int32),
            pltpu.SemaphoreType.DMA((N_FETCHED,)),
        ],
    )


    lines = lax.axis_size("mesh")
    paired = merged and lines == 4
    if paired:
        strip = width // lines
        narrow = hid // lines
        rows_of = (3 * strip + TAIL, strip + 2 * halo, 3 * strip + TAIL, strip)
        message_shapes = [shape((n, hid), bf16) for n in rows_of]
        message_shapes += [shape((narrow + k % 2 * (halo // 2), width), bf16) for k in range(lines)]
    else:
        message_shapes = [shape((peers, chunk + TAIL, hid), bf16)]
        message_shapes += [shape((n, hid), bf16) for n in piece]
    normed, local, target, *messages = call(
        functools.partial(edge_kernel, (peers, chunk, n_halo, paired)),
        [shape((rows, width), f32), shape((rows, hid), f32), shape((rows, hid), bf16)]
        + message_shapes,
        node, pre, pick, collect, spread, scatter, packed, other, gain, cot, *arrived,
        scratch=[
            pltpu.VMEM((hid, width), bf16),
            pltpu.VMEM((2 * halo, hid), bf16),
            pltpu.VMEM((2, width, hid), bf16),
        ],
    )

    def node_terms(*returned):
        return call(
            paired_node_kernel if paired else node_kernel,
            shape((rows, width), bf16),
            send, local, target, packed, *returned,
        )

    if paired:
        (src_grad, dst_grad, out_grad, tail), node_part = paired_sums(
            messages, lines, strip, narrow, width, hid, node_terms
        )
    else:
        node_part = node_terms(
            *[shifted(x, axis, -by) for x, (axis, by) in zip(messages[1:], routes)]
        )
        exchanged = lax.all_to_all(messages[0], ("mesh", "sub"), 0, 0)
        reduced, bias_grad, gain_grad = call(
            functools.partial(sum_kernel, chunk),
            [shape((peers, chunk, hid), bf16), shape((1, hid), f32), shape((1, width), f32)],
            exchanged,
        )
        gathered = lax.all_to_all(reduced, ("mesh", "sub"), 0, 0)
        src_grad, dst_grad, out_grad = call(
            unpack_kernel,
            [shape((width, hid), f32), shape((width, hid), f32), shape((hid, width), f32)],
            gathered.reshape(peers * chunk, hid),
        )
    finished = [shape((rows, width), f32), shape((rows, width), bf16)]
    ends = [cot, node, gain, normed, node_part, shifted(node_part, "lat", 1)]
    if paired:
        node_grad, updated, bias_grad, gain_grad = call(
            finish_kernel, finished + [shape((1, hid), f32), shape((1, width), f32)], *ends, tail
        )
    else:
        node_grad, updated = call(finish_kernel, finished, *ends)
    return (
        updated, node_grad, src_grad, dst_grad, out_grad,
        bias_grad.reshape(hid), gain_grad.reshape(width),
    )


def solution(mesh):
    nodes = P(("parts", "mesh", "sub"), None)
    slots = P(("parts", "mesh", "sub"))
    in_specs = (
        nodes,
        P(("parts", "mesh", "sub"), None, None),
        slots,
        slots,
        slots,
        P(None, "lat"),
        P(None, "lat"),
        P("lat"),
        P("lat", None),
        P(),
        nodes,
    )
    out_specs = (
        nodes,
        nodes,
        P("parts", "lat"),
        P("parts", "lat"),
        P(("parts", "lat"), None),
        P(("parts", "lat")),
        P("parts"),
    )
    return jax.shard_map(shards, mesh=mesh, in_specs=in_specs, out_specs=out_specs, check_vma=False)
```

```python
import functools

import jax
import jax.numpy as jnp
from jax import lax
from jax.experimental import pallas as pl
from jax.experimental.pallas import tpu as pltpu
from jax.sharding import PartitionSpec as P

BLOCK = 128
EPSILON = 1e-05
TAIL = 16
N_FETCHED = 5
VMEM_LIMIT = 24 * 1024 * 1024

f32 = jnp.float32
bf16 = jnp.bfloat16

NN = (((1,), (0,)), ((), ()))
NT = (((1,), (1,)), ((), ()))
TN = (((0,), (0,)), ((), ()))


def dot(a, b, dims=NN):
    return lax.dot_general(a, b, dims, preferred_element_type=f32)


def iota(shape, dim):
    return lax.broadcasted_iota(jnp.int32, shape, dim)


def one_hot(condition):
    return jnp.where(condition, 1.0, 0.0).astype(bf16)


def split(x):
    high = x.astype(bf16)
    return high, (x - high.astype(f32)).astype(bf16)


def columns_of(row, lanes):
    return jnp.transpose(jnp.broadcast_to(row, (lanes, row.shape[1])))


def usable_row(count_ref, edges):
    lane = iota((1, BLOCK), 1)
    parts = [lane < count_ref[b] for b in range(edges // BLOCK)]
    return jnp.concatenate([jnp.where(p, 1, 0) for p in parts], axis=1)


def usable_columns(count_ref, edges, lanes):
    sub = iota((BLOCK, lanes), 0)
    return jnp.concatenate(
        [jnp.where(sub < count_ref[b], 1, 0) for b in range(edges // BLOCK)], axis=0
    )


def fetch(sems, *pairs):
    copies = [pltpu.make_async_copy(a, b, sems.at[i]) for i, (a, b) in enumerate(pairs)]
    for copy in copies:
        copy.start()
    return copies


def send_kernel(
    node_hbm, send_hbm, w_src_hbm, w_dst_hbm, w_out_hbm, bias_hbm,
    node_ref, send_ref, packed_ref, *rest,
):
    *out_refs, bias_ref, sems = rest
    hid = packed_ref.shape[1]
    width = w_src_hbm.shape[0]
    pairs = [(node_hbm, node_ref), (send_hbm, send_ref), (bias_hbm, bias_ref)]
    pairs += [(w_src_hbm, packed_ref.at[pl.ds(0, width)]), (w_dst_hbm, packed_ref.at[pl.ds(width, width)])]
    for k in range(width // hid):
        target = packed_ref.at[pl.ds(2 * width + k * hid, hid)]
        pairs.append((w_out_hbm.at[:, pl.ds(k * hid, hid)], target))
    copies = fetch(sems, *pairs)
    copies[0].wait()
    copies[1].wait()
    node = node_ref[...]
    rows = node.shape[0]
    halo = send_ref.shape[2]
    pieces = []
    for d in range(4):
        pick = one_hot(iota((rows, halo), 0) == send_ref[0, d : d + 1, :])
        pieces.append(dot(pick, node, TN).astype(bf16))
    out_refs[0][...] = pieces[0]
    out_refs[1][...] = pieces[1]
    if len(out_refs) == 3:
        out_refs[2][0:halo, :] = pieces[2]
        out_refs[2][halo:, :] = pieces[3]
    else:
        out_refs[2][...] = pieces[2]
        out_refs[3][...] = pieces[3]
    copies[2].wait()
    bias = bias_ref[...]
    parts = []
    for _ in range(3):
        parts.append(bias.astype(bf16).astype(f32))
        bias = bias - parts[-1]
    parts.append(jnp.zeros((TAIL - 3, hid), f32))
    packed_ref[packed_ref.shape[0] - TAIL :, :] = jnp.concatenate(parts, axis=0).astype(bf16)
    for copy in copies[3:]:
        copy.wait()


def unpacked(ref, width):
    hid = ref.shape[1]
    w_out = [ref[at : at + hid, :] for at in range(2 * width, 3 * width, hid)]
    tail = ref[ref.shape[0] - TAIL :, :].astype(f32)
    bias = tail[0:1] + tail[1:2] + tail[2:3]
    return ref[0:width, :], ref[width : 2 * width, :], jnp.concatenate(w_out, axis=1), bias


def local_kernel(node_ref, packed_ref, other_ref, *refs):
    ins, refs = refs[:N_FETCHED], refs[N_FETCHED:]
    pre_ref, pick_ref, collect_ref, spread_ref, scatter_ref, *refs = refs
    gain_ref, cot_ref, count_ref, src_ref, dst_ref, sems = refs
    copies = fetch(sems, *zip(ins, (src_ref, dst_ref, count_ref, gain_ref, cot_ref)))
    node = node_ref[...]
    rows, width = node.shape
    w_src, w_dst, _, bias = unpacked(packed_ref, width)
    w_src_other, w_dst_other, _, bias_other = unpacked(other_ref, width)
    projected = dot(node, jnp.concatenate([w_src, w_src_other, w_dst, w_dst_other], axis=1))
    both = projected.shape[1] // 2
    projected = jnp.concatenate([projected[:, :both], projected[:, both:]], axis=0)
    high, low = split(projected)
    for copy in copies:
        copy.wait()
    edges = src_ref.shape[1]
    scatter_ref[...] = one_hot(iota(scatter_ref.shape, 0) == src_ref[...])
    used = usable_row(count_ref, edges) > 0
    collect_ref[...] = one_hot((iota((rows, edges), 0) == dst_ref[...]) & used)
    source = columns_of(src_ref[...], 128)
    target = columns_of(dst_ref[...], 128)
    lane = iota(source.shape, 1)
    used = usable_columns(count_ref, edges, 128) > 0
    near = one_hot(source == lane)
    pick_ref[...] = one_hot(source == lane + rows)
    spread_ref[...] = one_hot((target == lane) & used)
    ends = jnp.concatenate([near, one_hot(target == lane)], axis=1)
    pre_ref[...] = dot(ends, high) + dot(ends, low) + jnp.concatenate([bias, bias_other], axis=1)


def twice(x):
    return jnp.concatenate([x, x], axis=1)


def stacked(x):
    return jnp.concatenate(split(x), axis=0)


def edge_kernel(
    geometry,
    node_ref, pre_ref, pick_ref, collect_ref, spread_ref, scatter_ref, packed_ref, other_ref, gain_ref, cot_ref,
    *rest,
):
    peers, chunk, n_halo, paired = geometry
    *rest, out_scratch, back_scratch, pair_scratch = rest
    halo_refs = rest[:n_halo]
    normed_ref, local_ref, target_ref, *message_refs = rest[n_halo:]
    node = node_ref[...]
    rows, width = node.shape
    hid = packed_ref.shape[1]
    halo_rows = jnp.concatenate([r[...] for r in halo_refs], axis=0)
    w_src, _, w_out, _ = unpacked(packed_ref, width)
    w_src_other, _, w_out_other, _ = unpacked(other_ref, width)

    far = stacked(dot(halo_rows, jnp.concatenate([w_src, w_src_other], axis=1)))
    pre = pre_ref[...] + dot(twice(pick_ref[...]), far)
    sig = 0.5 + 0.5 * jnp.tanh(0.5 * pre)
    hidden = dot(collect_ref[...], (pre * sig).astype(bf16))
    pre, sig = pre[:, :hid], sig[:, :hid]
    factor = sig * (1.0 + pre * (1.0 - sig))
    parts = []
    for at, w in ((0, w_out), (hid, w_out_other)):
        high, low = split(hidden[:, at : at + hid])
        parts.append(dot(high, w) + dot(low, w))
    hidden_low = hidden[:, :hid].astype(bf16)
    aggregate = parts[0] + parts[1]

    center = aggregate - jnp.mean(aggregate, axis=1, keepdims=True)
    variance = jnp.mean(center * center, axis=1, keepdims=True)
    inverse = lax.rsqrt(variance + EPSILON)
    normed = center * inverse
    gain = gain_ref[...]
    upstream = cot_ref[...].astype(f32)
    scaled = upstream * gain
    agg_grad = inverse * (
        scaled
        - jnp.mean(scaled, axis=1, keepdims=True)
        - normed * jnp.mean(scaled * normed, axis=1, keepdims=True)
    )
    agg_grad = agg_grad.astype(bf16)
    normed_ref[...] = normed
    gain_part = jnp.sum(upstream * normed, axis=0, keepdims=True)

    act_grad = dot(twice(spread_ref[...]), stacked(dot(agg_grad, w_out, NT)))
    pre_grad = (act_grad * factor).astype(bf16)

    table = jnp.concatenate([node, halo_rows], axis=0)
    by_source = dot(scatter_ref[...], pre_grad)
    by_target = dot(collect_ref[...], pre_grad)
    local_ref[...] = by_source[:rows]
    by_target_low = by_target.astype(bf16)
    by_source_low = by_source.astype(bf16)
    target_ref[...] = by_target_low

    bias_part = jnp.sum(by_target, axis=0, keepdims=True)
    src_part = dot(table, by_source_low, TN).astype(bf16)
    dst_part = dot(node, by_target_low, TN).astype(bf16)
    out_part = dot(hidden_low, agg_grad, TN).astype(bf16)
    vectors = [bias_part] + [gain_part[:, at : at + hid] for at in range(0, width, hid)]
    tail = tail_of(vectors)
    back = by_source_low[rows:]

    if paired:
        sends, keeps, out_refs = message_refs[:2], message_refs[2:4], message_refs[4:]
        sub = lax.axis_index("sub")
        mesh = lax.axis_index("mesh")
        lines = len(out_refs)
        halo = back.shape[0] // 4
        first = sub == 0
        pair_scratch[0] = jnp.where(first, dst_part, src_part)
        pair_scratch[1] = jnp.where(first, src_part, dst_part)
        strip = width // lines
        for slot, (far_ref, zero_ref) in enumerate((sends, keeps)):
            places = [(far_ref, at, k) for at, k in enumerate((3, 2, 1))] + [(zero_ref, 0, 0)]
            for ref, at, k in places:
                start = pl.multiple_of((mesh ^ k) * strip, strip)
                ref[at * strip : (at + 1) * strip, :] = pair_scratch[slot, pl.ds(start, strip), :]
            far_ref[3 * strip :, :] = tail
        sends[1][strip:, :] = back[2 * halo :]
        back_scratch[...] = back[: 2 * halo]
        out_scratch[...] = out_part
        strip = hid // len(out_refs)
        for k, ref in enumerate(out_refs):
            start = pl.multiple_of((mesh ^ k) * strip, strip)
            ref[0:strip, :] = out_scratch[pl.ds(start, strip), :]
            if k % 2 == 1:
                slot = (mesh + (k // 2) + 1) % 2
                start = pl.multiple_of(slot * halo, halo)
                rows_back = back_scratch[pl.ds(start, halo), :]
                ref[strip:, 0:hid] = rows_back[: halo // 2]
                ref[strip:, hid:] = rows_back[halo // 2 :]
        return

    message_ref, *back_refs = message_refs
    at = 0
    for ref in back_refs:
        ref[...] = back[at : at + ref.shape[0]]
        at += ref.shape[0]
    blocks = [src_part, dst_part]
    for at in range(0, width, hid):
        blocks.append(out_part[:, at : at + hid])
    done = 0
    for block in blocks:
        at = 0
        while at < block.shape[0]:
            peer, offset = divmod(done, chunk)
            take = min(chunk - offset, block.shape[0] - at)
            message_ref[peer, offset : offset + take, :] = block[at : at + take]
            at += take
            done += take
    while done < peers * chunk:
        peer, offset = divmod(done, chunk)
        take = chunk - offset
        message_ref[peer, offset : offset + take, :] = jnp.zeros((take, hid), bf16)
        done += take
    for peer in range(peers):
        message_ref[peer, chunk:, :] = tail


def tail_of(vectors):
    tail = []
    for v in vectors:
        high = v.astype(bf16).astype(f32)
        tail += [high, v - high]
    tail.append(jnp.zeros((TAIL - len(tail), vectors[0].shape[1]), f32))
    return jnp.concatenate(tail, axis=0).astype(bf16)


def tree(terms):
    while len(terms) > 1:
        terms = [terms[i] + terms[i + 1] for i in range(0, len(terms), 2)]
    return terms[0]


def far_kernel(arrived_ref, keep_ref, *refs):
    *line_refs, tail_ref = refs
    total = keep_ref[...].astype(f32) + arrived_ref[...].astype(f32)
    strip = line_refs[0].shape[0] - TAIL
    tail = total[len(line_refs) * strip :]
    tail = tail_of([tail[at : at + 1] + tail[at + 1 : at + 2] for at in range(0, 6, 2)])
    for k, ref in enumerate(line_refs):
        ref[0:strip, :] = total[k * strip : (k + 1) * strip].astype(bf16)
        ref[strip:, :] = tail
    tail_ref[...] = tail


def line_kernel(*refs):
    *terms, zero_ref, send_ref, keep_ref = refs
    rows, hid = keep_ref.shape
    total = tree([r[0:rows, :].astype(f32) for r in terms])
    first = lax.axis_index("sub") == 0
    left, right = total[:, :hid], total[:, hid:]
    send_ref[0:rows, :] = jnp.where(first, right, left).astype(bf16)
    send_ref[rows:, :] = zero_ref[...]
    keep_ref[...] = jnp.where(first, left, right).astype(bf16)


def own_kernel(*refs):
    *terms, keep_ref, vectors_ref, out_keep_ref, arrived_ref, own_ref, tail_ref = refs
    strip = keep_ref.shape[0]
    narrow = out_keep_ref.shape[0]
    zero = (keep_ref[...].astype(f32) + arrived_ref[narrow : narrow + strip, :].astype(f32)).astype(bf16)
    total = tree([r[0:strip, :].astype(f32) for r in terms] + [zero.astype(f32)])
    own_ref[0:strip, :] = total.astype(bf16)
    own_ref[strip:, :] = (out_keep_ref[...].astype(f32) + arrived_ref[0:narrow, :].astype(f32)).astype(bf16)
    tail_ref[...] = tree([r[strip:, :].astype(f32) for r in terms] + [vectors_ref[...].astype(f32)])


def write_vectors(tail, bias_ref, gain_ref):
    bias_ref[...] = tail[0:1] + tail[1:2]
    hid = tail.shape[1]
    for k in range(gain_ref.shape[1] // hid):
        gain_ref[:, k * hid : (k + 1) * hid] = tail[2 + 2 * k : 3 + 2 * k] + tail[3 + 2 * k : 4 + 2 * k]


def relay_kernel(*refs):
    *_, strip_ref, out_ref = refs
    out_ref[...] = strip_ref[...]


def place_kernel(lines, which, a_ref, b_ref, c_ref, d_ref, *refs):
    src_hbm, dst_hbm, out_hbm, src_ref, dst_ref, out_ref, sems = refs[-7:]
    first = lax.axis_index("sub") == 0
    mesh = lax.axis_index("mesh")
    strip, hid = src_ref.shape[1:]
    narrow = out_ref.shape[1]
    copies = []

    def put(ref, hbm, at, rows):
        start = pl.multiple_of((mesh ^ which[at]) * rows, rows)
        copies.append(pltpu.make_async_copy(ref.at[at], hbm.at[pl.ds(start, rows)], sems.at[len(copies)]))
        copies[-1].start()

    for at, (mine_ref, theirs_ref) in enumerate(((a_ref, c_ref), (b_ref, d_ref))):
        mine, theirs = mine_ref[...], theirs_ref[...]
        low = jnp.where(first, mine, theirs).astype(f32)
        high = jnp.where(first, theirs, mine).astype(f32)
        src_ref[at] = low[:strip]
        put(src_ref, src_hbm, at, strip)
        dst_ref[at] = high[:strip]
        put(dst_ref, dst_hbm, at, strip)
        out_ref[at, :, 0:hid] = low[strip:]
        out_ref[at, :, hid:] = high[strip:]
        put(out_ref, out_hbm, at, narrow)
    for copy in copies:
        copy.wait()


def sum_kernel(chunk, arrived_ref, out_ref, bias_ref, gain_ref):
    peers = arrived_ref.shape[0]
    total = arrived_ref[0].astype(f32)
    for peer in range(1, peers):
        total += arrived_ref[peer].astype(f32)
    low = total[:chunk].astype(bf16)
    for peer in range(peers):
        out_ref[peer] = low
    tail = total[chunk:]
    write_vectors(tail, bias_ref, gain_ref)


def unpack_kernel(arrived_ref, src_ref, dst_ref, out_ref):
    hid = src_ref.shape[1]
    rows = src_ref.shape[0]
    src_ref[...] = arrived_ref[0:rows, :].astype(f32)
    dst_ref[...] = arrived_ref[rows : 2 * rows, :].astype(f32)
    at = 2 * rows
    for k in range(out_ref.shape[1] // hid):
        out_ref[:, k * hid : (k + 1) * hid] = arrived_ref[at : at + out_ref.shape[0], :].astype(f32)
        at += out_ref.shape[0]


def node_part(send_ref, local_ref, target_ref, packed_ref, returned, out_ref):
    rows = local_ref.shape[0]
    halo = send_ref.shape[2]
    picks = [one_hot(iota((rows, halo), 0) == send_ref[0, d : d + 1, :]) for d in range(4)]
    total = local_ref[...] + dot(jnp.concatenate(picks, axis=1), jnp.concatenate(returned, axis=0))
    w_src, w_dst, _, _ = unpacked(packed_ref, out_ref.shape[1])
    out_ref[...] = (dot(total.astype(bf16), w_src, NT) + dot(target_ref[...], w_dst, NT)).astype(bf16)


def node_kernel(send_ref, local_ref, target_ref, packed_ref, *rest):
    *back_refs, out_ref = rest
    returned = [r[...] for r in back_refs]
    node_part(send_ref, local_ref, target_ref, packed_ref, returned, out_ref)


def paired_node_kernel(
    send_ref, local_ref, target_ref, packed_ref, three_ref, one_ref, pair_ref, out_ref
):
    even = lax.axis_index("mesh") % 2 == 0
    halo = send_ref.shape[2]
    hid = local_ref.shape[1]
    at = one_ref.shape[0] - halo // 2
    one, three = [
        jnp.concatenate([r[at:, :hid], r[at:, hid:]], axis=0) for r in (one_ref, three_ref)
    ]
    returned = [
        jnp.where(even, one, three), jnp.where(even, three, one), pair_ref[pair_ref.shape[0] - 2 * halo :, :]
    ]
    node_part(send_ref, local_ref, target_ref, packed_ref, returned, out_ref)


def finish_kernel(cot_ref, node_ref, gain_ref, normed_ref, own_ref, other_ref, *rest):
    if len(rest) == 5:
        tail_ref, *rest, bias_out_ref, gain_out_ref = rest
        write_vectors(tail_ref[...], bias_out_ref, gain_out_ref)
    grad_ref, updated_ref = rest
    grad_ref[...] = cot_ref[...].astype(f32) + (
        own_ref[...].astype(f32) + other_ref[...].astype(f32)
    )
    updated_ref[...] = (node_ref[...].astype(f32) + gain_ref[...] * normed_ref[...]).astype(bf16)


VMEM = pl.BlockSpec(memory_space=pltpu.VMEM)
SMEM = pl.BlockSpec(memory_space=pltpu.SMEM)
HBM = pl.BlockSpec(memory_space=pltpu.HBM)


def shape(dims, dtype):
    return jax.ShapeDtypeStruct(dims, dtype)


def call(kernel, outs, *args, specs=None, out_specs=None, flops=10**8, scratch=(), **options):
    return pl.pallas_call(
        kernel,
        out_shape=outs,
        in_specs=specs or [VMEM] * len(args),
        out_specs=out_specs or jax.tree.map(lambda _: VMEM, outs),
        scratch_shapes=scratch,
        **options,
        compiler_params=pltpu.CompilerParams(vmem_limit_bytes=VMEM_LIMIT),
        cost_estimate=pl.CostEstimate(flops=flops, bytes_accessed=10**6, transcendentals=0),
    )(*args)


def shifted(x, axis, by):
    count = lax.axis_size(axis)
    return lax.ppermute(x, axis, [(i, (i + by) % count) for i in range(count)])


def across(x, axis, k):
    count = lax.axis_size(axis)
    return lax.ppermute(x, axis, [(i, i ^ k) for i in range(count)])


def diagonal(x):
    lines, pairs = lax.axis_size("mesh"), lax.axis_size("sub")
    moves = [(m * pairs + p, (m ^ 1) * pairs + (p ^ 1)) for m in range(lines) for p in range(pairs)]
    return lax.ppermute(x, ("mesh", "sub"), moves)


def paired_sums(messages, lines, strip, narrow, width, hid, node_terms):
    sends, keeps, outs = messages[:2], messages[2:4], messages[4:]
    order = range(lines - 1, 0, -1)
    block = shape((strip + TAIL, hid), bf16)
    far = across(sends[0], "sub", 1)
    out_terms = {k: across(outs[k], "mesh", k) for k in order}
    line = {}
    line[3], line[2], line[1], tail = call(
        far_kernel, [block] * 3 + [shape((TAIL, hid), bf16)], far, keeps[0]
    )
    line_terms = {k: across(line[k], "mesh", k) for k in order}
    out_send, out_keep = call(
        line_kernel,
        [shape((narrow + sends[1].shape[0], hid), bf16), shape((narrow, hid), bf16)],
        *[out_terms[k] for k in order], outs[0], sends[1], flops=10**8,
    )
    near = across(out_send, "sub", 1)
    node_part = node_terms(out_terms[3], out_terms[1], near)
    own, tail = call(
        own_kernel,
        [shape((strip + narrow, hid), bf16), shape((TAIL, hid), f32)],
        *[line_terms[k] for k in order], keeps[1], tail, out_keep, near, flops=10**8,
    )
    mine = {k: across(own, "mesh", k) for k in order}
    mine[0] = own
    theirs = {0: across(own, "sub", 1), 1: diagonal(own)}
    early = (mine[0], mine[1], theirs[0], theirs[1])
    theirs[2] = across(mine[2], "sub", 1)
    theirs[3] = across(mine[3], "sub", 1)
    wholes = [shape((width, hid), f32), shape((width, hid), f32), shape((hid, width), f32)]
    scratch = [
        pltpu.VMEM((2, strip, hid), f32), pltpu.VMEM((2, strip, hid), f32), pltpu.VMEM((2, narrow, width), f32),
        pltpu.SemaphoreType.DMA((6,)),
    ]
    grads = call(
        functools.partial(place_kernel, lines, (0, 1)), wholes, *early,
        out_specs=[HBM] * 3, scratch=scratch, flops=10**8,
    )
    grads = call(
        functools.partial(place_kernel, lines, (2, 3)), wholes,
        mine[2], mine[3], theirs[2], theirs[3], *grads,
        specs=[VMEM] * 4 + [HBM] * 3, out_specs=[HBM] * 3, scratch=scratch,
        input_output_aliases={4: 0, 5: 1, 6: 2},
    )
    return (*grads, tail), node_part


def shards(
    node_state,
    send_rows,
    edge_src,
    edge_dst,
    block_count,
    w_src,
    w_dst,
    hidden_bias,
    w_out,
    norm_gain,
    cotangent,
):
    rows, width = node_state.shape
    hid = w_src.shape[1]
    halo = send_rows.shape[2]
    edges = edge_src.shape[0]
    peers = lax.axis_size("mesh") * lax.axis_size("sub")
    merged = lax.axis_size("sub") == 2
    total_rows = 2 * width + (width // hid) * hid
    chunk = -(-total_rows // (peers * 16)) * 16

    piece = [halo, halo, 2 * halo] if merged else [halo] * 4
    routes = [("mesh", 1), ("mesh", -1), ("sub", 1)] + ([] if merged else [("sub", -1)])
    n_halo = len(piece)

    def in_hbm(x):
        return pltpu.with_memory_space_constraint(x, pltpu.HBM)

    bias = hidden_bias.reshape(1, hid)
    operands = [node_state, send_rows, w_src, w_dst, w_out, bias]
    node, send, packed, *outgoing = call(
        send_kernel,
        [
            shape((rows, width), bf16),
            shape(send_rows.shape, jnp.int32),
            shape((3 * width + TAIL, hid), bf16),
        ]
        + [shape((n, width), bf16) for n in piece],
        *[in_hbm(x) for x in operands],
        specs=[HBM] * len(operands),
        scratch=[pltpu.VMEM((1, hid), f32), pltpu.SemaphoreType.DMA((5 + width // hid,))],
    )
    arrived = [shifted(x, axis, by) for x, (axis, by) in zip(outgoing, routes)]

    other = shifted(packed, "lat", 1)

    fetched = [
        edge_src.reshape(1, edges), edge_dst.reshape(1, edges), block_count,
        norm_gain.reshape(1, width), cotangent,
    ]
    pre, pick, collect, spread, scatter, gain, cot = call(
        local_kernel,
        [
            shape((edges, 2 * hid), f32),
            shape((edges, 4 * halo), bf16),
            shape((rows, edges), bf16),
            shape((edges, rows), bf16),
            shape((rows + 4 * halo, edges), bf16),
            shape((1, width), f32),
            shape((rows, width), bf16),
        ],
        node, packed, other, *[in_hbm(x) for x in fetched],
        specs=[VMEM] * 3 + [HBM] * len(fetched),
        scratch=[
            pltpu.SMEM(block_count.shape, jnp.int32),
            pltpu.VMEM((1, edges), jnp.int32),
            pltpu.VMEM((1, edges), jnp.int32),
            pltpu.SemaphoreType.DMA((N_FETCHED,)),
        ],
    )


    lines = lax.axis_size("mesh")
    paired = merged and lines == 4
    if paired:
        strip = width // lines
        narrow = hid // lines
        rows_of = (3 * strip + TAIL, strip + 2 * halo, 3 * strip + TAIL, strip)
        message_shapes = [shape((n, hid), bf16) for n in rows_of]
        message_shapes += [shape((narrow + k % 2 * (halo // 2), width), bf16) for k in range(lines)]
    else:
        message_shapes = [shape((peers, chunk + TAIL, hid), bf16)]
        message_shapes += [shape((n, hid), bf16) for n in piece]
    normed, local, target, *messages = call(
        functools.partial(edge_kernel, (peers, chunk, n_halo, paired)),
        [shape((rows, width), f32), shape((rows, hid), f32), shape((rows, hid), bf16)]
        + message_shapes,
        node, pre, pick, collect, spread, scatter, packed, other, gain, cot, *arrived,
        scratch=[
            pltpu.VMEM((hid, width), bf16),
            pltpu.VMEM((2 * halo, hid), bf16),
            pltpu.VMEM((2, width, hid), bf16),
        ],
    )

    def node_terms(*returned):
        return call(
            paired_node_kernel if paired else node_kernel,
            shape((rows, width), bf16),
            send, local, target, packed, *returned,
        )

    if paired:
        (src_grad, dst_grad, out_grad, tail), node_part = paired_sums(
            messages, lines, strip, narrow, width, hid, node_terms
        )
    else:
        node_part = node_terms(
            *[shifted(x, axis, -by) for x, (axis, by) in zip(messages[1:], routes)]
        )
        exchanged = lax.all_to_all(messages[0], ("mesh", "sub"), 0, 0)
        reduced, bias_grad, gain_grad = call(
            functools.partial(sum_kernel, chunk),
            [shape((peers, chunk, hid), bf16), shape((1, hid), f32), shape((1, width), f32)],
            exchanged,
        )
        gathered = lax.all_to_all(reduced, ("mesh", "sub"), 0, 0)
        src_grad, dst_grad, out_grad = call(
            unpack_kernel,
            [shape((width, hid), f32), shape((width, hid), f32), shape((hid, width), f32)],
            gathered.reshape(peers * chunk, hid),
        )
    finished = [shape((rows, width), f32), shape((rows, width), bf16)]
    ends = [cot, node, gain, normed, node_part, shifted(node_part, "lat", 1)]
    if paired:
        node_grad, updated, bias_grad, gain_grad = call(
            finish_kernel, finished + [shape((1, hid), f32), shape((1, width), f32)], *ends, tail
        )
    else:
        node_grad, updated = call(finish_kernel, finished, *ends)
    return (
        updated, node_grad, src_grad, dst_grad, out_grad,
        bias_grad.reshape(hid), gain_grad.reshape(width),
    )


def solution(mesh):
    nodes = P(("parts", "mesh", "sub"), None)
    slots = P(("parts", "mesh", "sub"))
    in_specs = (
        nodes,
        P(("parts", "mesh", "sub"), None, None),
        slots,
        slots,
        slots,
        P(None, "lat"),
        P(None, "lat"),
        P("lat"),
        P("lat", None),
        P(),
        nodes,
    )
    out_specs = (
        nodes,
        nodes,
        P("parts", "lat"),
        P("parts", "lat"),
        P(("parts", "lat"), None),
        P(("parts", "lat")),
        P("parts"),
    )
    return jax.shard_map(shards, mesh=mesh, in_specs=in_specs, out_specs=out_specs, check_vma=False)
```

```python
import functools

import jax
import jax.numpy as jnp
from jax import lax
from jax.experimental import pallas as pl
from jax.experimental.pallas import tpu as pltpu
from jax.sharding import PartitionSpec as P

BLOCK = 128
EPSILON = 1e-05
TAIL = 16
N_FETCHED = 5
VMEM_LIMIT = 24 * 1024 * 1024

f32 = jnp.float32
bf16 = jnp.bfloat16

NN = (((1,), (0,)), ((), ()))
NT = (((1,), (1,)), ((), ()))
TN = (((0,), (0,)), ((), ()))


def dot(a, b, dims=NN):
    return lax.dot_general(a, b, dims, preferred_element_type=f32)


def iota(shape, dim):
    return lax.broadcasted_iota(jnp.int32, shape, dim)


def one_hot(condition):
    return jnp.where(condition, 1.0, 0.0).astype(bf16)


def split(x):
    high = x.astype(bf16)
    return high, (x - high.astype(f32)).astype(bf16)


def columns_of(row, lanes):
    return jnp.transpose(jnp.broadcast_to(row, (lanes, row.shape[1])))


def usable_row(count_ref, edges):
    lane = iota((1, BLOCK), 1)
    parts = [lane < count_ref[b] for b in range(edges // BLOCK)]
    return jnp.concatenate([jnp.where(p, 1, 0) for p in parts], axis=1)


def usable_columns(count_ref, edges, lanes):
    sub = iota((BLOCK, lanes), 0)
    return jnp.concatenate(
        [jnp.where(sub < count_ref[b], 1, 0) for b in range(edges // BLOCK)], axis=0
    )


def fetch(sems, *pairs):
    copies = [pltpu.make_async_copy(a, b, sems.at[i]) for i, (a, b) in enumerate(pairs)]
    for copy in copies:
        copy.start()
    return copies


def send_kernel(
    node_hbm, send_hbm, w_src_hbm, w_dst_hbm, w_out_hbm, bias_hbm,
    node_ref, send_ref, packed_ref, *rest,
):
    *out_refs, bias_ref, sems = rest
    hid = packed_ref.shape[1]
    width = w_src_hbm.shape[0]
    pairs = [(node_hbm, node_ref), (send_hbm, send_ref), (bias_hbm, bias_ref)]
    pairs += [(w_src_hbm, packed_ref.at[pl.ds(0, width)]), (w_dst_hbm, packed_ref.at[pl.ds(width, width)])]
    for k in range(width // hid):
        target = packed_ref.at[pl.ds(2 * width + k * hid, hid)]
        pairs.append((w_out_hbm.at[:, pl.ds(k * hid, hid)], target))
    copies = fetch(sems, *pairs)
    copies[0].wait()
    copies[1].wait()
    node = node_ref[...]
    rows = node.shape[0]
    halo = send_ref.shape[2]
    pieces = []
    for d in range(4):
        pick = one_hot(iota((rows, halo), 0) == send_ref[0, d : d + 1, :])
        pieces.append(dot(pick, node, TN).astype(bf16))
    out_refs[0][...] = pieces[0]
    out_refs[1][...] = pieces[1]
    if len(out_refs) == 3:
        out_refs[2][0:halo, :] = pieces[2]
        out_refs[2][halo:, :] = pieces[3]
    else:
        out_refs[2][...] = pieces[2]
        out_refs[3][...] = pieces[3]
    copies[2].wait()
    bias = bias_ref[...]
    parts = []
    for _ in range(3):
        parts.append(bias.astype(bf16).astype(f32))
        bias = bias - parts[-1]
    parts.append(jnp.zeros((TAIL - 3, hid), f32))
    packed_ref[packed_ref.shape[0] - TAIL :, :] = jnp.concatenate(parts, axis=0).astype(bf16)
    for copy in copies[3:]:
        copy.wait()


def unpacked(ref, width):
    hid = ref.shape[1]
    w_out = [ref[at : at + hid, :] for at in range(2 * width, 3 * width, hid)]
    tail = ref[ref.shape[0] - TAIL :, :].astype(f32)
    bias = tail[0:1] + tail[1:2] + tail[2:3]
    return ref[0:width, :], ref[width : 2 * width, :], jnp.concatenate(w_out, axis=1), bias


def local_kernel(node_ref, packed_ref, other_ref, *refs):
    ins, refs = refs[:N_FETCHED], refs[N_FETCHED:]
    pre_ref, pick_ref, collect_ref, spread_ref, scatter_ref, *refs = refs
    gain_ref, cot_ref, count_ref, src_ref, dst_ref, sems = refs
    copies = fetch(sems, *zip(ins, (src_ref, dst_ref, count_ref, gain_ref, cot_ref)))
    node = node_ref[...]
    rows, width = node.shape
    w_src, w_dst, _, bias = unpacked(packed_ref, width)
    w_src_other, w_dst_other, _, bias_other = unpacked(other_ref, width)
    projected = dot(node, jnp.concatenate([w_src, w_src_other, w_dst, w_dst_other], axis=1))
    both = projected.shape[1] // 2
    projected = jnp.concatenate([projected[:, :both], projected[:, both:]], axis=0)
    high, low = split(projected)
    for copy in copies:
        copy.wait()
    edges = src_ref.shape[1]
    scatter_ref[...] = one_hot(iota(scatter_ref.shape, 0) == src_ref[...])
    used = usable_row(count_ref, edges) > 0
    collect_ref[...] = one_hot((iota((rows, edges), 0) == dst_ref[...]) & used)
    source = columns_of(src_ref[...], 128)
    target = columns_of(dst_ref[...], 128)
    lane = iota(source.shape, 1)
    used = usable_columns(count_ref, edges, 128) > 0
    near = one_hot(source == lane)
    pick_ref[...] = one_hot(source == lane + rows)
    spread_ref[...] = one_hot((target == lane) & used)
    ends = jnp.concatenate([near, one_hot(target == lane)], axis=1)
    pre_ref[...] = dot(ends, high) + dot(ends, low) + jnp.concatenate([bias, bias_other], axis=1)


def twice(x):
    return jnp.concatenate([x, x], axis=1)


def stacked(x):
    return jnp.concatenate(split(x), axis=0)


def edge_kernel(
    geometry,
    node_ref, pre_ref, pick_ref, collect_ref, spread_ref, scatter_ref, packed_ref, other_ref, gain_ref, cot_ref,
    *rest,
):
    peers, chunk, n_halo, paired = geometry
    *rest, out_scratch, back_scratch, pair_scratch = rest
    halo_refs = rest[:n_halo]
    normed_ref, local_ref, target_ref, *message_refs = rest[n_halo:]
    node = node_ref[...]
    rows, width = node.shape
    hid = packed_ref.shape[1]
    halo_rows = jnp.concatenate([r[...] for r in halo_refs], axis=0)
    w_src, _, w_out, _ = unpacked(packed_ref, width)
    w_src_other, _, w_out_other, _ = unpacked(other_ref, width)

    far = stacked(dot(halo_rows, jnp.concatenate([w_src, w_src_other], axis=1)))
    pre = pre_ref[...] + dot(twice(pick_ref[...]), far)
    sig = 0.5 + 0.5 * jnp.tanh(0.5 * pre)
    hidden = dot(collect_ref[...], (pre * sig).astype(bf16))
    pre, sig = pre[:, :hid], sig[:, :hid]
    factor = sig * (1.0 + pre * (1.0 - sig))
    parts = []
    for at, w in ((0, w_out), (hid, w_out_other)):
        high, low = split(hidden[:, at : at + hid])
        parts.append(dot(high, w) + dot(low, w))
    hidden_low = hidden[:, :hid].astype(bf16)
    aggregate = parts[0] + parts[1]

    center = aggregate - jnp.mean(aggregate, axis=1, keepdims=True)
    variance = jnp.mean(center * center, axis=1, keepdims=True)
    inverse = lax.rsqrt(variance + EPSILON)
    normed = center * inverse
    gain = gain_ref[...]
    upstream = cot_ref[...].astype(f32)
    scaled = upstream * gain
    agg_grad = inverse * (
        scaled
        - jnp.mean(scaled, axis=1, keepdims=True)
        - normed * jnp.mean(scaled * normed, axis=1, keepdims=True)
    )
    agg_grad = agg_grad.astype(bf16)
    normed_ref[...] = normed
    gain_part = jnp.sum(upstream * normed, axis=0, keepdims=True)

    act_grad = dot(twice(spread_ref[...]), stacked(dot(agg_grad, w_out, NT)))
    pre_grad = (act_grad * factor).astype(bf16)

    table = jnp.concatenate([node, halo_rows], axis=0)
    by_source = dot(scatter_ref[...], pre_grad)
    by_target = dot(collect_ref[...], pre_grad)
    local_ref[...] = by_source[:rows]
    by_target_low = by_target.astype(bf16)
    by_source_low = by_source.astype(bf16)
    target_ref[...] = by_target_low

    bias_part = jnp.sum(by_target, axis=0, keepdims=True)
    src_part = dot(table, by_source_low, TN).astype(bf16)
    dst_part = dot(node, by_target_low, TN).astype(bf16)
    out_part = dot(hidden_low, agg_grad, TN).astype(bf16)
    vectors = [bias_part] + [gain_part[:, at : at + hid] for at in range(0, width, hid)]
    tail = tail_of(vectors)
    back = by_source_low[rows:]

    if paired:
        send_ref, keep_ref, *out_refs = message_refs
        sub = lax.axis_index("sub")
        mesh = lax.axis_index("mesh")
        lines = len(out_refs)
        halo = back.shape[0] // 4
        first = sub == 0
        pair_scratch[0] = jnp.where(first, dst_part, src_part)
        pair_scratch[1] = jnp.where(first, src_part, dst_part)
        strip = width // lines
        for slot, ref in enumerate((send_ref, keep_ref)):
            for at, k in enumerate((3, 2, 1, 0)):
                start = pl.multiple_of((mesh ^ k) * strip, strip)
                ref[at * strip : (at + 1) * strip, :] = pair_scratch[slot, pl.ds(start, strip), :]
            ref[width : width + TAIL, :] = tail
        send_ref[width + TAIL :, :] = back[2 * halo :]
        back_scratch[...] = back[: 2 * halo]
        out_scratch[...] = out_part
        strip = hid // len(out_refs)
        for k, ref in enumerate(out_refs):
            start = pl.multiple_of((mesh ^ k) * strip, strip)
            ref[0:strip, :] = out_scratch[pl.ds(start, strip), :]
            if k % 2 == 1:
                slot = (mesh + (k // 2) + 1) % 2
                start = pl.multiple_of(slot * halo, halo)
                rows_back = back_scratch[pl.ds(start, halo), :]
                ref[strip:, 0:hid] = rows_back[: halo // 2]
                ref[strip:, hid:] = rows_back[halo // 2 :]
        return

    message_ref, *back_refs = message_refs
    at = 0
    for ref in back_refs:
        ref[...] = back[at : at + ref.shape[0]]
        at += ref.shape[0]
    blocks = [src_part, dst_part]
    for at in range(0, width, hid):
        blocks.append(out_part[:, at : at + hid])
    done = 0
    for block in blocks:
        at = 0
        while at < block.shape[0]:
            peer, offset = divmod(done, chunk)
            take = min(chunk - offset, block.shape[0] - at)
            message_ref[peer, offset : offset + take, :] = block[at : at + take]
            at += take
            done += take
    while done < peers * chunk:
        peer, offset = divmod(done, chunk)
        take = chunk - offset
        message_ref[peer, offset : offset + take, :] = jnp.zeros((take, hid), bf16)
        done += take
    for peer in range(peers):
        message_ref[peer, chunk:, :] = tail


def tail_of(vectors):
    tail = []
    for v in vectors:
        high = v.astype(bf16).astype(f32)
        tail += [high, v - high]
    tail.append(jnp.zeros((TAIL - len(tail), vectors[0].shape[1]), f32))
    return jnp.concatenate(tail, axis=0).astype(bf16)


def tree(terms):
    while len(terms) > 1:
        terms = [terms[i] + terms[i + 1] for i in range(0, len(terms), 2)]
    return terms[0]


def turn_kernel(arrived_ref, keep_ref, *refs):
    full = keep_ref.shape[0]
    total = keep_ref[...].astype(f32) + arrived_ref[0:full, :].astype(f32)
    rows = full - TAIL
    strip = rows // len(refs)
    tail = total[rows:]
    tail = tail_of([tail[at : at + 1] + tail[at + 1 : at + 2] for at in range(0, 6, 2)])
    for k, ref in enumerate(refs):
        ref[0:strip, :] = total[k * strip : (k + 1) * strip].astype(bf16)
        ref[strip:, :] = tail


def line_kernel(*refs):
    *terms, send_ref, keep_ref = refs
    rows, hid = keep_ref.shape
    total = tree([r[0:rows, :].astype(f32) for r in terms])
    first = lax.axis_index("sub") == 0
    left, right = total[:, :hid], total[:, hid:]
    send_ref[...] = jnp.where(first, right, left).astype(bf16)
    keep_ref[...] = jnp.where(first, left, right).astype(bf16)


def own_kernel(*refs):
    *terms, out_keep_ref, out_arrived_ref, own_ref, tail_ref = refs
    total = tree([r[...].astype(f32) for r in terms])
    strip = own_ref.shape[0] - out_keep_ref.shape[0]
    own_ref[0:strip, :] = total[:strip].astype(bf16)
    own_ref[strip:, :] = (out_keep_ref[...].astype(f32) + out_arrived_ref[...].astype(f32)).astype(bf16)
    tail_ref[...] = total[strip:]


def write_vectors(tail, bias_ref, gain_ref):
    bias_ref[...] = tail[0:1] + tail[1:2]
    hid = tail.shape[1]
    for k in range(gain_ref.shape[1] // hid):
        gain_ref[:, k * hid : (k + 1) * hid] = tail[2 + 2 * k : 3 + 2 * k] + tail[3 + 2 * k : 4 + 2 * k]


def relay_kernel(*refs):
    *_, strip_ref, out_ref = refs
    out_ref[...] = strip_ref[...]


def place_kernel(lines, which, a_ref, b_ref, c_ref, d_ref, *refs):
    src_hbm, dst_hbm, out_hbm, src_ref, dst_ref, out_ref, sems = refs[-7:]
    first = lax.axis_index("sub") == 0
    mesh = lax.axis_index("mesh")
    strip, hid = src_ref.shape[1:]
    narrow = out_ref.shape[1]
    copies = []

    def put(ref, hbm, at, rows):
        start = pl.multiple_of((mesh ^ which[at]) * rows, rows)
        copies.append(pltpu.make_async_copy(ref.at[at], hbm.at[pl.ds(start, rows)], sems.at[len(copies)]))
        copies[-1].start()

    for at, (mine_ref, theirs_ref) in enumerate(((a_ref, c_ref), (b_ref, d_ref))):
        mine, theirs = mine_ref[...], theirs_ref[...]
        low = jnp.where(first, mine, theirs).astype(f32)
        high = jnp.where(first, theirs, mine).astype(f32)
        src_ref[at] = low[:strip]
        put(src_ref, src_hbm, at, strip)
        dst_ref[at] = high[:strip]
        put(dst_ref, dst_hbm, at, strip)
        out_ref[at, :, 0:hid] = low[strip:]
        out_ref[at, :, hid:] = high[strip:]
        put(out_ref, out_hbm, at, narrow)
    for copy in copies:
        copy.wait()


def sum_kernel(chunk, arrived_ref, out_ref, bias_ref, gain_ref):
    peers = arrived_ref.shape[0]
    total = arrived_ref[0].astype(f32)
    for peer in range(1, peers):
        total += arrived_ref[peer].astype(f32)
    low = total[:chunk].astype(bf16)
    for peer in range(peers):
        out_ref[peer] = low
    tail = total[chunk:]
    write_vectors(tail, bias_ref, gain_ref)


def unpack_kernel(arrived_ref, src_ref, dst_ref, out_ref):
    hid = src_ref.shape[1]
    rows = src_ref.shape[0]
    src_ref[...] = arrived_ref[0:rows, :].astype(f32)
    dst_ref[...] = arrived_ref[rows : 2 * rows, :].astype(f32)
    at = 2 * rows
    for k in range(out_ref.shape[1] // hid):
        out_ref[:, k * hid : (k + 1) * hid] = arrived_ref[at : at + out_ref.shape[0], :].astype(f32)
        at += out_ref.shape[0]


def node_part(send_ref, local_ref, target_ref, packed_ref, returned, out_ref):
    rows = local_ref.shape[0]
    halo = send_ref.shape[2]
    picks = [one_hot(iota((rows, halo), 0) == send_ref[0, d : d + 1, :]) for d in range(4)]
    total = local_ref[...] + dot(jnp.concatenate(picks, axis=1), jnp.concatenate(returned, axis=0))
    w_src, w_dst, _, _ = unpacked(packed_ref, out_ref.shape[1])
    out_ref[...] = (dot(total.astype(bf16), w_src, NT) + dot(target_ref[...], w_dst, NT)).astype(bf16)


def node_kernel(send_ref, local_ref, target_ref, packed_ref, *rest):
    *back_refs, out_ref = rest
    returned = [r[...] for r in back_refs]
    node_part(send_ref, local_ref, target_ref, packed_ref, returned, out_ref)


def paired_node_kernel(
    send_ref, local_ref, target_ref, packed_ref, three_ref, one_ref, pair_ref, out_ref
):
    even = lax.axis_index("mesh") % 2 == 0
    halo = send_ref.shape[2]
    hid = local_ref.shape[1]
    at = one_ref.shape[0] - halo // 2
    one, three = [
        jnp.concatenate([r[at:, :hid], r[at:, hid:]], axis=0) for r in (one_ref, three_ref)
    ]
    returned = [
        jnp.where(even, one, three), jnp.where(even, three, one), pair_ref[pair_ref.shape[0] - 2 * halo :, :]
    ]
    node_part(send_ref, local_ref, target_ref, packed_ref, returned, out_ref)


def finish_kernel(cot_ref, node_ref, gain_ref, normed_ref, own_ref, other_ref, *rest):
    if len(rest) == 5:
        tail_ref, *rest, bias_out_ref, gain_out_ref = rest
        write_vectors(tail_ref[...], bias_out_ref, gain_out_ref)
    grad_ref, updated_ref = rest
    grad_ref[...] = cot_ref[...].astype(f32) + (
        own_ref[...].astype(f32) + other_ref[...].astype(f32)
    )
    updated_ref[...] = (node_ref[...].astype(f32) + gain_ref[...] * normed_ref[...]).astype(bf16)


VMEM = pl.BlockSpec(memory_space=pltpu.VMEM)
SMEM = pl.BlockSpec(memory_space=pltpu.SMEM)
HBM = pl.BlockSpec(memory_space=pltpu.HBM)


def shape(dims, dtype):
    return jax.ShapeDtypeStruct(dims, dtype)


def call(kernel, outs, *args, specs=None, out_specs=None, flops=10**8, scratch=(), **options):
    return pl.pallas_call(
        kernel,
        out_shape=outs,
        in_specs=specs or [VMEM] * len(args),
        out_specs=out_specs or jax.tree.map(lambda _: VMEM, outs),
        scratch_shapes=scratch,
        **options,
        compiler_params=pltpu.CompilerParams(vmem_limit_bytes=VMEM_LIMIT),
        cost_estimate=pl.CostEstimate(flops=flops, bytes_accessed=10**6, transcendentals=0),
    )(*args)


def shifted(x, axis, by):
    count = lax.axis_size(axis)
    return lax.ppermute(x, axis, [(i, (i + by) % count) for i in range(count)])


def across(x, axis, k):
    count = lax.axis_size(axis)
    return lax.ppermute(x, axis, [(i, i ^ k) for i in range(count)])


def diagonal(x):
    lines, pairs = lax.axis_size("mesh"), lax.axis_size("sub")
    moves = [(m * pairs + p, (m ^ 1) * pairs + (p ^ 1)) for m in range(lines) for p in range(pairs)]
    return lax.ppermute(x, ("mesh", "sub"), moves)


def paired_sums(messages, lines, strip, narrow, width, hid, node_terms):
    send, keep, *outs = messages
    order = range(lines - 1, 0, -1)
    block = shape((strip + TAIL, hid), bf16)
    pair = across(send, "sub", 1)
    out_terms = {k: across(outs[k], "mesh", k) for k in order}
    line = call(turn_kernel, [block] * lines, pair, keep)[::-1]
    line_terms = {k: across(line[k], "mesh", k) for k in order}
    out_send, out_keep = call(
        line_kernel,
        [shape((narrow, hid), bf16)] * 2,
        *[out_terms[k] for k in order], outs[0],
        flops=10**10,
    )
    node_part = node_terms(out_terms[3], out_terms[1], pair)
    own, tail = call(
        own_kernel,
        [shape((strip + narrow, hid), bf16), shape((TAIL, hid), f32)],
        *[line_terms[k] for k in order], line[0], out_keep, across(out_send, "sub", 1),
        flops=10**8,
    )
    mine = {k: across(own, "mesh", k) for k in order}
    mine[0] = own
    theirs = {0: across(own, "sub", 1), 1: diagonal(own)}
    early = (mine[0], mine[1], theirs[0], theirs[1])
    theirs[2] = across(mine[2], "sub", 1)
    theirs[3] = across(mine[3], "sub", 1)
    wholes = [shape((width, hid), f32), shape((width, hid), f32), shape((hid, width), f32)]
    scratch = [
        pltpu.VMEM((2, strip, hid), f32), pltpu.VMEM((2, strip, hid), f32), pltpu.VMEM((2, narrow, width), f32),
        pltpu.SemaphoreType.DMA((6,)),
    ]
    grads = call(
        functools.partial(place_kernel, lines, (0, 1)), wholes, *early,
        out_specs=[HBM] * 3, scratch=scratch, flops=10**8,
    )
    grads = call(
        functools.partial(place_kernel, lines, (2, 3)), wholes,
        mine[2], mine[3], theirs[2], theirs[3], *grads,
        specs=[VMEM] * 4 + [HBM] * 3, out_specs=[HBM] * 3, scratch=scratch,
        input_output_aliases={4: 0, 5: 1, 6: 2},
    )
    return (*grads, tail), node_part


def shards(
    node_state,
    send_rows,
    edge_src,
    edge_dst,
    block_count,
    w_src,
    w_dst,
    hidden_bias,
    w_out,
    norm_gain,
    cotangent,
):
    rows, width = node_state.shape
    hid = w_src.shape[1]
    halo = send_rows.shape[2]
    edges = edge_src.shape[0]
    peers = lax.axis_size("mesh") * lax.axis_size("sub")
    merged = lax.axis_size("sub") == 2
    total_rows = 2 * width + (width // hid) * hid
    chunk = -(-total_rows // (peers * 16)) * 16

    piece = [halo, halo, 2 * halo] if merged else [halo] * 4
    routes = [("mesh", 1), ("mesh", -1), ("sub", 1)] + ([] if merged else [("sub", -1)])
    n_halo = len(piece)

    def in_hbm(x):
        return pltpu.with_memory_space_constraint(x, pltpu.HBM)

    bias = hidden_bias.reshape(1, hid)
    operands = [node_state, send_rows, w_src, w_dst, w_out, bias]
    node, send, packed, *outgoing = call(
        send_kernel,
        [
            shape((rows, width), bf16),
            shape(send_rows.shape, jnp.int32),
            shape((3 * width + TAIL, hid), bf16),
        ]
        + [shape((n, width), bf16) for n in piece],
        *[in_hbm(x) for x in operands],
        specs=[HBM] * len(operands),
        scratch=[pltpu.VMEM((1, hid), f32), pltpu.SemaphoreType.DMA((5 + width // hid,))],
    )
    arrived = [shifted(x, axis, by) for x, (axis, by) in zip(outgoing, routes)]

    other = shifted(packed, "lat", 1)

    fetched = [
        edge_src.reshape(1, edges), edge_dst.reshape(1, edges), block_count,
        norm_gain.reshape(1, width), cotangent,
    ]
    pre, pick, collect, spread, scatter, gain, cot = call(
        local_kernel,
        [
            shape((edges, 2 * hid), f32),
            shape((edges, 4 * halo), bf16),
            shape((rows, edges), bf16),
            shape((edges, rows), bf16),
            shape((rows + 4 * halo, edges), bf16),
            shape((1, width), f32),
            shape((rows, width), bf16),
        ],
        node, packed, other, *[in_hbm(x) for x in fetched],
        specs=[VMEM] * 3 + [HBM] * len(fetched),
        scratch=[
            pltpu.SMEM(block_count.shape, jnp.int32),
            pltpu.VMEM((1, edges), jnp.int32),
            pltpu.VMEM((1, edges), jnp.int32),
            pltpu.SemaphoreType.DMA((N_FETCHED,)),
        ],
    )


    lines = lax.axis_size("mesh")
    paired = merged and lines == 4
    if paired:
        strip = width // lines
        narrow = hid // lines
        rows_of = (width + TAIL + 2 * halo, width + TAIL)
        message_shapes = [shape((n, hid), bf16) for n in rows_of]
        message_shapes += [shape((narrow + k % 2 * (halo // 2), width), bf16) for k in range(lines)]
    else:
        message_shapes = [shape((peers, chunk + TAIL, hid), bf16)]
        message_shapes += [shape((n, hid), bf16) for n in piece]
    normed, local, target, *messages = call(
        functools.partial(edge_kernel, (peers, chunk, n_halo, paired)),
        [shape((rows, width), f32), shape((rows, hid), f32), shape((rows, hid), bf16)]
        + message_shapes,
        node, pre, pick, collect, spread, scatter, packed, other, gain, cot, *arrived,
        scratch=[
            pltpu.VMEM((hid, width), bf16),
            pltpu.VMEM((2 * halo, hid), bf16),
            pltpu.VMEM((2, width, hid), bf16),
        ],
    )

    def node_terms(*returned):
        return call(
            paired_node_kernel if paired else node_kernel,
            shape((rows, width), bf16),
            send, local, target, packed, *returned,
        )

    if paired:
        (src_grad, dst_grad, out_grad, tail), node_part = paired_sums(
            messages, lines, strip, narrow, width, hid, node_terms
        )
    else:
        node_part = node_terms(
            *[shifted(x, axis, -by) for x, (axis, by) in zip(messages[1:], routes)]
        )
        exchanged = lax.all_to_all(messages[0], ("mesh", "sub"), 0, 0)
        reduced, bias_grad, gain_grad = call(
            functools.partial(sum_kernel, chunk),
            [shape((peers, chunk, hid), bf16), shape((1, hid), f32), shape((1, width), f32)],
            exchanged,
        )
        gathered = lax.all_to_all(reduced, ("mesh", "sub"), 0, 0)
        src_grad, dst_grad, out_grad = call(
            unpack_kernel,
            [shape((width, hid), f32), shape((width, hid), f32), shape((hid, width), f32)],
            gathered.reshape(peers * chunk, hid),
        )
    finished = [shape((rows, width), f32), shape((rows, width), bf16)]
    ends = [cot, node, gain, normed, node_part, shifted(node_part, "lat", 1)]
    if paired:
        node_grad, updated, bias_grad, gain_grad = call(
            finish_kernel, finished + [shape((1, hid), f32), shape((1, width), f32)], *ends, tail
        )
    else:
        node_grad, updated = call(finish_kernel, finished, *ends)
    return (
        updated, node_grad, src_grad, dst_grad, out_grad,
        bias_grad.reshape(hid), gain_grad.reshape(width),
    )


def solution(mesh):
    nodes = P(("parts", "mesh", "sub"), None)
    slots = P(("parts", "mesh", "sub"))
    in_specs = (
        nodes,
        P(("parts", "mesh", "sub"), None, None),
        slots,
        slots,
        slots,
        P(None, "lat"),
        P(None, "lat"),
        P("lat"),
        P("lat", None),
        P(),
        nodes,
    )
    out_specs = (
        nodes,
        nodes,
        P("parts", "lat"),
        P("parts", "lat"),
        P(("parts", "lat"), None),
        P(("parts", "lat")),
        P("parts"),
    )
    return jax.shard_map(shards, mesh=mesh, in_specs=in_specs, out_specs=out_specs, check_vma=False)
```

```python
import functools

import jax
import jax.numpy as jnp
from jax import lax
from jax.experimental import pallas as pl
from jax.experimental.pallas import tpu as pltpu
from jax.sharding import PartitionSpec as P

BLOCK = 128
EPSILON = 1e-05
TAIL = 16
N_FETCHED = 5
VMEM_LIMIT = 24 * 1024 * 1024

f32 = jnp.float32
bf16 = jnp.bfloat16

NN = (((1,), (0,)), ((), ()))
NT = (((1,), (1,)), ((), ()))
TN = (((0,), (0,)), ((), ()))


def dot(a, b, dims=NN):
    return lax.dot_general(a, b, dims, preferred_element_type=f32)


def iota(shape, dim):
    return lax.broadcasted_iota(jnp.int32, shape, dim)


def one_hot(condition):
    return jnp.where(condition, 1.0, 0.0).astype(bf16)


def split(x):
    high = x.astype(bf16)
    return high, (x - high.astype(f32)).astype(bf16)


def columns_of(row, lanes):
    return jnp.transpose(jnp.broadcast_to(row, (lanes, row.shape[1])))


def usable_row(count_ref, edges):
    lane = iota((1, BLOCK), 1)
    parts = [lane < count_ref[b] for b in range(edges // BLOCK)]
    return jnp.concatenate([jnp.where(p, 1, 0) for p in parts], axis=1)


def usable_columns(count_ref, edges, lanes):
    sub = iota((BLOCK, lanes), 0)
    return jnp.concatenate(
        [jnp.where(sub < count_ref[b], 1, 0) for b in range(edges // BLOCK)], axis=0
    )


def fetch(sems, *pairs):
    copies = [pltpu.make_async_copy(a, b, sems.at[i]) for i, (a, b) in enumerate(pairs)]
    for copy in copies:
        copy.start()
    return copies


def send_kernel(
    node_hbm, send_hbm, w_src_hbm, w_dst_hbm, w_out_hbm, bias_hbm,
    node_ref, send_ref, packed_ref, *rest,
):
    *out_refs, bias_ref, sems = rest
    hid = packed_ref.shape[1]
    width = w_src_hbm.shape[0]
    pairs = [(node_hbm, node_ref), (send_hbm, send_ref), (bias_hbm, bias_ref)]
    pairs += [(w_src_hbm, packed_ref.at[pl.ds(0, width)]), (w_dst_hbm, packed_ref.at[pl.ds(width, width)])]
    for k in range(width // hid):
        target = packed_ref.at[pl.ds(2 * width + k * hid, hid)]
        pairs.append((w_out_hbm.at[:, pl.ds(k * hid, hid)], target))
    copies = fetch(sems, *pairs)
    copies[0].wait()
    copies[1].wait()
    node = node_ref[...]
    rows = node.shape[0]
    halo = send_ref.shape[2]
    pieces = []
    for d in range(4):
        pick = one_hot(iota((rows, halo), 0) == send_ref[0, d : d + 1, :])
        pieces.append(dot(pick, node, TN).astype(bf16))
    out_refs[0][...] = pieces[0]
    out_refs[1][...] = pieces[1]
    if len(out_refs) == 3:
        out_refs[2][0:halo, :] = pieces[2]
        out_refs[2][halo:, :] = pieces[3]
    else:
        out_refs[2][...] = pieces[2]
        out_refs[3][...] = pieces[3]
    copies[2].wait()
    bias = bias_ref[...]
    parts = []
    for _ in range(3):
        parts.append(bias.astype(bf16).astype(f32))
        bias = bias - parts[-1]
    parts.append(jnp.zeros((TAIL - 3, hid), f32))
    packed_ref[packed_ref.shape[0] - TAIL :, :] = jnp.concatenate(parts, axis=0).astype(bf16)
    for copy in copies[3:]:
        copy.wait()


def unpacked(ref, width):
    hid = ref.shape[1]
    w_out = [ref[at : at + hid, :] for at in range(2 * width, 3 * width, hid)]
    tail = ref[ref.shape[0] - TAIL :, :].astype(f32)
    bias = tail[0:1] + tail[1:2] + tail[2:3]
    return ref[0:width, :], ref[width : 2 * width, :], jnp.concatenate(w_out, axis=1), bias


def local_kernel(node_ref, packed_ref, other_ref, *refs):
    ins, refs = refs[:N_FETCHED], refs[N_FETCHED:]
    pre_ref, pick_ref, collect_ref, spread_ref, scatter_ref, *refs = refs
    gain_ref, cot_ref, count_ref, src_ref, dst_ref, sems = refs
    copies = fetch(sems, *zip(ins, (src_ref, dst_ref, count_ref, gain_ref, cot_ref)))
    node = node_ref[...]
    rows, width = node.shape
    w_src, w_dst, _, bias = unpacked(packed_ref, width)
    w_src_other, w_dst_other, _, bias_other = unpacked(other_ref, width)
    projected = dot(node, jnp.concatenate([w_src, w_src_other, w_dst, w_dst_other], axis=1))
    both = projected.shape[1] // 2
    projected = jnp.concatenate([projected[:, :both], projected[:, both:]], axis=0)
    high, low = split(projected)
    for copy in copies:
        copy.wait()
    edges = src_ref.shape[1]
    scatter_ref[...] = one_hot(iota(scatter_ref.shape, 0) == src_ref[...])
    used = usable_row(count_ref, edges) > 0
    collect_ref[...] = one_hot((iota((rows, edges), 0) == dst_ref[...]) & used)
    source = columns_of(src_ref[...], 128)
    target = columns_of(dst_ref[...], 128)
    lane = iota(source.shape, 1)
    used = usable_columns(count_ref, edges, 128) > 0
    near = one_hot(source == lane)
    pick_ref[...] = one_hot(source == lane + rows)
    spread_ref[...] = one_hot((target == lane) & used)
    ends = jnp.concatenate([near, one_hot(target == lane)], axis=1)
    pre_ref[...] = dot(ends, high) + dot(ends, low) + jnp.concatenate([bias, bias_other], axis=1)


def twice(x):
    return jnp.concatenate([x, x], axis=1)


def stacked(x):
    return jnp.concatenate(split(x), axis=0)


def edge_kernel(
    geometry,
    node_ref, pre_ref, pick_ref, collect_ref, spread_ref, scatter_ref, packed_ref, other_ref, gain_ref, cot_ref,
    *rest,
):
    peers, chunk, n_halo, paired = geometry
    *rest, out_scratch, back_scratch = rest
    halo_refs = rest[:n_halo]
    normed_ref, local_ref, target_ref, *message_refs = rest[n_halo:]
    node = node_ref[...]
    rows, width = node.shape
    hid = packed_ref.shape[1]
    halo_rows = jnp.concatenate([r[...] for r in halo_refs], axis=0)
    w_src, _, w_out, _ = unpacked(packed_ref, width)
    w_src_other, _, w_out_other, _ = unpacked(other_ref, width)

    far = stacked(dot(halo_rows, jnp.concatenate([w_src, w_src_other], axis=1)))
    pre = pre_ref[...] + dot(twice(pick_ref[...]), far)
    sig = 0.5 + 0.5 * jnp.tanh(0.5 * pre)
    hidden = dot(collect_ref[...], (pre * sig).astype(bf16))
    pre, sig = pre[:, :hid], sig[:, :hid]
    factor = sig * (1.0 + pre * (1.0 - sig))
    parts = []
    for at, w in ((0, w_out), (hid, w_out_other)):
        high, low = split(hidden[:, at : at + hid])
        parts.append(dot(high, w) + dot(low, w))
    hidden_low = hidden[:, :hid].astype(bf16)
    aggregate = parts[0] + parts[1]

    center = aggregate - jnp.mean(aggregate, axis=1, keepdims=True)
    variance = jnp.mean(center * center, axis=1, keepdims=True)
    inverse = lax.rsqrt(variance + EPSILON)
    normed = center * inverse
    gain = gain_ref[...]
    upstream = cot_ref[...].astype(f32)
    scaled = upstream * gain
    agg_grad = inverse * (
        scaled
        - jnp.mean(scaled, axis=1, keepdims=True)
        - normed * jnp.mean(scaled * normed, axis=1, keepdims=True)
    )
    agg_grad = agg_grad.astype(bf16)
    normed_ref[...] = normed
    gain_part = jnp.sum(upstream * normed, axis=0, keepdims=True)

    act_grad = dot(twice(spread_ref[...]), stacked(dot(agg_grad, w_out, NT)))
    pre_grad = (act_grad * factor).astype(bf16)

    table = jnp.concatenate([node, halo_rows], axis=0)
    by_source = dot(scatter_ref[...], pre_grad)
    by_target = dot(collect_ref[...], pre_grad)
    local_ref[...] = by_source[:rows]
    by_target_low = by_target.astype(bf16)
    by_source_low = by_source.astype(bf16)
    target_ref[...] = by_target_low

    bias_part = jnp.sum(by_target, axis=0, keepdims=True)
    src_part = dot(table, by_source_low, TN).astype(bf16)
    dst_part = dot(node, by_target_low, TN).astype(bf16)
    out_part = dot(hidden_low, agg_grad, TN).astype(bf16)
    vectors = [bias_part] + [gain_part[:, at : at + hid] for at in range(0, width, hid)]
    tail = tail_of(vectors)
    back = by_source_low[rows:]

    if paired:
        send_ref, keep_ref, *out_refs = message_refs
        sub = lax.axis_index("sub")
        mesh = lax.axis_index("mesh")
        lines = len(out_refs)
        halo = back.shape[0] // 4
        first = sub == 0
        strip = width // lines
        chosen = ((send_ref, dst_part, src_part), (keep_ref, src_part, dst_part))
        for ref, when_first, otherwise in chosen:
            value = jnp.where(first, when_first, otherwise)
            for j in range(lines):
                start = pl.multiple_of((lines - 1 - (mesh ^ j)) * strip, strip)
                ref[pl.ds(start, strip), :] = value[j * strip : (j + 1) * strip]
            ref[width : width + TAIL, :] = tail
        send_ref[width + TAIL :, :] = back[2 * halo :]
        back_scratch[...] = back[: 2 * halo]
        out_scratch[...] = out_part
        strip = hid // len(out_refs)
        for k, ref in enumerate(out_refs):
            start = pl.multiple_of((mesh ^ k) * strip, strip)
            ref[0:strip, :] = out_scratch[pl.ds(start, strip), :]
            if k % 2 == 1:
                slot = (mesh + (k // 2) + 1) % 2
                start = pl.multiple_of(slot * halo, halo)
                rows_back = back_scratch[pl.ds(start, halo), :]
                ref[strip:, 0:hid] = rows_back[: halo // 2]
                ref[strip:, hid:] = rows_back[halo // 2 :]
        return

    message_ref, *back_refs = message_refs
    at = 0
    for ref in back_refs:
        ref[...] = back[at : at + ref.shape[0]]
        at += ref.shape[0]
    blocks = [src_part, dst_part]
    for at in range(0, width, hid):
        blocks.append(out_part[:, at : at + hid])
    done = 0
    for block in blocks:
        at = 0
        while at < block.shape[0]:
            peer, offset = divmod(done, chunk)
            take = min(chunk - offset, block.shape[0] - at)
            message_ref[peer, offset : offset + take, :] = block[at : at + take]
            at += take
            done += take
    while done < peers * chunk:
        peer, offset = divmod(done, chunk)
        take = chunk - offset
        message_ref[peer, offset : offset + take, :] = jnp.zeros((take, hid), bf16)
        done += take
    for peer in range(peers):
        message_ref[peer, chunk:, :] = tail


def tail_of(vectors):
    tail = []
    for v in vectors:
        high = v.astype(bf16).astype(f32)
        tail += [high, v - high]
    tail.append(jnp.zeros((TAIL - len(tail), vectors[0].shape[1]), f32))
    return jnp.concatenate(tail, axis=0).astype(bf16)


def tree(terms):
    while len(terms) > 1:
        terms = [terms[i] + terms[i + 1] for i in range(0, len(terms), 2)]
    return terms[0]


def turn_kernel(arrived_ref, keep_ref, *refs):
    full = keep_ref.shape[0]
    total = keep_ref[...].astype(f32) + arrived_ref[0:full, :].astype(f32)
    rows = full - TAIL
    strip = rows // len(refs)
    tail = total[rows:]
    tail = tail_of([tail[at : at + 1] + tail[at + 1 : at + 2] for at in range(0, 6, 2)])
    for k, ref in enumerate(refs):
        ref[0:strip, :] = total[k * strip : (k + 1) * strip].astype(bf16)
        ref[strip:, :] = tail


def line_kernel(*refs):
    *terms, send_ref, keep_ref = refs
    rows, hid = keep_ref.shape
    total = tree([r[0:rows, :].astype(f32) for r in terms])
    first = lax.axis_index("sub") == 0
    left, right = total[:, :hid], total[:, hid:]
    send_ref[...] = jnp.where(first, right, left).astype(bf16)
    keep_ref[...] = jnp.where(first, left, right).astype(bf16)


def own_kernel(*refs):
    *terms, out_keep_ref, out_arrived_ref, own_ref, tail_ref = refs
    total = tree([r[...].astype(f32) for r in terms])
    strip = own_ref.shape[0] - out_keep_ref.shape[0]
    own_ref[0:strip, :] = total[:strip].astype(bf16)
    own_ref[strip:, :] = (out_keep_ref[...].astype(f32) + out_arrived_ref[...].astype(f32)).astype(bf16)
    tail_ref[...] = total[strip:]


def write_vectors(tail, bias_ref, gain_ref):
    bias_ref[...] = tail[0:1] + tail[1:2]
    hid = tail.shape[1]
    for k in range(gain_ref.shape[1] // hid):
        gain_ref[:, k * hid : (k + 1) * hid] = tail[2 + 2 * k : 3 + 2 * k] + tail[3 + 2 * k : 4 + 2 * k]


def place_kernel(which, *refs):
    count = len(which)
    src_hbm, dst_hbm, out_hbm, src_ref, dst_ref, out_ref, sems = refs[-7:]
    first = lax.axis_index("sub") == 0
    mesh = lax.axis_index("mesh")
    strip, hid = src_ref.shape[1:]
    narrow = out_ref.shape[1]
    copies = []

    def put(ref, hbm, at, rows):
        start = pl.multiple_of((mesh ^ which[at]) * rows, rows)
        copies.append(pltpu.make_async_copy(ref.at[at], hbm.at[pl.ds(start, rows)], sems.at[len(copies)]))
        copies[-1].start()

    for at in range(count):
        mine, theirs = refs[at][...], refs[count + at][...]
        low = jnp.where(first, mine, theirs).astype(f32)
        high = jnp.where(first, theirs, mine).astype(f32)
        src_ref[at] = low[:strip]
        put(src_ref, src_hbm, at, strip)
        dst_ref[at] = high[:strip]
        put(dst_ref, dst_hbm, at, strip)
        out_ref[at, :, 0:hid] = low[strip:]
        out_ref[at, :, hid:] = high[strip:]
        put(out_ref, out_hbm, at, narrow)
    for copy in copies:
        copy.wait()


def sum_kernel(chunk, arrived_ref, out_ref, bias_ref, gain_ref):
    peers = arrived_ref.shape[0]
    total = arrived_ref[0].astype(f32)
    for peer in range(1, peers):
        total += arrived_ref[peer].astype(f32)
    low = total[:chunk].astype(bf16)
    for peer in range(peers):
        out_ref[peer] = low
    tail = total[chunk:]
    write_vectors(tail, bias_ref, gain_ref)


def unpack_kernel(arrived_ref, src_ref, dst_ref, out_ref):
    hid = src_ref.shape[1]
    rows = src_ref.shape[0]
    src_ref[...] = arrived_ref[0:rows, :].astype(f32)
    dst_ref[...] = arrived_ref[rows : 2 * rows, :].astype(f32)
    at = 2 * rows
    for k in range(out_ref.shape[1] // hid):
        out_ref[:, k * hid : (k + 1) * hid] = arrived_ref[at : at + out_ref.shape[0], :].astype(f32)
        at += out_ref.shape[0]


def node_part(send_ref, local_ref, target_ref, packed_ref, returned, out_ref):
    rows = local_ref.shape[0]
    halo = send_ref.shape[2]
    picks = [one_hot(iota((rows, halo), 0) == send_ref[0, d : d + 1, :]) for d in range(4)]
    total = local_ref[...] + dot(jnp.concatenate(picks, axis=1), jnp.concatenate(returned, axis=0))
    w_src, w_dst, _, _ = unpacked(packed_ref, out_ref.shape[1])
    out_ref[...] = (dot(total.astype(bf16), w_src, NT) + dot(target_ref[...], w_dst, NT)).astype(bf16)


def node_kernel(send_ref, local_ref, target_ref, packed_ref, *rest):
    *back_refs, out_ref = rest
    returned = [r[...] for r in back_refs]
    node_part(send_ref, local_ref, target_ref, packed_ref, returned, out_ref)


def paired_node_kernel(
    send_ref, local_ref, target_ref, packed_ref, three_ref, one_ref, pair_ref, out_ref
):
    even = lax.axis_index("mesh") % 2 == 0
    halo = send_ref.shape[2]
    hid = local_ref.shape[1]
    at = one_ref.shape[0] - halo // 2
    one, three = [
        jnp.concatenate([r[at:, :hid], r[at:, hid:]], axis=0) for r in (one_ref, three_ref)
    ]
    returned = [
        jnp.where(even, one, three), jnp.where(even, three, one), pair_ref[pair_ref.shape[0] - 2 * halo :, :]
    ]
    node_part(send_ref, local_ref, target_ref, packed_ref, returned, out_ref)


def finish_kernel(cot_ref, node_ref, gain_ref, normed_ref, own_ref, other_ref, *rest):
    if len(rest) == 5:
        tail_ref, *rest, bias_out_ref, gain_out_ref = rest
        write_vectors(tail_ref[...], bias_out_ref, gain_out_ref)
    grad_ref, updated_ref = rest
    grad_ref[...] = cot_ref[...].astype(f32) + (
        own_ref[...].astype(f32) + other_ref[...].astype(f32)
    )
    updated_ref[...] = (node_ref[...].astype(f32) + gain_ref[...] * normed_ref[...]).astype(bf16)


VMEM = pl.BlockSpec(memory_space=pltpu.VMEM)
SMEM = pl.BlockSpec(memory_space=pltpu.SMEM)
HBM = pl.BlockSpec(memory_space=pltpu.HBM)


def shape(dims, dtype):
    return jax.ShapeDtypeStruct(dims, dtype)


def call(kernel, outs, *args, specs=None, out_specs=None, flops=10**8, scratch=(), **options):
    return pl.pallas_call(
        kernel,
        out_shape=outs,
        in_specs=specs or [VMEM] * len(args),
        out_specs=out_specs or jax.tree.map(lambda _: VMEM, outs),
        scratch_shapes=scratch,
        **options,
        compiler_params=pltpu.CompilerParams(vmem_limit_bytes=VMEM_LIMIT),
        cost_estimate=pl.CostEstimate(flops=flops, bytes_accessed=10**6, transcendentals=0),
    )(*args)


def shifted(x, axis, by):
    count = lax.axis_size(axis)
    return lax.ppermute(x, axis, [(i, (i + by) % count) for i in range(count)])


def across(x, axis, k):
    count = lax.axis_size(axis)
    return lax.ppermute(x, axis, [(i, i ^ k) for i in range(count)])


def diagonal(x):
    lines, pairs = lax.axis_size("mesh"), lax.axis_size("sub")
    moves = [(m * pairs + p, (m ^ 1) * pairs + (p ^ 1)) for m in range(lines) for p in range(pairs)]
    return lax.ppermute(x, ("mesh", "sub"), moves)


def paired_sums(messages, lines, strip, narrow, width, hid, node_terms):
    send, keep, *outs = messages
    order = range(lines - 1, 0, -1)
    block = shape((strip + TAIL, hid), bf16)
    pair = across(send, "sub", 1)
    out_terms = {k: across(outs[k], "mesh", k) for k in order}
    line = call(turn_kernel, [block] * lines, pair, keep)[::-1]
    line_terms = {k: across(line[k], "mesh", k) for k in order}
    out_send, out_keep = call(
        line_kernel,
        [shape((narrow, hid), bf16)] * 2,
        *[out_terms[k] for k in order], outs[0],
        flops=10**10,
    )
    node_part = node_terms(out_terms[3], out_terms[1], pair)
    own, tail = call(
        own_kernel,
        [shape((strip + narrow, hid), bf16), shape((TAIL, hid), f32)],
        *[line_terms[k] for k in order], line[0], out_keep, across(out_send, "sub", 1),
        flops=10**8,
    )
    mine = {k: across(own, "mesh", k) for k in order}
    mine[0] = own
    theirs = {0: across(own, "sub", 1), 1: diagonal(own)}
    theirs |= {k: across(mine[k], "sub", 1) for k in (3, 2)}
    wholes = [shape((width, hid), f32), shape((width, hid), f32), shape((hid, width), f32)]

    def placed(which, *before):
        count = len(which)
        return call(
            functools.partial(place_kernel, which), wholes,
            *[mine[k] for k in which], *[theirs[k] for k in which], *before,
            specs=[VMEM] * (2 * count) + [HBM] * len(before),
            out_specs=[HBM] * 3,
            scratch=[
                pltpu.VMEM((count, strip, hid), f32), pltpu.VMEM((count, strip, hid), f32),
                pltpu.VMEM((count, narrow, width), f32), pltpu.SemaphoreType.DMA((3 * count,)),
            ],
            input_output_aliases={2 * count + i: i for i in range(len(before))},
        )

    grads = placed((2,), *placed((0,1,3)))
    return (*grads, tail), node_part


def shards(
    node_state,
    send_rows,
    edge_src,
    edge_dst,
    block_count,
    w_src,
    w_dst,
    hidden_bias,
    w_out,
    norm_gain,
    cotangent,
):
    rows, width = node_state.shape
    hid = w_src.shape[1]
    halo = send_rows.shape[2]
    edges = edge_src.shape[0]
    peers = lax.axis_size("mesh") * lax.axis_size("sub")
    merged = lax.axis_size("sub") == 2
    total_rows = 2 * width + (width // hid) * hid
    chunk = -(-total_rows // (peers * 16)) * 16

    piece = [halo, halo, 2 * halo] if merged else [halo] * 4
    routes = [("mesh", 1), ("mesh", -1), ("sub", 1)] + ([] if merged else [("sub", -1)])
    n_halo = len(piece)

    def in_hbm(x):
        return pltpu.with_memory_space_constraint(x, pltpu.HBM)

    bias = hidden_bias.reshape(1, hid)
    operands = [node_state, send_rows, w_src, w_dst, w_out, bias]
    node, send, packed, *outgoing = call(
        send_kernel,
        [
            shape((rows, width), bf16),
            shape(send_rows.shape, jnp.int32),
            shape((3 * width + TAIL, hid), bf16),
        ]
        + [shape((n, width), bf16) for n in piece],
        *[in_hbm(x) for x in operands],
        specs=[HBM] * len(operands),
        scratch=[pltpu.VMEM((1, hid), f32), pltpu.SemaphoreType.DMA((5 + width // hid,))],
    )
    arrived = [shifted(x, axis, by) for x, (axis, by) in zip(outgoing, routes)]

    other = shifted(packed, "lat", 1)

    fetched = [
        edge_src.reshape(1, edges), edge_dst.reshape(1, edges), block_count,
        norm_gain.reshape(1, width), cotangent,
    ]
    pre, pick, collect, spread, scatter, gain, cot = call(
        local_kernel,
        [
            shape((edges, 2 * hid), f32),
            shape((edges, 4 * halo), bf16),
            shape((rows, edges), bf16),
            shape((edges, rows), bf16),
            shape((rows + 4 * halo, edges), bf16),
            shape((1, width), f32),
            shape((rows, width), bf16),
        ],
        node, packed, other, *[in_hbm(x) for x in fetched],
        specs=[VMEM] * 3 + [HBM] * len(fetched),
        scratch=[
            pltpu.SMEM(block_count.shape, jnp.int32),
            pltpu.VMEM((1, edges), jnp.int32),
            pltpu.VMEM((1, edges), jnp.int32),
            pltpu.SemaphoreType.DMA((N_FETCHED,)),
        ],
    )


    lines = lax.axis_size("mesh")
    paired = merged and lines == 4
    if paired:
        strip = width // lines
        narrow = hid // lines
        rows_of = (width + TAIL + 2 * halo, width + TAIL)
        message_shapes = [shape((n, hid), bf16) for n in rows_of]
        message_shapes += [shape((narrow + k % 2 * (halo // 2), width), bf16) for k in range(lines)]
    else:
        message_shapes = [shape((peers, chunk + TAIL, hid), bf16)]
        message_shapes += [shape((n, hid), bf16) for n in piece]
    normed, local, target, *messages = call(
        functools.partial(edge_kernel, (peers, chunk, n_halo, paired)),
        [shape((rows, width), f32), shape((rows, hid), f32), shape((rows, hid), bf16)]
        + message_shapes,
        node, pre, pick, collect, spread, scatter, packed, other, gain, cot, *arrived,
        scratch=[
            pltpu.VMEM((hid, width), bf16),
            pltpu.VMEM((2 * halo, hid), bf16),
        ],
    )

    def node_terms(*returned):
        return call(
            paired_node_kernel if paired else node_kernel,
            shape((rows, width), bf16),
            send, local, target, packed, *returned,
        )

    if paired:
        (src_grad, dst_grad, out_grad, tail), node_part = paired_sums(
            messages, lines, strip, narrow, width, hid, node_terms
        )
    else:
        node_part = node_terms(
            *[shifted(x, axis, -by) for x, (axis, by) in zip(messages[1:], routes)]
        )
        exchanged = lax.all_to_all(messages[0], ("mesh", "sub"), 0, 0)
        reduced, bias_grad, gain_grad = call(
            functools.partial(sum_kernel, chunk),
            [shape((peers, chunk, hid), bf16), shape((1, hid), f32), shape((1, width), f32)],
            exchanged,
        )
        gathered = lax.all_to_all(reduced, ("mesh", "sub"), 0, 0)
        src_grad, dst_grad, out_grad = call(
            unpack_kernel,
            [shape((width, hid), f32), shape((width, hid), f32), shape((hid, width), f32)],
            gathered.reshape(peers * chunk, hid),
        )
    finished = [shape((rows, width), f32), shape((rows, width), bf16)]
    ends = [cot, node, gain, normed, node_part, shifted(node_part, "lat", 1)]
    if paired:
        node_grad, updated, bias_grad, gain_grad = call(
            finish_kernel, finished + [shape((1, hid), f32), shape((1, width), f32)], *ends, tail
        )
    else:
        node_grad, updated = call(finish_kernel, finished, *ends)
    return (
        updated, node_grad, src_grad, dst_grad, out_grad,
        bias_grad.reshape(hid), gain_grad.reshape(width),
    )


def solution(mesh):
    nodes = P(("parts", "mesh", "sub"), None)
    slots = P(("parts", "mesh", "sub"))
    in_specs = (
        nodes,
        P(("parts", "mesh", "sub"), None, None),
        slots,
        slots,
        slots,
        P(None, "lat"),
        P(None, "lat"),
        P("lat"),
        P("lat", None),
        P(),
        nodes,
    )
    out_specs = (
        nodes,
        nodes,
        P("parts", "lat"),
        P("parts", "lat"),
        P(("parts", "lat"), None),
        P(("parts", "lat")),
        P("parts"),
    )
    return jax.shard_map(shards, mesh=mesh, in_specs=in_specs, out_specs=out_specs, check_vma=False)
```

```python
import functools

import jax
import jax.numpy as jnp
from jax import lax
from jax.experimental import pallas as pl
from jax.experimental.pallas import tpu as pltpu
from jax.sharding import PartitionSpec as P

BLOCK = 128
EPSILON = 1e-05
TAIL = 16
N_FETCHED = 5
VMEM_LIMIT = 24 * 1024 * 1024

f32 = jnp.float32
bf16 = jnp.bfloat16

NN = (((1,), (0,)), ((), ()))
NT = (((1,), (1,)), ((), ()))
TN = (((0,), (0,)), ((), ()))


def dot(a, b, dims=NN):
    return lax.dot_general(a, b, dims, preferred_element_type=f32)


def iota(shape, dim):
    return lax.broadcasted_iota(jnp.int32, shape, dim)


def one_hot(condition):
    return jnp.where(condition, 1.0, 0.0).astype(bf16)


def split(x):
    high = x.astype(bf16)
    return high, (x - high.astype(f32)).astype(bf16)


def columns_of(row, lanes):
    return jnp.transpose(jnp.broadcast_to(row, (lanes, row.shape[1])))


def usable_row(count_ref, edges):
    lane = iota((1, BLOCK), 1)
    parts = [lane < count_ref[b] for b in range(edges // BLOCK)]
    return jnp.concatenate([jnp.where(p, 1, 0) for p in parts], axis=1)


def usable_columns(count_ref, edges, lanes):
    sub = iota((BLOCK, lanes), 0)
    return jnp.concatenate(
        [jnp.where(sub < count_ref[b], 1, 0) for b in range(edges // BLOCK)], axis=0
    )


def fetch(sems, *pairs):
    copies = [pltpu.make_async_copy(a, b, sems.at[i]) for i, (a, b) in enumerate(pairs)]
    for copy in copies:
        copy.start()
    return copies


def send_kernel(
    node_hbm, send_hbm, w_src_hbm, w_dst_hbm, w_out_hbm, bias_hbm,
    node_ref, send_ref, packed_ref, *rest,
):
    *out_refs, bias_ref, sems = rest
    hid = packed_ref.shape[1]
    width = w_src_hbm.shape[0]
    pairs = [(node_hbm, node_ref), (send_hbm, send_ref), (bias_hbm, bias_ref)]
    pairs += [(w_src_hbm, packed_ref.at[pl.ds(0, width)]), (w_dst_hbm, packed_ref.at[pl.ds(width, width)])]
    for k in range(width // hid):
        target = packed_ref.at[pl.ds(2 * width + k * hid, hid)]
        pairs.append((w_out_hbm.at[:, pl.ds(k * hid, hid)], target))
    copies = fetch(sems, *pairs)
    copies[0].wait()
    copies[1].wait()
    node = node_ref[...]
    rows = node.shape[0]
    halo = send_ref.shape[2]
    pieces = []
    for d in range(4):
        pick = one_hot(iota((rows, halo), 0) == send_ref[0, d : d + 1, :])
        pieces.append(dot(pick, node, TN).astype(bf16))
    out_refs[0][...] = pieces[0]
    out_refs[1][...] = pieces[1]
    if len(out_refs) == 3:
        out_refs[2][0:halo, :] = pieces[2]
        out_refs[2][halo:, :] = pieces[3]
    else:
        out_refs[2][...] = pieces[2]
        out_refs[3][...] = pieces[3]
    copies[2].wait()
    bias = bias_ref[...]
    parts = []
    for _ in range(3):
        parts.append(bias.astype(bf16).astype(f32))
        bias = bias - parts[-1]
    parts.append(jnp.zeros((TAIL - 3, hid), f32))
    packed_ref[packed_ref.shape[0] - TAIL :, :] = jnp.concatenate(parts, axis=0).astype(bf16)
    for copy in copies[3:]:
        copy.wait()


def unpacked(ref, width):
    hid = ref.shape[1]
    w_out = [ref[at : at + hid, :] for at in range(2 * width, 3 * width, hid)]
    tail = ref[ref.shape[0] - TAIL :, :].astype(f32)
    bias = tail[0:1] + tail[1:2] + tail[2:3]
    return ref[0:width, :], ref[width : 2 * width, :], jnp.concatenate(w_out, axis=1), bias


def local_kernel(node_ref, packed_ref, other_ref, *refs):
    ins, refs = refs[:N_FETCHED], refs[N_FETCHED:]
    pre_ref, pick_ref, collect_ref, spread_ref, scatter_ref, *refs = refs
    gain_ref, cot_ref, count_ref, src_ref, dst_ref, sems = refs
    copies = fetch(sems, *zip(ins, (src_ref, dst_ref, count_ref, gain_ref, cot_ref)))
    node = node_ref[...]
    rows, width = node.shape
    w_src, w_dst, _, bias = unpacked(packed_ref, width)
    w_src_other, w_dst_other, _, bias_other = unpacked(other_ref, width)
    projected = dot(node, jnp.concatenate([w_src, w_src_other, w_dst, w_dst_other], axis=1))
    both = projected.shape[1] // 2
    projected = jnp.concatenate([projected[:, :both], projected[:, both:]], axis=0)
    high, low = split(projected)
    for copy in copies:
        copy.wait()
    edges = src_ref.shape[1]
    scatter_ref[...] = one_hot(iota(scatter_ref.shape, 0) == src_ref[...])
    used = usable_row(count_ref, edges) > 0
    collect_ref[...] = one_hot((iota((rows, edges), 0) == dst_ref[...]) & used)
    source = columns_of(src_ref[...], 128)
    target = columns_of(dst_ref[...], 128)
    lane = iota(source.shape, 1)
    used = usable_columns(count_ref, edges, 128) > 0
    near = one_hot(source == lane)
    pick_ref[...] = one_hot(source == lane + rows)
    spread_ref[...] = one_hot((target == lane) & used)
    ends = jnp.concatenate([near, one_hot(target == lane)], axis=1)
    pre_ref[...] = dot(ends, high) + dot(ends, low) + jnp.concatenate([bias, bias_other], axis=1)


def twice(x):
    return jnp.concatenate([x, x], axis=1)


def stacked(x):
    return jnp.concatenate(split(x), axis=0)


def edge_kernel(
    geometry,
    node_ref, pre_ref, pick_ref, collect_ref, spread_ref, scatter_ref, packed_ref, other_ref, gain_ref, cot_ref,
    *rest,
):
    peers, chunk, n_halo, paired = geometry
    *rest, out_scratch, back_scratch = rest
    halo_refs = rest[:n_halo]
    normed_ref, local_ref, target_ref, *message_refs = rest[n_halo:]
    node = node_ref[...]
    rows, width = node.shape
    hid = packed_ref.shape[1]
    halo_rows = jnp.concatenate([r[...] for r in halo_refs], axis=0)
    w_src, _, w_out, _ = unpacked(packed_ref, width)
    w_src_other, _, w_out_other, _ = unpacked(other_ref, width)

    far = stacked(dot(halo_rows, jnp.concatenate([w_src, w_src_other], axis=1)))
    pre = pre_ref[...] + dot(twice(pick_ref[...]), far)
    sig = 0.5 + 0.5 * jnp.tanh(0.5 * pre)
    hidden = dot(collect_ref[...], (pre * sig).astype(bf16))
    pre, sig = pre[:, :hid], sig[:, :hid]
    factor = sig * (1.0 + pre * (1.0 - sig))
    parts = []
    for at, w in ((0, w_out), (hid, w_out_other)):
        high, low = split(hidden[:, at : at + hid])
        parts.append(dot(high, w) + dot(low, w))
    hidden_low = hidden[:, :hid].astype(bf16)
    aggregate = parts[0] + parts[1]

    center = aggregate - jnp.mean(aggregate, axis=1, keepdims=True)
    variance = jnp.mean(center * center, axis=1, keepdims=True)
    inverse = lax.rsqrt(variance + EPSILON)
    normed = center * inverse
    gain = gain_ref[...]
    upstream = cot_ref[...].astype(f32)
    scaled = upstream * gain
    agg_grad = inverse * (
        scaled
        - jnp.mean(scaled, axis=1, keepdims=True)
        - normed * jnp.mean(scaled * normed, axis=1, keepdims=True)
    )
    agg_grad = agg_grad.astype(bf16)
    normed_ref[...] = normed
    gain_part = jnp.sum(upstream * normed, axis=0, keepdims=True)

    act_grad = dot(twice(spread_ref[...]), stacked(dot(agg_grad, w_out, NT)))
    pre_grad = (act_grad * factor).astype(bf16)

    table = jnp.concatenate([node, halo_rows], axis=0)
    by_source = dot(scatter_ref[...], pre_grad)
    by_target = dot(collect_ref[...], pre_grad)
    local_ref[...] = by_source[:rows]
    by_target_low = by_target.astype(bf16)
    by_source_low = by_source.astype(bf16)
    target_ref[...] = by_target_low

    bias_part = jnp.sum(by_target, axis=0, keepdims=True)
    src_part = dot(table, by_source_low, TN).astype(bf16)
    dst_part = dot(node, by_target_low, TN).astype(bf16)
    out_part = dot(hidden_low, agg_grad, TN).astype(bf16)
    vectors = [bias_part] + [gain_part[:, at : at + hid] for at in range(0, width, hid)]
    tail = tail_of(vectors)
    back = by_source_low[rows:]

    if paired:
        send_ref, keep_ref, *out_refs = message_refs
        sub = lax.axis_index("sub")
        mesh = lax.axis_index("mesh")
        lines = len(out_refs)
        halo = back.shape[0] // 4
        first = sub == 0
        strip = width // lines
        chosen = ((send_ref, dst_part, src_part), (keep_ref, src_part, dst_part))
        for ref, when_first, otherwise in chosen:
            value = jnp.where(first, when_first, otherwise)
            for j in range(lines):
                start = pl.multiple_of((lines - 1 - (mesh ^ j)) * strip, strip)
                ref[pl.ds(start, strip), :] = value[j * strip : (j + 1) * strip]
            ref[width : width + TAIL, :] = tail
        send_ref[width + TAIL :, :] = back[2 * halo :]
        back_scratch[...] = back[: 2 * halo]
        out_scratch[...] = out_part
        strip = hid // len(out_refs)
        for k, ref in enumerate(out_refs):
            start = pl.multiple_of((mesh ^ k) * strip, strip)
            ref[0:strip, :] = out_scratch[pl.ds(start, strip), :]
            if k % 2 == 1:
                slot = (mesh + (k // 2) + 1) % 2
                start = pl.multiple_of(slot * halo, halo)
                rows_back = back_scratch[pl.ds(start, halo), :]
                ref[strip:, 0:hid] = rows_back[: halo // 2]
                ref[strip:, hid:] = rows_back[halo // 2 :]
        return

    message_ref, *back_refs = message_refs
    at = 0
    for ref in back_refs:
        ref[...] = back[at : at + ref.shape[0]]
        at += ref.shape[0]
    blocks = [src_part, dst_part]
    for at in range(0, width, hid):
        blocks.append(out_part[:, at : at + hid])
    done = 0
    for block in blocks:
        at = 0
        while at < block.shape[0]:
            peer, offset = divmod(done, chunk)
            take = min(chunk - offset, block.shape[0] - at)
            message_ref[peer, offset : offset + take, :] = block[at : at + take]
            at += take
            done += take
    while done < peers * chunk:
        peer, offset = divmod(done, chunk)
        take = chunk - offset
        message_ref[peer, offset : offset + take, :] = jnp.zeros((take, hid), bf16)
        done += take
    for peer in range(peers):
        message_ref[peer, chunk:, :] = tail


def tail_of(vectors):
    tail = []
    for v in vectors:
        high = v.astype(bf16).astype(f32)
        tail += [high, v - high]
    tail.append(jnp.zeros((TAIL - len(tail), vectors[0].shape[1]), f32))
    return jnp.concatenate(tail, axis=0).astype(bf16)


def tree(terms):
    while len(terms) > 1:
        terms = [terms[i] + terms[i + 1] for i in range(0, len(terms), 2)]
    return terms[0]


def turn_kernel(arrived_ref, keep_ref, *refs):
    full = keep_ref.shape[0]
    total = keep_ref[...].astype(f32) + arrived_ref[0:full, :].astype(f32)
    rows = full - TAIL
    strip = rows // len(refs)
    tail = total[rows:]
    tail = tail_of([tail[at : at + 1] + tail[at + 1 : at + 2] for at in range(0, 6, 2)])
    for k, ref in enumerate(refs):
        ref[0:strip, :] = total[k * strip : (k + 1) * strip].astype(bf16)
        ref[strip:, :] = tail


def line_kernel(*refs):
    *terms, send_ref, keep_ref = refs
    rows, hid = keep_ref.shape
    total = tree([r[0:rows, :].astype(f32) for r in terms])
    first = lax.axis_index("sub") == 0
    left, right = total[:, :hid], total[:, hid:]
    send_ref[...] = jnp.where(first, right, left).astype(bf16)
    keep_ref[...] = jnp.where(first, left, right).astype(bf16)


def own_kernel(*refs):
    *terms, out_keep_ref, out_arrived_ref, own_ref, tail_ref = refs
    total = tree([r[...].astype(f32) for r in terms])
    strip = own_ref.shape[0] - out_keep_ref.shape[0]
    own_ref[0:strip, :] = total[:strip].astype(bf16)
    own_ref[strip:, :] = (out_keep_ref[...].astype(f32) + out_arrived_ref[...].astype(f32)).astype(bf16)
    tail_ref[...] = total[strip:]


def write_vectors(tail, bias_ref, gain_ref):
    bias_ref[...] = tail[0:1] + tail[1:2]
    hid = tail.shape[1]
    for k in range(gain_ref.shape[1] // hid):
        gain_ref[:, k * hid : (k + 1) * hid] = tail[2 + 2 * k : 3 + 2 * k] + tail[3 + 2 * k : 4 + 2 * k]


def place_kernel(which, *refs):
    count = len(which)
    src_hbm, dst_hbm, out_hbm, src_ref, dst_ref, out_ref, sems = refs[-7:]
    first = lax.axis_index("sub") == 0
    mesh = lax.axis_index("mesh")
    strip, hid = src_ref.shape[1:]
    narrow = out_ref.shape[1]
    copies = []

    def put(ref, hbm, at, rows):
        start = pl.multiple_of((mesh ^ which[at]) * rows, rows)
        copies.append(pltpu.make_async_copy(ref.at[at], hbm.at[pl.ds(start, rows)], sems.at[len(copies)]))
        copies[-1].start()

    for at in range(count):
        mine, theirs = refs[at][...], refs[count + at][...]
        low = jnp.where(first, mine, theirs).astype(f32)
        high = jnp.where(first, theirs, mine).astype(f32)
        src_ref[at] = low[:strip]
        put(src_ref, src_hbm, at, strip)
        dst_ref[at] = high[:strip]
        put(dst_ref, dst_hbm, at, strip)
        out_ref[at, :, 0:hid] = low[strip:]
        out_ref[at, :, hid:] = high[strip:]
        put(out_ref, out_hbm, at, narrow)
    for copy in copies:
        copy.wait()


def sum_kernel(chunk, arrived_ref, out_ref, bias_ref, gain_ref):
    peers = arrived_ref.shape[0]
    total = arrived_ref[0].astype(f32)
    for peer in range(1, peers):
        total += arrived_ref[peer].astype(f32)
    low = total[:chunk].astype(bf16)
    for peer in range(peers):
        out_ref[peer] = low
    tail = total[chunk:]
    write_vectors(tail, bias_ref, gain_ref)


def unpack_kernel(arrived_ref, src_ref, dst_ref, out_ref):
    hid = src_ref.shape[1]
    rows = src_ref.shape[0]
    src_ref[...] = arrived_ref[0:rows, :].astype(f32)
    dst_ref[...] = arrived_ref[rows : 2 * rows, :].astype(f32)
    at = 2 * rows
    for k in range(out_ref.shape[1] // hid):
        out_ref[:, k * hid : (k + 1) * hid] = arrived_ref[at : at + out_ref.shape[0], :].astype(f32)
        at += out_ref.shape[0]


def node_part(send_ref, local_ref, target_ref, packed_ref, returned, out_ref):
    rows = local_ref.shape[0]
    halo = send_ref.shape[2]
    picks = [one_hot(iota((rows, halo), 0) == send_ref[0, d : d + 1, :]) for d in range(4)]
    total = local_ref[...] + dot(jnp.concatenate(picks, axis=1), jnp.concatenate(returned, axis=0))
    w_src, w_dst, _, _ = unpacked(packed_ref, out_ref.shape[1])
    out_ref[...] = (dot(total.astype(bf16), w_src, NT) + dot(target_ref[...], w_dst, NT)).astype(bf16)


def node_kernel(send_ref, local_ref, target_ref, packed_ref, *rest):
    *back_refs, out_ref = rest
    returned = [r[...] for r in back_refs]
    node_part(send_ref, local_ref, target_ref, packed_ref, returned, out_ref)


def paired_node_kernel(
    send_ref, local_ref, target_ref, packed_ref, three_ref, one_ref, pair_ref, out_ref
):
    even = lax.axis_index("mesh") % 2 == 0
    halo = send_ref.shape[2]
    hid = local_ref.shape[1]
    at = one_ref.shape[0] - halo // 2
    one, three = [
        jnp.concatenate([r[at:, :hid], r[at:, hid:]], axis=0) for r in (one_ref, three_ref)
    ]
    returned = [
        jnp.where(even, one, three), jnp.where(even, three, one), pair_ref[pair_ref.shape[0] - 2 * halo :, :]
    ]
    node_part(send_ref, local_ref, target_ref, packed_ref, returned, out_ref)


def finish_kernel(cot_ref, node_ref, gain_ref, normed_ref, own_ref, other_ref, *rest):
    if len(rest) == 5:
        tail_ref, *rest, bias_out_ref, gain_out_ref = rest
        write_vectors(tail_ref[...], bias_out_ref, gain_out_ref)
    grad_ref, updated_ref = rest
    grad_ref[...] = cot_ref[...].astype(f32) + (
        own_ref[...].astype(f32) + other_ref[...].astype(f32)
    )
    updated_ref[...] = (node_ref[...].astype(f32) + gain_ref[...] * normed_ref[...]).astype(bf16)


VMEM = pl.BlockSpec(memory_space=pltpu.VMEM)
SMEM = pl.BlockSpec(memory_space=pltpu.SMEM)
HBM = pl.BlockSpec(memory_space=pltpu.HBM)


def shape(dims, dtype):
    return jax.ShapeDtypeStruct(dims, dtype)


def call(kernel, outs, *args, specs=None, out_specs=None, flops=10**8, scratch=(), **options):
    return pl.pallas_call(
        kernel,
        out_shape=outs,
        in_specs=specs or [VMEM] * len(args),
        out_specs=out_specs or jax.tree.map(lambda _: VMEM, outs),
        scratch_shapes=scratch,
        **options,
        compiler_params=pltpu.CompilerParams(vmem_limit_bytes=VMEM_LIMIT),
        cost_estimate=pl.CostEstimate(flops=flops, bytes_accessed=10**6, transcendentals=0),
    )(*args)


def shifted(x, axis, by):
    count = lax.axis_size(axis)
    return lax.ppermute(x, axis, [(i, (i + by) % count) for i in range(count)])


def across(x, axis, k):
    count = lax.axis_size(axis)
    return lax.ppermute(x, axis, [(i, i ^ k) for i in range(count)])


def diagonal(x):
    lines, pairs = lax.axis_size("mesh"), lax.axis_size("sub")
    moves = [(m * pairs + p, (m ^ 1) * pairs + (p ^ 1)) for m in range(lines) for p in range(pairs)]
    return lax.ppermute(x, ("mesh", "sub"), moves)


def paired_sums(messages, lines, strip, narrow, width, hid, node_terms):
    send, keep, *outs = messages
    order = range(lines - 1, 0, -1)
    block = shape((strip + TAIL, hid), bf16)
    pair = across(send, "sub", 1)
    out_terms = {k: across(outs[k], "mesh", k) for k in order}
    line = call(turn_kernel, [block] * lines, pair, keep)[::-1]
    line_terms = {k: across(line[k], "mesh", k) for k in order}
    out_send, out_keep = call(
        line_kernel,
        [shape((narrow, hid), bf16)] * 2,
        *[out_terms[k] for k in order], outs[0],
        flops=10**10,
    )
    node_part = node_terms(out_terms[3], out_terms[1], pair)
    own, tail = call(
        own_kernel,
        [shape((strip + narrow, hid), bf16), shape((TAIL, hid), f32)],
        *[line_terms[k] for k in (2, 3, 1)], line[0], out_keep, across(out_send, "sub", 1),
        flops=10**8,
    )
    mine = {k: across(own, "mesh", k) for k in order}
    mine[0] = own
    theirs = {0: across(own, "sub", 1), 1: diagonal(own)}
    theirs |= {k: across(mine[k], "sub", 1) for k in (3, 2)}
    wholes = [shape((width, hid), f32), shape((width, hid), f32), shape((hid, width), f32)]

    def placed(which, *before):
        count = len(which)
        return call(
            functools.partial(place_kernel, which), wholes,
            *[mine[k] for k in which], *[theirs[k] for k in which], *before,
            specs=[VMEM] * (2 * count) + [HBM] * len(before),
            out_specs=[HBM] * 3,
            scratch=[
                pltpu.VMEM((count, strip, hid), f32), pltpu.VMEM((count, strip, hid), f32),
                pltpu.VMEM((count, narrow, width), f32), pltpu.SemaphoreType.DMA((3 * count,)),
            ],
            input_output_aliases={2 * count + i: i for i in range(len(before))},
        )

    grads = placed((2,), *placed((0,1,3)))
    return (*grads, tail), node_part


def shards(
    node_state,
    send_rows,
    edge_src,
    edge_dst,
    block_count,
    w_src,
    w_dst,
    hidden_bias,
    w_out,
    norm_gain,
    cotangent,
):
    rows, width = node_state.shape
    hid = w_src.shape[1]
    halo = send_rows.shape[2]
    edges = edge_src.shape[0]
    peers = lax.axis_size("mesh") * lax.axis_size("sub")
    merged = lax.axis_size("sub") == 2
    total_rows = 2 * width + (width // hid) * hid
    chunk = -(-total_rows // (peers * 16)) * 16

    piece = [halo, halo, 2 * halo] if merged else [halo] * 4
    routes = [("mesh", 1), ("mesh", -1), ("sub", 1)] + ([] if merged else [("sub", -1)])
    n_halo = len(piece)

    def in_hbm(x):
        return pltpu.with_memory_space_constraint(x, pltpu.HBM)

    bias = hidden_bias.reshape(1, hid)
    operands = [node_state, send_rows, w_src, w_dst, w_out, bias]
    node, send, packed, *outgoing = call(
        send_kernel,
        [
            shape((rows, width), bf16),
            shape(send_rows.shape, jnp.int32),
            shape((3 * width + TAIL, hid), bf16),
        ]
        + [shape((n, width), bf16) for n in piece],
        *[in_hbm(x) for x in operands],
        specs=[HBM] * len(operands),
        scratch=[pltpu.VMEM((1, hid), f32), pltpu.SemaphoreType.DMA((5 + width // hid,))],
    )
    arrived = [shifted(x, axis, by) for x, (axis, by) in zip(outgoing, routes)]

    other = shifted(packed, "lat", 1)

    fetched = [
        edge_src.reshape(1, edges), edge_dst.reshape(1, edges), block_count,
        norm_gain.reshape(1, width), cotangent,
    ]
    pre, pick, collect, spread, scatter, gain, cot = call(
        local_kernel,
        [
            shape((edges, 2 * hid), f32),
            shape((edges, 4 * halo), bf16),
            shape((rows, edges), bf16),
            shape((edges, rows), bf16),
            shape((rows + 4 * halo, edges), bf16),
            shape((1, width), f32),
            shape((rows, width), bf16),
        ],
        node, packed, other, *[in_hbm(x) for x in fetched],
        specs=[VMEM] * 3 + [HBM] * len(fetched),
        scratch=[
            pltpu.SMEM(block_count.shape, jnp.int32),
            pltpu.VMEM((1, edges), jnp.int32),
            pltpu.VMEM((1, edges), jnp.int32),
            pltpu.SemaphoreType.DMA((N_FETCHED,)),
        ],
    )


    lines = lax.axis_size("mesh")
    paired = merged and lines == 4
    if paired:
        strip = width // lines
        narrow = hid // lines
        rows_of = (width + TAIL + 2 * halo, width + TAIL)
        message_shapes = [shape((n, hid), bf16) for n in rows_of]
        message_shapes += [shape((narrow + k % 2 * (halo // 2), width), bf16) for k in range(lines)]
    else:
        message_shapes = [shape((peers, chunk + TAIL, hid), bf16)]
        message_shapes += [shape((n, hid), bf16) for n in piece]
    normed, local, target, *messages = call(
        functools.partial(edge_kernel, (peers, chunk, n_halo, paired)),
        [shape((rows, width), f32), shape((rows, hid), f32), shape((rows, hid), bf16)]
        + message_shapes,
        node, pre, pick, collect, spread, scatter, packed, other, gain, cot, *arrived,
        scratch=[
            pltpu.VMEM((hid, width), bf16),
            pltpu.VMEM((2 * halo, hid), bf16),
        ],
    )

    def node_terms(*returned):
        return call(
            paired_node_kernel if paired else node_kernel,
            shape((rows, width), bf16),
            send, local, target, packed, *returned,
        )

    if paired:
        (src_grad, dst_grad, out_grad, tail), node_part = paired_sums(
            messages, lines, strip, narrow, width, hid, node_terms
        )
    else:
        node_part = node_terms(
            *[shifted(x, axis, -by) for x, (axis, by) in zip(messages[1:], routes)]
        )
        exchanged = lax.all_to_all(messages[0], ("mesh", "sub"), 0, 0)
        reduced, bias_grad, gain_grad = call(
            functools.partial(sum_kernel, chunk),
            [shape((peers, chunk, hid), bf16), shape((1, hid), f32), shape((1, width), f32)],
            exchanged,
        )
        gathered = lax.all_to_all(reduced, ("mesh", "sub"), 0, 0)
        src_grad, dst_grad, out_grad = call(
            unpack_kernel,
            [shape((width, hid), f32), shape((width, hid), f32), shape((hid, width), f32)],
            gathered.reshape(peers * chunk, hid),
        )
    finished = [shape((rows, width), f32), shape((rows, width), bf16)]
    ends = [cot, node, gain, normed, node_part, shifted(node_part, "lat", 1)]
    if paired:
        node_grad, updated, bias_grad, gain_grad = call(
            finish_kernel, finished + [shape((1, hid), f32), shape((1, width), f32)], *ends, tail
        )
    else:
        node_grad, updated = call(finish_kernel, finished, *ends)
    return (
        updated, node_grad, src_grad, dst_grad, out_grad,
        bias_grad.reshape(hid), gain_grad.reshape(width),
    )


def solution(mesh):
    nodes = P(("parts", "mesh", "sub"), None)
    slots = P(("parts", "mesh", "sub"))
    in_specs = (
        nodes,
        P(("parts", "mesh", "sub"), None, None),
        slots,
        slots,
        slots,
        P(None, "lat"),
        P(None, "lat"),
        P("lat"),
        P("lat", None),
        P(),
        nodes,
    )
    out_specs = (
        nodes,
        nodes,
        P("parts", "lat"),
        P("parts", "lat"),
        P(("parts", "lat"), None),
        P(("parts", "lat")),
        P("parts"),
    )
    return jax.shard_map(shards, mesh=mesh, in_specs=in_specs, out_specs=out_specs, check_vma=False)
```

```python
import functools

import jax
import jax.numpy as jnp
from jax import lax
from jax.experimental import pallas as pl
from jax.experimental.pallas import tpu as pltpu
from jax.sharding import PartitionSpec as P

BLOCK = 128
EPSILON = 1e-05
TAIL = 16
N_FETCHED = 5
VMEM_LIMIT = 24 * 1024 * 1024

f32 = jnp.float32
bf16 = jnp.bfloat16

NN = (((1,), (0,)), ((), ()))
NT = (((1,), (1,)), ((), ()))
TN = (((0,), (0,)), ((), ()))


def dot(a, b, dims=NN):
    return lax.dot_general(a, b, dims, preferred_element_type=f32)


def iota(shape, dim):
    return lax.broadcasted_iota(jnp.int32, shape, dim)


def one_hot(condition):
    return jnp.where(condition, 1.0, 0.0).astype(bf16)


def split(x):
    high = x.astype(bf16)
    return high, (x - high.astype(f32)).astype(bf16)


def columns_of(row, lanes):
    return jnp.transpose(jnp.broadcast_to(row, (lanes, row.shape[1])))


def usable_row(count_ref, edges):
    lane = iota((1, BLOCK), 1)
    parts = [lane < count_ref[b] for b in range(edges // BLOCK)]
    return jnp.concatenate([jnp.where(p, 1, 0) for p in parts], axis=1)


def usable_columns(count_ref, edges, lanes):
    sub = iota((BLOCK, lanes), 0)
    return jnp.concatenate(
        [jnp.where(sub < count_ref[b], 1, 0) for b in range(edges // BLOCK)], axis=0
    )


def fetch(sems, *pairs):
    copies = [pltpu.make_async_copy(a, b, sems.at[i]) for i, (a, b) in enumerate(pairs)]
    for copy in copies:
        copy.start()
    return copies


def send_kernel(
    node_hbm, send_hbm, w_src_hbm, w_dst_hbm, w_out_hbm, bias_hbm,
    node_ref, send_ref, packed_ref, *rest,
):
    *out_refs, bias_ref, sems = rest
    hid = packed_ref.shape[1]
    width = w_src_hbm.shape[0]
    pairs = [(node_hbm, node_ref), (send_hbm, send_ref), (bias_hbm, bias_ref)]
    pairs += [(w_src_hbm, packed_ref.at[pl.ds(0, width)]), (w_dst_hbm, packed_ref.at[pl.ds(width, width)])]
    for k in range(width // hid):
        target = packed_ref.at[pl.ds(2 * width + k * hid, hid)]
        pairs.append((w_out_hbm.at[:, pl.ds(k * hid, hid)], target))
    copies = fetch(sems, *pairs)
    copies[0].wait()
    copies[1].wait()
    node = node_ref[...]
    rows = node.shape[0]
    halo = send_ref.shape[2]
    pieces = []
    for d in range(4):
        pick = one_hot(iota((rows, halo), 0) == send_ref[0, d : d + 1, :])
        pieces.append(dot(pick, node, TN).astype(bf16))
    out_refs[0][...] = pieces[0]
    out_refs[1][...] = pieces[1]
    if len(out_refs) == 3:
        out_refs[2][0:halo, :] = pieces[2]
        out_refs[2][halo:, :] = pieces[3]
    else:
        out_refs[2][...] = pieces[2]
        out_refs[3][...] = pieces[3]
    copies[2].wait()
    bias = bias_ref[...]
    parts = []
    for _ in range(3):
        parts.append(bias.astype(bf16).astype(f32))
        bias = bias - parts[-1]
    parts.append(jnp.zeros((TAIL - 3, hid), f32))
    packed_ref[packed_ref.shape[0] - TAIL :, :] = jnp.concatenate(parts, axis=0).astype(bf16)
    for copy in copies[3:]:
        copy.wait()


def unpacked(ref, width):
    hid = ref.shape[1]
    w_out = [ref[at : at + hid, :] for at in range(2 * width, 3 * width, hid)]
    tail = ref[ref.shape[0] - TAIL :, :].astype(f32)
    bias = tail[0:1] + tail[1:2] + tail[2:3]
    return ref[0:width, :], ref[width : 2 * width, :], jnp.concatenate(w_out, axis=1), bias


def local_kernel(node_ref, packed_ref, other_ref, *refs):
    ins, refs = refs[:N_FETCHED], refs[N_FETCHED:]
    pre_ref, pick_ref, collect_ref, spread_ref, scatter_ref, *refs = refs
    gain_ref, cot_ref, count_ref, src_ref, dst_ref, sems = refs
    copies = fetch(sems, *zip(ins, (src_ref, dst_ref, count_ref, gain_ref, cot_ref)))
    node = node_ref[...]
    rows, width = node.shape
    w_src, w_dst, _, bias = unpacked(packed_ref, width)
    w_src_other, w_dst_other, _, bias_other = unpacked(other_ref, width)
    projected = dot(node, jnp.concatenate([w_src, w_src_other, w_dst, w_dst_other], axis=1))
    both = projected.shape[1] // 2
    projected = jnp.concatenate([projected[:, :both], projected[:, both:]], axis=0)
    high, low = split(projected)
    for copy in copies:
        copy.wait()
    edges = src_ref.shape[1]
    scatter_ref[...] = one_hot(iota(scatter_ref.shape, 0) == src_ref[...])
    used = usable_row(count_ref, edges) > 0
    collect_ref[...] = one_hot((iota((rows, edges), 0) == dst_ref[...]) & used)
    source = columns_of(src_ref[...], 128)
    target = columns_of(dst_ref[...], 128)
    lane = iota(source.shape, 1)
    used = usable_columns(count_ref, edges, 128) > 0
    near = one_hot(source == lane)
    pick_ref[...] = one_hot(source == lane + rows)
    spread_ref[...] = one_hot((target == lane) & used)
    ends = jnp.concatenate([near, one_hot(target == lane)], axis=1)
    pre_ref[...] = dot(ends, high) + dot(ends, low) + jnp.concatenate([bias, bias_other], axis=1)


def twice(x):
    return jnp.concatenate([x, x], axis=1)


def stacked(x):
    return jnp.concatenate(split(x), axis=0)


def edge_kernel(
    geometry,
    node_ref, pre_ref, pick_ref, collect_ref, spread_ref, scatter_ref, packed_ref, other_ref, gain_ref, cot_ref,
    *rest,
):
    peers, chunk, n_halo, paired = geometry
    *rest, out_scratch, back_scratch = rest
    halo_refs = rest[:n_halo]
    normed_ref, local_ref, target_ref, *message_refs = rest[n_halo:]
    node = node_ref[...]
    rows, width = node.shape
    hid = packed_ref.shape[1]
    halo_rows = jnp.concatenate([r[...] for r in halo_refs], axis=0)
    w_src, _, w_out, _ = unpacked(packed_ref, width)
    w_src_other, _, w_out_other, _ = unpacked(other_ref, width)

    far = stacked(dot(halo_rows, jnp.concatenate([w_src, w_src_other], axis=1)))
    pre = pre_ref[...] + dot(twice(pick_ref[...]), far)
    sig = 0.5 + 0.5 * jnp.tanh(0.5 * pre)
    hidden = dot(collect_ref[...], (pre * sig).astype(bf16))
    pre, sig = pre[:, :hid], sig[:, :hid]
    factor = sig * (1.0 + pre * (1.0 - sig))
    parts = []
    for at, w in ((0, w_out), (hid, w_out_other)):
        high, low = split(hidden[:, at : at + hid])
        parts.append(dot(high, w) + dot(low, w))
    hidden_low = hidden[:, :hid].astype(bf16)
    aggregate = parts[0] + parts[1]

    center = aggregate - jnp.mean(aggregate, axis=1, keepdims=True)
    variance = jnp.mean(center * center, axis=1, keepdims=True)
    inverse = lax.rsqrt(variance + EPSILON)
    normed = center * inverse
    gain = gain_ref[...]
    upstream = cot_ref[...].astype(f32)
    scaled = upstream * gain
    agg_grad = inverse * (
        scaled
        - jnp.mean(scaled, axis=1, keepdims=True)
        - normed * jnp.mean(scaled * normed, axis=1, keepdims=True)
    )
    agg_grad = agg_grad.astype(bf16)
    normed_ref[...] = normed
    gain_part = jnp.sum(upstream * normed, axis=0, keepdims=True)

    act_grad = dot(twice(spread_ref[...]), stacked(dot(agg_grad, w_out, NT)))
    pre_grad = (act_grad * factor).astype(bf16)

    table = jnp.concatenate([node, halo_rows], axis=0)
    by_source = dot(scatter_ref[...], pre_grad)
    by_target = dot(collect_ref[...], pre_grad)
    local_ref[...] = by_source[:rows]
    by_target_low = by_target.astype(bf16)
    by_source_low = by_source.astype(bf16)
    target_ref[...] = by_target_low

    bias_part = jnp.sum(by_target, axis=0, keepdims=True)
    src_part = dot(table, by_source_low, TN).astype(bf16)
    dst_part = dot(node, by_target_low, TN).astype(bf16)
    out_part = dot(hidden_low, agg_grad, TN).astype(bf16)
    vectors = [bias_part] + [gain_part[:, at : at + hid] for at in range(0, width, hid)]
    tail = tail_of(vectors)
    back = by_source_low[rows:]

    if paired:
        send_ref, keep_ref, *out_refs = message_refs
        sub = lax.axis_index("sub")
        mesh = lax.axis_index("mesh")
        lines = len(out_refs)
        halo = back.shape[0] // 4
        first = sub == 0
        strip = width // lines
        chosen = ((send_ref, dst_part, src_part), (keep_ref, src_part, dst_part))
        for ref, when_first, otherwise in chosen:
            value = jnp.where(first, when_first, otherwise)
            for j in range(lines):
                start = pl.multiple_of((lines - 1 - (mesh ^ j)) * strip, strip)
                ref[pl.ds(start, strip), :] = value[j * strip : (j + 1) * strip]
            ref[width : width + TAIL, :] = tail
        send_ref[width + TAIL :, :] = back[2 * halo :]
        back_scratch[...] = back[: 2 * halo]
        out_scratch[...] = out_part
        strip = hid // len(out_refs)
        for k, ref in enumerate(out_refs):
            start = pl.multiple_of((mesh ^ k) * strip, strip)
            ref[0:strip, :] = out_scratch[pl.ds(start, strip), :]
            if k % 2 == 1:
                slot = (mesh + (k // 2) + 1) % 2
                start = pl.multiple_of(slot * halo, halo)
                rows_back = back_scratch[pl.ds(start, halo), :]
                ref[strip:, 0:hid] = rows_back[: halo // 2]
                ref[strip:, hid:] = rows_back[halo // 2 :]
        return

    message_ref, *back_refs = message_refs
    at = 0
    for ref in back_refs:
        ref[...] = back[at : at + ref.shape[0]]
        at += ref.shape[0]
    blocks = [src_part, dst_part]
    for at in range(0, width, hid):
        blocks.append(out_part[:, at : at + hid])
    done = 0
    for block in blocks:
        at = 0
        while at < block.shape[0]:
            peer, offset = divmod(done, chunk)
            take = min(chunk - offset, block.shape[0] - at)
            message_ref[peer, offset : offset + take, :] = block[at : at + take]
            at += take
            done += take
    while done < peers * chunk:
        peer, offset = divmod(done, chunk)
        take = chunk - offset
        message_ref[peer, offset : offset + take, :] = jnp.zeros((take, hid), bf16)
        done += take
    for peer in range(peers):
        message_ref[peer, chunk:, :] = tail


def tail_of(vectors):
    tail = []
    for v in vectors:
        high = v.astype(bf16).astype(f32)
        tail += [high, v - high]
    tail.append(jnp.zeros((TAIL - len(tail), vectors[0].shape[1]), f32))
    return jnp.concatenate(tail, axis=0).astype(bf16)


def tree(terms):
    while len(terms) > 1:
        terms = [terms[i] + terms[i + 1] for i in range(0, len(terms), 2)]
    return terms[0]


def turn_kernel(arrived_ref, keep_ref, *refs):
    full = keep_ref.shape[0]
    total = keep_ref[...].astype(f32) + arrived_ref[0:full, :].astype(f32)
    rows = full - TAIL
    strip = rows // len(refs)
    tail = total[rows:]
    tail = tail_of([tail[at : at + 1] + tail[at + 1 : at + 2] for at in range(0, 6, 2)])
    for k, ref in enumerate(refs):
        ref[0:strip, :] = total[k * strip : (k + 1) * strip].astype(bf16)
        ref[strip:, :] = tail


def line_kernel(*refs):
    *terms, send_ref, keep_ref = refs
    rows, hid = keep_ref.shape
    total = tree([r[0:rows, :].astype(f32) for r in terms])
    first = lax.axis_index("sub") == 0
    left, right = total[:, :hid], total[:, hid:]
    send_ref[...] = jnp.where(first, right, left).astype(bf16)
    keep_ref[...] = jnp.where(first, left, right).astype(bf16)


def own_kernel(*refs):
    *terms, out_keep_ref, out_arrived_ref, own_ref, tail_ref = refs
    total = tree([r[...].astype(f32) for r in terms])
    strip = own_ref.shape[0] - out_keep_ref.shape[0]
    own_ref[0:strip, :] = total[:strip].astype(bf16)
    own_ref[strip:, :] = (out_keep_ref[...].astype(f32) + out_arrived_ref[...].astype(f32)).astype(bf16)
    tail_ref[...] = total[strip:]


def write_vectors(tail, bias_ref, gain_ref):
    bias_ref[...] = tail[0:1] + tail[1:2]
    hid = tail.shape[1]
    for k in range(gain_ref.shape[1] // hid):
        gain_ref[:, k * hid : (k + 1) * hid] = tail[2 + 2 * k : 3 + 2 * k] + tail[3 + 2 * k : 4 + 2 * k]


def place_kernel(which, *refs):
    count = len(which)
    src_hbm, dst_hbm, out_hbm, src_ref, dst_ref, out_ref, sems = refs[-7:]
    first = lax.axis_index("sub") == 0
    mesh = lax.axis_index("mesh")
    strip, hid = src_ref.shape[1:]
    narrow = out_ref.shape[1]
    copies = []

    def put(ref, hbm, at, rows):
        start = pl.multiple_of((mesh ^ which[at]) * rows, rows)
        copies.append(pltpu.make_async_copy(ref.at[at], hbm.at[pl.ds(start, rows)], sems.at[len(copies)]))
        copies[-1].start()

    for at in range(count):
        mine, theirs = refs[at][...], refs[count + at][...]
        low = jnp.where(first, mine, theirs).astype(f32)
        high = jnp.where(first, theirs, mine).astype(f32)
        src_ref[at] = low[:strip]
        put(src_ref, src_hbm, at, strip)
        dst_ref[at] = high[:strip]
        put(dst_ref, dst_hbm, at, strip)
        out_ref[at, :, 0:hid] = low[strip:]
        out_ref[at, :, hid:] = high[strip:]
        put(out_ref, out_hbm, at, narrow)
    for copy in copies:
        copy.wait()


def sum_kernel(chunk, arrived_ref, out_ref, bias_ref, gain_ref):
    peers = arrived_ref.shape[0]
    total = arrived_ref[0].astype(f32)
    for peer in range(1, peers):
        total += arrived_ref[peer].astype(f32)
    low = total[:chunk].astype(bf16)
    for peer in range(peers):
        out_ref[peer] = low
    tail = total[chunk:]
    write_vectors(tail, bias_ref, gain_ref)


def unpack_kernel(arrived_ref, src_ref, dst_ref, out_ref):
    hid = src_ref.shape[1]
    rows = src_ref.shape[0]
    src_ref[...] = arrived_ref[0:rows, :].astype(f32)
    dst_ref[...] = arrived_ref[rows : 2 * rows, :].astype(f32)
    at = 2 * rows
    for k in range(out_ref.shape[1] // hid):
        out_ref[:, k * hid : (k + 1) * hid] = arrived_ref[at : at + out_ref.shape[0], :].astype(f32)
        at += out_ref.shape[0]


def node_part(send_ref, local_ref, target_ref, packed_ref, returned, out_ref):
    rows = local_ref.shape[0]
    halo = send_ref.shape[2]
    picks = [one_hot(iota((rows, halo), 0) == send_ref[0, d : d + 1, :]) for d in range(4)]
    total = local_ref[...] + dot(jnp.concatenate(picks, axis=1), jnp.concatenate(returned, axis=0))
    w_src, w_dst, _, _ = unpacked(packed_ref, out_ref.shape[1])
    out_ref[...] = (dot(total.astype(bf16), w_src, NT) + dot(target_ref[...], w_dst, NT)).astype(bf16)


def node_kernel(send_ref, local_ref, target_ref, packed_ref, *rest):
    *back_refs, out_ref = rest
    returned = [r[...] for r in back_refs]
    node_part(send_ref, local_ref, target_ref, packed_ref, returned, out_ref)


def paired_node_kernel(
    send_ref, local_ref, target_ref, packed_ref, three_ref, one_ref, pair_ref, out_ref
):
    even = lax.axis_index("mesh") % 2 == 0
    halo = send_ref.shape[2]
    hid = local_ref.shape[1]
    at = one_ref.shape[0] - halo // 2
    one, three = [
        jnp.concatenate([r[at:, :hid], r[at:, hid:]], axis=0) for r in (one_ref, three_ref)
    ]
    returned = [
        jnp.where(even, one, three), jnp.where(even, three, one), pair_ref[pair_ref.shape[0] - 2 * halo :, :]
    ]
    node_part(send_ref, local_ref, target_ref, packed_ref, returned, out_ref)


def finish_kernel(cot_ref, node_ref, gain_ref, normed_ref, own_ref, other_ref, *rest):
    if len(rest) == 5:
        tail_ref, *rest, bias_out_ref, gain_out_ref = rest
        write_vectors(tail_ref[...], bias_out_ref, gain_out_ref)
    grad_ref, updated_ref = rest
    grad_ref[...] = cot_ref[...].astype(f32) + (
        own_ref[...].astype(f32) + other_ref[...].astype(f32)
    )
    updated_ref[...] = (node_ref[...].astype(f32) + gain_ref[...] * normed_ref[...]).astype(bf16)


VMEM = pl.BlockSpec(memory_space=pltpu.VMEM)
SMEM = pl.BlockSpec(memory_space=pltpu.SMEM)
HBM = pl.BlockSpec(memory_space=pltpu.HBM)


def shape(dims, dtype):
    return jax.ShapeDtypeStruct(dims, dtype)


def call(kernel, outs, *args, specs=None, out_specs=None, flops=10**8, scratch=(), **options):
    return pl.pallas_call(
        kernel,
        out_shape=outs,
        in_specs=specs or [VMEM] * len(args),
        out_specs=out_specs or jax.tree.map(lambda _: VMEM, outs),
        scratch_shapes=scratch,
        **options,
        compiler_params=pltpu.CompilerParams(vmem_limit_bytes=VMEM_LIMIT),
        cost_estimate=pl.CostEstimate(flops=flops, bytes_accessed=10**6, transcendentals=0),
    )(*args)


def shifted(x, axis, by):
    count = lax.axis_size(axis)
    return lax.ppermute(x, axis, [(i, (i + by) % count) for i in range(count)])


def across(x, axis, k):
    count = lax.axis_size(axis)
    return lax.ppermute(x, axis, [(i, i ^ k) for i in range(count)])


def diagonal(x):
    lines, pairs = lax.axis_size("mesh"), lax.axis_size("sub")
    moves = [(m * pairs + p, (m ^ 1) * pairs + (p ^ 1)) for m in range(lines) for p in range(pairs)]
    return lax.ppermute(x, ("mesh", "sub"), moves)


def paired_sums(messages, lines, strip, narrow, width, hid, node_terms):
    send, keep, *outs = messages
    order = range(lines - 1, 0, -1)
    block = shape((strip + TAIL, hid), bf16)
    pair = across(send, "sub", 1)
    out_terms = {k: across(outs[k], "mesh", k) for k in order}
    line = call(turn_kernel, [block] * lines, pair, keep)[::-1]
    line_terms = {k: across(line[k], "mesh", k) for k in order}
    out_send, out_keep = call(
        line_kernel,
        [shape((narrow, hid), bf16)] * 2,
        *[out_terms[k] for k in order], outs[0],
        flops=10**10,
    )
    node_part = node_terms(out_terms[3], out_terms[1], pair)
    own, tail = call(
        own_kernel,
        [shape((strip + narrow, hid), bf16), shape((TAIL, hid), f32)],
        *[line_terms[k] for k in (2, 3, 1)], line[0], out_keep, across(out_send, "sub", 1),
        flops=10**8,
    )
    mine = {k: across(own, "mesh", k) for k in order}
    mine[0] = own
    theirs = {0: across(own, "sub", 1), 1: diagonal(own)}
    theirs |= {k: across(mine[k], "sub", 1) for k in (3, 2)}
    wholes = [shape((width, hid), f32), shape((width, hid), f32), shape((hid, width), f32)]

    def placed(which, *before):
        count = len(which)
        return call(
            functools.partial(place_kernel, which), wholes,
            *[mine[k] for k in which], *[theirs[k] for k in which], *before,
            specs=[VMEM] * (2 * count) + [HBM] * len(before),
            out_specs=[HBM] * 3,
            scratch=[
                pltpu.VMEM((count, strip, hid), f32), pltpu.VMEM((count, strip, hid), f32),
                pltpu.VMEM((count, narrow, width), f32), pltpu.SemaphoreType.DMA((3 * count,)),
            ],
            input_output_aliases={2 * count + i: i for i in range(len(before))},
        )

    grads = placed((3,), *placed((0, 1, 2)))
    return (*grads, tail), node_part


def shards(
    node_state,
    send_rows,
    edge_src,
    edge_dst,
    block_count,
    w_src,
    w_dst,
    hidden_bias,
    w_out,
    norm_gain,
    cotangent,
):
    rows, width = node_state.shape
    hid = w_src.shape[1]
    halo = send_rows.shape[2]
    edges = edge_src.shape[0]
    peers = lax.axis_size("mesh") * lax.axis_size("sub")
    merged = lax.axis_size("sub") == 2
    total_rows = 2 * width + (width // hid) * hid
    chunk = -(-total_rows // (peers * 16)) * 16

    piece = [halo, halo, 2 * halo] if merged else [halo] * 4
    routes = [("mesh", 1), ("mesh", -1), ("sub", 1)] + ([] if merged else [("sub", -1)])
    n_halo = len(piece)

    def in_hbm(x):
        return pltpu.with_memory_space_constraint(x, pltpu.HBM)

    bias = hidden_bias.reshape(1, hid)
    operands = [node_state, send_rows, w_src, w_dst, w_out, bias]
    node, send, packed, *outgoing = call(
        send_kernel,
        [
            shape((rows, width), bf16),
            shape(send_rows.shape, jnp.int32),
            shape((3 * width + TAIL, hid), bf16),
        ]
        + [shape((n, width), bf16) for n in piece],
        *[in_hbm(x) for x in operands],
        specs=[HBM] * len(operands),
        scratch=[pltpu.VMEM((1, hid), f32), pltpu.SemaphoreType.DMA((5 + width // hid,))],
    )
    arrived = [shifted(x, axis, by) for x, (axis, by) in zip(outgoing, routes)]

    other = shifted(packed, "lat", 1)

    fetched = [
        edge_src.reshape(1, edges), edge_dst.reshape(1, edges), block_count,
        norm_gain.reshape(1, width), cotangent,
    ]
    pre, pick, collect, spread, scatter, gain, cot = call(
        local_kernel,
        [
            shape((edges, 2 * hid), f32),
            shape((edges, 4 * halo), bf16),
            shape((rows, edges), bf16),
            shape((edges, rows), bf16),
            shape((rows + 4 * halo, edges), bf16),
            shape((1, width), f32),
            shape((rows, width), bf16),
        ],
        node, packed, other, *[in_hbm(x) for x in fetched],
        specs=[VMEM] * 3 + [HBM] * len(fetched),
        scratch=[
            pltpu.SMEM(block_count.shape, jnp.int32),
            pltpu.VMEM((1, edges), jnp.int32),
            pltpu.VMEM((1, edges), jnp.int32),
            pltpu.SemaphoreType.DMA((N_FETCHED,)),
        ],
    )


    lines = lax.axis_size("mesh")
    paired = merged and lines == 4
    if paired:
        strip = width // lines
        narrow = hid // lines
        rows_of = (width + TAIL + 2 * halo, width + TAIL)
        message_shapes = [shape((n, hid), bf16) for n in rows_of]
        message_shapes += [shape((narrow + k % 2 * (halo // 2), width), bf16) for k in range(lines)]
    else:
        message_shapes = [shape((peers, chunk + TAIL, hid), bf16)]
        message_shapes += [shape((n, hid), bf16) for n in piece]
    normed, local, target, *messages = call(
        functools.partial(edge_kernel, (peers, chunk, n_halo, paired)),
        [shape((rows, width), f32), shape((rows, hid), f32), shape((rows, hid), bf16)]
        + message_shapes,
        node, pre, pick, collect, spread, scatter, packed, other, gain, cot, *arrived,
        scratch=[
            pltpu.VMEM((hid, width), bf16),
            pltpu.VMEM((2 * halo, hid), bf16),
        ],
    )

    def node_terms(*returned):
        return call(
            paired_node_kernel if paired else node_kernel,
            shape((rows, width), bf16),
            send, local, target, packed, *returned,
        )

    if paired:
        (src_grad, dst_grad, out_grad, tail), node_part = paired_sums(
            messages, lines, strip, narrow, width, hid, node_terms
        )
    else:
        node_part = node_terms(
            *[shifted(x, axis, -by) for x, (axis, by) in zip(messages[1:], routes)]
        )
        exchanged = lax.all_to_all(messages[0], ("mesh", "sub"), 0, 0)
        reduced, bias_grad, gain_grad = call(
            functools.partial(sum_kernel, chunk),
            [shape((peers, chunk, hid), bf16), shape((1, hid), f32), shape((1, width), f32)],
            exchanged,
        )
        gathered = lax.all_to_all(reduced, ("mesh", "sub"), 0, 0)
        src_grad, dst_grad, out_grad = call(
            unpack_kernel,
            [shape((width, hid), f32), shape((width, hid), f32), shape((hid, width), f32)],
            gathered.reshape(peers * chunk, hid),
        )
    finished = [shape((rows, width), f32), shape((rows, width), bf16)]
    ends = [cot, node, gain, normed, node_part, shifted(node_part, "lat", 1)]
    if paired:
        node_grad, updated, bias_grad, gain_grad = call(
            finish_kernel, finished + [shape((1, hid), f32), shape((1, width), f32)], *ends, tail
        )
    else:
        node_grad, updated = call(finish_kernel, finished, *ends)
    return (
        updated, node_grad, src_grad, dst_grad, out_grad,
        bias_grad.reshape(hid), gain_grad.reshape(width),
    )


def solution(mesh):
    nodes = P(("parts", "mesh", "sub"), None)
    slots = P(("parts", "mesh", "sub"))
    in_specs = (
        nodes,
        P(("parts", "mesh", "sub"), None, None),
        slots,
        slots,
        slots,
        P(None, "lat"),
        P(None, "lat"),
        P("lat"),
        P("lat", None),
        P(),
        nodes,
    )
    out_specs = (
        nodes,
        nodes,
        P("parts", "lat"),
        P("parts", "lat"),
        P(("parts", "lat"), None),
        P(("parts", "lat")),
        P("parts"),
    )
    return jax.shard_map(shards, mesh=mesh, in_specs=in_specs, out_specs=out_specs, check_vma=False)
```
